32 devices in a mesh: shard: 4 (over y, core), rep: 8 (over z, x).
Axes of the slice: x: 2, y: 2, z: 4, core: 2. Of those that a mesh axis runs over, the one named last changes fastest.
Arguments:
- layer_input: bfloat16 [256, 197, 768], P(('shard', 'rep')), may hold values from -6 to 6
- out_cotangent: bfloat16 [256, 197, 768], P(('shard', 'rep')), may hold values from -6 to 6
- attention_params: float32 [2363136], P('shard'), may hold values from -2 to 2.5
- attention_moments: float32 [2, 2363136], P(None, 'shard'), may hold values from -0.2 to 0.2, as said below
- feedforward_params: float32 [4723968], P('shard'), may hold values from -2 to 2.5
- feedforward_moments: float32 [2, 4723968], P(None, 'shard'), may hold values from -0.2 to 0.2, as said below
- step_count: int32 [1], replicated, may hold values from 1 to 20
Outputs:
- layer_output: bfloat16 [256, 197, 768], P(('shard', 'rep'))
- input_grad: bfloat16 [256, 197, 768], P(('shard', 'rep'))
- attention_grad: float32 [2363136], P('shard')
- feedforward_grad: float32 [4723968], P('shard')
- attention_change: float32 [2363136], P('shard')
- attention_moments_new: float32 [2, 2363136], P(None, 'shard')
- feedforward_change: float32 [4723968], P('shard')
- feedforward_moments_new: float32 [2, 4723968], P(None, 'shard')
The draws below stay inside these ranges and needn't reach their ends.
Inputs may be any that keep to these rules, and one draw needn't show every extreme that they name: `attention_moments`: row 1, the second moments, is positive. `feedforward_moments`: row 1, the second moments, is positive.
All inputs are finite; a program needn't handle non-finite values.
Results may differ from the reference program's by a relative error of at most 0.017.
The reference program's roundings to bfloat16 on the way count: a program that leaves them out, or rounds other values in their place, can miss the bound.
Values may be sent and summed in bfloat16 or wider, within the bound.
No kernel may reach another device: no remote copies, remote signals or barrier semaphores. Data moves between devices by JAX's collectives and lax.ppermute only.
A program may use at most 384 MiB of HBM per device.

```python
import math
import jax
import jax.numpy as jnp
from jax import lax

D = 768
HEADS = 12
HEAD_DIM = 64
FF = 3072
SEQ = 197
IMG_DEV = 8
IMAGES = 256
ATTN_FLAT = 2363136
FFN_FLAT = 4723968
N_SHARD = 4
N_REP = 8


def clipped_normal(key, count):
    return jnp.clip(jax.random.normal(key, (count,), jnp.float32), -4.0, 4.0)


def gain_entries(key, count):
    return jnp.exp(0.35 * jnp.clip(jax.random.normal(key, (count,), jnp.float32), -2.5, 2.5))


def moment_rows(key, count):
    keys_list = jax.random.split(key, 2)
    first_row = 0.05 * clipped_normal(keys_list[0], count)
    second_row = jnp.exp(jax.random.uniform(keys_list[1], (count,), jnp.float32, math.log(1e-05), math.log(0.0002)))
    return jnp.stack([first_row, second_row])


def draw_attention_params(key, part):
    keys_list = jax.random.split(key, 7)
    base = clipped_normal(keys_list[2], D * 3 * D).reshape(D, 3, D) * D ** (-0.5)
    return jnp.concatenate([gain_entries(keys_list[0], D), 0.4 * clipped_normal(keys_list[1], D), base.reshape(-1), 0.4 * clipped_normal(keys_list[3], D), 0.4 * clipped_normal(keys_list[4], D), clipped_normal(keys_list[5], D * D) * (4.0 * D ** (-0.5)), 0.4 * clipped_normal(keys_list[6], D)])


def draw_feedforward_params(key, part):
    keys_list = jax.random.split(key, 6)
    return jnp.concatenate([gain_entries(keys_list[0], D), 0.4 * clipped_normal(keys_list[1], D), clipped_normal(keys_list[2], D * FF) * D ** (-0.5), 0.4 * clipped_normal(keys_list[3], FF), clipped_normal(keys_list[4], FF * D) * FF ** (-0.5), 0.4 * clipped_normal(keys_list[5], D)])


def draw_attention_moments(key, part):
    return moment_rows(jax.random.fold_in(key, 11), ATTN_FLAT)


def draw_feedforward_moments(key, part):
    return moment_rows(jax.random.fold_in(key, 23), FFN_FLAT)


def shard_levels(rng, shape, shards, smallest, high):
    loudness, own = 1.0, jax.random.fold_in(rng, 6)
    for dim, parts in shards:
        draws = jnp.exp(jax.random.uniform(jax.random.fold_in(own, dim), (parts,), jnp.float32, smallest / len(shards), high / len(shards)))
        loudness = loudness * jnp.repeat(draws, shape[dim] // parts).reshape([-1 if axis == dim else 1 for axis in range(len(shape))])
    return loudness


def scatter_about(own_key, shape, width, limit, cuts=(), kind=jnp.bfloat16):
    gain = shard_levels(own_key, shape, cuts, -0.22, 0.18) if cuts else 1.0
    result = jax.random.normal(own_key, shape, jnp.float32) * width * gain
    return jnp.minimum(jnp.maximum(result, -limit), limit).astype(kind)


def setup_inputs(seed: int = 0) -> dict:
    streams_of = jax.random.split(jax.random.key(seed), 8)
    layer_input = scatter_about(streams_of[0], (IMAGES, SEQ, D), 1.0, 6.0, ((0, 32),))
    out_cotangent = scatter_about(streams_of[1], (IMAGES, SEQ, D), 1.0, 6.0, ((0, 32),))
    attention_params = draw_attention_params(jax.random.fold_in(streams_of[7], 71), 0)
    attention_moments = draw_attention_moments(jax.random.fold_in(streams_of[7], 71), 0)
    feedforward_params = draw_feedforward_params(jax.random.fold_in(streams_of[7], 71), 0)
    feedforward_moments = draw_feedforward_moments(jax.random.fold_in(streams_of[7], 71), 0)
    step_count = jax.random.randint(streams_of[6], (1,), 1, 21).astype(jnp.int32)
    return {"layer_input": layer_input, "out_cotangent": out_cotangent, "attention_params": attention_params, "attention_moments": attention_moments, "feedforward_params": feedforward_params, "feedforward_moments": feedforward_moments, "step_count": step_count}


ln_eps = 1e-06
beta_one = 0.9
beta_two = 0.999
adam_eps = 1e-08
rate_matrix = 0.01
rate_vector = 0.1
decay_matrix = 0.05
root_half = 0.7071067811865476
inv_root_tau = 0.3989422804014327

def product(form, left, right):
    return jnp.einsum(form, left.astype(jnp.float32), right.astype(jnp.float32))

def split_flat(flat_vec, lengths):
    starts = [0]
    for length in lengths:
        starts.append(starts[-1] + length)
    return [flat_vec[starts[position]:starts[position] + lengths[position]] for position in range(len(lengths))]

def attention_lengths(model_width):
    return [model_width, model_width, 3 * model_width * model_width, model_width, model_width, model_width * model_width, model_width]

def feedforward_lengths(model_width, hidden_width):
    return [model_width, model_width, model_width * hidden_width, hidden_width, hidden_width * model_width, model_width]

def matrix_mask(lengths, matrix_slots, positions):
    starts = [0]
    for length in lengths:
        starts.append(starts[-1] + length)
    is_matrix = jnp.zeros(positions.shape, bool)
    for matrix_slot in matrix_slots:
        inside = (positions >= starts[matrix_slot]) & (positions < starts[matrix_slot] + lengths[matrix_slot])
        is_matrix = is_matrix | inside
    return is_matrix

def unpack_weights(attention_flat, feedforward_flat, model_width, hidden_width):
    gain_one, shift_one, qkv_flat, query_bias, value_bias, proj_flat, proj_bias = split_flat(attention_flat, attention_lengths(model_width))
    gain_two, shift_two, up_flat, up_bias, down_flat, down_bias = split_flat(feedforward_flat, feedforward_lengths(model_width, hidden_width))
    return (gain_one, shift_one, qkv_flat.reshape(model_width, 3 * model_width), query_bias, value_bias, proj_flat.reshape(model_width, model_width), proj_bias, gain_two, shift_two, up_flat.reshape(model_width, hidden_width), up_bias, down_flat.reshape(hidden_width, model_width), down_bias)

def norm_forward(values, gain_vec, shift_vec):
    center = values - lax.optimization_barrier(jnp.mean(values, axis=-1, keepdims=True))
    spread = lax.rsqrt(lax.optimization_barrier(jnp.mean(center * center, axis=-1, keepdims=True)) + ln_eps)
    normed = center * spread
    return (normed * gain_vec.astype(jnp.float32) + shift_vec.astype(jnp.float32), normed, spread)

def norm_backward(grad_out, normed, spread, gain_vec):
    grad_normed = grad_out * gain_vec.astype(jnp.float32)
    return spread * (grad_normed - lax.optimization_barrier(jnp.mean(grad_normed, axis=-1, keepdims=True)) - normed * lax.optimization_barrier(jnp.mean(grad_normed * normed, axis=-1, keepdims=True)))

def gelu_value(values):
    return 0.5 * values * (1.0 + lax.erf(values * root_half))

def gelu_slope(values):
    return 0.5 * (1.0 + lax.erf(values * root_half)) + values * jnp.exp(-0.5 * values * values) * inv_root_tau

def forward_pass(inputs, weights):
    gain_one, shift_one, qkv_weight, query_bias, value_bias, proj_weight, proj_bias, gain_two, shift_two, up_weight, up_bias, down_weight, down_bias = weights
    image_count, seq_len, model_width = inputs.shape
    token_rows = inputs.reshape(image_count * seq_len, model_width).astype(jnp.float32)
    normed_out, normed_one, spread_one = norm_forward(token_rows, gain_one, shift_one)
    first_in = normed_out.astype(jnp.bfloat16)
    zero_bias = jnp.zeros(query_bias.shape, jnp.float32)
    qkv_bias = jnp.concatenate([query_bias.astype(jnp.float32), zero_bias, value_bias.astype(jnp.float32)])
    projected = jnp.dot(first_in, qkv_weight, preferred_element_type=jnp.float32) + qkv_bias
    projected = projected.astype(jnp.bfloat16).reshape(image_count, seq_len, 3, HEADS, HEAD_DIM)
    query_part = projected[:, :, 0]
    key_part = projected[:, :, 1]
    value_part = projected[:, :, 2]
    scores = product('bqhd,bkhd->bhqk', query_part, key_part) * HEAD_DIM ** (-0.5)
    row_top = lax.optimization_barrier(jnp.max(scores, axis=-1, keepdims=True))
    log_total = row_top + jnp.log(lax.optimization_barrier(jnp.sum(jnp.exp(scores - row_top), axis=-1, keepdims=True)))
    attn_probs = jnp.exp(scores - log_total).astype(jnp.bfloat16)
    attended = product('bhqk,bkhd->bqhd', attn_probs, value_part).astype(jnp.bfloat16)
    attended = attended.reshape(image_count * seq_len, model_width)
    hidden_rows = token_rows + jnp.dot(attended, proj_weight, preferred_element_type=jnp.float32) + proj_bias.astype(jnp.float32)
    second_out, normed_two, spread_two = norm_forward(hidden_rows, gain_two, shift_two)
    second_in = second_out.astype(jnp.bfloat16)
    pre_act = jnp.dot(second_in, up_weight, preferred_element_type=jnp.float32) + up_bias.astype(jnp.float32)
    act_low = gelu_value(pre_act).astype(jnp.bfloat16)
    result_rows = hidden_rows + jnp.dot(act_low, down_weight, preferred_element_type=jnp.float32) + down_bias.astype(jnp.float32)
    saved = (normed_one, spread_one, first_in, query_part, key_part, value_part, log_total, attended, normed_two, spread_two, second_in, pre_act, act_low)
    return (result_rows, saved)

def feedforward_backward(saved, cot_rows, weights):
    normed_one, spread_one, first_in, query_part, key_part, value_part, log_total, attended, normed_two, spread_two, second_in, pre_act, act_low = saved
    gain_one, shift_one, qkv_weight, query_bias, value_bias, proj_weight, proj_bias, gain_two, shift_two, up_weight, up_bias, down_weight, down_bias = weights
    cot_wide = cot_rows.astype(jnp.float32)
    grad_act = jnp.dot(cot_rows, down_weight.T, preferred_element_type=jnp.float32)
    grad_pre = grad_act * gelu_slope(pre_act)
    grad_pre_low = grad_pre.astype(jnp.bfloat16)
    grad_second = jnp.dot(grad_pre_low, up_weight.T, preferred_element_type=jnp.float32)
    grad_hidden = cot_wide + norm_backward(grad_second, normed_two, spread_two, gain_two)
    feed_grads = jnp.concatenate([lax.optimization_barrier(jnp.sum(grad_second * normed_two, axis=0)), lax.optimization_barrier(jnp.sum(grad_second, axis=0)), jnp.dot(second_in.T, grad_pre_low, preferred_element_type=jnp.float32).reshape(-1), lax.optimization_barrier(jnp.sum(grad_pre, axis=0)), jnp.dot(act_low.T, cot_rows, preferred_element_type=jnp.float32).reshape(-1), lax.optimization_barrier(jnp.sum(cot_wide, axis=0))])
    return (grad_hidden, feed_grads)

def attention_backward(saved, grad_hidden, weights):
    normed_one, spread_one, first_in, query_part, key_part, value_part, log_total, attended, normed_two, spread_two, second_in, pre_act, act_low = saved
    gain_one, shift_one, qkv_weight, query_bias, value_bias, proj_weight, proj_bias, gain_two, shift_two, up_weight, up_bias, down_weight, down_bias = weights
    image_count, seq_len = (query_part.shape[0], query_part.shape[1])
    token_count = image_count * seq_len
    model_width = HEADS * HEAD_DIM
    grad_hidden_low = grad_hidden.astype(jnp.bfloat16)
    grad_attended = jnp.dot(grad_hidden_low, proj_weight.T, preferred_element_type=jnp.float32).astype(jnp.bfloat16)
    grad_attended = grad_attended.reshape(image_count, seq_len, HEADS, HEAD_DIM)
    scores = product('bqhd,bkhd->bhqk', query_part, key_part) * HEAD_DIM ** (-0.5)
    probs_wide = jnp.exp(scores - log_total)
    attn_probs = probs_wide.astype(jnp.bfloat16)
    grad_values = product('bhqk,bqhd->bkhd', attn_probs, grad_attended)
    grad_probs = product('bqhd,bkhd->bhqk', grad_attended, value_part)
    row_delta = lax.optimization_barrier(jnp.sum(probs_wide * grad_probs, axis=-1, keepdims=True))
    grad_scores = (probs_wide * (grad_probs - row_delta) * HEAD_DIM ** (-0.5)).astype(jnp.bfloat16)
    grad_queries = product('bhqk,bkhd->bqhd', grad_scores, key_part)
    grad_keys = product('bhqk,bqhd->bkhd', grad_scores, query_part)
    grad_qkv = jnp.stack([grad_queries, grad_keys, grad_values], axis=2).astype(jnp.bfloat16)
    grad_qkv = grad_qkv.reshape(token_count, 3 * model_width)
    grad_first = jnp.dot(grad_qkv, qkv_weight.T, preferred_element_type=jnp.float32)
    grad_rows = grad_hidden + norm_backward(grad_first, normed_one, spread_one, gain_one)
    attn_grads = jnp.concatenate([lax.optimization_barrier(jnp.sum(grad_first * normed_one, axis=0)), lax.optimization_barrier(jnp.sum(grad_first, axis=0)), jnp.dot(first_in.T, grad_qkv, preferred_element_type=jnp.float32).reshape(-1), lax.optimization_barrier(jnp.sum(grad_queries.reshape(token_count, model_width), axis=0)), lax.optimization_barrier(jnp.sum(grad_values.reshape(token_count, model_width), axis=0)), jnp.dot(attended.T, grad_hidden_low, preferred_element_type=jnp.float32).reshape(-1), lax.optimization_barrier(jnp.sum(grad_hidden, axis=0))])
    return (grad_rows, attn_grads)

def adam_change(params, moments, grads, step_count, lengths, matrix_slots, offset):
    positions = jnp.arange(params.shape[0], dtype=jnp.int32) + offset
    is_matrix = matrix_mask(lengths, matrix_slots, positions)
    step_wide = step_count[0].astype(jnp.float32)
    first_moment = beta_one * moments[0] + (1.0 - beta_one) * grads
    second_moment = beta_two * moments[1] + (1.0 - beta_two) * grads * grads
    first_hat = first_moment / (1.0 - jnp.power(beta_one, step_wide))
    second_hat = second_moment / (1.0 - jnp.power(beta_two, step_wide))
    step_rate = jnp.where(is_matrix, rate_matrix, rate_vector)
    decay_rate = jnp.where(is_matrix, decay_matrix, 0.0)
    change = step_rate * (first_hat / (jnp.sqrt(second_hat) + adam_eps) + decay_rate * params)
    return (change, jnp.stack([first_moment, second_moment]))

def reference(layer_input, out_cotangent, attention_params, attention_moments, feedforward_params, feedforward_moments, step_count):
    weights = unpack_weights(attention_params.astype(jnp.bfloat16), feedforward_params.astype(jnp.bfloat16), D, FF)
    block_count = N_SHARD * N_REP
    input_blocks = layer_input.reshape(block_count, IMG_DEV, SEQ, D)
    cot_blocks = out_cotangent.reshape(block_count, IMG_DEV, SEQ, D)

    def one_block(carry, block_pair):
        attention_sum, feedforward_sum = carry
        inputs, cotangent = block_pair
        result_rows, saved = forward_pass(inputs, weights)
        cot_rows = cotangent.reshape(IMG_DEV * SEQ, D)
        grad_hidden, feed_grads = feedforward_backward(saved, cot_rows, weights)
        grad_rows, attn_grads = attention_backward(saved, grad_hidden, weights)
        outputs = (result_rows.astype(jnp.bfloat16).reshape(inputs.shape), grad_rows.astype(jnp.bfloat16).reshape(inputs.shape))
        return ((attention_sum + attn_grads, feedforward_sum + feed_grads), outputs)
    start_carry = (jnp.zeros(attention_params.shape, jnp.float32), jnp.zeros(feedforward_params.shape, jnp.float32))
    (attention_sum, feedforward_sum), (result_blocks, grad_blocks) = lax.scan(one_block, start_carry, (input_blocks, cot_blocks))
    attention_grad = attention_sum / IMAGES
    feedforward_grad = feedforward_sum / IMAGES
    zero_offset = jnp.zeros((), jnp.int32)
    attention_change, attention_moments_new = adam_change(attention_params, attention_moments, attention_grad, step_count, attention_lengths(D), [2, 5], zero_offset)
    feedforward_change, feedforward_moments_new = adam_change(feedforward_params, feedforward_moments, feedforward_grad, step_count, feedforward_lengths(D, FF), [2, 4], zero_offset)
    layer_output = result_blocks.reshape(IMAGES, SEQ, D)
    input_grad = grad_blocks.reshape(IMAGES, SEQ, D)
    return (layer_output, input_grad, attention_grad, feedforward_grad, attention_change, attention_moments_new, feedforward_change, feedforward_moments_new)
```

```python
import functools

import jax
import jax.numpy as jnp
from jax import lax
from jax.experimental import pallas as pl
from jax.experimental.pallas import tpu as pltpu
from jax.sharding import PartitionSpec as P

D = 768
HEADS = 12
FF = 3072
T = 208

F32 = jnp.float32
BF = jnp.bfloat16

ln_eps = 1e-06
beta_one = 0.9
beta_two = 0.999
adam_eps = 1e-08
rate_matrix = 0.01
rate_vector = 0.1
decay_matrix = 0.05
root_half = 0.7071067811865476
inv_root_tau = 0.3989422804014327

MB = 1 << 20
LANES = 128
MARGIN = 8

ATTN_START = (12, 5, -3, 2)
FEED_START = (12, 2, 15, 5)


def attn_parts(share):
    if share < 3:
        return [(16, 256 * part, 6 * part, 18) for part in range(3)]
    return [(48, 0, 0, 6)]


def feed_parts(share):
    if share < 2:
        return [(24, 768 * j + 384 * h, 12 * h + 6 * j, 24) for j in range(2) for h in range(2)]
    return [(96, 0, 0, 6)]


ATTN_EXTRA = (
    [(0, 0, 12), (12, 4602, 14)],
    [(25, 0, 5), (30, 4613, 3)],
    [(33, 0, 15), (48, 4605, 11)],
    [(58, 0, 2), (60, 4610, 6)],
)
FEED_EXTRA = (
    [(0, 0, 12), (12, 9204, 23)],
    [(34, 0, 2), (36, 9218, 9)],
    [(45, 0, 15), (60, 9225, 2)],
    [(61, 0, 5), (66, 9221, 6)],
)
ATTN_PUT = (
    [(0, 0, 12)],
    [(25, 0, 5), (30, 4613, 3)],
    [(48, 4605, 12)],
    [(58, 0, 2), (60, 4610, 6)],
)
FEED_PUT = (
    [(0, 0, 12)],
    [(34, 0, 2), (36, 9218, 9)],
    [(45, 0, 15)],
    [(61, 0, 5), (66, 9221, 6)],
)
EXTRA = 72


class Block:
    def __init__(self, start, parts, extra, put, rows, matrices):
        self.start, self.parts, self.extra, self.put = start, parts, extra, put
        self.rows = rows
        self.matrices = matrices


ATTN = Block(ATTN_START, attn_parts, ATTN_EXTRA, ATTN_PUT, 768, ((1536, 1771008), (1772544, 2362368)))
FEED = Block(FEED_START, feed_parts, FEED_EXTRA, FEED_PUT, 1536, ((1536, 2360832), (2363904, 4723200)))


def params(limit=56):
    return pltpu.CompilerParams(vmem_limit_bytes=limit * MB)


def dot(a, b):
    return lax.dot_general(a, b, (((1,), (0,)), ((), ())), preferred_element_type=F32)


def dot_nt(a, b):
    return lax.dot_general(a, b, (((1,), (1,)), ((), ())), preferred_element_type=F32)


def dot_tn(a, b):
    return lax.dot_general(a, b, (((0,), (0,)), ((), ())), preferred_element_type=F32)


def normed_of(values):
    center = values - jnp.mean(values, axis=-1, keepdims=True)
    spread = lax.rsqrt(jnp.mean(center * center, axis=-1, keepdims=True) + ln_eps)
    return center * spread, spread


def whole(array):
    rank = len(array.shape)
    return pl.BlockSpec(array.shape, lambda *i: (0,) * rank, pipeline_mode=pl.Buffered(1))


def rows_of(count, width):
    return pl.BlockSpec((count, width), lambda i: (i, 0))


SMEM = pl.BlockSpec(memory_space=pltpu.SMEM)


def sds(shape, dtype):
    return jax.ShapeDtypeStruct(shape, dtype)


CHUNK = 512


def prep_kernel(block, steps, shard_ref, flat_ref, box_ref, extra_ref, held):
    step = pl.program_id(0)
    held[pl.ds(pl.multiple_of(MARGIN + CHUNK * step, 8), CHUNK), :] = flat_ref[...].reshape(CHUNK, LANES)

    @pl.when(step == steps - 1)
    def _():
        low = lax.broadcasted_iota(jnp.int32, (8, LANES), 1) < 64
        low_one = lax.broadcasted_iota(jnp.int32, (1, LANES), 1) < 64
        extra_ref[...] = jnp.zeros_like(extra_ref)
        for share in range(4):

            @pl.when(shard_ref[0] == share)
            def _(share=share):
                odd = share % 2 == 1

                def tile(first, stride):
                    here = held[pl.ds(first, 8, stride=stride), :]
                    if not odd:
                        return here
                    ahead = held[pl.ds(first - 1, 8, stride=stride), :]
                    return jnp.where(low, pltpu.roll(ahead, 64, 1), pltpu.roll(here, 64, 1))

                for groups, box_row, flat_row, stride in block.parts(share):
                    base = MARGIN + block.start[share] + flat_row

                    def body(group, carry, base=base, box_row=box_row, stride=stride):
                        for j in range(6):
                            first = base + 16 * stride * group + j
                            both = jnp.concatenate([tile(first, stride), tile(first + 8 * stride, stride)], axis=0)
                            at = pl.multiple_of(box_row + 16 * group, 16)
                            box_ref[pl.ds(at, 16), LANES * j : LANES * j + LANES] = both.astype(BF)
                        return carry

                    lax.fori_loop(0, groups, body, 0)
                count = flat_rows(block, share)
                for to, row, length in block.extra[share]:
                    for k in range(length):
                        at = MARGIN + row + k
                        value = held[at : at + 1, :]
                        if odd:
                            ahead = held[at - 1 : at, :]
                            value = jnp.where(low_one, pltpu.roll(ahead, 64, 1), pltpu.roll(value, 64, 1))
                            if row + k == 0:
                                value = jnp.where(low_one, 0.0, value)
                        elif row + k == count:
                            value = jnp.where(low_one, value, 0.0)
                        extra_ref[to + k : to + k + 1, :] = value.astype(BF).astype(F32)


def flat_rows(block, share):
    return 4615 if block is ATTN else 9226


def prep(block, flat, shard):
    steps = -(-flat.shape[0] // (CHUNK * LANES))
    return pl.pallas_call(
        functools.partial(prep_kernel, block, steps),
        grid=(steps,),
        in_specs=[SMEM, pl.BlockSpec((CHUNK * LANES,), lambda i: (i,))],
        out_specs=[
            pl.BlockSpec((block.rows, D), lambda i: (0, 0)),
            pl.BlockSpec((EXTRA, LANES), lambda i: (0, 0)),
        ],
        out_shape=[sds((block.rows, D), BF), sds((EXTRA, LANES), F32)],
        scratch_shapes=[pltpu.VMEM((MARGIN + CHUNK * steps + MARGIN, LANES), F32)],
        compiler_params=params(),
    )(shard, flat)


def spread_row(extra_ref, first, count):
    return jnp.concatenate([extra_ref[first + k : first + k + 1, :] for k in range(count)], axis=1)


def patch_row(ref, row, values):
    at = row // 16 * 16
    rows = lax.broadcasted_iota(jnp.int32, (16, values.shape[1]), 0)
    old = ref[at : at + 16, :].astype(F32)
    ref[at : at + 16, :] = jnp.where(rows == row - at, values, old).astype(BF)


def assemble_attn(shard_ref, extra_ref, a0, a1, a2, a3, qkv_ref, proj_ref, vec_ref, bias_ref, sems):
    shard = shard_ref[0]
    for wait in (False, True):
        for k, box in enumerate((a0, a1, a2, a3)):
            share = jnp.bitwise_xor(shard, k)

            @pl.when(share == 3)
            def _(box=box, k=k):
                copy = pltpu.make_async_copy(box, proj_ref, sems.at[k, 0])
                copy.wait() if wait else copy.start()

            @pl.when(share != 3)
            def _(box=box, k=k, share=share):
                for part in range(3):
                    copy = pltpu.make_async_copy(
                        box.at[pl.ds(256 * part, 256), :],
                        qkv_ref.at[pl.ds(pl.multiple_of(768 * part + 256 * share, 256), 256), :],
                        sems.at[k, part],
                    )
                    copy.wait() if wait else copy.start()

    for part in range(3):
        patch_row(qkv_ref, 768 * part + 255, spread_row(extra_ref, 12 + 6 * part, 6))
        patch_row(qkv_ref, 768 * part + 512, spread_row(extra_ref, 30 + 6 * part, 6))
    vec_ref[...] = jnp.zeros_like(vec_ref)
    for row, first in enumerate((0, 6, 60, EXTRA + 0, EXTRA + 6)):
        vec_ref[row : row + 1, :] = spread_row(extra_ref, first, 6)
    bias_ref[...] = jnp.zeros_like(bias_ref)
    bias_ref[0:1, 0:768] = spread_row(extra_ref, 48, 6)
    bias_ref[0:1, 1536:2304] = spread_row(extra_ref, 54, 6)


def call_assemble_attn(shard, extra, boxes):
    anywhere = pl.BlockSpec(memory_space=pl.ANY)
    return pl.pallas_call(
        assemble_attn,
        in_specs=[SMEM, pl.BlockSpec(memory_space=pltpu.VMEM)] + [anywhere] * 4,
        out_specs=[pl.BlockSpec(memory_space=pltpu.VMEM)] * 4,
        out_shape=[sds((2304, D), BF), sds((D, D), BF), sds((8, D), F32), sds((8, 2304), F32)],
        scratch_shapes=[pltpu.SemaphoreType.DMA((4, 3))],
        compiler_params=params(),
    )(shard, extra, *boxes)


def assemble_feed(shard_ref, extra_ref, a0, a1, a2, a3, up_ref, down_ref, ub_ref, db_ref, sems):
    shard = shard_ref[0]
    for wait in (False, True):
        for k, box in enumerate((a0, a1, a2, a3)):
            share = jnp.bitwise_xor(shard, k)

            @pl.when(share >= 2)
            def _(box=box, k=k, share=share):
                at = pl.multiple_of(1536 * (share - 2), 512)
                copy = pltpu.make_async_copy(box, down_ref.at[pl.ds(at, 1536), :], sems.at[k, 0])
                copy.wait() if wait else copy.start()

            @pl.when(share < 2)
            def _(box=box, k=k, share=share):
                for j in range(2):
                    for h in range(2):
                        copy = pltpu.make_async_copy(
                            box.at[pl.ds(768 * j + 384 * h, 384), :],
                            up_ref.at[pl.ds(pl.multiple_of(768 * (2 * h + j) + 384 * share, 128), 384), :],
                            sems.at[k, 2 * j + h],
                        )
                        copy.wait() if wait else copy.start()

    for part in range(4):
        patch_row(up_ref, 768 * part + 383, spread_row(extra_ref, EXTRA + 12 + 6 * part, 6))
    patch_row(down_ref, 1535, spread_row(extra_ref, EXTRA + 60, 6))
    ub_ref[...] = jnp.zeros_like(ub_ref)
    ub_ref[0:1, :] = spread_row(extra_ref, EXTRA + 36, 24)
    db_ref[...] = jnp.zeros_like(db_ref)
    db_ref[0:1, :] = spread_row(extra_ref, EXTRA + 66, 6)


def call_assemble_feed(shard, extra, boxes):
    anywhere = pl.BlockSpec(memory_space=pl.ANY)
    return pl.pallas_call(
        assemble_feed,
        in_specs=[SMEM, pl.BlockSpec(memory_space=pltpu.VMEM)] + [anywhere] * 4,
        out_specs=[pl.BlockSpec(memory_space=pltpu.VMEM)] * 4,
        out_shape=[sds((FF, D), BF), sds((FF, D), BF), sds((8, FF), F32), sds((8, D), F32)],
        scratch_shapes=[pltpu.SemaphoreType.DMA((4, 4))],
        compiler_params=params(),
    )(shard, extra, *boxes)


def attn_forward(seq, x_ref, vec_ref, bias_ref, qkv_w, proj_w, first_ref, qkv_ref, log_ref, att_ref, hid_ref, second_ref):
    x = x_ref[...].astype(F32)
    normed, _ = normed_of(x)
    first = (normed * vec_ref[0:1, :] + vec_ref[1:2, :]).astype(BF)
    first_ref[...] = first
    for part in range(3):
        cols = slice(768 * part, 768 * part + 768)
        qkv_ref[:, cols] = (dot(first, qkv_w[cols, :]) + bias_ref[0:1, cols]).astype(BF)
    low = lax.broadcasted_iota(jnp.int32, (T, LANES), 1) < 64
    real = lax.broadcasted_iota(jnp.int32, (T, T), 0) < seq
    for pair in range(HEADS // 2):
        at = LANES * pair
        q = qkv_ref[:, at : at + LANES] * jnp.asarray(0.125, BF)
        k = qkv_ref[:, 768 + at : 768 + at + LANES]
        v = qkv_ref[:, 1536 + at : 1536 + at + LANES]
        outs = []
        for half in range(2):
            own = low if half == 0 else ~low
            scores = dot_nt(k, jnp.where(own, q, jnp.zeros_like(q)))
            scores = jnp.where(real, scores, -1e30)
            top = jnp.max(scores, axis=0, keepdims=True)
            weight = jnp.exp(scores - top)
            total = jnp.sum(weight, axis=0, keepdims=True)
            head = 2 * pair + half
            log_ref[0, head : head + 1, :] = top + jnp.log(total)
            outs.append(dot_tn((weight * (1.0 / total)).astype(BF), v))
        att_ref[:, at : at + LANES] = jnp.where(low, outs[0], outs[1]).astype(BF)
    hidden = x + dot(att_ref[...], proj_w[...]) + vec_ref[2:3, :]
    hid_ref[...] = hidden
    normed, _ = normed_of(hidden)
    second_ref[...] = (normed * vec_ref[3:4, :] + vec_ref[4:5, :]).astype(BF)


def call_attn_forward(seq, x, vec, bias, qkv_w, proj_w):
    rows = x.shape[0]
    images = rows // T
    return pl.pallas_call(
        functools.partial(attn_forward, seq),
        grid=(images,),
        in_specs=[rows_of(T, D), whole(vec), whole(bias), whole(qkv_w), whole(proj_w)],
        out_specs=[
            rows_of(T, D),
            rows_of(T, 2304),
            pl.BlockSpec((1, HEADS, T), lambda i: (i, 0, 0)),
            rows_of(T, D),
            rows_of(T, D),
            rows_of(T, D),
        ],
        out_shape=[
            sds((rows, D), BF),
            sds((rows, 2304), BF),
            sds((images, HEADS, T), F32),
            sds((rows, D), BF),
            sds((rows, D), F32),
            sds((rows, D), BF),
        ],
        compiler_params=params(),
    )(x, vec, bias, qkv_w, proj_w)


def feed(seq, width, second_ref, cot_ref, hid_ref, up_w, ub_ref, down_w, db_ref, act_ref, pre_ref, out_ref, gs_ref, sum_ref, cot_sum):
    second = second_ref[...]
    cot = cot_ref[...]
    result = hid_ref[...] + db_ref[0:1, :]
    grad_second = jnp.zeros_like(result)

    @pl.when(pl.program_id(0) == 0)
    def _():
        sum_ref[...] = jnp.zeros_like(sum_ref)
        cot_sum[...] = jnp.zeros_like(cot_sum)

    cot_sum[0:1, :] += jnp.sum(cot.astype(F32), axis=0, keepdims=True)
    for part in range(FF // width):
        cols = slice(width * part, width * part + width)
        pre = dot(second, up_w[cols, :]) + ub_ref[0:1, cols]
        grad_act = dot_nt(cot, down_w[cols, :])
        half = 0.5 * (1.0 + lax.erf(pre * root_half))
        act = (pre * half).astype(BF)
        grad_pre = grad_act * (half + pre * jnp.exp(-0.5 * pre * pre) * inv_root_tau)
        low = grad_pre.astype(BF)
        act_ref[:, cols] = act
        pre_ref[:, cols] = low
        sum_ref[0:1, cols] += jnp.sum(grad_pre, axis=0, keepdims=True)
        result = result + dot(act, down_w[cols, :])
        grad_second = grad_second + dot_nt(low, up_w[cols, :])
    for image in range(result.shape[0] // T):
        out_ref[image] = result[T * image : T * image + seq].astype(BF)
    gs_ref[...] = grad_second


def call_feed(seq, second, cot, hidden, up_w, ub, down_w, db):
    rows = second.shape[0]
    images = rows // T
    step = 2 if images % 2 == 0 else 1
    tall = step * T
    return pl.pallas_call(
        functools.partial(feed, seq, D),
        grid=(images // step,),
        in_specs=[rows_of(tall, D)] * 3 + [whole(up_w), whole(ub), whole(down_w), whole(db)],
        out_specs=[
            rows_of(tall, FF),
            rows_of(tall, FF),
            pl.BlockSpec((step, seq, D), lambda i: (i, 0, 0)),
            rows_of(tall, D),
            pl.BlockSpec((8, FF), lambda i: (0, 0)),
            pl.BlockSpec((8, D), lambda i: (0, 0)),
        ],
        out_shape=[
            sds((rows, FF), BF),
            sds((rows, FF), BF),
            sds((images, seq, D), BF),
            sds((rows, D), F32),
            sds((8, FF), F32),
            sds((8, D), F32),
        ],
        compiler_params=params(),
    )(second, cot, hidden, up_w, ub, down_w, db)


def over_tokens(left_ref, right_ref, out_ref):
    out_ref[...] = dot_tn(left_ref[...], right_ref[...]).astype(out_ref.dtype).reshape(out_ref.shape)


def call_over_tokens(left, right, grid, left_block, right_block, out_shape, out_block):
    count = left.shape[0]
    return pl.pallas_call(
        over_tokens,
        grid=grid,
        in_specs=[
            pl.BlockSpec((count, left_block[0]), left_block[1]),
            pl.BlockSpec((count, right_block[0]), right_block[1]),
        ],
        out_specs=pl.BlockSpec(*out_block),
        out_shape=sds(out_shape, BF),
        compiler_params=params(),
    )(left, right)


def attn_backward(seq, gs_ref, hid_ref, cot_ref, log_ref, qkv_ref, vec_ref, proj_w, grad_ref, low_ref, gh_ref, sum_ref, head_sum, ga_ref):
    @pl.when(pl.program_id(0) == 0)
    def _():
        sum_ref[...] = jnp.zeros_like(sum_ref)
        head_sum[...] = jnp.zeros_like(head_sum)

    gs = gs_ref[...]
    normed, spread = normed_of(hid_ref[...])
    gn = gs * vec_ref[3:4, :]
    gh = cot_ref[...].astype(F32) + spread * (
        gn - jnp.mean(gn, axis=-1, keepdims=True) - normed * jnp.mean(gn * normed, axis=-1, keepdims=True)
    )
    sum_ref[0:1, :] += jnp.sum(gs * normed, axis=0, keepdims=True)
    sum_ref[1:2, :] += jnp.sum(gs, axis=0, keepdims=True)
    sum_ref[2:3, :] += jnp.sum(gh, axis=0, keepdims=True)
    gh_ref[...] = gh
    gh_low = gh.astype(BF)
    low_ref[...] = gh_low
    ga_ref[...] = dot_nt(gh_low, proj_w[...]).astype(BF)
    low = lax.broadcasted_iota(jnp.int32, (T, LANES), 1) < 64
    real = lax.broadcasted_iota(jnp.int32, (T, T), 0) < seq
    eighth = jnp.asarray(0.125, BF)
    for pair in range(HEADS // 2):
        at = LANES * pair
        cols = slice(at, at + LANES)
        q = qkv_ref[:, cols] * eighth
        k = qkv_ref[:, 768 + at : 768 + at + LANES]
        v = qkv_ref[:, 1536 + at : 1536 + at + LANES]
        k_small = k * eighth
        grad_out = ga_ref[:, cols]
        zero = jnp.zeros_like(q)
        grads = ([], [], [])
        for half in range(2):
            own = low if half == 0 else ~low
            head = 2 * pair + half
            scores = dot_nt(k, jnp.where(own, q, zero))
            probs = jnp.where(real, jnp.exp(scores - log_ref[0, head : head + 1, :]), 0.0)
            grads[2].append(dot(probs.astype(BF), grad_out))
            grad_probs = dot_nt(v, jnp.where(own, grad_out, zero))
            delta = jnp.sum(probs * grad_probs, axis=0, keepdims=True)
            grad_scores = (probs * (grad_probs - delta)).astype(BF)
            grads[1].append(dot(grad_scores, q))
            grads[0].append(dot_tn(grad_scores, k_small))
        for part in range(3):
            grad = jnp.where(low, grads[part][0], grads[part][1])
            if part != 1:
                row = part // 2
                head_sum[row : row + 1, cols] += jnp.sum(grad, axis=0, keepdims=True)
            grad_ref[:, 768 * part + at : 768 * part + at + LANES] = grad.astype(BF)


def call_attn_backward(seq, gs, hidden, cot, log_total, qkv, vec, proj_w):
    rows = gs.shape[0]
    small = pl.BlockSpec((8, D), lambda i: (0, 0))
    return pl.pallas_call(
        functools.partial(attn_backward, seq),
        grid=(rows // T,),
        in_specs=[rows_of(T, D)] * 3
        + [pl.BlockSpec((1, HEADS, T), lambda i: (i, 0, 0)), rows_of(T, 2304), whole(vec), whole(proj_w)],
        out_specs=[rows_of(T, 2304), rows_of(T, D), rows_of(T, D), small, small],
        out_shape=[sds((rows, 2304), BF), sds((rows, D), BF), sds((rows, D), F32), sds((8, D), F32), sds((8, D), F32)],
        scratch_shapes=[pltpu.VMEM((T, D), BF)],
        compiler_params=params(),
    )(gs, hidden, cot, log_total, qkv, vec, proj_w)


def input_backward(seq, grad_ref, gh_ref, x_ref, vec_ref, qkv_w, out_ref, sum_ref):
    @pl.when(pl.program_id(0) == 0)
    def _():
        sum_ref[...] = jnp.zeros_like(sum_ref)

    grad_first = dot_nt(grad_ref[:, 0:768], qkv_w[0:768, :])
    for part in range(1, 3):
        cols = slice(768 * part, 768 * part + 768)
        grad_first = grad_first + dot_nt(grad_ref[:, cols], qkv_w[cols, :])
    normed, spread = normed_of(x_ref[...].astype(F32))
    gn = grad_first * vec_ref[0:1, :]
    grad = gh_ref[...] + spread * (
        gn - jnp.mean(gn, axis=-1, keepdims=True) - normed * jnp.mean(gn * normed, axis=-1, keepdims=True)
    )
    sum_ref[0:1, :] += jnp.sum(grad_first * normed, axis=0, keepdims=True)
    sum_ref[1:2, :] += jnp.sum(grad_first, axis=0, keepdims=True)
    for image in range(grad.shape[0] // T):
        out_ref[image] = grad[T * image : T * image + seq].astype(BF)


def call_input_backward(seq, grad, gh, x, vec, qkv_w):
    rows = gh.shape[0]
    images = rows // T
    step = 2 if images % 2 == 0 else 1
    tall = step * T
    return pl.pallas_call(
        functools.partial(input_backward, seq),
        grid=(images // step,),
        in_specs=[rows_of(tall, 2304), rows_of(tall, D), rows_of(tall, D), whole(vec), whole(qkv_w)],
        out_specs=[pl.BlockSpec((step, seq, D), lambda i: (i, 0, 0)), pl.BlockSpec((8, D), lambda i: (0, 0))],
        out_shape=[sds((images, seq, D), BF), sds((8, D), F32)],
        compiler_params=params(),
    )(grad, gh, x, vec, qkv_w)


def put_row(out_ref, first, values):
    for k in range(values.shape[1] // LANES):
        out_ref[first + k : first + k + 1, :] = values[:, LANES * k : LANES * k + LANES]


def pack_attn(last_sum, back_sum, head_sum, qkv_grad, out_ref):
    out_ref[...] = jnp.zeros_like(out_ref)
    put_row(out_ref, 0, last_sum[0:1, :])
    put_row(out_ref, 6, last_sum[1:2, :])
    for part in range(3):
        at = 256 * part
        put_row(out_ref, 12 + 6 * part, qkv_grad[0, at + 240 : at + 256, :].astype(F32)[15:16])
        put_row(out_ref, 30 + 6 * part, qkv_grad[2, at : at + 16, :].astype(F32)[0:1])
    put_row(out_ref, 48, head_sum[0:1, :])
    put_row(out_ref, 54, head_sum[1:2, :])
    put_row(out_ref, 60, back_sum[2:3, :])


def pack_feed(back_sum, pre_sum, cot_sum, up0, up1, down1, out_ref):
    put_row(out_ref, 0, back_sum[0:1, :])
    put_row(out_ref, 6, back_sum[1:2, :])
    for j, up in enumerate((up0, up1)):
        for h in range(2):
            put_row(out_ref, 12 + 12 * h + 6 * j, up[0, 384 * h + 368 : 384 * h + 384, :].astype(F32)[15:16])
    put_row(out_ref, 36, pre_sum[0:1, :])
    put_row(out_ref, 60, down1[0, 752:768, :].astype(F32)[15:16])
    put_row(out_ref, 66, cot_sum[0:1, :])


def call_pack(kernel, *arrays):
    return pl.pallas_call(
        kernel,
        in_specs=[pl.BlockSpec(memory_space=pltpu.VMEM)] * len(arrays),
        out_specs=pl.BlockSpec(memory_space=pltpu.VMEM),
        out_shape=sds((EXTRA, LANES), F32),
        compiler_params=params(),
    )(*arrays)


def adam_kernel(block, share_size, scale, boxes, shard_ref, power_ref, extra_ref, *refs):
    box_refs = refs[:boxes]
    flat_ref, mom_ref, grad_ref, change_ref, new_ref, held = refs[boxes:]
    step = pl.program_id(0)

    @pl.when(step == 0)
    def _():
        for share in range(4):

            @pl.when(shard_ref[0] == share)
            def _(share=share):
                for groups, box_row, flat_row, stride in block.parts(share):
                    base = MARGIN + block.start[share] + flat_row
                    for index in range(boxes):
                        first = max(box_row, 768 * index)
                        end = min(box_row + 16 * groups, 768 * index + 768)
                        if first >= end:
                            continue

                        def body(group, carry, index=index, first=first, base=base, box_row=box_row, stride=stride):
                            row = pl.multiple_of(first - 768 * index + 16 * group, 16)
                            for j in range(6):
                                both = box_refs[index][pl.ds(row, 16), LANES * j : LANES * j + LANES].astype(F32)
                                at = base + stride * (first - box_row + 16 * group) + j
                                held[pl.ds(at, 8, stride=stride), :] = both[0:8]
                                held[pl.ds(at + 8 * stride, 8, stride=stride), :] = both[8:16]
                            return carry

                        lax.fori_loop(0, (end - first) // 16, body, 0)
                for source, row, length in block.put[share]:
                    held[MARGIN + row : MARGIN + row + length, :] = extra_ref[source : source + length, :]

    start = pl.multiple_of(MARGIN + CHUNK * step, 8)
    shard = shard_ref[0]
    low = lax.broadcasted_iota(jnp.int32, (CHUNK, LANES), 1) < 64
    here = held[pl.ds(start, CHUNK), :]
    after = held[pl.ds(start + 1, CHUNK), :]
    shifted = jnp.where(low, pltpu.roll(here, 64, 1), pltpu.roll(after, 64, 1))
    grad = jnp.where(shard % 2 == 1, shifted, here) * scale
    position = (
        shard * share_size
        + step * (CHUNK * LANES)
        + lax.broadcasted_iota(jnp.int32, (CHUNK, LANES), 0) * LANES
        + lax.broadcasted_iota(jnp.int32, (CHUNK, LANES), 1)
    )
    matrix = jnp.zeros((CHUNK, LANES), jnp.bool_)
    for first, end in block.matrices:
        matrix = matrix | ((position >= first) & (position < end))
    size = CHUNK * LANES
    p = flat_ref[...].reshape(CHUNK, LANES)
    m = beta_one * mom_ref[0, :].reshape(CHUNK, LANES) + (1.0 - beta_one) * grad
    s = beta_two * mom_ref[1, :].reshape(CHUNK, LANES) + (1.0 - beta_two) * grad * grad
    ratio = (m * power_ref[0]) / (jnp.sqrt(s * power_ref[1]) + adam_eps)
    change = jnp.where(matrix, rate_matrix, rate_vector) * (ratio + jnp.where(matrix, decay_matrix, 0.0) * p)
    grad_ref[...] = grad.reshape(size)
    change_ref[...] = change.reshape(size)
    new_ref[0, :] = m.reshape(size)
    new_ref[1, :] = s.reshape(size)


def adam(block, shard, powers, extra, boxes, flat, moments, scale):
    count = flat.shape[0]
    steps = -(-count // (CHUNK * LANES))
    line = pl.BlockSpec((CHUNK * LANES,), lambda i: (i,))
    two = pl.BlockSpec((2, CHUNK * LANES), lambda i: (0, i))
    return pl.pallas_call(
        functools.partial(adam_kernel, block, count, scale, len(boxes)),
        grid=(steps,),
        in_specs=[SMEM, SMEM, whole(extra)] + [whole(box) for box in boxes] + [line, two],
        out_specs=[line, line, two],
        out_shape=[sds((count,), F32), sds((count,), F32), sds((2, count), F32)],
        scratch_shapes=[pltpu.VMEM((MARGIN + CHUNK * steps + MARGIN, LANES), F32)],
        compiler_params=params(),
    )(shard, powers, extra, *boxes, flat, moments)


def swap(value, axis, bit):
    pairs = [(i, i ^ bit) for i in range(lax.axis_size(axis))]
    return lax.ppermute(value, axis, pairs)


def turn(value, axis, unit, distance):
    size = lax.axis_size(axis)
    return lax.ppermute(value, axis, [(i, (i + unit * distance) % size) for i in range(size)])


def pick(array, index, axis=0):
    return lax.dynamic_index_in_dim(array, index, axis, keepdims=False)


def reduce_share(pieces):
    shard = lax.axis_index("shard")
    core, side = shard % 2, shard // 2
    rep = lax.axis_index("rep")
    near, far = rep % 2, rep // 2
    count = lax.axis_size("rep") // 2
    rows = pieces[0].shape[0]
    on = core == 0
    other = jnp.stack([jnp.where(on, pieces[1], pieces[0]), jnp.where(on, pieces[3], pieces[2])])
    mine = jnp.stack([jnp.where(on, pieces[0], pieces[1]), jnp.where(on, pieces[2], pieces[3])])
    came = swap(other, "shard", 1)
    total = mine.astype(F32) + came.astype(F32)
    came = swap(pick(total, 1 - side).astype(BF), "shard", 2)
    total = pick(total, side) + came.astype(F32)
    halves = total.reshape(2, rows // 2, D)
    came = swap(pick(halves, 1 - near).astype(BF), "rep", 1)
    half = pick(halves, near) + came.astype(F32)
    parts = half.reshape(count, rows // 2 // count, D)
    arrived = [
        turn(pick(parts, (far + step) % count).astype(BF), "rep", 2, step) for step in range(1, count)
    ]
    part = pick(parts, far)
    for value in arrived:
        part = part + value.astype(F32)
    part = part.astype(BF)
    others = [turn(part, "rep", 2, step) for step in range(1, count)]
    full = jnp.zeros((count, rows // 2 // count, D), BF)
    for step, value in enumerate([part] + others):
        full = lax.dynamic_update_slice_in_dim(full, value[None], (far + count - step) % count, 0)
    half = full.reshape(rows // 2, D)
    came = swap(half, "rep", 1)
    first = near == 0
    return jnp.concatenate([jnp.where(first, half, came), jnp.where(first, came, half)], axis=0)


def reduce_all(value):
    value = value + swap(value, "shard", 1)
    value = value + swap(value, "shard", 2)
    bit = 1
    while bit < lax.axis_size("rep"):
        value = value + swap(value, "rep", bit)
        bit *= 2
    return value


def gather_boxes(box):
    across = swap(box, "shard", 2)
    return box, swap(box, "shard", 1), across, swap(across, "shard", 1)


def body(layer_input, out_cotangent, attention_params, attention_moments, feedforward_params, feedforward_moments, step_count):
    images, seq, _ = layer_input.shape
    image_total = images * lax.axis_size("shard") * lax.axis_size("rep")
    scale = 1.0 / image_total
    shard = lax.axis_index("shard").astype(jnp.int32).reshape(1)
    attn_box, attn_extra = prep(ATTN, attention_params, shard)
    feed_box, feed_extra = prep(FEED, feedforward_params, shard)
    extra = jnp.concatenate([attn_extra, feed_extra], axis=0)
    extra = extra + swap(extra, "shard", 1)
    extra = extra + swap(extra, "shard", 2)
    pad = ((0, 0), (0, T - seq), (0, 0))
    x = jnp.pad(layer_input, pad).reshape(images * T, D)
    cot = jnp.pad(out_cotangent, pad).reshape(images * T, D)
    qkv_w, proj_w, vec, bias = call_assemble_attn(shard, extra, gather_boxes(attn_box))
    first, qkv, log_total, attended, hidden, second = call_attn_forward(seq, x, vec, bias, qkv_w, proj_w)
    up_w, down_w, ub, db = call_assemble_feed(shard, extra, gather_boxes(feed_box))
    act, pre, layer_output, gs, pre_sum, cot_sum = call_feed(seq, second, cot, hidden, up_w, ub, down_w, db)
    feed_boxes, ups, downs = [], [], []
    for j in range(2):
        up = call_over_tokens(
            second, pre, (2, 2), (384, lambda s, h: (0, s)), (768, lambda s, h, j=j: (0, 2 * h + j)),
            (2, 768, D), ((1, 384, D), lambda s, h: (s, h, 0)),
        )
        down = call_over_tokens(
            act, cot, (2,), (768, lambda s, j=j: (0, 2 * s + j)), (768, lambda s: (0, 0)),
            (2, 768, D), ((1, 768, D), lambda s: (s, 0, 0)),
        )
        ups.append(up)
        downs.append(down)
        feed_boxes.append(reduce_share([up[0], up[1], down[0], down[1]]))
    qkv_grad, gh_low, gh, back_sum, head_sum = call_attn_backward(seq, gs, hidden, cot, log_total, qkv, vec, proj_w)
    proj_grad = call_over_tokens(
        attended, gh_low, (1,), (768, lambda i: (0, 0)), (768, lambda i: (0, 0)), (D, D), ((D, D), lambda i: (0, 0)),
    )
    weight_grad = call_over_tokens(
        first, qkv_grad, (3, 3), (256, lambda s, b: (0, s)), (768, lambda s, b: (0, b)),
        (3, 768, D), ((1, 256, D), lambda s, b: (s, b, 0)),
    )
    attn_total = reduce_share([weight_grad[0], weight_grad[1], weight_grad[2], proj_grad])
    input_grad, last_sum = call_input_backward(seq, qkv_grad, gh, x, vec, qkv_w)
    feed_sums = reduce_all(call_pack(pack_feed, back_sum, pre_sum, cot_sum, ups[0], ups[1], downs[1]))
    attn_sums = reduce_all(call_pack(pack_attn, last_sum, back_sum, head_sum, weight_grad))
    time = step_count[0].astype(F32)
    powers = jnp.stack([1.0 / (1.0 - jnp.power(beta_one, time)), 1.0 / (1.0 - jnp.power(beta_two, time))])
    feed_grad, feed_change, feed_new = adam(
        FEED, shard, powers, feed_sums, feed_boxes, feedforward_params, feedforward_moments, scale
    )
    attn_grad, attn_change, attn_new = adam(
        ATTN, shard, powers, attn_sums, [attn_total], attention_params, attention_moments, scale
    )
    return (layer_output, input_grad, attn_grad, feed_grad, attn_change, attn_new, feed_change, feed_new)


def solution(mesh):
    tokens = P(("shard", "rep"), None, None)
    in_specs = (tokens, tokens, P("shard"), P(None, "shard"), P("shard"), P(None, "shard"), P())
    out_specs = (tokens, tokens, P("shard"), P("shard"), P("shard"), P(None, "shard"), P("shard"), P(None, "shard"))
    return jax.shard_map(body, mesh=mesh, in_specs=in_specs, out_specs=out_specs, check_vma=False)
```

```python
import functools

import jax
import jax.numpy as jnp
from jax import lax
from jax.experimental import pallas as pl
from jax.experimental.pallas import tpu as pltpu
from jax.sharding import PartitionSpec as P

D = 768
HEADS = 12
FF = 3072
T = 208

F32 = jnp.float32
BF = jnp.bfloat16

ln_eps = 1e-06
beta_one = 0.9
beta_two = 0.999
adam_eps = 1e-08
rate_matrix = 0.01
rate_vector = 0.1
decay_matrix = 0.05
root_half = 0.7071067811865476
inv_root_tau = 0.3989422804014327

MB = 1 << 20
LANES = 128
MARGIN = 8

ATTN_START = (12, 5, -3, 2)
FEED_START = (12, 2, 15, 5)


def attn_parts(share):
    if share < 3:
        return [(0, 16, 256 * part, 6 * part, 18) for part in range(3)]
    return [(0, 48, 0, 0, 6)]


def feed_parts(share):
    if share < 2:
        return [(j, 24, 384 * h, 12 * h + 6 * j, 24) for j in range(2) for h in range(2)]
    return [(j, 48, 0, 4608 * j, 6) for j in range(2)]


def attn_grad_parts(share):
    if share < 3:
        return [
            (g, 8, 128 * part, 3 * u, 3, 18 * 128 * u + 6 * part + 3 * g, 18)
            for g in range(2)
            for part in range(3)
            for u in range(2)
        ]
    return [(g, 24, 0, 0, 6, 6 * 384 * g, 6) for g in range(2)]


def feed_grad_parts(share):
    return [(box, groups, row, 0, 6, flat, stride) for box, groups, row, flat, stride in feed_parts(share)]


ATTN_EXTRA = (
    [(0, 0, 12), (12, 4602, 14)],
    [(25, 0, 5), (30, 4613, 3)],
    [(33, 0, 15), (48, 4605, 11)],
    [(58, 0, 2), (60, 4610, 6)],
)
FEED_EXTRA = (
    [(0, 0, 12), (12, 9204, 23)],
    [(34, 0, 2), (36, 9218, 9)],
    [(45, 0, 15), (60, 9225, 2)],
    [(61, 0, 5), (66, 9221, 6)],
)
ATTN_PUT = (
    [(0, 0, 12)],
    [(25, 0, 5), (30, 4613, 3)],
    [(48, 4605, 12)],
    [(58, 0, 2), (60, 4610, 6)],
)
FEED_PUT = (
    [(0, 0, 12)],
    [(34, 0, 2), (36, 9218, 9)],
    [(45, 0, 15)],
    [(61, 0, 5), (66, 9221, 6)],
)
EXTRA = 72


class Block:
    def __init__(self, base, boxes, start, parts, grad_parts, extra, put, matrices):
        self.base = base
        self.boxes, self.start, self.parts, self.grad_parts = boxes, start, parts, grad_parts
        self.extra, self.put = extra, put
        self.matrices = matrices


ATTN = Block(
    0, 1, ATTN_START, attn_parts, attn_grad_parts, ATTN_EXTRA, ATTN_PUT, ((1536, 1771008), (1772544, 2362368))
)
FEED = Block(
    EXTRA, 2, FEED_START, feed_parts, feed_grad_parts, FEED_EXTRA, FEED_PUT, ((1536, 2360832), (2363904, 4723200))
)


def params(limit=56):
    return pltpu.CompilerParams(vmem_limit_bytes=limit * MB)


def dot(a, b):
    return lax.dot_general(a, b, (((1,), (0,)), ((), ())), preferred_element_type=F32)


def dot_nt(a, b):
    return lax.dot_general(a, b, (((1,), (1,)), ((), ())), preferred_element_type=F32)


def dot_tn(a, b):
    return lax.dot_general(a, b, (((0,), (0,)), ((), ())), preferred_element_type=F32)


def normed_of(values):
    center = values - jnp.mean(values, axis=-1, keepdims=True)
    spread = lax.rsqrt(jnp.mean(center * center, axis=-1, keepdims=True) + ln_eps)
    return center * spread, spread


def whole(array):
    rank = len(array.shape)
    return pl.BlockSpec(array.shape, lambda *i: (0,) * rank, pipeline_mode=pl.Buffered(1))


def rows_of(count, width):
    return pl.BlockSpec((count, width), lambda i: (i, 0))


SMEM = pl.BlockSpec(memory_space=pltpu.SMEM)


def sds(shape, dtype):
    return jax.ShapeDtypeStruct(shape, dtype)


CHUNK = 2368


def prep_kernel(block, steps, shard_ref, flat_ref, *refs):
    *box_refs, extra_ref, held = refs
    step = pl.program_id(0)
    held[pl.ds(pl.multiple_of(MARGIN + CHUNK * step, 8), CHUNK), :] = flat_ref[...].reshape(CHUNK, LANES)

    @pl.when(step == steps - 1)
    def _():
        low = lax.broadcasted_iota(jnp.int32, (8, LANES), 1) < 64
        low_one = lax.broadcasted_iota(jnp.int32, (1, LANES), 1) < 64
        extra_ref[...] = jnp.zeros_like(extra_ref)
        for share in range(4):

            @pl.when(shard_ref[0] == share)
            def _(share=share):
                odd = share % 2 == 1

                def tile(first, stride):
                    here = held[pl.ds(first, 8, stride=stride), :]
                    if not odd:
                        return here
                    ahead = held[pl.ds(first - 1, 8, stride=stride), :]
                    return jnp.where(low, pltpu.roll(ahead, 64, 1), pltpu.roll(here, 64, 1))

                for box, groups, box_row, flat_row, stride in block.parts(share):
                    base = MARGIN + block.start[share] + flat_row

                    def body(group, carry, box=box, base=base, box_row=box_row, stride=stride):
                        for j in range(6):
                            first = base + 16 * stride * group + j
                            both = jnp.concatenate([tile(first, stride), tile(first + 8 * stride, stride)], axis=0)
                            at = pl.multiple_of(box_row + 16 * group, 16)
                            box_refs[box][pl.ds(at, 16), LANES * j : LANES * j + LANES] = both.astype(BF)
                        return carry

                    lax.fori_loop(0, groups, body, 0, unroll=8)
                count = flat_rows(block, share)
                for to, row, length in block.extra[share]:
                    for k in range(length):
                        at = MARGIN + row + k
                        value = held[at : at + 1, :]
                        if odd:
                            ahead = held[at - 1 : at, :]
                            value = jnp.where(low_one, pltpu.roll(ahead, 64, 1), pltpu.roll(value, 64, 1))
                            if row + k == 0:
                                value = jnp.where(low_one, 0.0, value)
                        elif row + k == count:
                            value = jnp.where(low_one, value, 0.0)
                        extra_ref[to + k : to + k + 1, :] = value.astype(BF).astype(F32)


def flat_rows(block, share):
    return 4615 if block is ATTN else 9226


def prep(block, flat, shard):
    steps = -(-flat.shape[0] // (CHUNK * LANES))
    return pl.pallas_call(
        functools.partial(prep_kernel, block, steps),
        grid=(steps,),
        in_specs=[SMEM, pl.BlockSpec((CHUNK * LANES,), lambda i: (i,))],
        out_specs=[pl.BlockSpec((D, D), lambda i: (0, 0))] * block.boxes
        + [pl.BlockSpec((EXTRA, LANES), lambda i: (0, 0))],
        out_shape=[sds((D, D), BF)] * block.boxes + [sds((EXTRA, LANES), F32)],
        scratch_shapes=[pltpu.VMEM((MARGIN + CHUNK * steps + MARGIN, LANES), F32)],
        compiler_params=params(),
    )(shard, flat)


def spread_row(extra_ref, first, count):
    return jnp.concatenate([extra_ref[first + k : first + k + 1, :] for k in range(count)], axis=1)


def patch_row(ref, row, values):
    at = row // 16 * 16
    rows = lax.broadcasted_iota(jnp.int32, (16, values.shape[1]), 0)
    old = ref[at : at + 16, :].astype(F32)
    ref[at : at + 16, :] = jnp.where(rows == row - at, values, old).astype(BF)


def load_attn(shard, boxes, qkv_ref, proj_ref, sems):
    for wait in (False, True):
        for k, box in enumerate(boxes):
            share = jnp.bitwise_xor(shard, k)

            @pl.when(share == 3)
            def _(box=box, k=k):
                copy = pltpu.make_async_copy(box, proj_ref, sems.at[k, 0])
                copy.wait() if wait else copy.start()

            @pl.when(share != 3)
            def _(box=box, k=k, share=share):
                for part in range(3):
                    copy = pltpu.make_async_copy(
                        box.at[pl.ds(256 * part, 256), :],
                        qkv_ref.at[pl.ds(pl.multiple_of(768 * part + 256 * share, 256), 256), :],
                        sems.at[k, part],
                    )
                    copy.wait() if wait else copy.start()


def load_feed(shard, boxes, up_ref, down_ref, sems):
    for wait in (False, True):
        for k, box in enumerate(boxes):
            share = jnp.bitwise_xor(shard, k)

            @pl.when(share >= 2)
            def _(box=box, k=k, share=share):
                at = pl.multiple_of(768 * (share - 2), 256)
                copy = pltpu.make_async_copy(box, down_ref.at[pl.ds(at, 768), :], sems.at[k, 0])
                copy.wait() if wait else copy.start()

            @pl.when(share < 2)
            def _(box=box, k=k, share=share):
                for h in range(2):
                    copy = pltpu.make_async_copy(
                        box.at[pl.ds(384 * h, 384), :],
                        up_ref.at[pl.ds(pl.multiple_of(768 * h + 384 * share, 128), 384), :],
                        sems.at[k, h],
                    )
                    copy.wait() if wait else copy.start()


ANYWHERE = pl.BlockSpec(memory_space=pl.ANY)


def attn_forward(seq, fresh, x_ref, *refs):
    if fresh:
        shard_ref, extra_ref, a0, a1, a2, a3, *refs = refs
        *refs, qkv_w, proj_w, vec_ref, bias_ref, sems = refs

        @pl.when(pl.program_id(0) == 0)
        def _():
            load_attn(shard_ref[0], (a0, a1, a2, a3), qkv_w, proj_w, sems)
            for part in range(3):
                patch_row(qkv_w, 768 * part + 255, spread_row(extra_ref, 12 + 6 * part, 6))
                patch_row(qkv_w, 768 * part + 512, spread_row(extra_ref, 30 + 6 * part, 6))
            vec_ref[...] = jnp.zeros_like(vec_ref)
            for row, first in enumerate((0, 6, 60, EXTRA + 0, EXTRA + 6)):
                vec_ref[row : row + 1, :] = spread_row(extra_ref, first, 6)
            bias_ref[...] = jnp.zeros_like(bias_ref)
            bias_ref[0:1, 0:768] = spread_row(extra_ref, 48, 6)
            bias_ref[0:1, 1536:2304] = spread_row(extra_ref, 54, 6)
    else:
        qkv_w, proj_w, vec_ref, bias_ref, *refs = refs
        refs = refs[6:]
    first_ref, qkv_ref, log_ref, att_ref, hid_ref, second_ref = refs
    x = x_ref[...].astype(F32)
    normed, _ = normed_of(x)
    first = (normed * vec_ref[0:1, :] + vec_ref[1:2, :]).astype(BF)
    first_ref[...] = first
    for part in range(3):
        cols = slice(768 * part, 768 * part + 768)
        qkv_ref[:, cols] = (dot(first, qkv_w[cols, :]) + bias_ref[0:1, cols]).astype(BF)
    low = lax.broadcasted_iota(jnp.int32, (T, LANES), 1) < 64
    real = lax.broadcasted_iota(jnp.int32, (T, T), 0) < seq
    for pair in range(HEADS // 2):
        at = LANES * pair
        q = qkv_ref[:, at : at + LANES] * jnp.asarray(0.125, BF)
        k = qkv_ref[:, 768 + at : 768 + at + LANES]
        v = qkv_ref[:, 1536 + at : 1536 + at + LANES]
        outs = []
        for half in range(2):
            own = low if half == 0 else ~low
            scores = dot_nt(k, jnp.where(own, q, jnp.zeros_like(q)))
            scores = jnp.where(real, scores, -1e30)
            top = jnp.max(scores, axis=0, keepdims=True)
            weight = jnp.exp(scores - top)
            total = jnp.sum(weight, axis=0, keepdims=True)
            head = 2 * pair + half
            log_ref[0, head : head + 1, :] = top + jnp.log(total)
            outs.append(dot_tn((weight * (1.0 / total)).astype(BF), v))
        att_ref[:, at : at + LANES] = jnp.where(low, outs[0], outs[1]).astype(BF)
    hidden = x + dot(att_ref[...], proj_w[...]) + vec_ref[2:3, :]
    hid_ref[...] = hidden
    normed, _ = normed_of(hidden)
    second_ref[...] = (normed * vec_ref[3:4, :] + vec_ref[4:5, :]).astype(BF)


def call_attn_forward(seq, x, weights, first_image, count, boxes=None, before=None):
    rows = x.shape[0]
    images = rows // T
    blocks = lambda width: pl.BlockSpec((T, width), lambda i: (i + first_image, 0))
    specs = [
        blocks(D),
        blocks(2304),
        pl.BlockSpec((1, HEADS, T), lambda i: (i + first_image, 0, 0)),
        blocks(D),
        blocks(D),
        blocks(D),
    ]
    shapes = [
        sds((rows, D), BF),
        sds((rows, 2304), BF),
        sds((images, HEADS, T), F32),
        sds((rows, D), BF),
        sds((rows, D), F32),
        sds((rows, D), BF),
    ]
    if boxes is not None:
        shard, extra = weights
        made = [sds((2304, D), BF), sds((D, D), BF), sds((8, D), F32), sds((8, 2304), F32)]
        return pl.pallas_call(
            functools.partial(attn_forward, seq, True),
            grid=(count,),
            in_specs=[blocks(D), SMEM, whole(extra)] + [ANYWHERE] * 4,
            out_specs=specs + [pl.BlockSpec(shape.shape, lambda i: (0, 0)) for shape in made],
            out_shape=shapes + made,
            scratch_shapes=[pltpu.SemaphoreType.DMA((4, 3))],
            compiler_params=params(),
        )(x, shard, extra, *boxes)
    return pl.pallas_call(
        functools.partial(attn_forward, seq, False),
        grid=(count,),
        in_specs=[blocks(D)] + [whole(weight) for weight in weights] + [ANYWHERE] * 6,
        out_specs=specs,
        out_shape=shapes,
        input_output_aliases={5 + i: i for i in range(6)},
        compiler_params=params(),
    )(x, *weights, *before)


HALF = FF // 2
ROW_STEPS = 4


def feed(seq, part, tall, shard_ref, extra_ref, a0, a1, a2, a3, second_ref, cot_ref, result_ref, *refs):
    last = part == 1
    if last:
        before_ref, out_ref, gs_ref, *refs = refs
    else:
        out_ref, gs_ref, cot_sum, *refs = refs
    sum_ref, edge_ref, other_ref, mine_ref, up_w, down_w, bias, second_all, cot_all, act_all, pre_all, sems = refs
    step = pl.program_id(0)
    shard = shard_ref[0]

    @pl.when(step == 0)
    def _():
        load_feed(shard, (a0, a1, a2, a3), up_w, down_w, sems)
        for h in range(2):
            patch_row(up_w, 768 * h + 383, spread_row(extra_ref, EXTRA + 12 + 12 * h + 6 * part, 6))
            bias[0:1, 768 * h : 768 * h + 768] = spread_row(extra_ref, EXTRA + 36 + 12 * h + 6 * part, 6)
        if last:
            patch_row(down_w, 767, spread_row(extra_ref, EXTRA + 60, 6))
        sum_ref[...] = jnp.zeros_like(sum_ref)
        edge_ref[...] = jnp.zeros_like(edge_ref)
        if not last:
            cot_sum[...] = jnp.zeros_like(cot_sum)

    @pl.when(step < ROW_STEPS)
    def _():
        at = pl.ds(pl.multiple_of(step * tall, 16), tall)
        second = second_ref[...]
        cot = cot_ref[...]
        second_all[at, :] = second
        cot_all[at, :] = cot
        if last:
            result = result_ref[...]
            grad_second = before_ref[...]
        else:
            result = result_ref[...] + spread_row(extra_ref, EXTRA + 66, 6)
            grad_second = jnp.zeros_like(result)
            cot_sum[0:1, :] += jnp.sum(cot.astype(F32), axis=0, keepdims=True)
        for h in range(2):
            cols = slice(768 * h, 768 * h + 768)
            pre = dot(second, up_w[cols, :]) + bias[0:1, cols]
            grad_act = dot_nt(cot, down_w[cols, :])
            half = 0.5 * (1.0 + lax.erf(pre * root_half))
            act = (pre * half).astype(BF)
            grad_pre = grad_act * (half + pre * jnp.exp(-0.5 * pre * pre) * inv_root_tau)
            low = grad_pre.astype(BF)
            act_all[at, cols] = act
            pre_all[at, cols] = low
            sum_ref[0:1, cols] += jnp.sum(grad_pre, axis=0, keepdims=True)
            result = result + dot(act, down_w[cols, :])
            grad_second = grad_second + dot_nt(low, up_w[cols, :])
        if last:
            for image in range(tall // T):
                out_ref[image] = result[T * image : T * image + seq].astype(BF)
        else:
            out_ref[...] = result
        gs_ref[...] = grad_second

    for index in range(4):
        out = other_ref if index < 2 else mine_ref
        side = jnp.bitwise_xor(shard // 2, index % 2)
        core = shard % 2 if index >= 2 else 1 - shard % 2

        @pl.when((step == ROW_STEPS + index) & (side == 0))
        def _(out=out, core=core):
            left = second_all[:, pl.ds(pl.multiple_of(384 * core, 128), 384)]
            for h in range(2):
                grad = dot_tn(left, pre_all[:, 768 * h : 768 * h + 768])
                out[0, 384 * h : 384 * h + 384, :] = grad.astype(BF)

                @pl.when(core == 0)
                def _(grad=grad, h=h):
                    edge_ref[0:1, 768 * h : 768 * h + 768] = grad[383:384]

        @pl.when((step == ROW_STEPS + index) & (side == 1))
        def _(out=out, core=core):
            left = act_all[:, pl.ds(pl.multiple_of(768 * core, 128), 768)]
            grad = dot_tn(left, cot_all[...])
            out[0] = grad.astype(BF)

            @pl.when(core == 0)
            def _():
                edge_ref[1:2, 0:768] = grad[767:768]


def call_feed(seq, part, shard, extra, boxes, second, cot, result, before=None):
    rows = second.shape[0]
    images = rows // T
    tall = rows // ROW_STEPS
    last = part == 1
    row = lambda i: jnp.minimum(i, ROW_STEPS - 1)
    block = pl.BlockSpec((tall, D), lambda i: (row(i), 0))
    out = pl.BlockSpec((tall // T, seq, D), lambda i: (row(i), 0, 0)) if last else block
    grads = lambda first: pl.BlockSpec((1, D, D), lambda i: (jnp.clip(i - ROW_STEPS - first, 0, 1), 0, 0))
    small = lambda width: pl.BlockSpec((8, width), lambda i: (0, 0))
    return pl.pallas_call(
        functools.partial(feed, seq, part, tall),
        grid=(ROW_STEPS + 4,),
        in_specs=[SMEM, whole(extra)] + [ANYWHERE] * 4 + [block] * (4 if last else 3),
        out_specs=[out, block] + ([] if last else [small(D)]) + [small(HALF), small(HALF), grads(0), grads(2)],
        out_shape=[sds((images, seq, D), BF) if last else sds((rows, D), F32), sds((rows, D), F32)]
        + ([] if last else [sds((8, D), F32)])
        + [sds((8, HALF), F32), sds((8, HALF), F32), sds((2, D, D), BF), sds((2, D, D), BF)],
        scratch_shapes=[
            pltpu.VMEM((HALF, D), BF),
            pltpu.VMEM((HALF, D), BF),
            pltpu.VMEM((8, HALF), F32),
            pltpu.VMEM((rows, D), BF),
            pltpu.VMEM((rows, D), BF),
            pltpu.VMEM((rows, HALF), BF),
            pltpu.VMEM((rows, HALF), BF),
            pltpu.SemaphoreType.DMA((4, 2)),
        ],
        compiler_params=params(60),
    )(shard, extra, *boxes, second, cot, result, *([before] if last else []))


WIDE = 384


def attn_backward(seq, images, group, shard_ref, log_ref, qkv_ref, first_ref, att_ref, *refs):
    step = pl.program_id(0)
    shard = shard_ref[0]
    if group == 0:
        gs_ref, hid_ref, cot_ref, vec_ref, proj_w, grad_ref, head_sum, low_ref, ga_ref, gh_ref, sum_ref, *refs = refs
    else:
        low_ref, ga_ref, grad_ref, head_sum, *refs = refs
    edge_ref, other_ref, mine_ref, grad_all, first_all, low_all, att_all = refs

    @pl.when(step == 0)
    def _():
        head_sum[...] = jnp.zeros_like(head_sum)
        edge_ref[...] = jnp.zeros_like(edge_ref)
        if group == 0:
            sum_ref[...] = jnp.zeros_like(sum_ref)

    @pl.when(step < images)
    def _():
        at_rows = pl.ds(pl.multiple_of(step * T, 16), T)
        first_all[at_rows, :] = first_ref[...]
        att_all[at_rows, :] = att_ref[...]
        if group == 0:
            gs = gs_ref[...]
            normed, spread = normed_of(hid_ref[...])
            gn = gs * vec_ref[3:4, :]
            gh = cot_ref[...].astype(F32) + spread * (
                gn - jnp.mean(gn, axis=-1, keepdims=True) - normed * jnp.mean(gn * normed, axis=-1, keepdims=True)
            )
            sum_ref[0:1, :] += jnp.sum(gs * normed, axis=0, keepdims=True)
            sum_ref[1:2, :] += jnp.sum(gs, axis=0, keepdims=True)
            sum_ref[2:3, :] += jnp.sum(gh, axis=0, keepdims=True)
            gh_ref[...] = gh
            gh_low = gh.astype(BF)
            low_ref[...] = gh_low
            ga_ref[...] = dot_nt(gh_low, proj_w[...]).astype(BF)
        low_all[at_rows, :] = low_ref[...]
        low = lax.broadcasted_iota(jnp.int32, (T, LANES), 1) < 64
        real = lax.broadcasted_iota(jnp.int32, (T, T), 0) < seq
        eighth = jnp.asarray(0.125, BF)
        for pair in range(3):
            at = LANES * pair
            full = WIDE * group + at
            q = qkv_ref[:, full : full + LANES] * eighth
            k = qkv_ref[:, 768 + full : 768 + full + LANES]
            v = qkv_ref[:, 1536 + full : 1536 + full + LANES]
            k_small = k * eighth
            grad_out = ga_ref[:, at : at + LANES]
            zero = jnp.zeros_like(q)
            grads = ([], [], [])
            for half in range(2):
                own = low if half == 0 else ~low
                head = 6 * group + 2 * pair + half
                scores = dot_nt(k, jnp.where(own, q, zero))
                probs = jnp.where(real, jnp.exp(scores - log_ref[0, head : head + 1, :]), 0.0)
                grads[2].append(dot(probs.astype(BF), grad_out))
                grad_probs = dot_nt(v, jnp.where(own, grad_out, zero))
                delta = jnp.sum(probs * grad_probs, axis=0, keepdims=True)
                grad_scores = (probs * (grad_probs - delta)).astype(BF)
                grads[1].append(dot(grad_scores, q))
                grads[0].append(dot_tn(grad_scores, k_small))
            for part in range(3):
                grad = jnp.where(low, grads[part][0], grads[part][1])
                if part != 1:
                    row = part // 2
                    head_sum[row : row + 1, at : at + LANES] += jnp.sum(grad, axis=0, keepdims=True)
                cols = slice(WIDE * part + at, WIDE * part + at + LANES)
                grad = grad.astype(BF)
                grad_ref[:, cols] = grad
                grad_all[at_rows, cols] = grad

    for index in range(4):
        out = other_ref if index < 2 else mine_ref
        side = jnp.bitwise_xor(shard // 2, index % 2)
        core = shard % 2 if index >= 2 else 1 - shard % 2
        share = 2 * side + core

        @pl.when((step == images + index) & (share == 3))
        def _(out=out):
            out[0] = dot_tn(att_all[...], low_all[...]).astype(BF)

        @pl.when((step == images + index) & (share != 3))
        def _(out=out, share=share):
            grad = dot_tn(first_all[:, pl.ds(pl.multiple_of(256 * share, 256), 256)], grad_all[...])
            for part in range(3):
                cols = slice(WIDE * part, WIDE * part + WIDE)
                for u in range(2):
                    out[0, 128 * part : 128 * part + 128, WIDE * u : WIDE * u + WIDE] = grad[
                        128 * u : 128 * u + 128, cols
                    ].astype(BF)

            @pl.when(share == 0)
            def _():
                edge_ref[0:1, :] = grad[255:256]

            @pl.when(share == 2)
            def _():
                edge_ref[1:2, :] = grad[0:1]


def call_attn_backward(seq, group, shard, log_total, qkv, first, attended, *more):
    rows = first.shape[0]
    images = rows // T
    row = lambda i: jnp.minimum(i, images - 1)
    block = lambda width, col=0: pl.BlockSpec((T, width), lambda i: (row(i), col))
    small = lambda width: pl.BlockSpec((8, width), lambda i: (0, 0))
    grads = lambda at: pl.BlockSpec((1, WIDE, D), lambda i: (jnp.clip(i - images - at, 0, 1), 0, 0))
    in_specs = [SMEM, pl.BlockSpec((1, HEADS, T), lambda i: (row(i), 0, 0)), block(2304), block(D), block(WIDE, group)]
    out_specs = [block(3 * WIDE), small(WIDE)]
    out_shape = [sds((rows, 3 * WIDE), BF), sds((8, WIDE), F32)]
    if group == 0:
        in_specs += [block(D)] * 3 + [whole(more[3]), whole(more[4])]
        out_specs += [block(D), block(D), block(D), small(D)]
        out_shape += [sds((rows, D), BF), sds((rows, D), BF), sds((rows, D), F32), sds((8, D), F32)]
    else:
        in_specs += [block(D), block(WIDE, 1)]
    return pl.pallas_call(
        functools.partial(attn_backward, seq, images, group),
        grid=(images + 4,),
        in_specs=in_specs,
        out_specs=out_specs + [small(3 * WIDE), grads(0), grads(2)],
        out_shape=out_shape + [sds((8, 3 * WIDE), F32), sds((2, WIDE, D), BF), sds((2, WIDE, D), BF)],
        scratch_shapes=[
            pltpu.VMEM((rows, 3 * WIDE), BF),
            pltpu.VMEM((rows, D), BF),
            pltpu.VMEM((rows, D), BF),
            pltpu.VMEM((rows, WIDE), BF),
        ],
        compiler_params=params(),
    )(shard, log_total, qkv, first, attended, *more)


def input_backward(seq, grad0, grad1, gh_ref, x_ref, vec_ref, qkv_w, out_ref, sum_ref):
    @pl.when(pl.program_id(0) == 0)
    def _():
        sum_ref[...] = jnp.zeros_like(sum_ref)

    grad_first = None
    for part in range(3):
        cols = slice(WIDE * part, WIDE * part + WIDE)
        both = jnp.concatenate([grad0[:, cols], grad1[:, cols]], axis=1)
        term = dot_nt(both, qkv_w[768 * part : 768 * part + 768, :])
        grad_first = term if part == 0 else grad_first + term
    normed, spread = normed_of(x_ref[...].astype(F32))
    gn = grad_first * vec_ref[0:1, :]
    grad = gh_ref[...] + spread * (
        gn - jnp.mean(gn, axis=-1, keepdims=True) - normed * jnp.mean(gn * normed, axis=-1, keepdims=True)
    )
    sum_ref[0:1, :] += jnp.sum(grad_first * normed, axis=0, keepdims=True)
    sum_ref[1:2, :] += jnp.sum(grad_first, axis=0, keepdims=True)
    for image in range(grad.shape[0] // T):
        out_ref[image] = grad[T * image : T * image + seq].astype(BF)


def call_input_backward(seq, grads, gh, x, vec, qkv_w):
    rows = gh.shape[0]
    images = rows // T
    step = 2 if images % 2 == 0 else 1
    tall = step * T
    return pl.pallas_call(
        functools.partial(input_backward, seq),
        grid=(images // step,),
        in_specs=[rows_of(tall, 3 * WIDE)] * 2 + [rows_of(tall, D), rows_of(tall, D), whole(vec), whole(qkv_w)],
        out_specs=[pl.BlockSpec((step, seq, D), lambda i: (i, 0, 0)), pl.BlockSpec((8, D), lambda i: (0, 0))],
        out_shape=[sds((images, seq, D), BF), sds((8, D), F32)],
        compiler_params=params(),
    )(*grads, gh, x, vec, qkv_w)


def pack(last_sum, back_sum, head0, head1, edge0, edge1, pre0, pre1, up0, up1, cot_sum, out_ref):
    out_ref[...] = jnp.zeros_like(out_ref)

    def put(first, ref, row, col, width):
        for k in range(width // LANES):
            at = col + LANES * k
            out_ref[first + k : first + k + 1, :] = ref[row : row + 1, at : at + LANES]

    put(0, last_sum, 0, 0, D)
    put(6, last_sum, 1, 0, D)
    for group, (head, edge) in enumerate(((head0, edge0), (head1, edge1))):
        for part in range(3):
            put(12 + 6 * part + 3 * group, edge, 0, WIDE * part, WIDE)
            put(30 + 6 * part + 3 * group, edge, 1, WIDE * part, WIDE)
        put(48 + 3 * group, head, 0, 0, WIDE)
        put(54 + 3 * group, head, 1, 0, WIDE)
    put(60, back_sum, 2, 0, D)
    put(EXTRA, back_sum, 0, 0, D)
    put(EXTRA + 6, back_sum, 1, 0, D)
    for j, (pre, up) in enumerate(((pre0, up0), (pre1, up1))):
        for h in range(2):
            put(EXTRA + 12 + 12 * h + 6 * j, up, 0, 768 * h, D)
            put(EXTRA + 36 + 12 * h + 6 * j, pre, 0, 768 * h, D)
    put(EXTRA + 60, up1, 1, 0, D)
    put(EXTRA + 66, cot_sum, 0, 0, D)


def call_pack(*arrays):
    return pl.pallas_call(
        pack,
        in_specs=[pl.BlockSpec(memory_space=pltpu.VMEM)] * len(arrays),
        out_specs=pl.BlockSpec(memory_space=pltpu.VMEM),
        out_shape=sds((2 * EXTRA, LANES), F32),
        compiler_params=params(),
    )(*arrays)


def adam_kernel(block, share_size, scale, boxes, shard_ref, power_ref, extra_ref, *refs):
    box_refs = refs[:boxes]
    flat_ref, mom_ref, grad_ref, change_ref, new_ref, held = refs[boxes:]
    step = pl.program_id(0)

    @pl.when(step == 0)
    def _():
        for share in range(4):

            @pl.when(shard_ref[0] == share)
            def _(share=share):
                for box, groups, box_row, col, cols, flat_row, stride in block.grad_parts(share):
                    base = MARGIN + block.start[share] + flat_row

                    def body(group, carry, box=box, box_row=box_row, col=col, cols=cols, base=base, stride=stride):
                        row = pl.multiple_of(box_row + 16 * group, 16)
                        for j in range(cols):
                            at = LANES * (col + j)
                            both = box_refs[box][pl.ds(row, 16), at : at + LANES].astype(F32)
                            to = base + 16 * stride * group + j
                            held[pl.ds(to, 8, stride=stride), :] = both[0:8]
                            held[pl.ds(to + 8 * stride, 8, stride=stride), :] = both[8:16]
                        return carry

                    lax.fori_loop(0, groups, body, 0, unroll=8)
                for source, row, length in block.put[share]:
                    held[MARGIN + row : MARGIN + row + length, :] = extra_ref[block.base + source : block.base + source + length, :]

    start = pl.multiple_of(MARGIN + CHUNK * step, 8)
    shard = shard_ref[0]
    low = lax.broadcasted_iota(jnp.int32, (CHUNK, LANES), 1) < 64
    here = held[pl.ds(start, CHUNK), :]
    after = held[pl.ds(start + 1, CHUNK), :]
    shifted = jnp.where(low, pltpu.roll(here, 64, 1), pltpu.roll(after, 64, 1))
    grad = jnp.where(shard % 2 == 1, shifted, here) * scale
    position = (
        shard * share_size
        + step * (CHUNK * LANES)
        + lax.broadcasted_iota(jnp.int32, (CHUNK, LANES), 0) * LANES
        + lax.broadcasted_iota(jnp.int32, (CHUNK, LANES), 1)
    )
    matrix = jnp.zeros((CHUNK, LANES), jnp.bool_)
    for first, end in block.matrices:
        matrix = matrix | ((position >= first) & (position < end))
    size = CHUNK * LANES
    p = flat_ref[...].reshape(CHUNK, LANES)
    m = beta_one * mom_ref[0, :].reshape(CHUNK, LANES) + (1.0 - beta_one) * grad
    s = beta_two * mom_ref[1, :].reshape(CHUNK, LANES) + (1.0 - beta_two) * grad * grad
    ratio = (m * power_ref[0]) / (jnp.sqrt(s * power_ref[1]) + adam_eps)
    change = jnp.where(matrix, rate_matrix, rate_vector) * (ratio + jnp.where(matrix, decay_matrix, 0.0) * p)
    grad_ref[...] = grad.reshape(size)
    change_ref[...] = change.reshape(size)
    new_ref[0, :] = m.reshape(size)
    new_ref[1, :] = s.reshape(size)


def adam(block, shard, powers, extra, boxes, flat, moments, scale):
    count = flat.shape[0]
    steps = -(-count // (CHUNK * LANES))
    line = pl.BlockSpec((CHUNK * LANES,), lambda i: (i,))
    two = pl.BlockSpec((2, CHUNK * LANES), lambda i: (0, i))
    return pl.pallas_call(
        functools.partial(adam_kernel, block, count, scale, len(boxes)),
        grid=(steps,),
        in_specs=[SMEM, SMEM, whole(extra)] + [whole(box) for box in boxes] + [line, two],
        out_specs=[line, line, two],
        out_shape=[sds((count,), F32), sds((count,), F32), sds((2, count), F32)],
        scratch_shapes=[pltpu.VMEM((MARGIN + CHUNK * steps + MARGIN, LANES), F32)],
        compiler_params=params(),
    )(shard, powers, extra, *boxes, flat, moments)


def swap(value, axis, bit):
    pairs = [(i, i ^ bit) for i in range(lax.axis_size(axis))]
    return lax.ppermute(value, axis, pairs)


def turn(value, axis, unit, distance):
    size = lax.axis_size(axis)
    return lax.ppermute(value, axis, [(i, (i + unit * distance) % size) for i in range(size)])


def pick(array, index, axis=0):
    return lax.dynamic_index_in_dim(array, index, axis, keepdims=False)


class Line:
    def __init__(self):
        self.last = None

    def __call__(self, step, *args):
        if self.last is not None:
            flat, tree = jax.tree.flatten(args)
            flat = lax.optimization_barrier((self.last, *flat))[1:]
            args = jax.tree.unflatten(tree, flat)
        out = step(*args)
        self.last = min(jax.tree.leaves(out), key=lambda leaf: leaf.size)
        return out


class Sum:
    def __init__(self, line, mine, other):
        self.line, self.mine = line, mine
        self.rows = mine.shape[1]
        rep = lax.axis_index("rep")
        self.near, self.far = rep % 2, rep // 2
        self.count = lax.axis_size("rep") // 2
        self.came = swap(other, "shard", 1)

    def side(self):
        send = self.line(lambda m, c: (m.astype(F32) + c.astype(F32)).astype(BF), self.mine[1], self.came[1])
        self.mine, self.here = self.mine[0], self.came[0]
        self.came = swap(send, "shard", 2)

    def close(self):
        def step(mine, here, came):
            total = mine.astype(F32) + here.astype(F32) + came.astype(F32)
            halves = total.reshape(2, self.rows // 2, D)
            return pick(halves, 1 - self.near).astype(BF), pick(halves, self.near)

        send, self.half = self.line(step, self.mine, self.here, self.came)
        self.came = swap(send, "rep", 1)

    def along(self):
        def step(half, came):
            parts = (half + came.astype(F32)).reshape(self.count, self.rows // 2 // self.count, D)
            sends = [pick(parts, (self.far + d) % self.count).astype(BF) for d in range(1, self.count)]
            return sends, pick(parts, self.far)

        sends, self.part = self.line(step, self.half, self.came)
        self.came = [turn(send, "rep", 2, d + 1) for d, send in enumerate(sends)]

    def back_along(self):
        def step(part, came):
            for value in came:
                part = part + value.astype(F32)
            return part.astype(BF)

        self.part = self.line(step, self.part, self.came)
        self.came = [turn(self.part, "rep", 2, d) for d in range(1, self.count)]

    def back_close(self):
        def step(part, came):
            full = jnp.zeros((self.count,) + part.shape, BF)
            for d, value in enumerate([part] + came):
                full = lax.dynamic_update_slice_in_dim(full, value[None], (self.far + self.count - d) % self.count, 0)
            return full.reshape(self.rows // 2, D)

        self.half = self.line(step, self.part, self.came)
        self.came = swap(self.half, "rep", 1)

    def end(self):
        def step(half, came):
            first = self.near == 0
            return jnp.concatenate([jnp.where(first, half, came), jnp.where(first, came, half)], axis=0)

        return self.line(step, self.half, self.came)


class SumAll:
    def __init__(self, line, value):
        self.line, self.value = line, value
        self.hops = [("shard", 1), ("shard", 2)]
        bit = 1
        while bit < lax.axis_size("rep"):
            self.hops.append(("rep", bit))
            bit *= 2
        self.came = swap(value, *self.hops.pop(0))

    def hop(self):
        self.value = self.line(lambda a, b: a + b, self.value, self.came)
        if self.hops:
            self.came = swap(self.value, *self.hops.pop(0))
            return False
        return True


def body(layer_input, out_cotangent, attention_params, attention_moments, feedforward_params, feedforward_moments, step_count):
    images, seq, _ = layer_input.shape
    rows = images * T
    image_total = images * lax.axis_size("shard") * lax.axis_size("rep")
    scale = 1.0 / image_total
    shard = lax.axis_index("shard").astype(jnp.int32).reshape(1)
    time = step_count[0].astype(F32)
    powers = jnp.stack([1.0 / (1.0 - jnp.power(beta_one, time)), 1.0 / (1.0 - jnp.power(beta_two, time))])
    pad = ((0, 0), (0, T - seq), (0, 0))
    padded = lambda tokens: jnp.pad(tokens, pad).reshape(rows, D)
    line = Line()

    attn_box, attn_extra = line(functools.partial(prep, ATTN), attention_params, shard)
    attn_across = swap(attn_box, "shard", 2)
    attn_near = swap(attn_box, "shard", 1)
    box0, box1, feed_extra = line(functools.partial(prep, FEED), feedforward_params, shard)
    extra = line(lambda a, b: jnp.concatenate([a, b], axis=0), attn_extra, feed_extra)
    came = swap(extra, "shard", 1)
    x = line(padded, layer_input)
    extra = line(lambda a, b: a + b, extra, came)
    came = swap(extra, "shard", 2)
    cot = line(padded, out_cotangent)
    extra = line(lambda a, b: a + b, extra, came)
    near0, near1 = swap(box0, "shard", 1), swap(box1, "shard", 1)
    across, send0 = line(lambda a, b: lax.optimization_barrier((a, b)), attn_across, box0)
    attn_both = swap(across, "shard", 1)
    across0 = swap(send0, "shard", 2)
    boxes = (attn_box, attn_near, attn_across, attn_both)
    count = images // 2
    *saved, qkv_w, proj_w, vec, bias = line(
        lambda x, w, b: call_attn_forward(seq, x, w, 0, count, boxes=b), x, (shard, extra), boxes
    )
    across, send1 = line(lambda a, b: lax.optimization_barrier((a, b)), across0, box1)
    both0 = swap(across, "shard", 1)
    across1 = swap(send1, "shard", 2)
    first, qkv, log_total, attended, hidden, second = line(
        lambda x, w, b: call_attn_forward(seq, x, w, count, images - count, before=b), x, (qkv_w, proj_w, vec, bias), saved
    )
    boxes = (box0, near0, across0, both0)
    result, gs, cot_sum, pre0, up0, other0, mine0 = line(
        lambda *a: call_feed(seq, 0, *a), shard, extra, boxes, second, cot, hidden
    )
    feed0 = Sum(line, mine0, other0)
    both1 = swap(line(lambda a: a, across1), "shard", 1)
    boxes = (box1, near1, across1, both1)
    layer_output, gs, pre1, up1, other1, mine1 = line(
        lambda *a: call_feed(seq, 1, *a), shard, extra, boxes, second, cot, result, gs
    )
    feed1 = Sum(line, mine1, other1)
    feed0.side()
    grad0, head0, gh_low, ga, gh, back_sum, edge0, other2, mine2 = line(
        lambda *a: call_attn_backward(seq, 0, *a), shard, log_total, qkv, first, attended, gs, hidden, cot, vec, proj_w
    )
    attn0 = Sum(line, mine2, other2)
    feed0.close()
    feed1.side()
    grad1, head1, edge1, other3, mine3 = line(
        lambda *a: call_attn_backward(seq, 1, *a), shard, log_total, qkv, first, attended, gh_low, ga
    )
    attn1 = Sum(line, mine3, other3)
    feed0.along()
    feed1.close()
    attn0.side()
    input_grad, last_sum = line(lambda *a: call_input_backward(seq, *a), (grad0, grad1), gh, x, vec, qkv_w)
    sums = line(call_pack, last_sum, back_sum, head0, head1, edge0, edge1, pre0, pre1, up0, up1, cot_sum)
    sums = SumAll(line, sums)
    attn1.side()
    feed0.back_along()
    feed1.along()
    attn0.close()
    sums.hop()
    feed0.back_close()
    feed1.back_along()
    attn0.along()
    attn1.close()
    sums.hop()
    feed1.back_close()
    attn0.back_along()
    attn1.along()
    feed_box0 = feed0.end()
    while not sums.hop():
        pass
    feed_box1 = feed1.end()
    attn1.back_along()
    attn0.back_close()
    attn1.back_close()
    feed_grad, feed_change, feed_new = line(
        lambda *a: adam(FEED, *a, scale), shard, powers, sums.value, [feed_box0, feed_box1], feedforward_params, feedforward_moments
    )
    attn_grad, attn_change, attn_new = line(
        lambda *a: adam(ATTN, *a, scale), shard, powers, sums.value, [attn0.end(), attn1.end()], attention_params, attention_moments
    )
    return (layer_output, input_grad, attn_grad, feed_grad, attn_change, attn_new, feed_change, feed_new)


def solution(mesh):
    tokens = P(("shard", "rep"), None, None)
    in_specs = (tokens, tokens, P("shard"), P(None, "shard"), P("shard"), P(None, "shard"), P())
    out_specs = (tokens, tokens, P("shard"), P("shard"), P("shard"), P(None, "shard"), P("shard"), P(None, "shard"))
    return jax.shard_map(body, mesh=mesh, in_specs=in_specs, out_specs=out_specs, check_vma=False)
```

```python
import functools

import jax
import jax.numpy as jnp
from jax import lax
from jax.experimental import pallas as pl
from jax.experimental.pallas import tpu as pltpu
from jax.sharding import PartitionSpec as P

D = 768
HEADS = 12
FF = 3072
T = 208

F32 = jnp.float32
BF = jnp.bfloat16

ln_eps = 1e-06
beta_one = 0.9
beta_two = 0.999
adam_eps = 1e-08
rate_matrix = 0.01
rate_vector = 0.1
decay_matrix = 0.05
root_half = 0.7071067811865476
inv_root_tau = 0.3989422804014327

MB = 1 << 20
LANES = 128
MARGIN = 8

ATTN_START = (12, 5, -3, 2)
FEED_START = (12, 2, 15, 5)


def attn_parts(share):
    if share < 3:
        return [(0, 16, 256 * part, 6 * part, 18) for part in range(3)]
    return [(0, 48, 0, 0, 6)]


def feed_parts(share):
    if share < 2:
        return [(j, 24, 384 * h, 12 * h + 6 * j, 24) for j in range(2) for h in range(2)]
    return [(j, 48, 0, 4608 * j, 6) for j in range(2)]


def attn_grad_parts(share):
    if share < 3:
        return [
            (g, 8, 128 * part, 3 * u, 3, 18 * 128 * u + 6 * part + 3 * g, 18)
            for g in range(2)
            for part in range(3)
            for u in range(2)
        ]
    return [(g, 24, 0, 0, 6, 6 * 384 * g, 6) for g in range(2)]


def feed_grad_parts(share):
    return [(box, groups, row, 0, 6, flat, stride) for box, groups, row, flat, stride in feed_parts(share)]


ATTN_EXTRA = (
    [(0, 0, 12), (12, 4602, 14)],
    [(25, 0, 5), (30, 4613, 3)],
    [(33, 0, 15), (48, 4605, 11)],
    [(58, 0, 2), (60, 4610, 6)],
)
FEED_EXTRA = (
    [(0, 0, 12), (12, 9204, 23)],
    [(34, 0, 2), (36, 9218, 9)],
    [(45, 0, 15), (60, 9225, 2)],
    [(61, 0, 5), (66, 9221, 6)],
)
ATTN_PUT = (
    [(0, 0, 12)],
    [(25, 0, 5), (30, 4613, 3)],
    [(48, 4605, 12)],
    [(58, 0, 2), (60, 4610, 6)],
)
FEED_PUT = (
    [(0, 0, 12)],
    [(34, 0, 2), (36, 9218, 9)],
    [(45, 0, 15)],
    [(61, 0, 5), (66, 9221, 6)],
)
EXTRA = 72


class Block:
    def __init__(self, base, boxes, start, parts, grad_parts, extra, put, matrices):
        self.base = base
        self.boxes, self.start, self.parts, self.grad_parts = boxes, start, parts, grad_parts
        self.extra, self.put = extra, put
        self.matrices = matrices


ATTN = Block(
    0, 1, ATTN_START, attn_parts, attn_grad_parts, ATTN_EXTRA, ATTN_PUT, ((1536, 1771008), (1772544, 2362368))
)
FEED = Block(
    EXTRA, 2, FEED_START, feed_parts, feed_grad_parts, FEED_EXTRA, FEED_PUT, ((1536, 2360832), (2363904, 4723200))
)


def params(limit=56):
    return pltpu.CompilerParams(vmem_limit_bytes=limit * MB)


def dot(a, b):
    return lax.dot_general(a, b, (((1,), (0,)), ((), ())), preferred_element_type=F32)


def dot_nt(a, b):
    return lax.dot_general(a, b, (((1,), (1,)), ((), ())), preferred_element_type=F32)


def dot_tn(a, b):
    return lax.dot_general(a, b, (((0,), (0,)), ((), ())), preferred_element_type=F32)


def normed_of(values):
    center = values - jnp.mean(values, axis=-1, keepdims=True)
    spread = lax.rsqrt(jnp.mean(center * center, axis=-1, keepdims=True) + ln_eps)
    return center * spread, spread


def whole(array):
    rank = len(array.shape)
    return pl.BlockSpec(array.shape, lambda *i: (0,) * rank, pipeline_mode=pl.Buffered(1))


def rows_of(count, width):
    return pl.BlockSpec((count, width), lambda i: (i, 0))


SMEM = pl.BlockSpec(memory_space=pltpu.SMEM)


def sds(shape, dtype):
    return jax.ShapeDtypeStruct(shape, dtype)


CHUNK = 2368


def prep_kernel(block, steps, shard_ref, flat_ref, *refs):
    *box_refs, extra_ref, held = refs
    step = pl.program_id(0)
    held[pl.ds(pl.multiple_of(MARGIN + CHUNK * step, 8), CHUNK), :] = flat_ref[...].reshape(CHUNK, LANES)

    @pl.when(step == steps - 1)
    def _():
        low = lax.broadcasted_iota(jnp.int32, (8, LANES), 1) < 64
        low_one = lax.broadcasted_iota(jnp.int32, (1, LANES), 1) < 64
        extra_ref[...] = jnp.zeros_like(extra_ref)
        for share in range(4):

            @pl.when(shard_ref[0] == share)
            def _(share=share):
                odd = share % 2 == 1

                def tile(first, stride):
                    here = held[pl.ds(first, 8, stride=stride), :]
                    if not odd:
                        return here
                    ahead = held[pl.ds(first - 1, 8, stride=stride), :]
                    return jnp.where(low, pltpu.roll(ahead, 64, 1), pltpu.roll(here, 64, 1))

                for box, groups, box_row, flat_row, stride in block.parts(share):
                    base = MARGIN + block.start[share] + flat_row

                    def body(group, carry, box=box, base=base, box_row=box_row, stride=stride):
                        for j in range(6):
                            first = base + 16 * stride * group + j
                            both = jnp.concatenate([tile(first, stride), tile(first + 8 * stride, stride)], axis=0)
                            at = pl.multiple_of(box_row + 16 * group, 16)
                            box_refs[box][pl.ds(at, 16), LANES * j : LANES * j + LANES] = both.astype(BF)
                        return carry

                    lax.fori_loop(0, groups, body, 0, unroll=8)
                count = flat_rows(block, share)
                for to, row, length in block.extra[share]:
                    for k in range(length):
                        at = MARGIN + row + k
                        value = held[at : at + 1, :]
                        if odd:
                            ahead = held[at - 1 : at, :]
                            value = jnp.where(low_one, pltpu.roll(ahead, 64, 1), pltpu.roll(value, 64, 1))
                            if row + k == 0:
                                value = jnp.where(low_one, 0.0, value)
                        elif row + k == count:
                            value = jnp.where(low_one, value, 0.0)
                        extra_ref[to + k : to + k + 1, :] = value.astype(BF).astype(F32)


def flat_rows(block, share):
    return 4615 if block is ATTN else 9226


def prep(block, flat, shard):
    steps = -(-flat.shape[0] // (CHUNK * LANES))
    return pl.pallas_call(
        functools.partial(prep_kernel, block, steps),
        grid=(steps,),
        in_specs=[SMEM, pl.BlockSpec((CHUNK * LANES,), lambda i: (i,))],
        out_specs=[pl.BlockSpec((D, D), lambda i: (0, 0))] * block.boxes
        + [pl.BlockSpec((EXTRA, LANES), lambda i: (0, 0))],
        out_shape=[sds((D, D), BF)] * block.boxes + [sds((EXTRA, LANES), F32)],
        scratch_shapes=[pltpu.VMEM((MARGIN + CHUNK * steps + MARGIN, LANES), F32)],
        compiler_params=params(),
    )(shard, flat)


def spread_row(extra_ref, first, count):
    return jnp.concatenate([extra_ref[first + k : first + k + 1, :] for k in range(count)], axis=1)


def patch_row(ref, row, values):
    at = row // 16 * 16
    rows = lax.broadcasted_iota(jnp.int32, (16, values.shape[1]), 0)
    old = ref[at : at + 16, :].astype(F32)
    ref[at : at + 16, :] = jnp.where(rows == row - at, values, old).astype(BF)


def load_attn(shard, boxes, qkv_ref, proj_ref, sems):
    for wait in (False, True):
        for k, box in enumerate(boxes):
            share = jnp.bitwise_xor(shard, k)

            @pl.when(share == 3)
            def _(box=box, k=k):
                copy = pltpu.make_async_copy(box, proj_ref, sems.at[k, 0])
                copy.wait() if wait else copy.start()

            @pl.when(share != 3)
            def _(box=box, k=k, share=share):
                for part in range(3):
                    copy = pltpu.make_async_copy(
                        box.at[pl.ds(256 * part, 256), :],
                        qkv_ref.at[pl.ds(pl.multiple_of(768 * part + 256 * share, 256), 256), :],
                        sems.at[k, part],
                    )
                    copy.wait() if wait else copy.start()


def load_feed(shard, boxes, up_ref, down_ref, sems):
    for wait in (False, True):
        for k, box in enumerate(boxes):
            share = jnp.bitwise_xor(shard, k)

            @pl.when(share >= 2)
            def _(box=box, k=k, share=share):
                at = pl.multiple_of(768 * (share - 2), 256)
                copy = pltpu.make_async_copy(box, down_ref.at[pl.ds(at, 768), :], sems.at[k, 0])
                copy.wait() if wait else copy.start()

            @pl.when(share < 2)
            def _(box=box, k=k, share=share):
                for h in range(2):
                    copy = pltpu.make_async_copy(
                        box.at[pl.ds(384 * h, 384), :],
                        up_ref.at[pl.ds(pl.multiple_of(768 * h + 384 * share, 128), 384), :],
                        sems.at[k, h],
                    )
                    copy.wait() if wait else copy.start()


ANYWHERE = pl.BlockSpec(memory_space=pl.ANY)


def half_masks():
    lane = lax.broadcasted_iota(jnp.int32, (1, LANES), 1)
    return (lane < 64).astype(F32).astype(BF), (lane >= 64).astype(F32).astype(BF)


def two_heads(pair, masks):
    return jnp.concatenate([pair * masks[0], pair * masks[1]], axis=0)


def attn_forward(seq, x_ref, shard_ref, extra_ref, a0, a1, a2, a3, *refs):
    *refs, qkv_w, proj_w, vec_ref, bias_ref, sems = refs

    @pl.when(pl.program_id(0) == 0)
    def _():
        load_attn(shard_ref[0], (a0, a1, a2, a3), qkv_w, proj_w, sems)
        for part in range(3):
            patch_row(qkv_w, 768 * part + 255, spread_row(extra_ref, 12 + 6 * part, 6))
            patch_row(qkv_w, 768 * part + 512, spread_row(extra_ref, 30 + 6 * part, 6))
        vec_ref[...] = jnp.zeros_like(vec_ref)
        for row, first in enumerate((0, 6, 60, EXTRA + 0, EXTRA + 6)):
            vec_ref[row : row + 1, :] = spread_row(extra_ref, first, 6)
        bias_ref[...] = jnp.zeros_like(bias_ref)
        bias_ref[0:1, 0:768] = spread_row(extra_ref, 48, 6)
        bias_ref[0:1, 1536:2304] = spread_row(extra_ref, 54, 6)

    first_ref, qkv_ref, log_ref, att_ref, hid_ref, second_ref = refs
    x = x_ref[...].astype(F32)
    normed, _ = normed_of(x)
    first = (normed * vec_ref[0:1, :] + vec_ref[1:2, :]).astype(BF)
    first_ref[...] = first
    for part in range(3):
        cols = slice(768 * part, 768 * part + 768)
        qkv_ref[:, cols] = (dot(first, qkv_w[cols, :]) + bias_ref[0:1, cols]).astype(BF)
    masks = half_masks()
    real = lax.broadcasted_iota(jnp.int32, (2, T, T), 1) < seq
    for pair in range(HEADS // 2):
        at = LANES * pair
        q = qkv_ref[:, at : at + LANES] * jnp.asarray(0.125, BF)
        k = two_heads(qkv_ref[:, 768 + at : 768 + at + LANES], masks)
        v = two_heads(qkv_ref[:, 1536 + at : 1536 + at + LANES], masks)
        scores = dot_nt(k, q).reshape(2, T, T)
        scores = jnp.where(real, scores, -1e30)
        top = jnp.max(scores, axis=1, keepdims=True)
        weight = jnp.exp(scores - top)
        total = jnp.sum(weight, axis=1, keepdims=True)
        logs = top + jnp.log(total)
        log_ref[0, 2 * pair : 2 * pair + 1, :] = logs[0]
        log_ref[0, 2 * pair + 1 : 2 * pair + 2, :] = logs[1]
        probs = (weight * (1.0 / total)).astype(BF).reshape(2 * T, T)
        att_ref[:, at : at + LANES] = dot_tn(probs, v).astype(BF)
    hidden = x + dot(att_ref[...], proj_w[...]) + vec_ref[2:3, :]
    hid_ref[...] = hidden
    normed, _ = normed_of(hidden)
    second_ref[...] = (normed * vec_ref[3:4, :] + vec_ref[4:5, :]).astype(BF)


def call_attn_forward(seq, x, weights, boxes):
    shard, extra = weights
    rows = x.shape[0]
    images = rows // T
    made = [sds((2304, D), BF), sds((D, D), BF), sds((8, D), F32), sds((8, 2304), F32)]
    return pl.pallas_call(
        functools.partial(attn_forward, seq),
        grid=(images,),
        in_specs=[rows_of(T, D), SMEM, whole(extra)] + [ANYWHERE] * 4,
        out_specs=[
            rows_of(T, D),
            rows_of(T, 2304),
            pl.BlockSpec((1, HEADS, T), lambda i: (i, 0, 0)),
            rows_of(T, D),
            rows_of(T, D),
            rows_of(T, D),
        ]
        + [pl.BlockSpec(shape.shape, lambda i: (0, 0)) for shape in made],
        out_shape=[
            sds((rows, D), BF),
            sds((rows, 2304), BF),
            sds((images, HEADS, T), F32),
            sds((rows, D), BF),
            sds((rows, D), F32),
            sds((rows, D), BF),
        ]
        + made,
        scratch_shapes=[pltpu.SemaphoreType.DMA((4, 3))],
        compiler_params=params(),
    )(x, shard, extra, *boxes)


HALF = FF // 2
ROW_STEPS = 4


def feed(seq, part, tall, shard_ref, extra_ref, a0, a1, a2, a3, second_ref, cot_ref, result_ref, *refs):
    last = part == 1
    if last:
        before_ref, out_ref, gs_ref, *refs = refs
    else:
        out_ref, gs_ref, cot_sum, *refs = refs
    sum_ref, edge_ref, other_ref, mine_ref, up_w, down_w, bias, second_all, cot_all, act_all, pre_all, box, sems = refs
    step = pl.program_id(0)
    shard = shard_ref[0]

    @pl.when(step == 0)
    def _():
        load_feed(shard, (a0, a1, a2, a3), up_w, down_w, sems)
        for h in range(2):
            patch_row(up_w, 768 * h + 383, spread_row(extra_ref, EXTRA + 12 + 12 * h + 6 * part, 6))
            bias[0:1, 768 * h : 768 * h + 768] = spread_row(extra_ref, EXTRA + 36 + 12 * h + 6 * part, 6)
        if last:
            patch_row(down_w, 767, spread_row(extra_ref, EXTRA + 60, 6))
        sum_ref[...] = jnp.zeros_like(sum_ref)
        edge_ref[...] = jnp.zeros_like(edge_ref)
        if not last:
            cot_sum[...] = jnp.zeros_like(cot_sum)

    @pl.when(step < ROW_STEPS)
    def _():
        at = pl.ds(pl.multiple_of(step * tall, 16), tall)
        second = second_ref[...]
        cot = cot_ref[...]
        second_all[at, :] = second
        cot_all[at, :] = cot
        if last:
            result = result_ref[...]
            grad_second = before_ref[...]
        else:
            result = result_ref[...] + spread_row(extra_ref, EXTRA + 66, 6)
            grad_second = jnp.zeros_like(result)
            cot_sum[0:1, :] += jnp.sum(cot.astype(F32), axis=0, keepdims=True)
        for h in range(2):
            cols = slice(768 * h, 768 * h + 768)
            pre = dot(second, up_w[cols, :]) + bias[0:1, cols]
            grad_act = dot_nt(cot, down_w[cols, :])
            half = 0.5 * (1.0 + lax.erf(pre * root_half))
            act = (pre * half).astype(BF)
            grad_pre = grad_act * (half + pre * jnp.exp(-0.5 * pre * pre) * inv_root_tau)
            low = grad_pre.astype(BF)
            act_all[at, cols] = act
            pre_all[at, cols] = low
            sum_ref[0:1, cols] += jnp.sum(grad_pre, axis=0, keepdims=True)
            result = result + dot(act, down_w[cols, :])
            grad_second = grad_second + dot_nt(low, up_w[cols, :])
        if last:
            for image in range(tall // T):
                out_ref[image] = result[T * image : T * image + seq].astype(BF)
        else:
            out_ref[...] = result
        gs_ref[...] = grad_second

    index = step - ROW_STEPS
    side = jnp.bitwise_xor(shard // 2, index % 2)
    core = jnp.where(index >= 2, shard % 2, 1 - shard % 2)

    @pl.when((index >= 0) & (side == 0))
    def _():
        left = second_all[:, pl.ds(pl.multiple_of(384 * core, 128), 384)]
        for h in range(2):
            grad = dot_tn(left, pre_all[:, 768 * h : 768 * h + 768])
            box[384 * h : 384 * h + 384, :] = grad.astype(BF)

            @pl.when(core == 0)
            def _(grad=grad, h=h):
                edge_ref[0:1, 768 * h : 768 * h + 768] = grad[383:384]

    @pl.when((index >= 0) & (side == 1))
    def _():
        left = act_all[:, pl.ds(pl.multiple_of(768 * core, 128), 768)]
        grad = dot_tn(left, cot_all[...])
        box[...] = grad.astype(BF)

        @pl.when(core == 0)
        def _():
            edge_ref[1:2, 0:768] = grad[767:768]

    @pl.when((index >= 0) & (index < 2))
    def _():
        other_ref[0] = box[...]

    @pl.when(index >= 2)
    def _():
        mine_ref[0] = box[...]


def call_feed(seq, part, shard, extra, boxes, second, cot, result, before=None):
    rows = second.shape[0]
    images = rows // T
    tall = rows // ROW_STEPS
    last = part == 1
    row = lambda i: jnp.minimum(i, ROW_STEPS - 1)
    block = pl.BlockSpec((tall, D), lambda i: (row(i), 0))
    out = pl.BlockSpec((tall // T, seq, D), lambda i: (row(i), 0, 0)) if last else block
    grads = lambda first: pl.BlockSpec((1, D, D), lambda i: (jnp.clip(i - ROW_STEPS - first, 0, 1), 0, 0))
    small = lambda width: pl.BlockSpec((8, width), lambda i: (0, 0))
    return pl.pallas_call(
        functools.partial(feed, seq, part, tall),
        grid=(ROW_STEPS + 4,),
        in_specs=[SMEM, whole(extra)] + [ANYWHERE] * 4 + [block] * (4 if last else 3),
        out_specs=[out, block] + ([] if last else [small(D)]) + [small(HALF), small(HALF), grads(0), grads(2)],
        out_shape=[sds((images, seq, D), BF) if last else sds((rows, D), F32), sds((rows, D), F32)]
        + ([] if last else [sds((8, D), F32)])
        + [sds((8, HALF), F32), sds((8, HALF), F32), sds((2, D, D), BF), sds((2, D, D), BF)],
        scratch_shapes=[
            pltpu.VMEM((HALF, D), BF),
            pltpu.VMEM((HALF, D), BF),
            pltpu.VMEM((8, HALF), F32),
            pltpu.VMEM((rows, D), BF),
            pltpu.VMEM((rows, D), BF),
            pltpu.VMEM((rows, HALF), BF),
            pltpu.VMEM((rows, HALF), BF),
            pltpu.VMEM((D, D), BF),
            pltpu.SemaphoreType.DMA((4, 2)),
        ],
        compiler_params=params(60),
    )(shard, extra, *boxes, second, cot, result, *([before] if last else []))


WIDE = 384


def attn_backward(seq, images, group, shard_ref, log_ref, qkv_ref, first_ref, att_ref, *refs):
    step = pl.program_id(0)
    shard = shard_ref[0]
    if group == 0:
        gs_ref, hid_ref, cot_ref, vec_ref, proj_w, grad_ref, head_sum, low_ref, ga_ref, gh_ref, sum_ref, *refs = refs
    else:
        low_ref, ga_ref, grad_ref, head_sum, *refs = refs
    edge_ref, other_ref, mine_ref, grad_all, first_all, low_all, att_all, box = refs

    @pl.when(step == 0)
    def _():
        head_sum[...] = jnp.zeros_like(head_sum)
        edge_ref[...] = jnp.zeros_like(edge_ref)
        if group == 0:
            sum_ref[...] = jnp.zeros_like(sum_ref)

    @pl.when(step < images)
    def _():
        at_rows = pl.ds(pl.multiple_of(step * T, 16), T)
        first_all[at_rows, :] = first_ref[...]
        att_all[at_rows, :] = att_ref[...]
        if group == 0:
            gs = gs_ref[...]
            normed, spread = normed_of(hid_ref[...])
            gn = gs * vec_ref[3:4, :]
            gh = cot_ref[...].astype(F32) + spread * (
                gn - jnp.mean(gn, axis=-1, keepdims=True) - normed * jnp.mean(gn * normed, axis=-1, keepdims=True)
            )
            sum_ref[0:1, :] += jnp.sum(gs * normed, axis=0, keepdims=True)
            sum_ref[1:2, :] += jnp.sum(gs, axis=0, keepdims=True)
            sum_ref[2:3, :] += jnp.sum(gh, axis=0, keepdims=True)
            gh_ref[...] = gh
            gh_low = gh.astype(BF)
            low_ref[...] = gh_low
            ga_ref[...] = dot_nt(gh_low, proj_w[...]).astype(BF)
        low_all[at_rows, :] = low_ref[...]
        low = lax.broadcasted_iota(jnp.int32, (T, LANES), 1) < 64
        real = lax.broadcasted_iota(jnp.int32, (2, T, T), 1) < seq
        eighth = jnp.asarray(0.125, BF)
        masks = half_masks()
        for pair in range(3):
            at = LANES * pair
            full = WIDE * group + at
            head = 6 * group + 2 * pair
            q = qkv_ref[:, full : full + LANES] * eighth
            k = two_heads(qkv_ref[:, 768 + full : 768 + full + LANES], masks)
            v = two_heads(qkv_ref[:, 1536 + full : 1536 + full + LANES], masks)
            grad_out = ga_ref[:, at : at + LANES]
            scores = dot_nt(k, q).reshape(2, T, T)
            logs = jnp.concatenate([log_ref[0:1, head : head + 1, :], log_ref[0:1, head + 1 : head + 2, :]], axis=0)
            probs = jnp.where(real, jnp.exp(scores - logs), 0.0)
            grad_v = dot(probs.astype(BF).reshape(2 * T, T), grad_out)
            grad_probs = dot_nt(v, grad_out).reshape(2, T, T)
            delta = jnp.sum(probs * grad_probs, axis=1, keepdims=True)
            grad_scores = (probs * (grad_probs - delta)).astype(BF).reshape(2 * T, T)
            grad_k = dot(grad_scores, q)
            grads = (
                dot_tn(grad_scores, k * eighth),
                jnp.where(low, grad_k[:T], grad_k[T:]),
                jnp.where(low, grad_v[:T], grad_v[T:]),
            )
            for part, grad in enumerate(grads):
                if part != 1:
                    row = part // 2
                    head_sum[row : row + 1, at : at + LANES] += jnp.sum(grad, axis=0, keepdims=True)
                cols = slice(WIDE * part + at, WIDE * part + at + LANES)
                grad = grad.astype(BF)
                grad_ref[:, cols] = grad
                grad_all[at_rows, cols] = grad

    index = step - images
    side = jnp.bitwise_xor(shard // 2, index % 2)
    core = jnp.where(index >= 2, shard % 2, 1 - shard % 2)
    share = 2 * side + core

    @pl.when((index >= 0) & (share == 3))
    def _():
        box[...] = dot_tn(att_all[...], low_all[...]).astype(BF)

    @pl.when((index >= 0) & (share != 3))
    def _():
        grad = dot_tn(first_all[:, pl.ds(pl.multiple_of(256 * share, 256), 256)], grad_all[...])
        for part in range(3):
            cols = slice(WIDE * part, WIDE * part + WIDE)
            for u in range(2):
                box[128 * part : 128 * part + 128, WIDE * u : WIDE * u + WIDE] = grad[
                    128 * u : 128 * u + 128, cols
                ].astype(BF)

        @pl.when(share == 0)
        def _():
            edge_ref[0:1, :] = grad[255:256]

        @pl.when(share == 2)
        def _():
            edge_ref[1:2, :] = grad[0:1]

    @pl.when((index >= 0) & (index < 2))
    def _():
        other_ref[0] = box[...]

    @pl.when(index >= 2)
    def _():
        mine_ref[0] = box[...]


def call_attn_backward(seq, group, shard, log_total, qkv, first, attended, *more):
    rows = first.shape[0]
    images = rows // T
    row = lambda i: jnp.minimum(i, images - 1)
    block = lambda width, col=0: pl.BlockSpec((T, width), lambda i: (row(i), col))
    small = lambda width: pl.BlockSpec((8, width), lambda i: (0, 0))
    grads = lambda at: pl.BlockSpec((1, WIDE, D), lambda i: (jnp.clip(i - images - at, 0, 1), 0, 0))
    in_specs = [SMEM, pl.BlockSpec((1, HEADS, T), lambda i: (row(i), 0, 0)), block(2304), block(D), block(WIDE, group)]
    out_specs = [block(3 * WIDE), small(WIDE)]
    out_shape = [sds((rows, 3 * WIDE), BF), sds((8, WIDE), F32)]
    if group == 0:
        in_specs += [block(D)] * 3 + [whole(more[3]), whole(more[4])]
        out_specs += [block(D), block(D), block(D), small(D)]
        out_shape += [sds((rows, D), BF), sds((rows, D), BF), sds((rows, D), F32), sds((8, D), F32)]
    else:
        in_specs += [block(D), block(WIDE, 1)]
    return pl.pallas_call(
        functools.partial(attn_backward, seq, images, group),
        grid=(images + 4,),
        in_specs=in_specs,
        out_specs=out_specs + [small(3 * WIDE), grads(0), grads(2)],
        out_shape=out_shape + [sds((8, 3 * WIDE), F32), sds((2, WIDE, D), BF), sds((2, WIDE, D), BF)],
        scratch_shapes=[
            pltpu.VMEM((rows, 3 * WIDE), BF),
            pltpu.VMEM((rows, D), BF),
            pltpu.VMEM((rows, D), BF),
            pltpu.VMEM((rows, WIDE), BF),
            pltpu.VMEM((WIDE, D), BF),
        ],
        compiler_params=params(),
    )(shard, log_total, qkv, first, attended, *more)


def input_backward(seq, grad0, grad1, gh_ref, x_ref, vec_ref, qkv_w, out_ref, sum_ref):
    @pl.when(pl.program_id(0) == 0)
    def _():
        sum_ref[...] = jnp.zeros_like(sum_ref)

    grad_first = None
    for part in range(3):
        cols = slice(WIDE * part, WIDE * part + WIDE)
        both = jnp.concatenate([grad0[:, cols], grad1[:, cols]], axis=1)
        term = dot_nt(both, qkv_w[768 * part : 768 * part + 768, :])
        grad_first = term if part == 0 else grad_first + term
    normed, spread = normed_of(x_ref[...].astype(F32))
    gn = grad_first * vec_ref[0:1, :]
    grad = gh_ref[...] + spread * (
        gn - jnp.mean(gn, axis=-1, keepdims=True) - normed * jnp.mean(gn * normed, axis=-1, keepdims=True)
    )
    sum_ref[0:1, :] += jnp.sum(grad_first * normed, axis=0, keepdims=True)
    sum_ref[1:2, :] += jnp.sum(grad_first, axis=0, keepdims=True)
    for image in range(grad.shape[0] // T):
        out_ref[image] = grad[T * image : T * image + seq].astype(BF)


def call_input_backward(seq, grads, gh, x, vec, qkv_w):
    rows = gh.shape[0]
    images = rows // T
    step = 2 if images % 2 == 0 else 1
    tall = step * T
    return pl.pallas_call(
        functools.partial(input_backward, seq),
        grid=(images // step,),
        in_specs=[rows_of(tall, 3 * WIDE)] * 2 + [rows_of(tall, D), rows_of(tall, D), whole(vec), whole(qkv_w)],
        out_specs=[pl.BlockSpec((step, seq, D), lambda i: (i, 0, 0)), pl.BlockSpec((8, D), lambda i: (0, 0))],
        out_shape=[sds((images, seq, D), BF), sds((8, D), F32)],
        compiler_params=params(),
    )(*grads, gh, x, vec, qkv_w)


def pack(last_sum, back_sum, head0, head1, edge0, edge1, pre0, pre1, up0, up1, cot_sum, out_ref):
    out_ref[...] = jnp.zeros_like(out_ref)

    def put(first, ref, row, col, width):
        for k in range(width // LANES):
            at = col + LANES * k
            out_ref[first + k : first + k + 1, :] = ref[row : row + 1, at : at + LANES]

    put(0, last_sum, 0, 0, D)
    put(6, last_sum, 1, 0, D)
    for group, (head, edge) in enumerate(((head0, edge0), (head1, edge1))):
        for part in range(3):
            put(12 + 6 * part + 3 * group, edge, 0, WIDE * part, WIDE)
            put(30 + 6 * part + 3 * group, edge, 1, WIDE * part, WIDE)
        put(48 + 3 * group, head, 0, 0, WIDE)
        put(54 + 3 * group, head, 1, 0, WIDE)
    put(60, back_sum, 2, 0, D)
    put(EXTRA, back_sum, 0, 0, D)
    put(EXTRA + 6, back_sum, 1, 0, D)
    for j, (pre, up) in enumerate(((pre0, up0), (pre1, up1))):
        for h in range(2):
            put(EXTRA + 12 + 12 * h + 6 * j, up, 0, 768 * h, D)
            put(EXTRA + 36 + 12 * h + 6 * j, pre, 0, 768 * h, D)
    put(EXTRA + 60, up1, 1, 0, D)
    put(EXTRA + 66, cot_sum, 0, 0, D)


def call_pack(*arrays):
    return pl.pallas_call(
        pack,
        in_specs=[pl.BlockSpec(memory_space=pltpu.VMEM)] * len(arrays),
        out_specs=pl.BlockSpec(memory_space=pltpu.VMEM),
        out_shape=sds((2 * EXTRA, LANES), F32),
        compiler_params=params(),
    )(*arrays)


def adam_kernel(block, share_size, scale, boxes, shard_ref, power_ref, extra_ref, *refs):
    box_refs = refs[:boxes]
    flat_ref, mom_ref, grad_ref, change_ref, new_ref, held = refs[boxes:]
    step = pl.program_id(0)

    @pl.when(step == 0)
    def _():
        for share in range(4):

            @pl.when(shard_ref[0] == share)
            def _(share=share):
                for box, groups, box_row, col, cols, flat_row, stride in block.grad_parts(share):
                    base = MARGIN + block.start[share] + flat_row

                    def body(group, carry, box=box, box_row=box_row, col=col, cols=cols, base=base, stride=stride):
                        row = pl.multiple_of(box_row + 16 * group, 16)
                        for j in range(cols):
                            at = LANES * (col + j)
                            both = box_refs[box][pl.ds(row, 16), at : at + LANES].astype(F32)
                            to = base + 16 * stride * group + j
                            held[pl.ds(to, 8, stride=stride), :] = both[0:8]
                            held[pl.ds(to + 8 * stride, 8, stride=stride), :] = both[8:16]
                        return carry

                    lax.fori_loop(0, groups, body, 0, unroll=8)
                for source, row, length in block.put[share]:
                    held[MARGIN + row : MARGIN + row + length, :] = extra_ref[block.base + source : block.base + source + length, :]

    start = pl.multiple_of(MARGIN + CHUNK * step, 8)
    shard = shard_ref[0]
    low = lax.broadcasted_iota(jnp.int32, (CHUNK, LANES), 1) < 64
    here = held[pl.ds(start, CHUNK), :]
    after = held[pl.ds(start + 1, CHUNK), :]
    shifted = jnp.where(low, pltpu.roll(here, 64, 1), pltpu.roll(after, 64, 1))
    grad = jnp.where(shard % 2 == 1, shifted, here) * scale
    position = (
        shard * share_size
        + step * (CHUNK * LANES)
        + lax.broadcasted_iota(jnp.int32, (CHUNK, LANES), 0) * LANES
        + lax.broadcasted_iota(jnp.int32, (CHUNK, LANES), 1)
    )
    matrix = jnp.zeros((CHUNK, LANES), jnp.bool_)
    for first, end in block.matrices:
        matrix = matrix | ((position >= first) & (position < end))
    size = CHUNK * LANES
    p = flat_ref[...].reshape(CHUNK, LANES)
    m = beta_one * mom_ref[0, :].reshape(CHUNK, LANES) + (1.0 - beta_one) * grad
    s = beta_two * mom_ref[1, :].reshape(CHUNK, LANES) + (1.0 - beta_two) * grad * grad
    ratio = (m * power_ref[0]) / (jnp.sqrt(s * power_ref[1]) + adam_eps)
    change = jnp.where(matrix, rate_matrix, rate_vector) * (ratio + jnp.where(matrix, decay_matrix, 0.0) * p)
    grad_ref[...] = grad.reshape(size)
    change_ref[...] = change.reshape(size)
    new_ref[0, :] = m.reshape(size)
    new_ref[1, :] = s.reshape(size)


def adam(block, shard, powers, extra, boxes, flat, moments, scale):
    count = flat.shape[0]
    steps = -(-count // (CHUNK * LANES))
    line = pl.BlockSpec((CHUNK * LANES,), lambda i: (i,))
    two = pl.BlockSpec((2, CHUNK * LANES), lambda i: (0, i))
    return pl.pallas_call(
        functools.partial(adam_kernel, block, count, scale, len(boxes)),
        grid=(steps,),
        in_specs=[SMEM, SMEM, whole(extra)] + [whole(box) for box in boxes] + [line, two],
        out_specs=[line, line, two],
        out_shape=[sds((count,), F32), sds((count,), F32), sds((2, count), F32)],
        scratch_shapes=[pltpu.VMEM((MARGIN + CHUNK * steps + MARGIN, LANES), F32)],
        compiler_params=params(),
    )(shard, powers, extra, *boxes, flat, moments)


def swap(value, axis, bit):
    pairs = [(i, i ^ bit) for i in range(lax.axis_size(axis))]
    return lax.ppermute(value, axis, pairs)


def turn(value, axis, unit, distance):
    size = lax.axis_size(axis)
    return lax.ppermute(value, axis, [(i, (i + unit * distance) % size) for i in range(size)])


def pick(array, index, axis=0):
    return lax.dynamic_index_in_dim(array, index, axis, keepdims=False)


class Line:
    def __init__(self):
        self.last = None

    def __call__(self, step, *args):
        if self.last is not None:
            flat, tree = jax.tree.flatten(args)
            flat = lax.optimization_barrier((self.last, *flat))[1:]
            args = jax.tree.unflatten(tree, flat)
        out = step(*args)
        self.last = min(jax.tree.leaves(out), key=lambda leaf: leaf.size)
        return out


class Sum:
    def __init__(self, line, mine, other):
        self.line, self.mine = line, mine
        self.rows = mine.shape[1]
        rep = lax.axis_index("rep")
        self.near, self.far = rep % 2, rep // 2
        self.count = lax.axis_size("rep") // 2
        self.came = swap(other, "shard", 1)

    def side(self):
        send = self.line(lambda m, c: (m.astype(F32) + c.astype(F32)).astype(BF), self.mine[1], self.came[1])
        self.mine, self.here = self.mine[0], self.came[0]
        self.came = swap(send, "shard", 2)

    def close(self):
        def step(mine, here, came):
            total = mine.astype(F32) + here.astype(F32) + came.astype(F32)
            halves = total.reshape(2, self.rows // 2, D)
            return pick(halves, 1 - self.near).astype(BF), pick(halves, self.near)

        send, self.half = self.line(step, self.mine, self.here, self.came)
        self.came = swap(send, "rep", 1)

    def along(self):
        def step(half, came):
            parts = (half + came.astype(F32)).reshape(self.count, self.rows // 2 // self.count, D)
            sends = [pick(parts, (self.far + d) % self.count).astype(BF) for d in range(1, self.count)]
            return sends, pick(parts, self.far)

        sends, self.part = self.line(step, self.half, self.came)
        self.came = [turn(send, "rep", 2, d + 1) for d, send in enumerate(sends)]

    def back_along(self):
        def step(part, came):
            for value in came:
                part = part + value.astype(F32)
            return part.astype(BF)

        self.part = self.line(step, self.part, self.came)
        self.came = [turn(self.part, "rep", 2, d) for d in range(1, self.count)]

    def back_close(self):
        def step(part, came):
            full = jnp.zeros((self.count,) + part.shape, BF)
            for d, value in enumerate([part] + came):
                full = lax.dynamic_update_slice_in_dim(full, value[None], (self.far + self.count - d) % self.count, 0)
            return full.reshape(self.rows // 2, D)

        self.half = self.line(step, self.part, self.came)
        self.came = swap(self.half, "rep", 1)

    def end(self):
        def step(half, came):
            first = self.near == 0
            return jnp.concatenate([jnp.where(first, half, came), jnp.where(first, came, half)], axis=0)

        return self.line(step, self.half, self.came)


class SumAll:
    def __init__(self, line, value):
        self.line, self.value = line, value
        self.hops = [("shard", 1), ("shard", 2)]
        bit = 1
        while bit < lax.axis_size("rep"):
            self.hops.append(("rep", bit))
            bit *= 2
        self.came = swap(value, *self.hops.pop(0))

    def hop(self):
        self.value = self.line(lambda a, b: a + b, self.value, self.came)
        if self.hops:
            self.came = swap(self.value, *self.hops.pop(0))
            return False
        return True


def body(layer_input, out_cotangent, attention_params, attention_moments, feedforward_params, feedforward_moments, step_count):
    images, seq, _ = layer_input.shape
    rows = images * T
    image_total = images * lax.axis_size("shard") * lax.axis_size("rep")
    scale = 1.0 / image_total
    shard = lax.axis_index("shard").astype(jnp.int32).reshape(1)
    time = step_count[0].astype(F32)
    powers = jnp.stack([1.0 / (1.0 - jnp.power(beta_one, time)), 1.0 / (1.0 - jnp.power(beta_two, time))])
    pad = ((0, 0), (0, T - seq), (0, 0))
    padded = lambda tokens: jnp.pad(tokens, pad).reshape(rows, D)
    line = Line()

    attn_box, attn_extra = line(functools.partial(prep, ATTN), attention_params, shard)
    attn_across = swap(attn_box, "shard", 2)
    attn_near = swap(attn_box, "shard", 1)
    box0, box1, feed_extra = line(functools.partial(prep, FEED), feedforward_params, shard)
    extra = line(lambda a, b: jnp.concatenate([a, b], axis=0), attn_extra, feed_extra)
    came = swap(extra, "shard", 1)
    x = line(padded, layer_input)
    extra = line(lambda a, b: a + b, extra, came)
    came = swap(extra, "shard", 2)
    cot = line(padded, out_cotangent)
    extra = line(lambda a, b: a + b, extra, came)
    near0, near1 = swap(box0, "shard", 1), swap(box1, "shard", 1)
    across, send0 = line(lambda a, b: lax.optimization_barrier((a, b)), attn_across, box0)
    attn_both = swap(across, "shard", 1)
    across0 = swap(send0, "shard", 2)
    boxes = (attn_box, attn_near, attn_across, attn_both)
    first, qkv, log_total, attended, hidden, second, qkv_w, proj_w, vec, bias = line(
        lambda x, w, b: call_attn_forward(seq, x, w, b), x, (shard, extra), boxes
    )
    across, send1 = line(lambda a, b: lax.optimization_barrier((a, b)), across0, box1)
    both0 = swap(across, "shard", 1)
    across1 = swap(send1, "shard", 2)
    boxes = (box0, near0, across0, both0)
    result, gs, cot_sum, pre0, up0, other0, mine0 = line(
        lambda *a: call_feed(seq, 0, *a), shard, extra, boxes, second, cot, hidden
    )
    both1 = swap(line(lambda a: a, across1), "shard", 1)
    feed0 = Sum(line, mine0, other0)
    feed0.side()
    boxes = (box1, near1, across1, both1)
    layer_output, gs, pre1, up1, other1, mine1 = line(
        lambda *a: call_feed(seq, 1, *a), shard, extra, boxes, second, cot, result, gs
    )
    feed1 = Sum(line, mine1, other1)
    feed0.close()
    feed1.side()
    grad0, head0, gh_low, ga, gh, back_sum, edge0, other2, mine2 = line(
        lambda *a: call_attn_backward(seq, 0, *a), shard, log_total, qkv, first, attended, gs, hidden, cot, vec, proj_w
    )
    attn0 = Sum(line, mine2, other2)
    feed0.along()
    feed1.close()
    attn0.side()
    grad1, head1, edge1, other3, mine3 = line(
        lambda *a: call_attn_backward(seq, 1, *a), shard, log_total, qkv, first, attended, gh_low, ga
    )
    attn1 = Sum(line, mine3, other3)
    feed0.back_along()
    feed1.along()
    attn1.side()
    attn0.close()
    input_grad, last_sum = line(lambda *a: call_input_backward(seq, *a), (grad0, grad1), gh, x, vec, qkv_w)
    sums = line(call_pack, last_sum, back_sum, head0, head1, edge0, edge1, pre0, pre1, up0, up1, cot_sum)
    sums = SumAll(line, sums)
    feed0.back_close()
    feed1.back_along()
    attn0.along()
    sums.hop()
    attn1.close()
    sums.hop()
    feed1.back_close()
    attn0.back_along()
    attn1.along()
    sums.hop()
    feed_box0 = feed0.end()
    while not sums.hop():
        pass
    attn0.back_close()
    attn1.back_along()
    feed_box1 = feed1.end()
    attn_box0 = attn0.end()
    attn1.back_close()
    feed_grad, feed_change, feed_new = line(
        lambda *a: adam(FEED, *a, scale), shard, powers, sums.value, [feed_box0, feed_box1], feedforward_params, feedforward_moments
    )
    attn_grad, attn_change, attn_new = line(
        lambda *a: adam(ATTN, *a, scale), shard, powers, sums.value, [attn_box0, attn1.end()], attention_params, attention_moments
    )
    return (layer_output, input_grad, attn_grad, feed_grad, attn_change, attn_new, feed_change, feed_new)


def solution(mesh):
    tokens = P(("shard", "rep"), None, None)
    in_specs = (tokens, tokens, P("shard"), P(None, "shard"), P("shard"), P(None, "shard"), P())
    out_specs = (tokens, tokens, P("shard"), P("shard"), P("shard"), P(None, "shard"), P("shard"), P(None, "shard"))
    return jax.shard_map(body, mesh=mesh, in_specs=in_specs, out_specs=out_specs, check_vma=False)
```

```python
import functools

import jax
import jax.numpy as jnp
from jax import lax
from jax.experimental import pallas as pl
from jax.experimental.pallas import tpu as pltpu
from jax.sharding import PartitionSpec as P

D = 768
HEADS = 12
FF = 3072
T = 208

F32 = jnp.float32
BF = jnp.bfloat16

ln_eps = 1e-06
beta_one = 0.9
beta_two = 0.999
adam_eps = 1e-08
rate_matrix = 0.01
rate_vector = 0.1
decay_matrix = 0.05
root_half = 0.7071067811865476
inv_root_tau = 0.3989422804014327

MB = 1 << 20
LANES = 128
MARGIN = 8

ATTN_START = (12, 5, -3, 2)
FEED_START = (12, 2, 15, 5)


def attn_parts(share):
    if share < 3:
        return [(0, 16, 256 * part, 6 * part, 18) for part in range(3)]
    return [(0, 48, 0, 0, 6)]


def feed_parts(share):
    if share < 2:
        return [(j, 24, 384 * h, 12 * h + 6 * j, 24) for j in range(2) for h in range(2)]
    return [(j, 48, 0, 4608 * j, 6) for j in range(2)]


def attn_grad_parts(share):
    if share < 3:
        return [
            (g, 8, 128 * part, 3 * u, 3, 18 * 128 * u + 6 * part + 3 * g, 18)
            for g in range(2)
            for part in range(3)
            for u in range(2)
        ]
    return [(g, 24, 0, 0, 6, 6 * 384 * g, 6) for g in range(2)]


def feed_grad_parts(share):
    return [(box, groups, row, 0, 6, flat, stride) for box, groups, row, flat, stride in feed_parts(share)]


ATTN_EXTRA = (
    [(0, 0, 12), (12, 4602, 14)],
    [(25, 0, 5), (30, 4613, 3)],
    [(33, 0, 15), (48, 4605, 11)],
    [(58, 0, 2), (60, 4610, 6)],
)
FEED_EXTRA = (
    [(0, 0, 12), (12, 9204, 23)],
    [(34, 0, 2), (36, 9218, 9)],
    [(45, 0, 15), (60, 9225, 2)],
    [(61, 0, 5), (66, 9221, 6)],
)
ATTN_PUT = (
    [(0, 0, 12)],
    [(25, 0, 5), (30, 4613, 3)],
    [(48, 4605, 12)],
    [(58, 0, 2), (60, 4610, 6)],
)
FEED_PUT = (
    [(0, 0, 12)],
    [(34, 0, 2), (36, 9218, 9)],
    [(45, 0, 15)],
    [(61, 0, 5), (66, 9221, 6)],
)
EXTRA = 72


class Block:
    def __init__(self, base, boxes, start, parts, grad_parts, extra, put, matrices):
        self.base = base
        self.boxes, self.start, self.parts, self.grad_parts = boxes, start, parts, grad_parts
        self.extra, self.put = extra, put
        self.matrices = matrices


ATTN = Block(
    0, 1, ATTN_START, attn_parts, attn_grad_parts, ATTN_EXTRA, ATTN_PUT, ((1536, 1771008), (1772544, 2362368))
)
FEED = Block(
    EXTRA, 2, FEED_START, feed_parts, feed_grad_parts, FEED_EXTRA, FEED_PUT, ((1536, 2360832), (2363904, 4723200))
)


def params(limit=56):
    return pltpu.CompilerParams(vmem_limit_bytes=limit * MB)


def dot(a, b):
    return lax.dot_general(a, b, (((1,), (0,)), ((), ())), preferred_element_type=F32)


def dot_nt(a, b):
    return lax.dot_general(a, b, (((1,), (1,)), ((), ())), preferred_element_type=F32)


def dot_tn(a, b):
    return lax.dot_general(a, b, (((0,), (0,)), ((), ())), preferred_element_type=F32)


def normed_of(values):
    center = values - jnp.mean(values, axis=-1, keepdims=True)
    spread = lax.rsqrt(jnp.mean(center * center, axis=-1, keepdims=True) + ln_eps)
    return center * spread, spread


def whole(array):
    rank = len(array.shape)
    return pl.BlockSpec(array.shape, lambda *i: (0,) * rank, pipeline_mode=pl.Buffered(1))


def rows_of(count, width):
    return pl.BlockSpec((count, width), lambda i: (i, 0))


SMEM = pl.BlockSpec(memory_space=pltpu.SMEM)


def sds(shape, dtype):
    return jax.ShapeDtypeStruct(shape, dtype)


CHUNK = 2368


def prep_kernel(block, steps, shard_ref, flat_ref, *refs):
    *box_refs, extra_ref, held = refs
    step = pl.program_id(0)
    held[pl.ds(pl.multiple_of(MARGIN + CHUNK * step, 8), CHUNK), :] = flat_ref[...].reshape(CHUNK, LANES)

    @pl.when(step == steps - 1)
    def _():
        low = lax.broadcasted_iota(jnp.int32, (8, LANES), 1) < 64
        low_one = lax.broadcasted_iota(jnp.int32, (1, LANES), 1) < 64
        extra_ref[...] = jnp.zeros_like(extra_ref)
        for share in range(4):

            @pl.when(shard_ref[0] == share)
            def _(share=share):
                odd = share % 2 == 1

                def tile(first, stride):
                    here = held[pl.ds(first, 8, stride=stride), :]
                    if not odd:
                        return here
                    ahead = held[pl.ds(first - 1, 8, stride=stride), :]
                    return jnp.where(low, pltpu.roll(ahead, 64, 1), pltpu.roll(here, 64, 1))

                for box, groups, box_row, flat_row, stride in block.parts(share):
                    base = MARGIN + block.start[share] + flat_row

                    def body(group, carry, box=box, base=base, box_row=box_row, stride=stride):
                        for j in range(6):
                            first = base + 16 * stride * group + j
                            both = jnp.concatenate([tile(first, stride), tile(first + 8 * stride, stride)], axis=0)
                            at = pl.multiple_of(box_row + 16 * group, 16)
                            box_refs[box][pl.ds(at, 16), LANES * j : LANES * j + LANES] = both.astype(BF)
                        return carry

                    lax.fori_loop(0, groups, body, 0, unroll=8)
                count = flat_rows(block, share)
                for to, row, length in block.extra[share]:
                    for k in range(length):
                        at = MARGIN + row + k
                        value = held[at : at + 1, :]
                        if odd:
                            ahead = held[at - 1 : at, :]
                            value = jnp.where(low_one, pltpu.roll(ahead, 64, 1), pltpu.roll(value, 64, 1))
                            if row + k == 0:
                                value = jnp.where(low_one, 0.0, value)
                        elif row + k == count:
                            value = jnp.where(low_one, value, 0.0)
                        extra_ref[to + k : to + k + 1, :] = value.astype(BF).astype(F32)


def flat_rows(block, share):
    return 4615 if block is ATTN else 9226


def prep(block, flat, shard):
    steps = -(-flat.shape[0] // (CHUNK * LANES))
    return pl.pallas_call(
        functools.partial(prep_kernel, block, steps),
        grid=(steps,),
        in_specs=[SMEM, pl.BlockSpec((CHUNK * LANES,), lambda i: (i,))],
        out_specs=[pl.BlockSpec((D, D), lambda i: (0, 0))] * block.boxes
        + [pl.BlockSpec((EXTRA, LANES), lambda i: (0, 0))],
        out_shape=[sds((D, D), BF)] * block.boxes + [sds((EXTRA, LANES), F32)],
        scratch_shapes=[pltpu.VMEM((MARGIN + CHUNK * steps + MARGIN, LANES), F32)],
        compiler_params=params(),
    )(shard, flat)


def spread_row(extra_ref, first, count):
    return jnp.concatenate([extra_ref[first + k : first + k + 1, :] for k in range(count)], axis=1)


def patch_row(ref, row, values):
    at = row // 16 * 16
    rows = lax.broadcasted_iota(jnp.int32, (16, values.shape[1]), 0)
    old = ref[at : at + 16, :].astype(F32)
    ref[at : at + 16, :] = jnp.where(rows == row - at, values, old).astype(BF)


def load_attn(shard, boxes, qkv_ref, proj_ref, sems):
    for wait in (False, True):
        for k, box in enumerate(boxes):
            share = jnp.bitwise_xor(shard, k)

            @pl.when(share == 3)
            def _(box=box, k=k):
                copy = pltpu.make_async_copy(box, proj_ref, sems.at[k, 0])
                copy.wait() if wait else copy.start()

            @pl.when(share != 3)
            def _(box=box, k=k, share=share):
                for part in range(3):
                    copy = pltpu.make_async_copy(
                        box.at[pl.ds(256 * part, 256), :],
                        qkv_ref.at[pl.ds(pl.multiple_of(768 * part + 256 * share, 256), 256), :],
                        sems.at[k, part],
                    )
                    copy.wait() if wait else copy.start()


def load_feed(shard, boxes, up_ref, down_ref, sems):
    for wait in (False, True):
        for k, box in enumerate(boxes):
            share = jnp.bitwise_xor(shard, k)

            @pl.when(share >= 2)
            def _(box=box, k=k, share=share):
                at = pl.multiple_of(768 * (share - 2), 256)
                copy = pltpu.make_async_copy(box, down_ref.at[pl.ds(at, 768), :], sems.at[k, 0])
                copy.wait() if wait else copy.start()

            @pl.when(share < 2)
            def _(box=box, k=k, share=share):
                for h in range(2):
                    copy = pltpu.make_async_copy(
                        box.at[pl.ds(384 * h, 384), :],
                        up_ref.at[pl.ds(pl.multiple_of(768 * h + 384 * share, 128), 384), :],
                        sems.at[k, h],
                    )
                    copy.wait() if wait else copy.start()


ANYWHERE = pl.BlockSpec(memory_space=pl.ANY)


def half_masks():
    lane = lax.broadcasted_iota(jnp.int32, (1, LANES), 1)
    return (lane < 64).astype(F32).astype(BF), (lane >= 64).astype(F32).astype(BF)


def two_heads(pair, masks):
    return jnp.concatenate([pair * masks[0], pair * masks[1]], axis=0)


def attn_forward(seq, x_ref, shard_ref, extra_ref, a0, a1, a2, a3, *refs):
    *refs, qkv_w, proj_w, vec_ref, bias_ref, sems = refs

    @pl.when(pl.program_id(0) == 0)
    def _():
        load_attn(shard_ref[0], (a0, a1, a2, a3), qkv_w, proj_w, sems)
        for part in range(3):
            patch_row(qkv_w, 768 * part + 255, spread_row(extra_ref, 12 + 6 * part, 6))
            patch_row(qkv_w, 768 * part + 512, spread_row(extra_ref, 30 + 6 * part, 6))
        vec_ref[...] = jnp.zeros_like(vec_ref)
        for row, first in enumerate((0, 6, 60, EXTRA + 0, EXTRA + 6)):
            vec_ref[row : row + 1, :] = spread_row(extra_ref, first, 6)
        bias_ref[...] = jnp.zeros_like(bias_ref)
        bias_ref[0:1, 0:768] = spread_row(extra_ref, 48, 6)
        bias_ref[0:1, 1536:2304] = spread_row(extra_ref, 54, 6)

    first_ref, qkv_ref, log_ref, att_ref, hid_ref, second_ref = refs
    x = x_ref[...].astype(F32)
    normed, _ = normed_of(x)
    first = (normed * vec_ref[0:1, :] + vec_ref[1:2, :]).astype(BF)
    first_ref[...] = first
    for part in range(3):
        cols = slice(768 * part, 768 * part + 768)
        qkv_ref[:, cols] = (dot(first, qkv_w[cols, :]) + bias_ref[0:1, cols]).astype(BF)
    masks = half_masks()
    real = lax.broadcasted_iota(jnp.int32, (2, T, T), 1) < seq
    for pair in range(HEADS // 2):
        at = LANES * pair
        q = qkv_ref[:, at : at + LANES] * jnp.asarray(0.125, BF)
        k = two_heads(qkv_ref[:, 768 + at : 768 + at + LANES], masks)
        v = two_heads(qkv_ref[:, 1536 + at : 1536 + at + LANES], masks)
        scores = dot_nt(k, q).reshape(2, T, T)
        scores = jnp.where(real, scores, -1e30)
        top = jnp.max(scores, axis=1, keepdims=True)
        weight = jnp.exp(scores - top)
        total = jnp.sum(weight, axis=1, keepdims=True)
        logs = top + jnp.log(total)
        log_ref[0, 2 * pair : 2 * pair + 1, :] = logs[0]
        log_ref[0, 2 * pair + 1 : 2 * pair + 2, :] = logs[1]
        probs = (weight * (1.0 / total)).astype(BF).reshape(2 * T, T)
        att_ref[:, at : at + LANES] = dot_tn(probs, v).astype(BF)
    hidden = x + dot(att_ref[...], proj_w[...]) + vec_ref[2:3, :]
    hid_ref[...] = hidden
    normed, _ = normed_of(hidden)
    second_ref[...] = (normed * vec_ref[3:4, :] + vec_ref[4:5, :]).astype(BF)


def call_attn_forward(seq, x, weights, boxes):
    shard, extra = weights
    rows = x.shape[0]
    images = rows // T
    made = [sds((2304, D), BF), sds((D, D), BF), sds((8, D), F32), sds((8, 2304), F32)]
    return pl.pallas_call(
        functools.partial(attn_forward, seq),
        grid=(images,),
        in_specs=[rows_of(T, D), SMEM, whole(extra)] + [ANYWHERE] * 4,
        out_specs=[
            rows_of(T, D),
            rows_of(T, 2304),
            pl.BlockSpec((1, HEADS, T), lambda i: (i, 0, 0)),
            rows_of(T, D),
            rows_of(T, D),
            rows_of(T, D),
        ]
        + [pl.BlockSpec(shape.shape, lambda i: (0, 0)) for shape in made],
        out_shape=[
            sds((rows, D), BF),
            sds((rows, 2304), BF),
            sds((images, HEADS, T), F32),
            sds((rows, D), BF),
            sds((rows, D), F32),
            sds((rows, D), BF),
        ]
        + made,
        scratch_shapes=[pltpu.SemaphoreType.DMA((4, 3))],
        compiler_params=params(),
    )(x, shard, extra, *boxes)


def hand_out(index, box, outs, sems):
    copies = [pltpu.make_async_copy(box.at[k], out, sems.at[k]) for k, out in enumerate(outs)]
    for k, copy in enumerate(copies):

        @pl.when(index == k)
        def _(copy=copy):
            copy.start()

    @pl.when(index == len(outs) - 1)
    def _():
        for copy in copies:
            copy.wait()


HALF = FF // 2
ROW_STEPS = 4


def feed(seq, part, tall, shard_ref, extra_ref, a0, a1, a2, a3, second_ref, cot_ref, result_ref, *refs):
    last = part == 1
    if last:
        before_ref, out_ref, gs_ref, *refs = refs
    else:
        out_ref, gs_ref, cot_sum, *refs = refs
    sum_ref, edge_ref, *outs, up_w, down_w, bias, second_all, cot_all, act_all, pre_all, box, sems, box_sems = refs
    step = pl.program_id(0)
    shard = shard_ref[0]

    @pl.when(step == 0)
    def _():
        load_feed(shard, (a0, a1, a2, a3), up_w, down_w, sems)
        for h in range(2):
            patch_row(up_w, 768 * h + 383, spread_row(extra_ref, EXTRA + 12 + 12 * h + 6 * part, 6))
            bias[0:1, 768 * h : 768 * h + 768] = spread_row(extra_ref, EXTRA + 36 + 12 * h + 6 * part, 6)
        if last:
            patch_row(down_w, 767, spread_row(extra_ref, EXTRA + 60, 6))
        sum_ref[...] = jnp.zeros_like(sum_ref)
        edge_ref[...] = jnp.zeros_like(edge_ref)
        if not last:
            cot_sum[...] = jnp.zeros_like(cot_sum)

    @pl.when(step < ROW_STEPS)
    def _():
        at = pl.ds(pl.multiple_of(step * tall, 16), tall)
        second = second_ref[...]
        cot = cot_ref[...]
        second_all[at, :] = second
        cot_all[at, :] = cot
        if last:
            result = result_ref[...]
            grad_second = before_ref[...]
        else:
            result = result_ref[...] + spread_row(extra_ref, EXTRA + 66, 6)
            grad_second = jnp.zeros_like(result)
            cot_sum[0:1, :] += jnp.sum(cot.astype(F32), axis=0, keepdims=True)
        for h in range(2):
            cols = slice(768 * h, 768 * h + 768)
            pre = dot(second, up_w[cols, :]) + bias[0:1, cols]
            grad_act = dot_nt(cot, down_w[cols, :])
            half = 0.5 * (1.0 + lax.erf(pre * root_half))
            act = (pre * half).astype(BF)
            grad_pre = grad_act * (half + pre * jnp.exp(-0.5 * pre * pre) * inv_root_tau)
            low = grad_pre.astype(BF)
            act_all[at, cols] = act
            pre_all[at, cols] = low
            sum_ref[0:1, cols] += jnp.sum(grad_pre, axis=0, keepdims=True)
            result = result + dot(act, down_w[cols, :])
            grad_second = grad_second + dot_nt(low, up_w[cols, :])
        if last:
            for image in range(tall // T):
                out_ref[image] = result[T * image : T * image + seq].astype(BF)
        else:
            out_ref[...] = result
        gs_ref[...] = grad_second

    index = step - ROW_STEPS
    side = jnp.bitwise_xor(shard // 2, 1 - index % 2)
    core = jnp.where(index >= 2, shard % 2, 1 - shard % 2)

    @pl.when((index >= 0) & (side == 0))
    def _():
        left = second_all[:, pl.ds(pl.multiple_of(384 * core, 128), 384)]
        for h in range(2):
            grad = dot_tn(left, pre_all[:, 768 * h : 768 * h + 768])
            box[index, 384 * h : 384 * h + 384, :] = grad.astype(BF)

            @pl.when(core == 0)
            def _(grad=grad, h=h):
                edge_ref[0:1, 768 * h : 768 * h + 768] = grad[383:384]

    @pl.when((index >= 0) & (side == 1))
    def _():
        left = act_all[:, pl.ds(pl.multiple_of(768 * core, 128), 768)]
        grad = dot_tn(left, cot_all[...])
        box[index] = grad.astype(BF)

        @pl.when(core == 0)
        def _():
            edge_ref[1:2, 0:768] = grad[767:768]

    hand_out(index, box, outs, box_sems)


def call_feed(seq, part, shard, extra, boxes, second, cot, result, before=None):
    rows = second.shape[0]
    images = rows // T
    tall = rows // ROW_STEPS
    last = part == 1
    row = lambda i: jnp.minimum(i, ROW_STEPS - 1)
    block = pl.BlockSpec((tall, D), lambda i: (row(i), 0))
    out = pl.BlockSpec((tall // T, seq, D), lambda i: (row(i), 0, 0)) if last else block
    small = lambda width: pl.BlockSpec((8, width), lambda i: (0, 0))
    return pl.pallas_call(
        functools.partial(feed, seq, part, tall),
        grid=(ROW_STEPS + 4,),
        in_specs=[SMEM, whole(extra)] + [ANYWHERE] * 4 + [block] * (4 if last else 3),
        out_specs=[out, block] + ([] if last else [small(D)]) + [small(HALF), small(HALF)] + [ANYWHERE] * 4,
        out_shape=[sds((images, seq, D), BF) if last else sds((rows, D), F32), sds((rows, D), F32)]
        + ([] if last else [sds((8, D), F32)])
        + [sds((8, HALF), F32), sds((8, HALF), F32)] + [sds((D, D), BF)] * 4,
        scratch_shapes=[
            pltpu.VMEM((HALF, D), BF),
            pltpu.VMEM((HALF, D), BF),
            pltpu.VMEM((8, HALF), F32),
            pltpu.VMEM((rows, D), BF),
            pltpu.VMEM((rows, D), BF),
            pltpu.VMEM((rows, HALF), BF),
            pltpu.VMEM((rows, HALF), BF),
            pltpu.VMEM((4, D, D), BF),
            pltpu.SemaphoreType.DMA((4, 2)),
            pltpu.SemaphoreType.DMA((4,)),
        ],
        compiler_params=params(60),
    )(shard, extra, *boxes, second, cot, result, *([before] if last else []))


WIDE = 384


def attn_backward(seq, group, base, count, last, shard_ref, log_ref, qkv_ref, first_ref, att_ref, *refs):
    step = pl.program_id(0)
    shard = shard_ref[0]
    if group == 0:
        gs_ref, hid_ref, cot_ref, vec_ref, proj_w, *refs = refs
    else:
        low_ref, ga_ref, *refs = refs
    if last:
        if group == 0:
            head_before, sum_before, first_any, att_any, low_any, grad_any, _, _, *refs = refs
        else:
            head_before, first_any, att_any, low_any, grad_any, *refs = refs
    grad_ref, head_sum, *refs = refs
    if group == 0:
        low_ref, ga_ref, gh_ref, sum_ref, *refs = refs
    if last:
        edge_ref, *outs, grad_all, first_all, low_all, att_all, box, box_sems, load_sems = refs
        done = pl.ds(0, base * T)
        loads = [
            pltpu.make_async_copy(grad_any.at[done], grad_all.at[done], load_sems.at[0]),
            pltpu.make_async_copy(first_any.at[done], first_all.at[done], load_sems.at[1]),
            pltpu.make_async_copy(low_any.at[done], low_all.at[done], load_sems.at[2]),
            pltpu.make_async_copy(
                att_any.at[done, pl.ds(WIDE * group, WIDE)], att_all.at[done], load_sems.at[3]
            ),
        ]

    @pl.when(step == 0)
    def _():
        if last:
            for load in loads:
                load.start()
            edge_ref[...] = jnp.zeros_like(edge_ref)
            head_sum[...] = head_before[...]
        else:
            head_sum[...] = jnp.zeros_like(head_sum)
        if group == 0:
            sum_ref[...] = sum_before[...] if last else jnp.zeros_like(sum_ref)

    @pl.when(step < count)
    def _():
        at_rows = pl.ds(pl.multiple_of((step + base) * T, 16), T)
        if last:
            first_all[at_rows, :] = first_ref[...]
            att_all[at_rows, :] = att_ref[...]
        if group == 0:
            gs = gs_ref[...]
            normed, spread = normed_of(hid_ref[...])
            gn = gs * vec_ref[3:4, :]
            gh = cot_ref[...].astype(F32) + spread * (
                gn - jnp.mean(gn, axis=-1, keepdims=True) - normed * jnp.mean(gn * normed, axis=-1, keepdims=True)
            )
            sum_ref[0:1, :] += jnp.sum(gs * normed, axis=0, keepdims=True)
            sum_ref[1:2, :] += jnp.sum(gs, axis=0, keepdims=True)
            sum_ref[2:3, :] += jnp.sum(gh, axis=0, keepdims=True)
            gh_ref[...] = gh
            gh_low = gh.astype(BF)
            low_ref[...] = gh_low
            ga_ref[...] = dot_nt(gh_low, proj_w[...]).astype(BF)
        if last:
            low_all[at_rows, :] = low_ref[...]
        low = lax.broadcasted_iota(jnp.int32, (T, LANES), 1) < 64
        real = lax.broadcasted_iota(jnp.int32, (2, T, T), 1) < seq
        eighth = jnp.asarray(0.125, BF)
        masks = half_masks()
        for pair in range(3):
            at = LANES * pair
            full = WIDE * group + at
            head = 6 * group + 2 * pair
            q = qkv_ref[:, full : full + LANES] * eighth
            k = two_heads(qkv_ref[:, 768 + full : 768 + full + LANES], masks)
            v = two_heads(qkv_ref[:, 1536 + full : 1536 + full + LANES], masks)
            grad_out = ga_ref[:, at : at + LANES]
            scores = dot_nt(k, q).reshape(2, T, T)
            logs = jnp.concatenate([log_ref[0:1, head : head + 1, :], log_ref[0:1, head + 1 : head + 2, :]], axis=0)
            probs = jnp.where(real, jnp.exp(scores - logs), 0.0)
            grad_v = dot(probs.astype(BF).reshape(2 * T, T), grad_out)
            grad_probs = dot_nt(v, grad_out).reshape(2, T, T)
            delta = jnp.sum(probs * grad_probs, axis=1, keepdims=True)
            grad_scores = (probs * (grad_probs - delta)).astype(BF).reshape(2 * T, T)
            grad_k = dot(grad_scores, q)
            grads = (
                dot_tn(grad_scores, k * eighth),
                jnp.where(low, grad_k[:T], grad_k[T:]),
                jnp.where(low, grad_v[:T], grad_v[T:]),
            )
            for part, grad in enumerate(grads):
                if part != 1:
                    row = part // 2
                    head_sum[row : row + 1, at : at + LANES] += jnp.sum(grad, axis=0, keepdims=True)
                cols = slice(WIDE * part + at, WIDE * part + at + LANES)
                grad = grad.astype(BF)
                grad_ref[:, cols] = grad
                if last:
                    grad_all[at_rows, cols] = grad

    if not last:
        return

    @pl.when(step == count)
    def _():
        for load in loads:
            load.wait()

    index = step - count
    side = jnp.bitwise_xor(shard // 2, 1 - index % 2)
    core = jnp.where(index >= 2, shard % 2, 1 - shard % 2)
    share = 2 * side + core

    @pl.when((index >= 0) & (share == 3))
    def _():
        box[index] = dot_tn(att_all[...], low_all[...]).astype(BF)

    @pl.when((index >= 0) & (share != 3))
    def _():
        grad = dot_tn(first_all[:, pl.ds(pl.multiple_of(256 * share, 256), 256)], grad_all[...])
        for part in range(3):
            cols = slice(WIDE * part, WIDE * part + WIDE)
            for u in range(2):
                box[index, 128 * part : 128 * part + 128, WIDE * u : WIDE * u + WIDE] = grad[
                    128 * u : 128 * u + 128, cols
                ].astype(BF)

        @pl.when(share == 0)
        def _():
            edge_ref[0:1, :] = grad[255:256]

        @pl.when(share == 2)
        def _():
            edge_ref[1:2, :] = grad[0:1]

    hand_out(index, box, outs, box_sems)


def call_attn_backward(seq, group, base, count, shard, log_total, qkv, first, attended, *more, before=()):
    rows = first.shape[0]
    last = len(before) > 0
    row = lambda i: jnp.minimum(i, count - 1) + base
    block = lambda width, col=0: pl.BlockSpec((T, width), lambda i: (row(i), col))
    small = lambda width: pl.BlockSpec((8, width), lambda i: (0, 0))
    in_specs = [SMEM, pl.BlockSpec((1, HEADS, T), lambda i: (row(i), 0, 0)), block(2304), block(D), block(WIDE, group)]
    out_specs = [block(3 * WIDE), small(WIDE)]
    out_shape = [sds((rows, 3 * WIDE), BF), sds((8, WIDE), F32)]
    if group == 0:
        in_specs += [block(D)] * 3 + [whole(more[3]), whole(more[4])]
        out_specs += [block(D), block(D), block(D), small(D)]
        out_shape += [sds((rows, D), BF), sds((rows, D), BF), sds((rows, D), F32), sds((8, D), F32)]
    else:
        in_specs += [block(D), block(WIDE, 1)]
    aliases, scratch, extra = {}, [], []
    if last:
        at = len(in_specs)
        if group == 0:
            grad, head, low, ga, gh, total = before
            extra = [head, total, first, attended, low, grad, ga, gh]
            in_specs += [whole(head), whole(total)] + [ANYWHERE] * 6
            aliases = {at + 4: 2, at + 5: 0, at + 6: 3, at + 7: 4}
        else:
            grad, head = before
            extra = [head, first, attended, more[0], grad]
            in_specs += [whole(head)] + [ANYWHERE] * 4
            aliases = {at + 4: 0}
        out_specs += [small(3 * WIDE)] + [ANYWHERE] * 4
        out_shape += [sds((8, 3 * WIDE), F32)] + [sds((WIDE, D), BF)] * 4
        scratch = [
            pltpu.VMEM((rows, 3 * WIDE), BF),
            pltpu.VMEM((rows, D), BF),
            pltpu.VMEM((rows, D), BF),
            pltpu.VMEM((rows, WIDE), BF),
            pltpu.VMEM((4, WIDE, D), BF),
            pltpu.SemaphoreType.DMA((4,)),
            pltpu.SemaphoreType.DMA((4,)),
        ]
    return pl.pallas_call(
        functools.partial(attn_backward, seq, group, base, count, last),
        grid=(count + 4 if last else count,),
        in_specs=in_specs,
        out_specs=out_specs,
        out_shape=out_shape,
        input_output_aliases=aliases,
        scratch_shapes=scratch,
        compiler_params=params(),
    )(shard, log_total, qkv, first, attended, *more, *extra)


def input_backward(seq, grad0, grad1, gh_ref, x_ref, vec_ref, qkv_w, out_ref, sum_ref):
    @pl.when(pl.program_id(0) == 0)
    def _():
        sum_ref[...] = jnp.zeros_like(sum_ref)

    grad_first = None
    for part in range(3):
        cols = slice(WIDE * part, WIDE * part + WIDE)
        both = jnp.concatenate([grad0[:, cols], grad1[:, cols]], axis=1)
        term = dot_nt(both, qkv_w[768 * part : 768 * part + 768, :])
        grad_first = term if part == 0 else grad_first + term
    normed, spread = normed_of(x_ref[...].astype(F32))
    gn = grad_first * vec_ref[0:1, :]
    grad = gh_ref[...] + spread * (
        gn - jnp.mean(gn, axis=-1, keepdims=True) - normed * jnp.mean(gn * normed, axis=-1, keepdims=True)
    )
    sum_ref[0:1, :] += jnp.sum(grad_first * normed, axis=0, keepdims=True)
    sum_ref[1:2, :] += jnp.sum(grad_first, axis=0, keepdims=True)
    for image in range(grad.shape[0] // T):
        out_ref[image] = grad[T * image : T * image + seq].astype(BF)


def call_input_backward(seq, grads, gh, x, vec, qkv_w):
    rows = gh.shape[0]
    images = rows // T
    step = 2 if images % 2 == 0 else 1
    tall = step * T
    return pl.pallas_call(
        functools.partial(input_backward, seq),
        grid=(images // step,),
        in_specs=[rows_of(tall, 3 * WIDE)] * 2 + [rows_of(tall, D), rows_of(tall, D), whole(vec), whole(qkv_w)],
        out_specs=[pl.BlockSpec((step, seq, D), lambda i: (i, 0, 0)), pl.BlockSpec((8, D), lambda i: (0, 0))],
        out_shape=[sds((images, seq, D), BF), sds((8, D), F32)],
        compiler_params=params(),
    )(*grads, gh, x, vec, qkv_w)


def putter(out_ref):
    out_ref[...] = jnp.zeros_like(out_ref)

    def put(first, ref, row, col, width):
        for k in range(width // LANES):
            at = col + LANES * k
            out_ref[first + k : first + k + 1, :] = ref[row : row + 1, at : at + LANES]

    return put


def pack(last_sum, back_sum, head0, head1, edge0, edge1, pre0, pre1, up0, up1, cot_sum, out_ref):
    put = putter(out_ref)
    put(0, last_sum, 0, 0, D)
    put(6, last_sum, 1, 0, D)
    for group, (head, edge) in enumerate(((head0, edge0), (head1, edge1))):
        for part in range(3):
            put(12 + 6 * part + 3 * group, edge, 0, WIDE * part, WIDE)
            put(30 + 6 * part + 3 * group, edge, 1, WIDE * part, WIDE)
        put(48 + 3 * group, head, 0, 0, WIDE)
        put(54 + 3 * group, head, 1, 0, WIDE)
    put(60, back_sum, 2, 0, D)
    put(EXTRA, back_sum, 0, 0, D)
    put(EXTRA + 6, back_sum, 1, 0, D)
    for j, (pre, up) in enumerate(((pre0, up0), (pre1, up1))):
        for h in range(2):
            put(EXTRA + 12 + 12 * h + 6 * j, up, 0, 768 * h, D)
            put(EXTRA + 36 + 12 * h + 6 * j, pre, 0, 768 * h, D)
    put(EXTRA + 60, up1, 1, 0, D)
    put(EXTRA + 66, cot_sum, 0, 0, D)


def call_pack(*arrays):
    return pl.pallas_call(
        pack,
        in_specs=[pl.BlockSpec(memory_space=pltpu.VMEM)] * len(arrays),
        out_specs=pl.BlockSpec(memory_space=pltpu.VMEM),
        out_shape=sds((2 * EXTRA, LANES), F32),
        compiler_params=params(),
    )(*arrays)


def adam_kernel(block, share_size, scale, boxes, shard_ref, power_ref, extra_ref, *refs):
    box_refs = refs[:boxes]
    flat_ref, mom_ref, grad_ref, change_ref, new_ref, held = refs[boxes:]
    step = pl.program_id(0)

    @pl.when(step == 0)
    def _():
        for share in range(4):

            @pl.when(shard_ref[0] == share)
            def _(share=share):
                for box, groups, box_row, col, cols, flat_row, stride in block.grad_parts(share):
                    base = MARGIN + block.start[share] + flat_row

                    def body(group, carry, box=box, box_row=box_row, col=col, cols=cols, base=base, stride=stride):
                        row = pl.multiple_of(box_row + 16 * group, 16)
                        for j in range(cols):
                            at = LANES * (col + j)
                            both = box_refs[box][pl.ds(row, 16), at : at + LANES].astype(F32)
                            to = base + 16 * stride * group + j
                            held[pl.ds(to, 8, stride=stride), :] = both[0:8]
                            held[pl.ds(to + 8 * stride, 8, stride=stride), :] = both[8:16]
                        return carry

                    lax.fori_loop(0, groups, body, 0, unroll=8)
                for source, row, length in block.put[share]:
                    held[MARGIN + row : MARGIN + row + length, :] = extra_ref[block.base + source : block.base + source + length, :]

    start = pl.multiple_of(MARGIN + CHUNK * step, 8)
    shard = shard_ref[0]
    low = lax.broadcasted_iota(jnp.int32, (CHUNK, LANES), 1) < 64
    here = held[pl.ds(start, CHUNK), :]
    after = held[pl.ds(start + 1, CHUNK), :]
    shifted = jnp.where(low, pltpu.roll(here, 64, 1), pltpu.roll(after, 64, 1))
    grad = jnp.where(shard % 2 == 1, shifted, here) * scale
    position = (
        shard * share_size
        + step * (CHUNK * LANES)
        + lax.broadcasted_iota(jnp.int32, (CHUNK, LANES), 0) * LANES
        + lax.broadcasted_iota(jnp.int32, (CHUNK, LANES), 1)
    )
    matrix = jnp.zeros((CHUNK, LANES), jnp.bool_)
    for first, end in block.matrices:
        matrix = matrix | ((position >= first) & (position < end))
    size = CHUNK * LANES
    p = flat_ref[...].reshape(CHUNK, LANES)
    m = beta_one * mom_ref[0, :].reshape(CHUNK, LANES) + (1.0 - beta_one) * grad
    s = beta_two * mom_ref[1, :].reshape(CHUNK, LANES) + (1.0 - beta_two) * grad * grad
    ratio = (m * power_ref[0]) / (jnp.sqrt(s * power_ref[1]) + adam_eps)
    change = jnp.where(matrix, rate_matrix, rate_vector) * (ratio + jnp.where(matrix, decay_matrix, 0.0) * p)
    grad_ref[...] = grad.reshape(size)
    change_ref[...] = change.reshape(size)
    new_ref[0, :] = m.reshape(size)
    new_ref[1, :] = s.reshape(size)


def adam(block, shard, powers, extra, boxes, flat, moments, scale):
    count = flat.shape[0]
    steps = -(-count // (CHUNK * LANES))
    line = pl.BlockSpec((CHUNK * LANES,), lambda i: (i,))
    two = pl.BlockSpec((2, CHUNK * LANES), lambda i: (0, i))
    return pl.pallas_call(
        functools.partial(adam_kernel, block, count, scale, len(boxes)),
        grid=(steps,),
        in_specs=[SMEM, SMEM, whole(extra)] + [whole(box) for box in boxes] + [line, two],
        out_specs=[line, line, two],
        out_shape=[sds((count,), F32), sds((count,), F32), sds((2, count), F32)],
        scratch_shapes=[pltpu.VMEM((MARGIN + CHUNK * steps + MARGIN, LANES), F32)],
        compiler_params=params(),
    )(shard, powers, extra, *boxes, flat, moments)


def swap(value, axis, bit):
    pairs = [(i, i ^ bit) for i in range(lax.axis_size(axis))]
    return lax.ppermute(value, axis, pairs)


def turn(value, axis, unit, distance):
    size = lax.axis_size(axis)
    return lax.ppermute(value, axis, [(i, (i + unit * distance) % size) for i in range(size)])


def pick(array, index, axis=0):
    return lax.dynamic_index_in_dim(array, index, axis, keepdims=False)


class Line:
    def __init__(self):
        self.last = None

    def __call__(self, step, *args):
        if self.last is not None:
            flat, tree = jax.tree.flatten(args)
            flat = lax.optimization_barrier((self.last, *flat))[1:]
            args = jax.tree.unflatten(tree, flat)
        out = step(*args)
        self.last = min(jax.tree.leaves(out), key=lambda leaf: leaf.size)
        return out


def pause_kernel(in_ref, out_ref):
    out_ref[...] = in_ref[...]


def pause(line, value):
    return line(
        pl.pallas_call(
            pause_kernel,
            out_shape=sds(value.shape, value.dtype),
            cost_estimate=pl.CostEstimate(flops=10**11, bytes_accessed=10**8, transcendentals=0),
        ),
        value,
    )


class Sum:
    def __init__(self, line, across, same, mine_across, mine):
        self.line, self.mine_across, self.mine = line, mine_across, mine
        self.rows = mine.shape[0]
        rep = lax.axis_index("rep")
        self.near, self.far = rep % 2, rep // 2
        self.count = lax.axis_size("rep") // 2
        self.came_across, self.here = swap(across, "shard", 1), swap(same, "shard", 1)

    def side(self):
        add = lambda a, b: a.astype(F32) + b.astype(F32)
        send = self.line(lambda a, b: add(a, b).astype(BF), self.mine_across, self.came_across)
        self.came = swap(send, "shard", 2)
        self.mine = self.line(add, self.mine, self.here)

    def close(self):
        def step(mine, came):
            halves = (mine + came.astype(F32)).reshape(2, self.rows // 2, D)
            return pick(halves, 1 - self.near).astype(BF), pick(halves, self.near)

        send, self.half = self.line(step, self.mine, self.came)
        self.came = swap(send, "rep", 1)

    def level(self, bit):
        if bit == 2:
            self.part = self.line(lambda a, b: (a + b.astype(F32)).astype(BF), self.half, self.came)
        else:
            self.part = self.line(lambda a, b: (a.astype(F32) + b.astype(F32)).astype(BF), self.part, self.came)
        self.came = swap(self.part, "rep", bit)

    def back_level(self):
        self.half = self.line(lambda a, b: (a.astype(F32) + b.astype(F32)).astype(BF), self.part, self.came)
        self.came = swap(self.half, "rep", 1)

    def along(self):
        def step(half, came):
            parts = (half + came.astype(F32)).reshape(self.count, self.rows // 2 // self.count, D)
            sends = [pick(parts, (self.far + d) % self.count).astype(BF) for d in range(1, self.count)]
            return sends, pick(parts, self.far)

        sends, self.part = self.line(step, self.half, self.came)
        self.came = [turn(send, "rep", 2, d + 1) for d, send in enumerate(sends)]

    def back_along(self):
        def step(part, came):
            for value in came:
                part = part + value.astype(F32)
            return part.astype(BF)

        self.part = self.line(step, self.part, self.came)
        self.came = [turn(self.part, "rep", 2, d) for d in range(1, self.count)]

    def gather(self):
        def step(part, came):
            for value in came:
                part = part + value.astype(F32)
            return part.astype(BF)

        self.part = self.line(step, self.part, self.came)
        self.came = lax.all_gather(self.part, "rep", axis=0, tiled=True)

    def gathered(self):
        def step(came):
            parts = came.reshape(self.count, 2, self.rows // 2 // self.count, D)
            return jnp.swapaxes(parts, 0, 1).reshape(self.rows, D)

        return self.line(step, self.came)

    def back_close(self):
        def step(part, came):
            full = jnp.zeros((self.count,) + part.shape, BF)
            for d, value in enumerate([part] + came):
                full = lax.dynamic_update_slice_in_dim(full, value[None], (self.far + self.count - d) % self.count, 0)
            return full.reshape(self.rows // 2, D)

        self.half = self.line(step, self.part, self.came)
        self.came = swap(self.half, "rep", 1)

    def end(self):
        def step(half, came):
            first = self.near == 0
            return jnp.concatenate([jnp.where(first, half, came), jnp.where(first, came, half)], axis=0)

        return self.line(step, self.half, self.came)


class SumAll:
    def __init__(self, line, value):
        self.line, self.value = line, value
        self.hops = [("shard", 1), ("shard", 2)]
        bit = 2
        while bit < lax.axis_size("rep"):
            self.hops.append(("rep", bit))
            bit *= 2
        self.hops.append(("rep", 1))
        self.came = swap(value, *self.hops.pop(0))

    def hop(self):
        self.value = self.line(lambda a, b: a + b, self.value, self.came)
        if self.hops:
            self.came = swap(self.value, *self.hops.pop(0))
            return False
        return True


def body(layer_input, out_cotangent, attention_params, attention_moments, feedforward_params, feedforward_moments, step_count):
    images, seq, _ = layer_input.shape
    rows = images * T
    image_total = images * lax.axis_size("shard") * lax.axis_size("rep")
    scale = 1.0 / image_total
    shard = lax.axis_index("shard").astype(jnp.int32).reshape(1)
    time = step_count[0].astype(F32)
    powers = jnp.stack([1.0 / (1.0 - jnp.power(beta_one, time)), 1.0 / (1.0 - jnp.power(beta_two, time))])
    pad = ((0, 0), (0, T - seq), (0, 0))
    padded = lambda tokens: jnp.pad(tokens, pad).reshape(rows, D)
    line = Line()

    attn_box, attn_extra = line(functools.partial(prep, ATTN), attention_params, shard)
    attn_across = swap(attn_box, "shard", 2)
    attn_near = swap(attn_box, "shard", 1)
    box0, box1, feed_extra = line(functools.partial(prep, FEED), feedforward_params, shard)
    extra = line(lambda a, b: jnp.concatenate([a, b], axis=0), attn_extra, feed_extra)
    came = swap(extra, "shard", 1)
    x = line(padded, layer_input)
    extra = line(lambda a, b: a + b, extra, came)
    came = swap(extra, "shard", 2)
    cot = line(padded, out_cotangent)
    extra = line(lambda a, b: a + b, extra, came)
    near0, near1 = swap(box0, "shard", 1), swap(box1, "shard", 1)
    across, send0 = line(lambda a, b: lax.optimization_barrier((a, b)), attn_across, box0)
    attn_both = swap(across, "shard", 1)
    across0 = swap(send0, "shard", 2)
    boxes = (attn_box, attn_near, attn_across, attn_both)
    first, qkv, log_total, attended, hidden, second, qkv_w, proj_w, vec, bias = line(
        lambda x, w, b: call_attn_forward(seq, x, w, b), x, (shard, extra), boxes
    )
    across, send1 = line(lambda a, b: lax.optimization_barrier((a, b)), across0, box1)
    both0 = swap(across, "shard", 1)
    across1 = swap(send1, "shard", 2)
    boxes = (box0, near0, across0, both0)
    result, gs, cot_sum, pre0, up0, *grads = line(
        lambda *a: call_feed(seq, 0, *a), shard, extra, boxes, second, cot, hidden
    )
    feed0 = Sum(line, *grads)
    both1 = swap(line(lambda a: a, across1), "shard", 1)
    feed0.side()
    boxes = (box1, near1, across1, both1)
    layer_output, gs, pre1, up1, *grads = line(
        lambda *a: call_feed(seq, 1, *a), shard, extra, boxes, second, cot, result, gs
    )
    feed1 = Sum(line, *grads)
    feed0.close()
    feed1.side()
    half = images // 2
    common = (shard, log_total, qkv, first, attended)
    more = (gs, hidden, cot, vec, proj_w)
    before = line(lambda *a: call_attn_backward(seq, 0, 0, half, *a), *common, *more)
    feed0.along()
    grad0, head0, gh_low, ga, gh, back_sum, edge0, *grads = line(
        lambda b, *a: call_attn_backward(seq, 0, half, images - half, *a, before=b), tuple(before), *common, *more
    )
    attn0 = Sum(line, *grads)
    feed0.gather()
    feed1.close()
    attn0.side()
    more = (gh_low, ga)
    before = line(lambda *a: call_attn_backward(seq, 1, 0, half, *a), *common, *more)
    feed1.along()
    grad1, head1, edge1, *grads = line(
        lambda b, *a: call_attn_backward(seq, 1, half, images - half, *a, before=b), tuple(before), *common, *more
    )
    attn1 = Sum(line, *grads)
    feed1.back_along()
    attn0.close()
    head1 = pause(line, head1)
    attn1.side()
    input_grad, last_sum = line(lambda *a: call_input_backward(seq, *a), (grad0, grad1), gh, x, vec, qkv_w)
    sums = line(call_pack, last_sum, back_sum, head0, head1, edge0, edge1, pre0, pre1, up0, up1, cot_sum)
    bits = [2 << k for k in range((lax.axis_size("rep") // 2).bit_length() - 1)]
    sums = SumAll(line, sums)
    attn1.close()
    attn0.level(2)
    feed1.back_close()
    sums.hop()
    sums.hop()
    for bit in bits[1:]:
        attn0.level(bit)
    attn1.level(2)
    sums.hop()
    feed_box0 = feed0.gathered()
    while not sums.hop():
        pass
    feed_box1 = feed1.end()
    attn0.back_level()
    for bit in bits[1:]:
        attn1.level(bit)
    feed_grad, feed_change, feed_new = line(
        lambda *a: adam(FEED, *a, scale), shard, powers, sums.value, [feed_box0, feed_box1], feedforward_params, feedforward_moments
    )
    attn1.back_level()
    attn_box0 = attn0.end()
    attn_grad, attn_change, attn_new = line(
        lambda *a: adam(ATTN, *a, scale), shard, powers, sums.value, [attn_box0, attn1.end()], attention_params, attention_moments
    )
    return (layer_output, input_grad, attn_grad, feed_grad, attn_change, attn_new, feed_change, feed_new)


def solution(mesh):
    tokens = P(("shard", "rep"), None, None)
    in_specs = (tokens, tokens, P("shard"), P(None, "shard"), P("shard"), P(None, "shard"), P())
    out_specs = (tokens, tokens, P("shard"), P("shard"), P("shard"), P(None, "shard"), P("shard"), P(None, "shard"))
    return jax.shard_map(body, mesh=mesh, in_specs=in_specs, out_specs=out_specs, check_vma=False)
```

```python
import functools

import jax
import jax.numpy as jnp
from jax import lax
from jax.experimental import pallas as pl
from jax.experimental.pallas import tpu as pltpu
from jax.sharding import PartitionSpec as P

D = 768
HEADS = 12
FF = 3072
T = 208

F32 = jnp.float32
BF = jnp.bfloat16

ln_eps = 1e-06
beta_one = 0.9
beta_two = 0.999
adam_eps = 1e-08
rate_matrix = 0.01
rate_vector = 0.1
decay_matrix = 0.05
root_half = 0.7071067811865476
inv_root_tau = 0.3989422804014327

MB = 1 << 20
LANES = 128
MARGIN = 8

ATTN_START = (12, 5, -3, 2)
FEED_START = (12, 2, 15, 5)


def attn_parts(share):
    if share < 3:
        return [(0, 16, 256 * part, 6 * part, 18) for part in range(3)]
    return [(0, 48, 0, 0, 6)]


def feed_parts(share):
    if share < 2:
        return [(j, 24, 384 * h, 12 * h + 6 * j, 24) for j in range(2) for h in range(2)]
    return [(j, 48, 0, 4608 * j, 6) for j in range(2)]


def attn_grad_parts(share):
    if share < 3:
        return [
            (g, 8, 128 * part, 3 * u, 3, 18 * 128 * u + 6 * part + 3 * g, 18)
            for g in range(2)
            for part in range(3)
            for u in range(2)
        ]
    return [(g, 24, 0, 0, 6, 6 * 384 * g, 6) for g in range(2)]


def feed_grad_parts(share):
    return [(box, groups, row, 0, 6, flat, stride) for box, groups, row, flat, stride in feed_parts(share)]


ATTN_EXTRA = (
    [(0, 0, 12), (12, 4602, 14)],
    [(25, 0, 5), (30, 4613, 3)],
    [(33, 0, 15), (48, 4605, 11)],
    [(58, 0, 2), (60, 4610, 6)],
)
FEED_EXTRA = (
    [(0, 0, 12), (12, 9204, 23)],
    [(34, 0, 2), (36, 9218, 9)],
    [(45, 0, 15), (60, 9225, 2)],
    [(61, 0, 5), (66, 9221, 6)],
)
ATTN_PUT = (
    [(0, 0, 12)],
    [(25, 0, 5), (30, 4613, 3)],
    [(48, 4605, 12)],
    [(58, 0, 2), (60, 4610, 6)],
)
FEED_PUT = (
    [(0, 0, 12)],
    [(34, 0, 2), (36, 9218, 9)],
    [(45, 0, 15)],
    [(61, 0, 5), (66, 9221, 6)],
)
EXTRA = 72


class Block:
    def __init__(self, base, boxes, start, parts, grad_parts, extra, put, matrices):
        self.base = base
        self.boxes, self.start, self.parts, self.grad_parts = boxes, start, parts, grad_parts
        self.extra, self.put = extra, put
        self.matrices = matrices


ATTN = Block(
    0, 1, ATTN_START, attn_parts, attn_grad_parts, ATTN_EXTRA, ATTN_PUT, ((1536, 1771008), (1772544, 2362368))
)
FEED = Block(
    EXTRA, 2, FEED_START, feed_parts, feed_grad_parts, FEED_EXTRA, FEED_PUT, ((1536, 2360832), (2363904, 4723200))
)


def params(limit=56):
    return pltpu.CompilerParams(vmem_limit_bytes=limit * MB)


def dot(a, b):
    return lax.dot_general(a, b, (((1,), (0,)), ((), ())), preferred_element_type=F32)


def dot_nt(a, b):
    return lax.dot_general(a, b, (((1,), (1,)), ((), ())), preferred_element_type=F32)


def dot_tn(a, b):
    return lax.dot_general(a, b, (((0,), (0,)), ((), ())), preferred_element_type=F32)


def normed_of(values):
    center = values - jnp.mean(values, axis=-1, keepdims=True)
    spread = lax.rsqrt(jnp.mean(center * center, axis=-1, keepdims=True) + ln_eps)
    return center * spread, spread


def whole(array):
    rank = len(array.shape)
    return pl.BlockSpec(array.shape, lambda *i: (0,) * rank, pipeline_mode=pl.Buffered(1))


def rows_of(count, width):
    return pl.BlockSpec((count, width), lambda i: (i, 0))


SMEM = pl.BlockSpec(memory_space=pltpu.SMEM)


def sds(shape, dtype):
    return jax.ShapeDtypeStruct(shape, dtype)


CHUNK = 2368


def prep_kernel(block, steps, shard_ref, flat_ref, *refs):
    *box_refs, extra_ref, held = refs
    step = pl.program_id(0)
    held[pl.ds(pl.multiple_of(MARGIN + CHUNK * step, 8), CHUNK), :] = flat_ref[...].reshape(CHUNK, LANES)

    @pl.when(step == steps - 1)
    def _():
        low = lax.broadcasted_iota(jnp.int32, (8, LANES), 1) < 64
        low_one = lax.broadcasted_iota(jnp.int32, (1, LANES), 1) < 64
        extra_ref[...] = jnp.zeros_like(extra_ref)
        for share in range(4):

            @pl.when(shard_ref[0] == share)
            def _(share=share):
                odd = share % 2 == 1

                def tile(first, stride):
                    here = held[pl.ds(first, 8, stride=stride), :]
                    if not odd:
                        return here
                    ahead = held[pl.ds(first - 1, 8, stride=stride), :]
                    return jnp.where(low, pltpu.roll(ahead, 64, 1), pltpu.roll(here, 64, 1))

                for box, groups, box_row, flat_row, stride in block.parts(share):
                    base = MARGIN + block.start[share] + flat_row

                    def body(group, carry, box=box, base=base, box_row=box_row, stride=stride):
                        for j in range(6):
                            first = base + 16 * stride * group + j
                            both = jnp.concatenate([tile(first, stride), tile(first + 8 * stride, stride)], axis=0)
                            at = pl.multiple_of(box_row + 16 * group, 16)
                            box_refs[box][pl.ds(at, 16), LANES * j : LANES * j + LANES] = both.astype(BF)
                        return carry

                    lax.fori_loop(0, groups, body, 0, unroll=8)
                count = flat_rows(block, share)
                for to, row, length in block.extra[share]:
                    for k in range(length):
                        at = MARGIN + row + k
                        value = held[at : at + 1, :]
                        if odd:
                            ahead = held[at - 1 : at, :]
                            value = jnp.where(low_one, pltpu.roll(ahead, 64, 1), pltpu.roll(value, 64, 1))
                            if row + k == 0:
                                value = jnp.where(low_one, 0.0, value)
                        elif row + k == count:
                            value = jnp.where(low_one, value, 0.0)
                        extra_ref[to + k : to + k + 1, :] = value.astype(BF).astype(F32)


def flat_rows(block, share):
    return 4615 if block is ATTN else 9226


def prep(block, flat, shard):
    steps = -(-flat.shape[0] // (CHUNK * LANES))
    return pl.pallas_call(
        functools.partial(prep_kernel, block, steps),
        grid=(steps,),
        in_specs=[SMEM, pl.BlockSpec((CHUNK * LANES,), lambda i: (i,))],
        out_specs=[pl.BlockSpec((D, D), lambda i: (0, 0))] * block.boxes
        + [pl.BlockSpec((EXTRA, LANES), lambda i: (0, 0))],
        out_shape=[sds((D, D), BF)] * block.boxes + [sds((EXTRA, LANES), F32)],
        scratch_shapes=[pltpu.VMEM((MARGIN + CHUNK * steps + MARGIN, LANES), F32)],
        compiler_params=params(),
    )(shard, flat)


def spread_row(extra_ref, first, count):
    return jnp.concatenate([extra_ref[first + k : first + k + 1, :] for k in range(count)], axis=1)


def patch_row(ref, row, values):
    at = row // 16 * 16
    rows = lax.broadcasted_iota(jnp.int32, (16, values.shape[1]), 0)
    old = ref[at : at + 16, :].astype(F32)
    ref[at : at + 16, :] = jnp.where(rows == row - at, values, old).astype(BF)


def load_attn(shard, boxes, qkv_ref, proj_ref, sems):
    for wait in (False, True):
        for k, box in enumerate(boxes):
            share = jnp.bitwise_xor(shard, k)

            @pl.when(share == 3)
            def _(box=box, k=k):
                copy = pltpu.make_async_copy(box, proj_ref, sems.at[k, 0])
                copy.wait() if wait else copy.start()

            @pl.when(share != 3)
            def _(box=box, k=k, share=share):
                for part in range(3):
                    copy = pltpu.make_async_copy(
                        box.at[pl.ds(256 * part, 256), :],
                        qkv_ref.at[pl.ds(pl.multiple_of(768 * part + 256 * share, 256), 256), :],
                        sems.at[k, part],
                    )
                    copy.wait() if wait else copy.start()


def load_feed(shard, boxes, up_ref, down_ref, sems):
    for wait in (False, True):
        for k, box in enumerate(boxes):
            share = jnp.bitwise_xor(shard, k)

            @pl.when(share >= 2)
            def _(box=box, k=k, share=share):
                at = pl.multiple_of(768 * (share - 2), 256)
                copy = pltpu.make_async_copy(box, down_ref.at[pl.ds(at, 768), :], sems.at[k, 0])
                copy.wait() if wait else copy.start()

            @pl.when(share < 2)
            def _(box=box, k=k, share=share):
                for h in range(2):
                    copy = pltpu.make_async_copy(
                        box.at[pl.ds(384 * h, 384), :],
                        up_ref.at[pl.ds(pl.multiple_of(768 * h + 384 * share, 128), 384), :],
                        sems.at[k, h],
                    )
                    copy.wait() if wait else copy.start()


ANYWHERE = pl.BlockSpec(memory_space=pl.ANY)


def half_masks():
    lane = lax.broadcasted_iota(jnp.int32, (1, LANES), 1)
    return (lane < 64).astype(F32).astype(BF), (lane >= 64).astype(F32).astype(BF)


def two_heads(pair, masks):
    return jnp.concatenate([pair * masks[0], pair * masks[1]], axis=0)


def attn_forward(seq, x_ref, shard_ref, extra_ref, a0, a1, a2, a3, *refs):
    *refs, qkv_w, proj_w, vec_ref, bias_ref, sems = refs

    @pl.when(pl.program_id(0) == 0)
    def _():
        load_attn(shard_ref[0], (a0, a1, a2, a3), qkv_w, proj_w, sems)
        for part in range(3):
            patch_row(qkv_w, 768 * part + 255, spread_row(extra_ref, 12 + 6 * part, 6))
            patch_row(qkv_w, 768 * part + 512, spread_row(extra_ref, 30 + 6 * part, 6))
        vec_ref[...] = jnp.zeros_like(vec_ref)
        for row, first in enumerate((0, 6, 60, EXTRA + 0, EXTRA + 6)):
            vec_ref[row : row + 1, :] = spread_row(extra_ref, first, 6)
        bias_ref[...] = jnp.zeros_like(bias_ref)
        bias_ref[0:1, 0:768] = spread_row(extra_ref, 48, 6)
        bias_ref[0:1, 1536:2304] = spread_row(extra_ref, 54, 6)

    first_ref, qkv_ref, log_ref, att_ref, hid_ref, second_ref = refs
    x = x_ref[...].astype(F32)
    normed, _ = normed_of(x)
    first = (normed * vec_ref[0:1, :] + vec_ref[1:2, :]).astype(BF)
    first_ref[...] = first
    for part in range(3):
        cols = slice(768 * part, 768 * part + 768)
        qkv_ref[:, cols] = (dot(first, qkv_w[cols, :]) + bias_ref[0:1, cols]).astype(BF)
    masks = half_masks()
    real = lax.broadcasted_iota(jnp.int32, (2, T, T), 1) < seq
    for pair in range(HEADS // 2):
        at = LANES * pair
        for image in range(x_ref.shape[0] // T):
            own = slice(T * image, T * image + T)
            q = qkv_ref[own, at : at + LANES] * jnp.asarray(0.125, BF)
            k = two_heads(qkv_ref[own, 768 + at : 768 + at + LANES], masks)
            v = two_heads(qkv_ref[own, 1536 + at : 1536 + at + LANES], masks)
            scores = dot_nt(k, q).reshape(2, T, T)
            scores = jnp.where(real, scores, -1e30)
            top = jnp.max(scores, axis=1, keepdims=True)
            weight = jnp.exp(scores - top)
            total = jnp.sum(weight, axis=1, keepdims=True)
            logs = top + jnp.log(total)
            log_ref[image, 2 * pair : 2 * pair + 1, :] = logs[0]
            log_ref[image, 2 * pair + 1 : 2 * pair + 2, :] = logs[1]
            probs = (weight * (1.0 / total)).astype(BF).reshape(2 * T, T)
            att_ref[own, at : at + LANES] = dot_tn(probs, v).astype(BF)
    hidden = x + dot(att_ref[...], proj_w[...]) + vec_ref[2:3, :]
    hid_ref[...] = hidden
    normed, _ = normed_of(hidden)
    second_ref[...] = (normed * vec_ref[3:4, :] + vec_ref[4:5, :]).astype(BF)


FORWARD_IMAGES = 2


def call_attn_forward(seq, x, weights, boxes):
    shard, extra = weights
    rows = x.shape[0]
    images = rows // T
    step = FORWARD_IMAGES if images % FORWARD_IMAGES == 0 else 1
    tall = step * T
    made = [sds((2304, D), BF), sds((D, D), BF), sds((8, D), F32), sds((8, 2304), F32)]
    return pl.pallas_call(
        functools.partial(attn_forward, seq),
        grid=(images // step,),
        in_specs=[rows_of(tall, D), SMEM, whole(extra)] + [ANYWHERE] * 4,
        out_specs=[
            rows_of(tall, D),
            rows_of(tall, 2304),
            pl.BlockSpec((step, HEADS, T), lambda i: (i, 0, 0)),
            rows_of(tall, D),
            rows_of(tall, D),
            rows_of(tall, D),
        ]
        + [pl.BlockSpec(shape.shape, lambda i: (0, 0)) for shape in made],
        out_shape=[
            sds((rows, D), BF),
            sds((rows, 2304), BF),
            sds((images, HEADS, T), F32),
            sds((rows, D), BF),
            sds((rows, D), F32),
            sds((rows, D), BF),
        ]
        + made,
        scratch_shapes=[pltpu.SemaphoreType.DMA((4, 3))],
        compiler_params=params(),
    )(x, shard, extra, *boxes)


def hand_out(index, box, outs, sems):
    copies = [pltpu.make_async_copy(box.at[k], out, sems.at[k]) for k, out in enumerate(outs)]
    for k, copy in enumerate(copies):

        @pl.when(index == k)
        def _(copy=copy):
            copy.start()

    @pl.when(index == len(outs) - 1)
    def _():
        for copy in copies:
            copy.wait()


HALF = FF // 2
ROW_STEPS = 4


def feed(seq, part, tall, shard_ref, extra_ref, a0, a1, a2, a3, second_ref, cot_ref, result_ref, *refs):
    last = part == 1
    if last:
        before_ref, out_ref, gs_ref, *refs = refs
    else:
        out_ref, gs_ref, cot_sum, *refs = refs
    sum_ref, edge_ref, *outs, up_w, down_w, bias, second_all, cot_all, act_all, pre_all, box, sems, box_sems = refs
    step = pl.program_id(0)
    shard = shard_ref[0]

    @pl.when(step == 0)
    def _():
        load_feed(shard, (a0, a1, a2, a3), up_w, down_w, sems)
        for h in range(2):
            patch_row(up_w, 768 * h + 383, spread_row(extra_ref, EXTRA + 12 + 12 * h + 6 * part, 6))
            bias[0:1, 768 * h : 768 * h + 768] = spread_row(extra_ref, EXTRA + 36 + 12 * h + 6 * part, 6)
        if last:
            patch_row(down_w, 767, spread_row(extra_ref, EXTRA + 60, 6))
        sum_ref[...] = jnp.zeros_like(sum_ref)
        edge_ref[...] = jnp.zeros_like(edge_ref)
        if not last:
            cot_sum[...] = jnp.zeros_like(cot_sum)

    @pl.when(step < ROW_STEPS)
    def _():
        at = pl.ds(pl.multiple_of(step * tall, 16), tall)
        second = second_ref[...]
        cot = cot_ref[...]
        second_all[at, :] = second
        cot_all[at, :] = cot
        if last:
            result = result_ref[...]
            grad_second = before_ref[...]
        else:
            result = result_ref[...] + spread_row(extra_ref, EXTRA + 66, 6)
            grad_second = jnp.zeros_like(result)
            cot_sum[0:1, :] += jnp.sum(cot.astype(F32), axis=0, keepdims=True)
        for h in range(2):
            cols = slice(768 * h, 768 * h + 768)
            pre = dot(second, up_w[cols, :]) + bias[0:1, cols]
            grad_act = dot_nt(cot, down_w[cols, :])
            half = 0.5 * (1.0 + lax.erf(pre * root_half))
            act = (pre * half).astype(BF)
            grad_pre = grad_act * (half + pre * jnp.exp(-0.5 * pre * pre) * inv_root_tau)
            low = grad_pre.astype(BF)
            act_all[at, cols] = act
            pre_all[at, cols] = low
            sum_ref[0:1, cols] += jnp.sum(grad_pre, axis=0, keepdims=True)
            result = result + dot(act, down_w[cols, :])
            grad_second = grad_second + dot_nt(low, up_w[cols, :])
        if last:
            for image in range(tall // T):
                out_ref[image] = result[T * image : T * image + seq].astype(BF)
        else:
            out_ref[...] = result
        gs_ref[...] = grad_second

    index = step - ROW_STEPS
    side = jnp.bitwise_xor(shard // 2, 1 - index % 2)
    core = jnp.where(index >= 2, shard % 2, 1 - shard % 2)

    @pl.when((index >= 0) & (side == 0))
    def _():
        left = second_all[:, pl.ds(pl.multiple_of(384 * core, 128), 384)]
        for h in range(2):
            grad = dot_tn(left, pre_all[:, 768 * h : 768 * h + 768])
            box[index, 384 * h : 384 * h + 384, :] = grad.astype(BF)

            @pl.when(core == 0)
            def _(grad=grad, h=h):
                edge_ref[0:1, 768 * h : 768 * h + 768] = grad[383:384]

    @pl.when((index >= 0) & (side == 1))
    def _():
        left = act_all[:, pl.ds(pl.multiple_of(768 * core, 128), 768)]
        grad = dot_tn(left, cot_all[...])
        box[index] = grad.astype(BF)

        @pl.when(core == 0)
        def _():
            edge_ref[1:2, 0:768] = grad[767:768]

    hand_out(index, box, outs, box_sems)


def call_feed(seq, part, shard, extra, boxes, second, cot, result, before=None):
    rows = second.shape[0]
    images = rows // T
    tall = rows // ROW_STEPS
    last = part == 1
    row = lambda i: jnp.minimum(i, ROW_STEPS - 1)
    block = pl.BlockSpec((tall, D), lambda i: (row(i), 0))
    out = pl.BlockSpec((tall // T, seq, D), lambda i: (row(i), 0, 0)) if last else block
    small = lambda width: pl.BlockSpec((8, width), lambda i: (0, 0))
    return pl.pallas_call(
        functools.partial(feed, seq, part, tall),
        grid=(ROW_STEPS + 4,),
        in_specs=[SMEM, whole(extra)] + [ANYWHERE] * 4 + [block] * (4 if last else 3),
        out_specs=[out, block] + ([] if last else [small(D)]) + [small(HALF), small(HALF)] + [ANYWHERE] * 4,
        out_shape=[sds((images, seq, D), BF) if last else sds((rows, D), F32), sds((rows, D), F32)]
        + ([] if last else [sds((8, D), F32)])
        + [sds((8, HALF), F32), sds((8, HALF), F32)] + [sds((D, D), BF)] * 4,
        scratch_shapes=[
            pltpu.VMEM((HALF, D), BF),
            pltpu.VMEM((HALF, D), BF),
            pltpu.VMEM((8, HALF), F32),
            pltpu.VMEM((rows, D), BF),
            pltpu.VMEM((rows, D), BF),
            pltpu.VMEM((rows, HALF), BF),
            pltpu.VMEM((rows, HALF), BF),
            pltpu.VMEM((4, D, D), BF),
            pltpu.SemaphoreType.DMA((4, 2)),
            pltpu.SemaphoreType.DMA((4,)),
        ],
        compiler_params=params(60),
    )(shard, extra, *boxes, second, cot, result, *([before] if last else []))


WIDE = 384


def attn_backward(seq, group, base, count, last, shard_ref, log_ref, qkv_ref, first_ref, att_ref, *refs):
    step = pl.program_id(0)
    shard = shard_ref[0]
    if group == 0:
        gs_ref, hid_ref, cot_ref, vec_ref, proj_w, *refs = refs
    else:
        low_ref, ga_ref, *refs = refs
    if last:
        if group == 0:
            head_before, sum_before, first_any, att_any, low_any, grad_any, _, _, *refs = refs
        else:
            head_before, first_any, att_any, low_any, grad_any, *refs = refs
    grad_ref, head_sum, *refs = refs
    if group == 0:
        low_ref, ga_ref, gh_ref, sum_ref, *refs = refs
    if last:
        edge_ref, *outs, grad_all, first_all, low_all, att_all, box, box_sems, load_sems = refs
        done = pl.ds(0, base * T)
        loads = [
            pltpu.make_async_copy(grad_any.at[done], grad_all.at[done], load_sems.at[0]),
            pltpu.make_async_copy(first_any.at[done], first_all.at[done], load_sems.at[1]),
            pltpu.make_async_copy(low_any.at[done], low_all.at[done], load_sems.at[2]),
            pltpu.make_async_copy(
                att_any.at[done, pl.ds(WIDE * group, WIDE)], att_all.at[done], load_sems.at[3]
            ),
        ]

    @pl.when(step == 0)
    def _():
        if last:
            for load in loads:
                load.start()
            edge_ref[...] = jnp.zeros_like(edge_ref)
            head_sum[...] = head_before[...]
        else:
            head_sum[...] = jnp.zeros_like(head_sum)
        if group == 0:
            sum_ref[...] = sum_before[...] if last else jnp.zeros_like(sum_ref)

    @pl.when(step < count)
    def _():
        at_rows = pl.ds(pl.multiple_of((step + base) * T, 16), T)
        if last:
            first_all[at_rows, :] = first_ref[...]
            att_all[at_rows, :] = att_ref[...]
        if group == 0:
            gs = gs_ref[...]
            normed, spread = normed_of(hid_ref[...])
            gn = gs * vec_ref[3:4, :]
            gh = cot_ref[...].astype(F32) + spread * (
                gn - jnp.mean(gn, axis=-1, keepdims=True) - normed * jnp.mean(gn * normed, axis=-1, keepdims=True)
            )
            sum_ref[0:1, :] += jnp.sum(gs * normed, axis=0, keepdims=True)
            sum_ref[1:2, :] += jnp.sum(gs, axis=0, keepdims=True)
            sum_ref[2:3, :] += jnp.sum(gh, axis=0, keepdims=True)
            gh_ref[...] = gh
            gh_low = gh.astype(BF)
            low_ref[...] = gh_low
            ga_ref[...] = dot_nt(gh_low, proj_w[...]).astype(BF)
        if last:
            low_all[at_rows, :] = low_ref[...]
        low = lax.broadcasted_iota(jnp.int32, (T, LANES), 1) < 64
        real = lax.broadcasted_iota(jnp.int32, (2, T, T), 1) < seq
        eighth = jnp.asarray(0.125, BF)
        masks = half_masks()
        for pair in range(3):
            at = LANES * pair
            full = WIDE * group + at
            head = 6 * group + 2 * pair
            q = qkv_ref[:, full : full + LANES] * eighth
            k = two_heads(qkv_ref[:, 768 + full : 768 + full + LANES], masks)
            v = two_heads(qkv_ref[:, 1536 + full : 1536 + full + LANES], masks)
            grad_out = ga_ref[:, at : at + LANES]
            scores = dot_nt(k, q).reshape(2, T, T)
            logs = jnp.concatenate([log_ref[0:1, head : head + 1, :], log_ref[0:1, head + 1 : head + 2, :]], axis=0)
            probs = jnp.where(real, jnp.exp(scores - logs), 0.0)
            grad_v = dot(probs.astype(BF).reshape(2 * T, T), grad_out)
            grad_probs = dot_nt(v, grad_out).reshape(2, T, T)
            delta = jnp.sum(probs * grad_probs, axis=1, keepdims=True)
            grad_scores = (probs * (grad_probs - delta)).astype(BF).reshape(2 * T, T)
            grad_k = dot(grad_scores, q)
            grads = (
                dot_tn(grad_scores, k * eighth),
                jnp.where(low, grad_k[:T], grad_k[T:]),
                jnp.where(low, grad_v[:T], grad_v[T:]),
            )
            for part, grad in enumerate(grads):
                if part != 1:
                    row = part // 2
                    head_sum[row : row + 1, at : at + LANES] += jnp.sum(grad, axis=0, keepdims=True)
                cols = slice(WIDE * part + at, WIDE * part + at + LANES)
                grad = grad.astype(BF)
                grad_ref[:, cols] = grad
                if last:
                    grad_all[at_rows, cols] = grad

    if not last:
        return

    @pl.when(step == count)
    def _():
        for load in loads:
            load.wait()

    index = step - count
    side = jnp.bitwise_xor(shard // 2, 1 - index % 2)
    core = jnp.where(index >= 2, shard % 2, 1 - shard % 2)
    share = 2 * side + core

    @pl.when((index >= 0) & (share == 3))
    def _():
        box[index] = dot_tn(att_all[...], low_all[...]).astype(BF)

    @pl.when((index >= 0) & (share != 3))
    def _():
        grad = dot_tn(first_all[:, pl.ds(pl.multiple_of(256 * share, 256), 256)], grad_all[...])
        for part in range(3):
            cols = slice(WIDE * part, WIDE * part + WIDE)
            for u in range(2):
                box[index, 128 * part : 128 * part + 128, WIDE * u : WIDE * u + WIDE] = grad[
                    128 * u : 128 * u + 128, cols
                ].astype(BF)

        @pl.when(share == 0)
        def _():
            edge_ref[0:1, :] = grad[255:256]

        @pl.when(share == 2)
        def _():
            edge_ref[1:2, :] = grad[0:1]

    hand_out(index, box, outs, box_sems)


def call_attn_backward(seq, group, base, count, shard, log_total, qkv, first, attended, *more, before=()):
    rows = first.shape[0]
    last = len(before) > 0
    row = lambda i: jnp.minimum(i, count - 1) + base
    block = lambda width, col=0: pl.BlockSpec((T, width), lambda i: (row(i), col))
    small = lambda width: pl.BlockSpec((8, width), lambda i: (0, 0))
    in_specs = [SMEM, pl.BlockSpec((1, HEADS, T), lambda i: (row(i), 0, 0)), block(2304), block(D), block(WIDE, group)]
    out_specs = [block(3 * WIDE), small(WIDE)]
    out_shape = [sds((rows, 3 * WIDE), BF), sds((8, WIDE), F32)]
    if group == 0:
        in_specs += [block(D)] * 3 + [whole(more[3]), whole(more[4])]
        out_specs += [block(D), block(D), block(D), small(D)]
        out_shape += [sds((rows, D), BF), sds((rows, D), BF), sds((rows, D), F32), sds((8, D), F32)]
    else:
        in_specs += [block(D), block(WIDE, 1)]
    aliases, scratch, extra = {}, [], []
    if last:
        at = len(in_specs)
        if group == 0:
            grad, head, low, ga, gh, total = before
            extra = [head, total, first, attended, low, grad, ga, gh]
            in_specs += [whole(head), whole(total)] + [ANYWHERE] * 6
            aliases = {at + 4: 2, at + 5: 0, at + 6: 3, at + 7: 4}
        else:
            grad, head = before
            extra = [head, first, attended, more[0], grad]
            in_specs += [whole(head)] + [ANYWHERE] * 4
            aliases = {at + 4: 0}
        out_specs += [small(3 * WIDE)] + [ANYWHERE] * 4
        out_shape += [sds((8, 3 * WIDE), F32)] + [sds((WIDE, D), BF)] * 4
        scratch = [
            pltpu.VMEM((rows, 3 * WIDE), BF),
            pltpu.VMEM((rows, D), BF),
            pltpu.VMEM((rows, D), BF),
            pltpu.VMEM((rows, WIDE), BF),
            pltpu.VMEM((4, WIDE, D), BF),
            pltpu.SemaphoreType.DMA((4,)),
            pltpu.SemaphoreType.DMA((4,)),
        ]
    return pl.pallas_call(
        functools.partial(attn_backward, seq, group, base, count, last),
        grid=(count + 4 if last else count,),
        in_specs=in_specs,
        out_specs=out_specs,
        out_shape=out_shape,
        input_output_aliases=aliases,
        scratch_shapes=scratch,
        compiler_params=params(),
    )(shard, log_total, qkv, first, attended, *more, *extra)


def input_backward(seq, grad0, grad1, gh_ref, x_ref, vec_ref, qkv_w, out_ref, sum_ref):
    @pl.when(pl.program_id(0) == 0)
    def _():
        sum_ref[...] = jnp.zeros_like(sum_ref)

    grad_first = None
    for part in range(3):
        cols = slice(WIDE * part, WIDE * part + WIDE)
        both = jnp.concatenate([grad0[:, cols], grad1[:, cols]], axis=1)
        term = dot_nt(both, qkv_w[768 * part : 768 * part + 768, :])
        grad_first = term if part == 0 else grad_first + term
    normed, spread = normed_of(x_ref[...].astype(F32))
    gn = grad_first * vec_ref[0:1, :]
    grad = gh_ref[...] + spread * (
        gn - jnp.mean(gn, axis=-1, keepdims=True) - normed * jnp.mean(gn * normed, axis=-1, keepdims=True)
    )
    sum_ref[0:1, :] += jnp.sum(grad_first * normed, axis=0, keepdims=True)
    sum_ref[1:2, :] += jnp.sum(grad_first, axis=0, keepdims=True)
    for image in range(grad.shape[0] // T):
        out_ref[image] = grad[T * image : T * image + seq].astype(BF)


def call_input_backward(seq, grads, gh, x, vec, qkv_w):
    rows = gh.shape[0]
    images = rows // T
    step = 2 if images % 2 == 0 else 1
    tall = step * T
    return pl.pallas_call(
        functools.partial(input_backward, seq),
        grid=(images // step,),
        in_specs=[rows_of(tall, 3 * WIDE)] * 2 + [rows_of(tall, D), rows_of(tall, D), whole(vec), whole(qkv_w)],
        out_specs=[pl.BlockSpec((step, seq, D), lambda i: (i, 0, 0)), pl.BlockSpec((8, D), lambda i: (0, 0))],
        out_shape=[sds((images, seq, D), BF), sds((8, D), F32)],
        compiler_params=params(),
    )(*grads, gh, x, vec, qkv_w)


def putter(out_ref):
    out_ref[...] = jnp.zeros_like(out_ref)

    def put(first, ref, row, col, width):
        for k in range(width // LANES):
            at = col + LANES * k
            out_ref[first + k : first + k + 1, :] = ref[row : row + 1, at : at + LANES]

    return put


def pack(last_sum, back_sum, head0, head1, edge0, edge1, pre0, pre1, up0, up1, cot_sum, out_ref):
    put = putter(out_ref)
    put(0, last_sum, 0, 0, D)
    put(6, last_sum, 1, 0, D)
    for group, (head, edge) in enumerate(((head0, edge0), (head1, edge1))):
        for part in range(3):
            put(12 + 6 * part + 3 * group, edge, 0, WIDE * part, WIDE)
            put(30 + 6 * part + 3 * group, edge, 1, WIDE * part, WIDE)
        put(48 + 3 * group, head, 0, 0, WIDE)
        put(54 + 3 * group, head, 1, 0, WIDE)
    put(60, back_sum, 2, 0, D)
    put(EXTRA, back_sum, 0, 0, D)
    put(EXTRA + 6, back_sum, 1, 0, D)
    for j, (pre, up) in enumerate(((pre0, up0), (pre1, up1))):
        for h in range(2):
            put(EXTRA + 12 + 12 * h + 6 * j, up, 0, 768 * h, D)
            put(EXTRA + 36 + 12 * h + 6 * j, pre, 0, 768 * h, D)
    put(EXTRA + 60, up1, 1, 0, D)
    put(EXTRA + 66, cot_sum, 0, 0, D)


def call_pack(*arrays):
    return pl.pallas_call(
        pack,
        in_specs=[pl.BlockSpec(memory_space=pltpu.VMEM)] * len(arrays),
        out_specs=pl.BlockSpec(memory_space=pltpu.VMEM),
        out_shape=sds((2 * EXTRA, LANES), F32),
        compiler_params=params(),
    )(*arrays)


def adam_kernel(block, share_size, scale, boxes, shard_ref, power_ref, extra_ref, *refs):
    box_refs = refs[:boxes]
    flat_ref, mom_ref, grad_ref, change_ref, new_ref, held = refs[boxes:]
    step = pl.program_id(0)

    @pl.when(step == 0)
    def _():
        for share in range(4):

            @pl.when(shard_ref[0] == share)
            def _(share=share):
                for box, groups, box_row, col, cols, flat_row, stride in block.grad_parts(share):
                    base = MARGIN + block.start[share] + flat_row

                    def body(group, carry, box=box, box_row=box_row, col=col, cols=cols, base=base, stride=stride):
                        row = pl.multiple_of(box_row + 16 * group, 16)
                        for j in range(cols):
                            at = LANES * (col + j)
                            both = box_refs[box][pl.ds(row, 16), at : at + LANES].astype(F32)
                            to = base + 16 * stride * group + j
                            held[pl.ds(to, 8, stride=stride), :] = both[0:8]
                            held[pl.ds(to + 8 * stride, 8, stride=stride), :] = both[8:16]
                        return carry

                    lax.fori_loop(0, groups, body, 0, unroll=8)
                for source, row, length in block.put[share]:
                    held[MARGIN + row : MARGIN + row + length, :] = extra_ref[block.base + source : block.base + source + length, :]

    start = pl.multiple_of(MARGIN + CHUNK * step, 8)
    shard = shard_ref[0]
    low = lax.broadcasted_iota(jnp.int32, (CHUNK, LANES), 1) < 64
    here = held[pl.ds(start, CHUNK), :]
    after = held[pl.ds(start + 1, CHUNK), :]
    shifted = jnp.where(low, pltpu.roll(here, 64, 1), pltpu.roll(after, 64, 1))
    grad = jnp.where(shard % 2 == 1, shifted, here) * scale
    position = (
        shard * share_size
        + step * (CHUNK * LANES)
        + lax.broadcasted_iota(jnp.int32, (CHUNK, LANES), 0) * LANES
        + lax.broadcasted_iota(jnp.int32, (CHUNK, LANES), 1)
    )
    matrix = jnp.zeros((CHUNK, LANES), jnp.bool_)
    for first, end in block.matrices:
        matrix = matrix | ((position >= first) & (position < end))
    size = CHUNK * LANES
    p = flat_ref[...].reshape(CHUNK, LANES)
    m = beta_one * mom_ref[0, :].reshape(CHUNK, LANES) + (1.0 - beta_one) * grad
    s = beta_two * mom_ref[1, :].reshape(CHUNK, LANES) + (1.0 - beta_two) * grad * grad
    ratio = (m * power_ref[0]) / (jnp.sqrt(s * power_ref[1]) + adam_eps)
    change = jnp.where(matrix, rate_matrix, rate_vector) * (ratio + jnp.where(matrix, decay_matrix, 0.0) * p)
    grad_ref[...] = grad.reshape(size)
    change_ref[...] = change.reshape(size)
    new_ref[0, :] = m.reshape(size)
    new_ref[1, :] = s.reshape(size)


def adam(block, shard, powers, extra, boxes, flat, moments, scale):
    count = flat.shape[0]
    steps = -(-count // (CHUNK * LANES))
    line = pl.BlockSpec((CHUNK * LANES,), lambda i: (i,))
    two = pl.BlockSpec((2, CHUNK * LANES), lambda i: (0, i))
    return pl.pallas_call(
        functools.partial(adam_kernel, block, count, scale, len(boxes)),
        grid=(steps,),
        in_specs=[SMEM, SMEM, whole(extra)] + [whole(box) for box in boxes] + [line, two],
        out_specs=[line, line, two],
        out_shape=[sds((count,), F32), sds((count,), F32), sds((2, count), F32)],
        scratch_shapes=[pltpu.VMEM((MARGIN + CHUNK * steps + MARGIN, LANES), F32)],
        compiler_params=params(),
    )(shard, powers, extra, *boxes, flat, moments)


def swap(value, axis, bit):
    pairs = [(i, i ^ bit) for i in range(lax.axis_size(axis))]
    return lax.ppermute(value, axis, pairs)


def turn(value, axis, unit, distance):
    size = lax.axis_size(axis)
    return lax.ppermute(value, axis, [(i, (i + unit * distance) % size) for i in range(size)])


def pick(array, index, axis=0):
    return lax.dynamic_index_in_dim(array, index, axis, keepdims=False)


class Line:
    def __init__(self):
        self.last = None

    def __call__(self, step, *args):
        if self.last is not None:
            flat, tree = jax.tree.flatten(args)
            flat = lax.optimization_barrier((self.last, *flat))[1:]
            args = jax.tree.unflatten(tree, flat)
        out = step(*args)
        self.last = min(jax.tree.leaves(out), key=lambda leaf: leaf.size)
        return out


def pause_kernel(in_ref, out_ref):
    out_ref[...] = in_ref[...]


def pause(line, value):
    return line(
        pl.pallas_call(
            pause_kernel,
            out_shape=sds(value.shape, value.dtype),
            cost_estimate=pl.CostEstimate(flops=10**11, bytes_accessed=10**8, transcendentals=0),
        ),
        value,
    )


class Sum:
    def __init__(self, line, across, same, mine_across, mine):
        self.line, self.mine_across, self.mine = line, mine_across, mine
        self.rows = mine.shape[0]
        rep = lax.axis_index("rep")
        self.near, self.far = rep % 2, rep // 2
        self.count = lax.axis_size("rep") // 2
        self.came_across, self.here = swap(across, "shard", 1), swap(same, "shard", 1)

    def side(self):
        add = lambda a, b: (a.astype(F32) + b.astype(F32)).astype(BF)
        send = self.line(add, self.mine_across, self.came_across)
        self.came = swap(send, "shard", 2)
        self.here = self.line(lambda a: a, self.here)

    def close(self):
        def step(mine, here, came):
            total = mine.astype(F32) + here.astype(F32) + came.astype(F32)
            halves = total.reshape(2, self.rows // 2, D)
            return pick(halves, 1 - self.near).astype(BF), pick(halves, self.near)

        send, self.half = self.line(step, self.mine, self.here, self.came)
        self.came = swap(send, "rep", 1)

    def level(self, bit):
        if bit == 2:
            self.part = self.line(lambda a, b: (a + b.astype(F32)).astype(BF), self.half, self.came)
        else:
            self.part = self.line(lambda a, b: (a.astype(F32) + b.astype(F32)).astype(BF), self.part, self.came)
        self.came = swap(self.part, "rep", bit)

    def back_level(self):
        self.half = self.line(lambda a, b: (a.astype(F32) + b.astype(F32)).astype(BF), self.part, self.came)
        self.came = swap(self.half, "rep", 1)

    def along(self):
        def step(half, came):
            parts = (half + came.astype(F32)).reshape(self.count, self.rows // 2 // self.count, D)
            sends = [pick(parts, (self.far + d) % self.count).astype(BF) for d in range(1, self.count)]
            return sends, pick(parts, self.far)

        sends, self.part = self.line(step, self.half, self.came)
        self.came = [turn(send, "rep", 2, d + 1) for d, send in enumerate(sends)]

    def back_along(self):
        def step(part, came):
            for value in came:
                part = part + value.astype(F32)
            return part.astype(BF)

        self.part = self.line(step, self.part, self.came)
        self.came = [turn(self.part, "rep", 2, d) for d in range(1, self.count)]

    def back_close(self):
        def step(part, came):
            full = jnp.zeros((self.count,) + part.shape, BF)
            for d, value in enumerate([part] + came):
                full = lax.dynamic_update_slice_in_dim(full, value[None], (self.far + self.count - d) % self.count, 0)
            return full.reshape(self.rows // 2, D)

        self.half = self.line(step, self.part, self.came)
        self.came = swap(self.half, "rep", 1)

    def end(self):
        def step(half, came):
            first = self.near == 0
            return jnp.concatenate([jnp.where(first, half, came), jnp.where(first, came, half)], axis=0)

        return self.line(step, self.half, self.came)


class SumAll:
    def __init__(self, line, value):
        self.line, self.value = line, value
        self.hops = [("shard", 1), ("shard", 2)]
        bit = 2
        while bit < lax.axis_size("rep"):
            self.hops.append(("rep", bit))
            bit *= 2
        self.hops.append(("rep", 1))
        self.came = swap(value, *self.hops.pop(0))

    def hop(self):
        self.value = self.line(lambda a, b: a + b, self.value, self.came)
        if self.hops:
            self.came = swap(self.value, *self.hops.pop(0))
            return False
        return True


def body(layer_input, out_cotangent, attention_params, attention_moments, feedforward_params, feedforward_moments, step_count):
    images, seq, _ = layer_input.shape
    rows = images * T
    image_total = images * lax.axis_size("shard") * lax.axis_size("rep")
    scale = 1.0 / image_total
    shard = lax.axis_index("shard").astype(jnp.int32).reshape(1)
    time = step_count[0].astype(F32)
    powers = jnp.stack([1.0 / (1.0 - jnp.power(beta_one, time)), 1.0 / (1.0 - jnp.power(beta_two, time))])
    pad = ((0, 0), (0, T - seq), (0, 0))
    turned = lambda tokens: jnp.swapaxes(tokens, 0, 1)
    padded = lambda tokens: jnp.pad(tokens, pad).reshape(rows, D)
    line = Line()

    attn_box, attn_extra = line(functools.partial(prep, ATTN), attention_params, shard)
    attn_across = swap(attn_box, "shard", 2)
    attn_near = swap(attn_box, "shard", 1)
    box0, box1, feed_extra = line(functools.partial(prep, FEED), feedforward_params, shard)
    extra = line(lambda a, b: jnp.concatenate([a, b], axis=0), attn_extra, feed_extra)
    came = swap(extra, "shard", 1)
    x = line(padded, layer_input)
    extra = line(lambda a, b: a + b, extra, came)
    came = swap(extra, "shard", 2)
    cot = line(padded, out_cotangent)
    extra = line(lambda a, b: a + b, extra, came)
    near0, near1 = swap(box0, "shard", 1), swap(box1, "shard", 1)
    across, send0 = line(lambda a, b: lax.optimization_barrier((a, b)), attn_across, box0)
    attn_both = swap(across, "shard", 1)
    across0 = swap(send0, "shard", 2)
    boxes = (attn_box, attn_near, attn_across, attn_both)
    first, qkv, log_total, attended, hidden, second, qkv_w, proj_w, vec, bias = line(
        lambda x, w, b: call_attn_forward(seq, x, w, b), x, (shard, extra), boxes
    )
    across, send1 = line(lambda a, b: lax.optimization_barrier((a, b)), across0, box1)
    both0 = swap(across, "shard", 1)
    across1 = swap(send1, "shard", 2)
    boxes = (box0, near0, across0, both0)
    result, gs, cot_sum, pre0, up0, *grads = line(
        lambda *a: call_feed(seq, 0, *a), shard, extra, boxes, second, cot, hidden
    )
    feed0 = Sum(line, *grads)
    both1 = swap(line(lambda a: a, across1), "shard", 1)
    feed0.side()
    boxes = (box1, near1, across1, both1)
    layer_output, gs, pre1, up1, *grads = line(
        lambda *a: call_feed(seq, 1, *a), shard, extra, boxes, second, cot, result, gs
    )
    feed1 = Sum(line, *grads)
    feed0.close()
    layer_output = line(turned, layer_output)
    feed1.side()
    half = images // 2
    common = (shard, log_total, qkv, first, attended)
    more = (gs, hidden, cot, vec, proj_w)
    before = line(lambda *a: call_attn_backward(seq, 0, 0, half, *a), *common, *more)
    feed0.along()
    grad0, head0, gh_low, ga, gh, back_sum, edge0, *grads = line(
        lambda b, *a: call_attn_backward(seq, 0, half, images - half, *a, before=b), tuple(before), *common, *more
    )
    attn0 = Sum(line, *grads)
    feed0.back_along()
    feed1.close()
    head0 = pause(line, head0)
    attn0.side()
    more = (gh_low, ga)
    before = line(lambda *a: call_attn_backward(seq, 1, 0, half, *a), *common, *more)
    feed0.back_close()
    feed1.along()
    grad1, head1, edge1, *grads = line(
        lambda b, *a: call_attn_backward(seq, 1, half, images - half, *a, before=b), tuple(before), *common, *more
    )
    attn1 = Sum(line, *grads)
    feed1.back_along()
    attn0.close()
    head1 = pause(line, head1)
    attn1.side()
    input_grad, last_sum = line(lambda *a: call_input_backward(seq, *a), (grad0, grad1), gh, x, vec, qkv_w)
    sums = line(call_pack, last_sum, back_sum, head0, head1, edge0, edge1, pre0, pre1, up0, up1, cot_sum)
    bits = [2 << k for k in range((lax.axis_size("rep") // 2).bit_length() - 1)]
    sums = SumAll(line, sums)
    attn1.close()
    attn0.level(2)
    feed1.back_close()
    sums.hop()
    input_grad = line(turned, input_grad)
    feed_box0 = feed0.end()
    sums.hop()
    for bit in bits[1:]:
        attn0.level(bit)
    attn1.level(2)
    sums.hop()
    while not sums.hop():
        pass
    feed_box1 = feed1.end()
    for bit in bits[1:]:
        attn1.level(bit)
    attn0.back_level()
    feed_grad, feed_change, feed_new = line(
        lambda *a: adam(FEED, *a, scale), shard, powers, sums.value, [feed_box0, feed_box1], feedforward_params, feedforward_moments
    )
    attn1.back_level()
    attn_box0 = attn0.end()
    attn_grad, attn_change, attn_new = line(
        lambda *a: adam(ATTN, *a, scale), shard, powers, sums.value, [attn_box0, attn1.end()], attention_params, attention_moments
    )
    return (turned(layer_output), turned(input_grad), attn_grad, feed_grad, attn_change, attn_new, feed_change, feed_new)


def solution(mesh):
    tokens = P(("shard", "rep"), None, None)
    in_specs = (tokens, tokens, P("shard"), P(None, "shard"), P("shard"), P(None, "shard"), P())
    out_specs = (tokens, tokens, P("shard"), P("shard"), P("shard"), P(None, "shard"), P("shard"), P(None, "shard"))
    return jax.shard_map(body, mesh=mesh, in_specs=in_specs, out_specs=out_specs, check_vma=False)
```

```python
import functools

import jax
import jax.numpy as jnp
from jax import lax
from jax.experimental import pallas as pl
from jax.experimental.pallas import tpu as pltpu
from jax.experimental.layout import Layout, with_layout_constraint
from jax.sharding import PartitionSpec as P

D = 768
HEADS = 12
FF = 3072
T = 208

F32 = jnp.float32
BF = jnp.bfloat16

ln_eps = 1e-06
beta_one = 0.9
beta_two = 0.999
adam_eps = 1e-08
rate_matrix = 0.01
rate_vector = 0.1
decay_matrix = 0.05
root_half = 0.7071067811865476
inv_root_tau = 0.3989422804014327

MB = 1 << 20
LANES = 128
MARGIN = 8

ATTN_START = (12, 5, -3, 2)
FEED_START = (12, 2, 15, 5)


def attn_parts(share):
    if share < 3:
        return [(0, 16, 256 * part, 6 * part, 18) for part in range(3)]
    return [(0, 48, 0, 0, 6)]


def feed_parts(share):
    if share < 2:
        return [(j, 24, 384 * h, 12 * h + 6 * j, 24) for j in range(2) for h in range(2)]
    return [(j, 48, 0, 4608 * j, 6) for j in range(2)]


def attn_grad_parts(share):
    if share < 3:
        return [
            (g, 8, 128 * part, 3 * u, 3, 18 * 128 * u + 6 * part + 3 * g, 18)
            for g in range(2)
            for part in range(3)
            for u in range(2)
        ]
    return [(g, 24, 0, 0, 6, 6 * 384 * g, 6) for g in range(2)]


def feed_grad_parts(share):
    return [(box, groups, row, 0, 6, flat, stride) for box, groups, row, flat, stride in feed_parts(share)]


ATTN_EXTRA = (
    [(0, 0, 12), (12, 4602, 14)],
    [(25, 0, 5), (30, 4613, 3)],
    [(33, 0, 15), (48, 4605, 11)],
    [(58, 0, 2), (60, 4610, 6)],
)
FEED_EXTRA = (
    [(0, 0, 12), (12, 9204, 23)],
    [(34, 0, 2), (36, 9218, 9)],
    [(45, 0, 15), (60, 9225, 2)],
    [(61, 0, 5), (66, 9221, 6)],
)
ATTN_PUT = (
    [(0, 0, 12)],
    [(25, 0, 5), (30, 4613, 3)],
    [(48, 4605, 12)],
    [(58, 0, 2), (60, 4610, 6)],
)
FEED_PUT = (
    [(0, 0, 12)],
    [(34, 0, 2), (36, 9218, 9)],
    [(45, 0, 15)],
    [(61, 0, 5), (66, 9221, 6)],
)
EXTRA = 72


class Block:
    def __init__(self, base, boxes, start, parts, grad_parts, extra, put, matrices):
        self.base = base
        self.boxes, self.start, self.parts, self.grad_parts = boxes, start, parts, grad_parts
        self.extra, self.put = extra, put
        self.matrices = matrices


ATTN = Block(
    0, 1, ATTN_START, attn_parts, attn_grad_parts, ATTN_EXTRA, ATTN_PUT, ((1536, 1771008), (1772544, 2362368))
)
FEED = Block(
    EXTRA, 2, FEED_START, feed_parts, feed_grad_parts, FEED_EXTRA, FEED_PUT, ((1536, 2360832), (2363904, 4723200))
)


def params(limit=56):
    return pltpu.CompilerParams(vmem_limit_bytes=limit * MB)


def dot(a, b):
    return lax.dot_general(a, b, (((1,), (0,)), ((), ())), preferred_element_type=F32)


def dot_nt(a, b):
    return lax.dot_general(a, b, (((1,), (1,)), ((), ())), preferred_element_type=F32)


def dot_tn(a, b):
    return lax.dot_general(a, b, (((0,), (0,)), ((), ())), preferred_element_type=F32)


def normed_of(values):
    center = values - jnp.mean(values, axis=-1, keepdims=True)
    spread = lax.rsqrt(jnp.mean(center * center, axis=-1, keepdims=True) + ln_eps)
    return center * spread, spread


def whole(array):
    rank = len(array.shape)
    return pl.BlockSpec(array.shape, lambda *i: (0,) * rank, pipeline_mode=pl.Buffered(1))


def rows_of(count, width):
    return pl.BlockSpec((count, width), lambda i: (i, 0))


SMEM = pl.BlockSpec(memory_space=pltpu.SMEM)


def sds(shape, dtype):
    return jax.ShapeDtypeStruct(shape, dtype)


CHUNK = 2368


def prep_kernel(block, steps, shard_ref, flat_ref, *refs):
    *box_refs, extra_ref, held = refs
    step = pl.program_id(0)
    held[pl.ds(pl.multiple_of(MARGIN + CHUNK * step, 8), CHUNK), :] = flat_ref[...].reshape(CHUNK, LANES)

    @pl.when(step == steps - 1)
    def _():
        low = lax.broadcasted_iota(jnp.int32, (8, LANES), 1) < 64
        low_one = lax.broadcasted_iota(jnp.int32, (1, LANES), 1) < 64
        extra_ref[...] = jnp.zeros_like(extra_ref)
        for share in range(4):

            @pl.when(shard_ref[0] == share)
            def _(share=share):
                odd = share % 2 == 1

                def tile(first, stride):
                    here = held[pl.ds(first, 8, stride=stride), :]
                    if not odd:
                        return here
                    ahead = held[pl.ds(first - 1, 8, stride=stride), :]
                    return jnp.where(low, pltpu.roll(ahead, 64, 1), pltpu.roll(here, 64, 1))

                for box, groups, box_row, flat_row, stride in block.parts(share):
                    base = MARGIN + block.start[share] + flat_row

                    def body(group, carry, box=box, base=base, box_row=box_row, stride=stride):
                        for j in range(6):
                            first = base + 16 * stride * group + j
                            both = jnp.concatenate([tile(first, stride), tile(first + 8 * stride, stride)], axis=0)
                            at = pl.multiple_of(box_row + 16 * group, 16)
                            box_refs[box][pl.ds(at, 16), LANES * j : LANES * j + LANES] = both.astype(BF)
                        return carry

                    lax.fori_loop(0, groups, body, 0, unroll=8)
                count = flat_rows(block, share)
                for to, row, length in block.extra[share]:
                    for k in range(length):
                        at = MARGIN + row + k
                        value = held[at : at + 1, :]
                        if odd:
                            ahead = held[at - 1 : at, :]
                            value = jnp.where(low_one, pltpu.roll(ahead, 64, 1), pltpu.roll(value, 64, 1))
                            if row + k == 0:
                                value = jnp.where(low_one, 0.0, value)
                        elif row + k == count:
                            value = jnp.where(low_one, value, 0.0)
                        extra_ref[to + k : to + k + 1, :] = value.astype(BF).astype(F32)


def flat_rows(block, share):
    return 4615 if block is ATTN else 9226


def prep(block, flat, shard):
    steps = -(-flat.shape[0] // (CHUNK * LANES))
    return pl.pallas_call(
        functools.partial(prep_kernel, block, steps),
        grid=(steps,),
        in_specs=[SMEM, pl.BlockSpec((CHUNK * LANES,), lambda i: (i,))],
        out_specs=[pl.BlockSpec((D, D), lambda i: (0, 0))] * block.boxes
        + [pl.BlockSpec((EXTRA, LANES), lambda i: (0, 0))],
        out_shape=[sds((D, D), BF)] * block.boxes + [sds((EXTRA, LANES), F32)],
        scratch_shapes=[pltpu.VMEM((MARGIN + CHUNK * steps + MARGIN, LANES), F32)],
        compiler_params=params(),
    )(shard, flat)


def spread_row(extra_ref, first, count):
    return jnp.concatenate([extra_ref[first + k : first + k + 1, :] for k in range(count)], axis=1)


def patch_row(ref, row, values):
    at = row // 16 * 16
    rows = lax.broadcasted_iota(jnp.int32, (16, values.shape[1]), 0)
    old = ref[at : at + 16, :].astype(F32)
    ref[at : at + 16, :] = jnp.where(rows == row - at, values, old).astype(BF)


def load_attn(shard, boxes, qkv_ref, proj_ref, sems):
    for wait in (False, True):
        for k, box in enumerate(boxes):
            share = jnp.bitwise_xor(shard, k)

            @pl.when(share == 3)
            def _(box=box, k=k):
                copy = pltpu.make_async_copy(box, proj_ref, sems.at[k, 0])
                copy.wait() if wait else copy.start()

            @pl.when(share != 3)
            def _(box=box, k=k, share=share):
                for part in range(3):
                    copy = pltpu.make_async_copy(
                        box.at[pl.ds(256 * part, 256), :],
                        qkv_ref.at[pl.ds(pl.multiple_of(768 * part + 256 * share, 256), 256), :],
                        sems.at[k, part],
                    )
                    copy.wait() if wait else copy.start()


def load_feed(shard, boxes, up_ref, down_ref, sems):
    for wait in (False, True):
        for k, box in enumerate(boxes):
            share = jnp.bitwise_xor(shard, k)

            @pl.when(share >= 2)
            def _(box=box, k=k, share=share):
                at = pl.multiple_of(768 * (share - 2), 256)
                copy = pltpu.make_async_copy(box, down_ref.at[pl.ds(at, 768), :], sems.at[k, 0])
                copy.wait() if wait else copy.start()

            @pl.when(share < 2)
            def _(box=box, k=k, share=share):
                for h in range(2):
                    copy = pltpu.make_async_copy(
                        box.at[pl.ds(384 * h, 384), :],
                        up_ref.at[pl.ds(pl.multiple_of(768 * h + 384 * share, 128), 384), :],
                        sems.at[k, h],
                    )
                    copy.wait() if wait else copy.start()


ANYWHERE = pl.BlockSpec(memory_space=pl.ANY)


def half_masks():
    lane = lax.broadcasted_iota(jnp.int32, (1, LANES), 1)
    return (lane < 64).astype(F32).astype(BF), (lane >= 64).astype(F32).astype(BF)


def two_heads(pair, masks):
    return jnp.concatenate([pair * masks[0], pair * masks[1]], axis=0)


def attn_forward(seq, x_ref, shard_ref, extra_ref, a0, a1, a2, a3, *refs):
    *refs, qkv_w, proj_w, vec_ref, bias_ref, sems = refs

    @pl.when(pl.program_id(0) == 0)
    def _():
        load_attn(shard_ref[0], (a0, a1, a2, a3), qkv_w, proj_w, sems)
        for part in range(3):
            patch_row(qkv_w, 768 * part + 255, spread_row(extra_ref, 12 + 6 * part, 6))
            patch_row(qkv_w, 768 * part + 512, spread_row(extra_ref, 30 + 6 * part, 6))
        vec_ref[...] = jnp.zeros_like(vec_ref)
        for row, first in enumerate((0, 6, 60, EXTRA + 0, EXTRA + 6)):
            vec_ref[row : row + 1, :] = spread_row(extra_ref, first, 6)
        bias_ref[...] = jnp.zeros_like(bias_ref)
        bias_ref[0:1, 0:768] = spread_row(extra_ref, 48, 6)
        bias_ref[0:1, 1536:2304] = spread_row(extra_ref, 54, 6)

    first_ref, qkv_ref, log_ref, att_ref, hid_ref, second_ref = refs
    x = x_ref[...].astype(F32)
    normed, _ = normed_of(x)
    first = (normed * vec_ref[0:1, :] + vec_ref[1:2, :]).astype(BF)
    first_ref[...] = first
    for part in range(3):
        cols = slice(768 * part, 768 * part + 768)
        qkv_ref[:, cols] = (dot(first, qkv_w[cols, :]) + bias_ref[0:1, cols]).astype(BF)
    masks = half_masks()
    real = lax.broadcasted_iota(jnp.int32, (2, T, T), 1) < seq
    for pair in range(HEADS // 2):
        at = LANES * pair
        for image in range(x_ref.shape[0] // T):
            own = slice(T * image, T * image + T)
            q = qkv_ref[own, at : at + LANES] * jnp.asarray(0.125, BF)
            k = two_heads(qkv_ref[own, 768 + at : 768 + at + LANES], masks)
            v = two_heads(qkv_ref[own, 1536 + at : 1536 + at + LANES], masks)
            scores = dot_nt(k, q).reshape(2, T, T)
            scores = jnp.where(real, scores, -1e30)
            top = jnp.max(scores, axis=1, keepdims=True)
            weight = jnp.exp(scores - top)
            total = jnp.sum(weight, axis=1, keepdims=True)
            logs = top + jnp.log(total)
            log_ref[image, 2 * pair : 2 * pair + 1, :] = logs[0]
            log_ref[image, 2 * pair + 1 : 2 * pair + 2, :] = logs[1]
            probs = (weight * (1.0 / total)).astype(BF).reshape(2 * T, T)
            att_ref[own, at : at + LANES] = dot_tn(probs, v).astype(BF)
    hidden = x + dot(att_ref[...], proj_w[...]) + vec_ref[2:3, :]
    hid_ref[...] = hidden
    normed, _ = normed_of(hidden)
    second_ref[...] = (normed * vec_ref[3:4, :] + vec_ref[4:5, :]).astype(BF)


FORWARD_IMAGES = 2


def call_attn_forward(seq, x, weights, boxes):
    shard, extra = weights
    rows = x.shape[0]
    images = rows // T
    step = FORWARD_IMAGES if images % FORWARD_IMAGES == 0 else 1
    tall = step * T
    made = [sds((2304, D), BF), sds((D, D), BF), sds((8, D), F32), sds((8, 2304), F32)]
    return pl.pallas_call(
        functools.partial(attn_forward, seq),
        grid=(images // step,),
        in_specs=[rows_of(tall, D), SMEM, whole(extra)] + [ANYWHERE] * 4,
        out_specs=[
            rows_of(tall, D),
            rows_of(tall, 2304),
            pl.BlockSpec((step, HEADS, T), lambda i: (i, 0, 0)),
            rows_of(tall, D),
            rows_of(tall, D),
            rows_of(tall, D),
        ]
        + [pl.BlockSpec(shape.shape, lambda i: (0, 0)) for shape in made],
        out_shape=[
            sds((rows, D), BF),
            sds((rows, 2304), BF),
            sds((images, HEADS, T), F32),
            sds((rows, D), BF),
            sds((rows, D), F32),
            sds((rows, D), BF),
        ]
        + made,
        scratch_shapes=[pltpu.SemaphoreType.DMA((4, 3))],
        compiler_params=params(),
    )(x, shard, extra, *boxes)


def hand_out(index, box, outs, sems):
    copies = [pltpu.make_async_copy(box.at[k], out, sems.at[k]) for k, out in enumerate(outs)]
    for k, copy in enumerate(copies):

        @pl.when(index == k)
        def _(copy=copy):
            copy.start()

    @pl.when(index == len(outs) - 1)
    def _():
        for copy in copies:
            copy.wait()


HALF = FF // 2
ROW_STEPS = 4


def feed(seq, part, tall, shard_ref, extra_ref, a0, a1, a2, a3, second_ref, cot_ref, result_ref, *refs):
    last = part == 1
    if last:
        before_ref, out_ref, gs_ref, *refs = refs
    else:
        out_ref, gs_ref, cot_sum, *refs = refs
    sum_ref, edge_ref, *outs, up_w, down_w, bias, second_all, cot_all, act_all, pre_all, box, sems, box_sems = refs
    step = pl.program_id(0)
    shard = shard_ref[0]

    @pl.when(step == 0)
    def _():
        load_feed(shard, (a0, a1, a2, a3), up_w, down_w, sems)
        for h in range(2):
            patch_row(up_w, 768 * h + 383, spread_row(extra_ref, EXTRA + 12 + 12 * h + 6 * part, 6))
            bias[0:1, 768 * h : 768 * h + 768] = spread_row(extra_ref, EXTRA + 36 + 12 * h + 6 * part, 6)
        if last:
            patch_row(down_w, 767, spread_row(extra_ref, EXTRA + 60, 6))
        sum_ref[...] = jnp.zeros_like(sum_ref)
        edge_ref[...] = jnp.zeros_like(edge_ref)
        if not last:
            cot_sum[...] = jnp.zeros_like(cot_sum)

    @pl.when(step < ROW_STEPS)
    def _():
        at = pl.ds(pl.multiple_of(step * tall, 16), tall)
        second = second_ref[...]
        cot = cot_ref[...]
        second_all[at, :] = second
        cot_all[at, :] = cot
        if last:
            result = result_ref[...]
            grad_second = before_ref[...]
        else:
            result = result_ref[...] + spread_row(extra_ref, EXTRA + 66, 6)
            grad_second = jnp.zeros_like(result)
            cot_sum[0:1, :] += jnp.sum(cot.astype(F32), axis=0, keepdims=True)
        for h in range(2):
            cols = slice(768 * h, 768 * h + 768)
            pre = dot(second, up_w[cols, :]) + bias[0:1, cols]
            grad_act = dot_nt(cot, down_w[cols, :])
            half = 0.5 * (1.0 + lax.erf(pre * root_half))
            act = (pre * half).astype(BF)
            grad_pre = grad_act * (half + pre * jnp.exp(-0.5 * pre * pre) * inv_root_tau)
            low = grad_pre.astype(BF)
            act_all[at, cols] = act
            pre_all[at, cols] = low
            sum_ref[0:1, cols] += jnp.sum(grad_pre, axis=0, keepdims=True)
            result = result + dot(act, down_w[cols, :])
            grad_second = grad_second + dot_nt(low, up_w[cols, :])
        if last:
            for image in range(tall // T):
                out_ref[image] = result[T * image : T * image + seq].astype(BF)
        else:
            out_ref[...] = result
        gs_ref[...] = grad_second

    index = step - ROW_STEPS
    side = jnp.bitwise_xor(shard // 2, 1 - index % 2)
    core = jnp.where(index >= 2, shard % 2, 1 - shard % 2)

    @pl.when((index >= 0) & (side == 0))
    def _():
        left = second_all[:, pl.ds(pl.multiple_of(384 * core, 128), 384)]
        for h in range(2):
            grad = dot_tn(left, pre_all[:, 768 * h : 768 * h + 768])
            box[index, 384 * h : 384 * h + 384, :] = grad.astype(BF)

            @pl.when(core == 0)
            def _(grad=grad, h=h):
                edge_ref[0:1, 768 * h : 768 * h + 768] = grad[383:384]

    @pl.when((index >= 0) & (side == 1))
    def _():
        left = act_all[:, pl.ds(pl.multiple_of(768 * core, 128), 768)]
        grad = dot_tn(left, cot_all[...])
        box[index] = grad.astype(BF)

        @pl.when(core == 0)
        def _():
            edge_ref[1:2, 0:768] = grad[767:768]

    hand_out(index, box, outs, box_sems)


def call_feed(seq, part, shard, extra, boxes, second, cot, result, before=None):
    rows = second.shape[0]
    images = rows // T
    tall = rows // ROW_STEPS
    last = part == 1
    row = lambda i: jnp.minimum(i, ROW_STEPS - 1)
    block = pl.BlockSpec((tall, D), lambda i: (row(i), 0))
    out = pl.BlockSpec((tall // T, seq, D), lambda i: (row(i), 0, 0)) if last else block
    small = lambda width: pl.BlockSpec((8, width), lambda i: (0, 0))
    return pl.pallas_call(
        functools.partial(feed, seq, part, tall),
        grid=(ROW_STEPS + 4,),
        in_specs=[SMEM, whole(extra)] + [ANYWHERE] * 4 + [block] * (4 if last else 3),
        out_specs=[out, block] + ([] if last else [small(D)]) + [small(HALF), small(HALF)] + [ANYWHERE] * 4,
        out_shape=[sds((images, seq, D), BF) if last else sds((rows, D), F32), sds((rows, D), F32)]
        + ([] if last else [sds((8, D), F32)])
        + [sds((8, HALF), F32), sds((8, HALF), F32)] + [sds((D, D), BF)] * 4,
        scratch_shapes=[
            pltpu.VMEM((HALF, D), BF),
            pltpu.VMEM((HALF, D), BF),
            pltpu.VMEM((8, HALF), F32),
            pltpu.VMEM((rows, D), BF),
            pltpu.VMEM((rows, D), BF),
            pltpu.VMEM((rows, HALF), BF),
            pltpu.VMEM((rows, HALF), BF),
            pltpu.VMEM((4, D, D), BF),
            pltpu.SemaphoreType.DMA((4, 2)),
            pltpu.SemaphoreType.DMA((4,)),
        ],
        compiler_params=params(60),
    )(shard, extra, *boxes, second, cot, result, *([before] if last else []))


WIDE = 384


def attn_backward(seq, group, base, count, last, shard_ref, log_ref, qkv_ref, first_ref, att_ref, *refs):
    step = pl.program_id(0)
    shard = shard_ref[0]
    if group == 0:
        gs_ref, hid_ref, cot_ref, vec_ref, proj_w, *refs = refs
    else:
        low_ref, ga_ref, *refs = refs
    if last:
        if group == 0:
            head_before, sum_before, first_any, att_any, low_any, grad_any, _, _, *refs = refs
        else:
            head_before, first_any, att_any, low_any, grad_any, *refs = refs
    grad_ref, head_sum, *refs = refs
    if group == 0:
        low_ref, ga_ref, gh_ref, sum_ref, *refs = refs
    if last:
        edge_ref, *outs, grad_all, first_all, low_all, att_all, box, box_sems, load_sems = refs
        done = pl.ds(0, base * T)
        loads = [
            pltpu.make_async_copy(grad_any.at[done], grad_all.at[done], load_sems.at[0]),
            pltpu.make_async_copy(first_any.at[done], first_all.at[done], load_sems.at[1]),
            pltpu.make_async_copy(low_any.at[done], low_all.at[done], load_sems.at[2]),
            pltpu.make_async_copy(
                att_any.at[done, pl.ds(WIDE * group, WIDE)], att_all.at[done], load_sems.at[3]
            ),
        ]

    @pl.when(step == 0)
    def _():
        if last:
            for load in loads:
                load.start()
            edge_ref[...] = jnp.zeros_like(edge_ref)
            head_sum[...] = head_before[...]
        else:
            head_sum[...] = jnp.zeros_like(head_sum)
        if group == 0:
            sum_ref[...] = sum_before[...] if last else jnp.zeros_like(sum_ref)

    @pl.when(step < count)
    def _():
        at_rows = pl.ds(pl.multiple_of((step + base) * T, 16), T)
        if last:
            first_all[at_rows, :] = first_ref[...]
            att_all[at_rows, :] = att_ref[...]
        if group == 0:
            gs = gs_ref[...]
            normed, spread = normed_of(hid_ref[...])
            gn = gs * vec_ref[3:4, :]
            gh = cot_ref[...].astype(F32) + spread * (
                gn - jnp.mean(gn, axis=-1, keepdims=True) - normed * jnp.mean(gn * normed, axis=-1, keepdims=True)
            )
            sum_ref[0:1, :] += jnp.sum(gs * normed, axis=0, keepdims=True)
            sum_ref[1:2, :] += jnp.sum(gs, axis=0, keepdims=True)
            sum_ref[2:3, :] += jnp.sum(gh, axis=0, keepdims=True)
            gh_ref[...] = gh
            gh_low = gh.astype(BF)
            low_ref[...] = gh_low
            ga_ref[...] = dot_nt(gh_low, proj_w[...]).astype(BF)
        if last:
            low_all[at_rows, :] = low_ref[...]
        low = lax.broadcasted_iota(jnp.int32, (T, LANES), 1) < 64
        real = lax.broadcasted_iota(jnp.int32, (2, T, T), 1) < seq
        eighth = jnp.asarray(0.125, BF)
        masks = half_masks()
        for pair in range(3):
            at = LANES * pair
            full = WIDE * group + at
            head = 6 * group + 2 * pair
            q = qkv_ref[:, full : full + LANES] * eighth
            k = two_heads(qkv_ref[:, 768 + full : 768 + full + LANES], masks)
            v = two_heads(qkv_ref[:, 1536 + full : 1536 + full + LANES], masks)
            grad_out = ga_ref[:, at : at + LANES]
            scores = dot_nt(k, q).reshape(2, T, T)
            logs = jnp.concatenate([log_ref[0:1, head : head + 1, :], log_ref[0:1, head + 1 : head + 2, :]], axis=0)
            probs = jnp.where(real, jnp.exp(scores - logs), 0.0)
            grad_v = dot(probs.astype(BF).reshape(2 * T, T), grad_out)
            grad_probs = dot_nt(v, grad_out).reshape(2, T, T)
            delta = jnp.sum(probs * grad_probs, axis=1, keepdims=True)
            grad_scores = (probs * (grad_probs - delta)).astype(BF).reshape(2 * T, T)
            grad_k = dot(grad_scores, q)
            grads = (
                dot_tn(grad_scores, k * eighth),
                jnp.where(low, grad_k[:T], grad_k[T:]),
                jnp.where(low, grad_v[:T], grad_v[T:]),
            )
            for part, grad in enumerate(grads):
                if part != 1:
                    row = part // 2
                    head_sum[row : row + 1, at : at + LANES] += jnp.sum(grad, axis=0, keepdims=True)
                cols = slice(WIDE * part + at, WIDE * part + at + LANES)
                grad = grad.astype(BF)
                grad_ref[:, cols] = grad
                if last:
                    grad_all[at_rows, cols] = grad

    if not last:
        return

    @pl.when(step == count)
    def _():
        for load in loads:
            load.wait()

    index = step - count
    side = jnp.bitwise_xor(shard // 2, 1 - index % 2)
    core = jnp.where(index >= 2, shard % 2, 1 - shard % 2)
    share = 2 * side + core

    @pl.when((index >= 0) & (share == 3))
    def _():
        box[index] = dot_tn(att_all[...], low_all[...]).astype(BF)

    @pl.when((index >= 0) & (share != 3))
    def _():
        grad = dot_tn(first_all[:, pl.ds(pl.multiple_of(256 * share, 256), 256)], grad_all[...])
        for part in range(3):
            cols = slice(WIDE * part, WIDE * part + WIDE)
            for u in range(2):
                box[index, 128 * part : 128 * part + 128, WIDE * u : WIDE * u + WIDE] = grad[
                    128 * u : 128 * u + 128, cols
                ].astype(BF)

        @pl.when(share == 0)
        def _():
            edge_ref[0:1, :] = grad[255:256]

        @pl.when(share == 2)
        def _():
            edge_ref[1:2, :] = grad[0:1]

    hand_out(index, box, outs, box_sems)


def call_attn_backward(seq, group, base, count, shard, log_total, qkv, first, attended, *more, before=()):
    rows = first.shape[0]
    last = len(before) > 0
    row = lambda i: jnp.minimum(i, count - 1) + base
    block = lambda width, col=0: pl.BlockSpec((T, width), lambda i: (row(i), col))
    small = lambda width: pl.BlockSpec((8, width), lambda i: (0, 0))
    in_specs = [SMEM, pl.BlockSpec((1, HEADS, T), lambda i: (row(i), 0, 0)), block(2304), block(D), block(WIDE, group)]
    out_specs = [block(3 * WIDE), small(WIDE)]
    out_shape = [sds((rows, 3 * WIDE), BF), sds((8, WIDE), F32)]
    if group == 0:
        in_specs += [block(D)] * 3 + [whole(more[3]), whole(more[4])]
        out_specs += [block(D), block(D), block(D), small(D)]
        out_shape += [sds((rows, D), BF), sds((rows, D), BF), sds((rows, D), F32), sds((8, D), F32)]
    else:
        in_specs += [block(D), block(WIDE, 1)]
    aliases, scratch, extra = {}, [], []
    if last:
        at = len(in_specs)
        if group == 0:
            grad, head, low, ga, gh, total = before
            extra = [head, total, first, attended, low, grad, ga, gh]
            in_specs += [whole(head), whole(total)] + [ANYWHERE] * 6
            aliases = {at + 4: 2, at + 5: 0, at + 6: 3, at + 7: 4}
        else:
            grad, head = before
            extra = [head, first, attended, more[0], grad]
            in_specs += [whole(head)] + [ANYWHERE] * 4
            aliases = {at + 4: 0}
        out_specs += [small(3 * WIDE)] + [ANYWHERE] * 4
        out_shape += [sds((8, 3 * WIDE), F32)] + [sds((WIDE, D), BF)] * 4
        scratch = [
            pltpu.VMEM((rows, 3 * WIDE), BF),
            pltpu.VMEM((rows, D), BF),
            pltpu.VMEM((rows, D), BF),
            pltpu.VMEM((rows, WIDE), BF),
            pltpu.VMEM((4, WIDE, D), BF),
            pltpu.SemaphoreType.DMA((4,)),
            pltpu.SemaphoreType.DMA((4,)),
        ]
    return pl.pallas_call(
        functools.partial(attn_backward, seq, group, base, count, last),
        grid=(count + 4 if last else count,),
        in_specs=in_specs,
        out_specs=out_specs,
        out_shape=out_shape,
        input_output_aliases=aliases,
        scratch_shapes=scratch,
        compiler_params=params(),
    )(shard, log_total, qkv, first, attended, *more, *extra)


def input_backward(seq, grad0, grad1, gh_ref, x_ref, vec_ref, qkv_w, out_ref, sum_ref):
    @pl.when(pl.program_id(0) == 0)
    def _():
        sum_ref[...] = jnp.zeros_like(sum_ref)

    grad_first = None
    for part in range(3):
        cols = slice(WIDE * part, WIDE * part + WIDE)
        both = jnp.concatenate([grad0[:, cols], grad1[:, cols]], axis=1)
        term = dot_nt(both, qkv_w[768 * part : 768 * part + 768, :])
        grad_first = term if part == 0 else grad_first + term
    normed, spread = normed_of(x_ref[...].astype(F32))
    gn = grad_first * vec_ref[0:1, :]
    grad = gh_ref[...] + spread * (
        gn - jnp.mean(gn, axis=-1, keepdims=True) - normed * jnp.mean(gn * normed, axis=-1, keepdims=True)
    )
    sum_ref[0:1, :] += jnp.sum(grad_first * normed, axis=0, keepdims=True)
    sum_ref[1:2, :] += jnp.sum(grad_first, axis=0, keepdims=True)
    for image in range(grad.shape[0] // T):
        out_ref[image] = grad[T * image : T * image + seq].astype(BF)


def call_input_backward(seq, grads, gh, x, vec, qkv_w):
    rows = gh.shape[0]
    images = rows // T
    step = 2 if images % 2 == 0 else 1
    tall = step * T
    return pl.pallas_call(
        functools.partial(input_backward, seq),
        grid=(images // step,),
        in_specs=[rows_of(tall, 3 * WIDE)] * 2 + [rows_of(tall, D), rows_of(tall, D), whole(vec), whole(qkv_w)],
        out_specs=[pl.BlockSpec((step, seq, D), lambda i: (i, 0, 0)), pl.BlockSpec((8, D), lambda i: (0, 0))],
        out_shape=[sds((images, seq, D), BF), sds((8, D), F32)],
        compiler_params=params(),
    )(*grads, gh, x, vec, qkv_w)


def putter(out_ref):
    out_ref[...] = jnp.zeros_like(out_ref)

    def put(first, ref, row, col, width):
        for k in range(width // LANES):
            at = col + LANES * k
            out_ref[first + k : first + k + 1, :] = ref[row : row + 1, at : at + LANES]

    return put


def pack(last_sum, back_sum, head0, head1, edge0, edge1, pre0, pre1, up0, up1, cot_sum, out_ref):
    put = putter(out_ref)
    put(0, last_sum, 0, 0, D)
    put(6, last_sum, 1, 0, D)
    for group, (head, edge) in enumerate(((head0, edge0), (head1, edge1))):
        for part in range(3):
            put(12 + 6 * part + 3 * group, edge, 0, WIDE * part, WIDE)
            put(30 + 6 * part + 3 * group, edge, 1, WIDE * part, WIDE)
        put(48 + 3 * group, head, 0, 0, WIDE)
        put(54 + 3 * group, head, 1, 0, WIDE)
    put(60, back_sum, 2, 0, D)
    put(EXTRA, back_sum, 0, 0, D)
    put(EXTRA + 6, back_sum, 1, 0, D)
    for j, (pre, up) in enumerate(((pre0, up0), (pre1, up1))):
        for h in range(2):
            put(EXTRA + 12 + 12 * h + 6 * j, up, 0, 768 * h, D)
            put(EXTRA + 36 + 12 * h + 6 * j, pre, 0, 768 * h, D)
    put(EXTRA + 60, up1, 1, 0, D)
    put(EXTRA + 66, cot_sum, 0, 0, D)


def call_pack(*arrays):
    return pl.pallas_call(
        pack,
        in_specs=[pl.BlockSpec(memory_space=pltpu.VMEM)] * len(arrays),
        out_specs=pl.BlockSpec(memory_space=pltpu.VMEM),
        out_shape=sds((2 * EXTRA, LANES), F32),
        compiler_params=params(),
    )(*arrays)


def adam_kernel(block, share_size, scale, boxes, shard_ref, power_ref, extra_ref, *refs):
    box_refs = refs[:boxes]
    flat_ref, mom_ref, grad_ref, change_ref, new_ref, held = refs[boxes:]
    step = pl.program_id(0)

    @pl.when(step == 0)
    def _():
        for share in range(4):

            @pl.when(shard_ref[0] == share)
            def _(share=share):
                for box, groups, box_row, col, cols, flat_row, stride in block.grad_parts(share):
                    base = MARGIN + block.start[share] + flat_row

                    def body(group, carry, box=box, box_row=box_row, col=col, cols=cols, base=base, stride=stride):
                        row = pl.multiple_of(box_row + 16 * group, 16)
                        for j in range(cols):
                            at = LANES * (col + j)
                            both = box_refs[box][pl.ds(row, 16), at : at + LANES].astype(F32)
                            to = base + 16 * stride * group + j
                            held[pl.ds(to, 8, stride=stride), :] = both[0:8]
                            held[pl.ds(to + 8 * stride, 8, stride=stride), :] = both[8:16]
                        return carry

                    lax.fori_loop(0, groups, body, 0, unroll=8)
                for source, row, length in block.put[share]:
                    held[MARGIN + row : MARGIN + row + length, :] = extra_ref[block.base + source : block.base + source + length, :]

    start = pl.multiple_of(MARGIN + CHUNK * step, 8)
    shard = shard_ref[0]
    low = lax.broadcasted_iota(jnp.int32, (CHUNK, LANES), 1) < 64
    here = held[pl.ds(start, CHUNK), :]
    after = held[pl.ds(start + 1, CHUNK), :]
    shifted = jnp.where(low, pltpu.roll(here, 64, 1), pltpu.roll(after, 64, 1))
    grad = jnp.where(shard % 2 == 1, shifted, here) * scale
    position = (
        shard * share_size
        + step * (CHUNK * LANES)
        + lax.broadcasted_iota(jnp.int32, (CHUNK, LANES), 0) * LANES
        + lax.broadcasted_iota(jnp.int32, (CHUNK, LANES), 1)
    )
    matrix = jnp.zeros((CHUNK, LANES), jnp.bool_)
    for first, end in block.matrices:
        matrix = matrix | ((position >= first) & (position < end))
    size = CHUNK * LANES
    p = flat_ref[...].reshape(CHUNK, LANES)
    m = beta_one * mom_ref[0, :].reshape(CHUNK, LANES) + (1.0 - beta_one) * grad
    s = beta_two * mom_ref[1, :].reshape(CHUNK, LANES) + (1.0 - beta_two) * grad * grad
    ratio = (m * power_ref[0]) / (jnp.sqrt(s * power_ref[1]) + adam_eps)
    change = jnp.where(matrix, rate_matrix, rate_vector) * (ratio + jnp.where(matrix, decay_matrix, 0.0) * p)
    grad_ref[...] = grad.reshape(size)
    change_ref[...] = change.reshape(size)
    new_ref[0, :] = m.reshape(size)
    new_ref[1, :] = s.reshape(size)


def adam(block, shard, powers, extra, boxes, flat, moments, scale):
    count = flat.shape[0]
    steps = -(-count // (CHUNK * LANES))
    line = pl.BlockSpec((CHUNK * LANES,), lambda i: (i,))
    two = pl.BlockSpec((2, CHUNK * LANES), lambda i: (0, i))
    return pl.pallas_call(
        functools.partial(adam_kernel, block, count, scale, len(boxes)),
        grid=(steps,),
        in_specs=[SMEM, SMEM, whole(extra)] + [whole(box) for box in boxes] + [line, two],
        out_specs=[line, line, two],
        out_shape=[sds((count,), F32), sds((count,), F32), sds((2, count), F32)],
        scratch_shapes=[pltpu.VMEM((MARGIN + CHUNK * steps + MARGIN, LANES), F32)],
        compiler_params=params(),
    )(shard, powers, extra, *boxes, flat, moments)


def swap(value, axis, bit):
    pairs = [(i, i ^ bit) for i in range(lax.axis_size(axis))]
    return lax.ppermute(value, axis, pairs)


def turn(value, axis, unit, distance):
    size = lax.axis_size(axis)
    return lax.ppermute(value, axis, [(i, (i + unit * distance) % size) for i in range(size)])


def pick(array, index, axis=0):
    return lax.dynamic_index_in_dim(array, index, axis, keepdims=False)


class Line:
    def __init__(self):
        self.last = None

    def __call__(self, step, *args):
        if self.last is not None:
            flat, tree = jax.tree.flatten(args)
            flat = lax.optimization_barrier((self.last, *flat))[1:]
            args = jax.tree.unflatten(tree, flat)
        out = step(*args)
        self.last = min(jax.tree.leaves(out), key=lambda leaf: leaf.size)
        return out


def pause_kernel(in_ref, out_ref):
    out_ref[...] = in_ref[...]


def pause(line, value):
    return line(
        pl.pallas_call(
            pause_kernel,
            out_shape=sds(value.shape, value.dtype),
            cost_estimate=pl.CostEstimate(flops=10**11, bytes_accessed=10**8, transcendentals=0),
        ),
        value,
    )


class Sum:
    def __init__(self, line, across, same, mine_across, mine):
        self.line, self.mine_across, self.mine = line, mine_across, mine
        self.rows = mine.shape[0]
        rep = lax.axis_index("rep")
        self.near, self.far = rep % 2, rep // 2
        self.count = lax.axis_size("rep") // 2
        self.came_across, self.here = swap(across, "shard", 1), swap(same, "shard", 1)

    def side(self):
        add = lambda a, b: (a.astype(F32) + b.astype(F32)).astype(BF)
        send = self.line(add, self.mine_across, self.came_across)
        self.came = swap(send, "shard", 2)
        self.here = self.line(lambda a: a, self.here)

    def close(self):
        def step(mine, here, came):
            total = mine.astype(F32) + here.astype(F32) + came.astype(F32)
            halves = total.reshape(2, self.rows // 2, D)
            return pick(halves, 1 - self.near).astype(BF), pick(halves, self.near)

        send, self.half = self.line(step, self.mine, self.here, self.came)
        self.came = swap(send, "rep", 1)

    def level(self, bit):
        if bit == 2:
            self.part = self.line(lambda a, b: (a + b.astype(F32)).astype(BF), self.half, self.came)
        else:
            self.part = self.line(lambda a, b: (a.astype(F32) + b.astype(F32)).astype(BF), self.part, self.came)
        self.came = swap(self.part, "rep", bit)

    def back_level(self):
        self.half = self.line(lambda a, b: (a.astype(F32) + b.astype(F32)).astype(BF), self.part, self.came)
        self.came = swap(self.half, "rep", 1)

    def along(self):
        def step(half, came):
            parts = (half + came.astype(F32)).reshape(self.count, self.rows // 2 // self.count, D)
            sends = [pick(parts, (self.far + d) % self.count).astype(BF) for d in range(1, self.count)]
            return sends, pick(parts, self.far)

        sends, self.part = self.line(step, self.half, self.came)
        self.came = [turn(send, "rep", 2, d + 1) for d, send in enumerate(sends)]

    def back_along(self):
        def step(part, came):
            for value in came:
                part = part + value.astype(F32)
            return part.astype(BF)

        self.part = self.line(step, self.part, self.came)
        self.came = [turn(self.part, "rep", 2, d) for d in range(1, self.count)]

    def back_close(self):
        def step(part, came):
            full = jnp.zeros((self.count,) + part.shape, BF)
            for d, value in enumerate([part] + came):
                full = lax.dynamic_update_slice_in_dim(full, value[None], (self.far + self.count - d) % self.count, 0)
            return full.reshape(self.rows // 2, D)

        self.half = self.line(step, self.part, self.came)
        self.came = swap(self.half, "rep", 1)

    def end(self):
        def step(half, came):
            first = self.near == 0
            return jnp.concatenate([jnp.where(first, half, came), jnp.where(first, came, half)], axis=0)

        return self.line(step, self.half, self.came)


class SumAll:
    def __init__(self, line, value):
        self.line, self.value = line, value
        self.hops = [("shard", 1), ("shard", 2)]
        bit = 2
        while bit < lax.axis_size("rep"):
            self.hops.append(("rep", bit))
            bit *= 2
        self.hops.append(("rep", 1))
        self.came = swap(value, *self.hops.pop(0))

    def hop(self):
        self.value = self.line(lambda a, b: a + b, self.value, self.came)
        if self.hops:
            self.came = swap(self.value, *self.hops.pop(0))
            return False
        return True


def body(layer_input, out_cotangent, attention_params, attention_moments, feedforward_params, feedforward_moments, step_count):
    images, seq, _ = layer_input.shape
    rows = images * T
    image_total = images * lax.axis_size("shard") * lax.axis_size("rep")
    scale = 1.0 / image_total
    shard = lax.axis_index("shard").astype(jnp.int32).reshape(1)
    time = step_count[0].astype(F32)
    powers = jnp.stack([1.0 / (1.0 - jnp.power(beta_one, time)), 1.0 / (1.0 - jnp.power(beta_two, time))])
    pad = ((0, 0), (0, T - seq), (0, 0))
    turned = lambda tokens: jnp.swapaxes(tokens, 0, 1)
    laid = lambda tokens: with_layout_constraint(turned(tokens), Layout((0, 1, 2)))
    padded = lambda tokens: jnp.pad(tokens, pad).reshape(rows, D)
    line = Line()

    attn_box, attn_extra = line(functools.partial(prep, ATTN), attention_params, shard)
    attn_across = swap(attn_box, "shard", 2)
    attn_near = swap(attn_box, "shard", 1)
    box0, box1, feed_extra = line(functools.partial(prep, FEED), feedforward_params, shard)
    extra = line(lambda a, b: jnp.concatenate([a, b], axis=0), attn_extra, feed_extra)
    came = swap(extra, "shard", 1)
    x = line(padded, layer_input)
    extra = line(lambda a, b: a + b, extra, came)
    came = swap(extra, "shard", 2)
    cot = line(padded, out_cotangent)
    extra = line(lambda a, b: a + b, extra, came)
    near0, near1 = swap(box0, "shard", 1), swap(box1, "shard", 1)
    across, send0 = line(lambda a, b: lax.optimization_barrier((a, b)), attn_across, box0)
    attn_both = swap(across, "shard", 1)
    across0 = swap(send0, "shard", 2)
    boxes = (attn_box, attn_near, attn_across, attn_both)
    first, qkv, log_total, attended, hidden, second, qkv_w, proj_w, vec, bias = line(
        lambda x, w, b: call_attn_forward(seq, x, w, b), x, (shard, extra), boxes
    )
    across, send1 = line(lambda a, b: lax.optimization_barrier((a, b)), across0, box1)
    both0 = swap(across, "shard", 1)
    across1 = swap(send1, "shard", 2)
    boxes = (box0, near0, across0, both0)
    result, gs, cot_sum, pre0, up0, *grads = line(
        lambda *a: call_feed(seq, 0, *a), shard, extra, boxes, second, cot, hidden
    )
    feed0 = Sum(line, *grads)
    both1 = swap(line(lambda a: a, across1), "shard", 1)
    feed0.side()
    boxes = (box1, near1, across1, both1)
    layer_output, gs, pre1, up1, *grads = line(
        lambda *a: call_feed(seq, 1, *a), shard, extra, boxes, second, cot, result, gs
    )
    feed1 = Sum(line, *grads)
    feed0.close()
    layer_output = line(laid, layer_output)
    feed1.side()
    half = images // 2
    common = (shard, log_total, qkv, first, attended)
    more = (gs, hidden, cot, vec, proj_w)
    before = line(lambda *a: call_attn_backward(seq, 0, 0, half, *a), *common, *more)
    feed0.along()
    grad0, head0, gh_low, ga, gh, back_sum, edge0, *grads = line(
        lambda b, *a: call_attn_backward(seq, 0, half, images - half, *a, before=b), tuple(before), *common, *more
    )
    attn0 = Sum(line, *grads)
    feed1.close()
    feed0.back_along()
    attn0.side()
    more = (gh_low, ga)
    before = line(lambda *a: call_attn_backward(seq, 1, 0, half, *a), *common, *more)
    feed0.back_close()
    feed1.along()
    grad1, head1, edge1, *grads = line(
        lambda b, *a: call_attn_backward(seq, 1, half, images - half, *a, before=b), tuple(before), *common, *more
    )
    attn1 = Sum(line, *grads)
    feed1.back_along()
    attn0.close()
    feed_box0 = feed0.end()
    head1 = pause(line, head1)
    attn1.side()
    input_grad, last_sum = line(lambda *a: call_input_backward(seq, *a), (grad0, grad1), gh, x, vec, qkv_w)
    sums = line(call_pack, last_sum, back_sum, head0, head1, edge0, edge1, pre0, pre1, up0, up1, cot_sum)
    bits = [2 << k for k in range((lax.axis_size("rep") // 2).bit_length() - 1)]
    sums = SumAll(line, sums)
    attn1.close()
    input_grad = line(laid, input_grad)
    attn0.level(2)
    sums.hop()
    feed1.back_close()
    sums.hop()
    attn1.level(2)
    for bit in bits[1:]:
        attn0.level(bit)
    while not sums.hop():
        pass
    feed_box1 = feed1.end()
    for bit in bits[1:]:
        attn1.level(bit)
    feed_grad, feed_change, feed_new = line(
        lambda *a: adam(FEED, *a, scale), shard, powers, sums.value, [feed_box0, feed_box1], feedforward_params, feedforward_moments
    )
    attn0.back_level()
    attn1.back_level()
    attn_box0 = attn0.end()
    attn_grad, attn_change, attn_new = line(
        lambda *a: adam(ATTN, *a, scale), shard, powers, sums.value, [attn_box0, attn1.end()], attention_params, attention_moments
    )
    return (turned(layer_output), turned(input_grad), attn_grad, feed_grad, attn_change, attn_new, feed_change, feed_new)


def solution(mesh):
    tokens = P(("shard", "rep"), None, None)
    in_specs = (tokens, tokens, P("shard"), P(None, "shard"), P("shard"), P(None, "shard"), P())
    out_specs = (tokens, tokens, P("shard"), P("shard"), P("shard"), P(None, "shard"), P("shard"), P(None, "shard"))
    return jax.shard_map(body, mesh=mesh, in_specs=in_specs, out_specs=out_specs, check_vma=False)
```

```python
import functools

import jax
import jax.numpy as jnp
from jax import lax
from jax.experimental import pallas as pl
from jax.experimental.pallas import tpu as pltpu
from jax.experimental.layout import Layout, with_layout_constraint
from jax.sharding import PartitionSpec as P

D = 768
HEADS = 12
FF = 3072
T = 208

F32 = jnp.float32
BF = jnp.bfloat16

ln_eps = 1e-06
beta_one = 0.9
beta_two = 0.999
adam_eps = 1e-08
rate_matrix = 0.01
rate_vector = 0.1
decay_matrix = 0.05
root_half = 0.7071067811865476
inv_root_tau = 0.3989422804014327

MB = 1 << 20
LANES = 128
MARGIN = 8

ATTN_START = (12, 5, -3, 2)
FEED_START = (12, 2, 15, 5)


def attn_parts(share):
    if share < 3:
        return [(0, 16, 256 * part, 6 * part, 18) for part in range(3)]
    return [(0, 48, 0, 0, 6)]


def feed_parts(share):
    if share < 2:
        return [(j, 24, 384 * h, 12 * h + 6 * j, 24) for j in range(2) for h in range(2)]
    return [(j, 48, 0, 4608 * j, 6) for j in range(2)]


def attn_grad_parts(share):
    if share < 3:
        return [
            (g, 8, 128 * part, 3 * u, 3, 18 * 128 * u + 6 * part + 3 * g, 18)
            for g in range(2)
            for part in range(3)
            for u in range(2)
        ]
    return [(g, 24, 0, 0, 6, 6 * 384 * g, 6) for g in range(2)]


def feed_grad_parts(share):
    return [(box, groups, row, 0, 6, flat, stride) for box, groups, row, flat, stride in feed_parts(share)]


ATTN_EXTRA = (
    [(0, 0, 12), (12, 4602, 14)],
    [(25, 0, 5), (30, 4613, 3)],
    [(33, 0, 15), (48, 4605, 11)],
    [(58, 0, 2), (60, 4610, 6)],
)
FEED_EXTRA = (
    [(0, 0, 12), (12, 9204, 23)],
    [(34, 0, 2), (36, 9218, 9)],
    [(45, 0, 15), (60, 9225, 2)],
    [(61, 0, 5), (66, 9221, 6)],
)
ATTN_PUT = (
    [(0, 0, 12)],
    [(25, 0, 5), (30, 4613, 3)],
    [(48, 4605, 12)],
    [(58, 0, 2), (60, 4610, 6)],
)
FEED_PUT = (
    [(0, 0, 12)],
    [(34, 0, 2), (36, 9218, 9)],
    [(45, 0, 15)],
    [(61, 0, 5), (66, 9221, 6)],
)
EXTRA = 72


class Block:
    def __init__(self, base, boxes, start, parts, grad_parts, extra, put, matrices):
        self.base = base
        self.boxes, self.start, self.parts, self.grad_parts = boxes, start, parts, grad_parts
        self.extra, self.put = extra, put
        self.matrices = matrices


ATTN = Block(
    0, 1, ATTN_START, attn_parts, attn_grad_parts, ATTN_EXTRA, ATTN_PUT, ((1536, 1771008), (1772544, 2362368))
)
FEED = Block(
    EXTRA, 2, FEED_START, feed_parts, feed_grad_parts, FEED_EXTRA, FEED_PUT, ((1536, 2360832), (2363904, 4723200))
)


def params(limit=56):
    return pltpu.CompilerParams(vmem_limit_bytes=limit * MB)


def dot(a, b):
    return lax.dot_general(a, b, (((1,), (0,)), ((), ())), preferred_element_type=F32)


def dot_nt(a, b):
    return lax.dot_general(a, b, (((1,), (1,)), ((), ())), preferred_element_type=F32)


def dot_tn(a, b):
    return lax.dot_general(a, b, (((0,), (0,)), ((), ())), preferred_element_type=F32)


def normed_of(values):
    center = values - jnp.mean(values, axis=-1, keepdims=True)
    spread = lax.rsqrt(jnp.mean(center * center, axis=-1, keepdims=True) + ln_eps)
    return center * spread, spread


def whole(array):
    rank = len(array.shape)
    return pl.BlockSpec(array.shape, lambda *i: (0,) * rank, pipeline_mode=pl.Buffered(1))


def rows_of(count, width):
    return pl.BlockSpec((count, width), lambda i: (i, 0))


SMEM = pl.BlockSpec(memory_space=pltpu.SMEM)


def sds(shape, dtype):
    return jax.ShapeDtypeStruct(shape, dtype)


CHUNK = 2368


def prep_kernel(block, steps, shard_ref, flat_ref, *refs):
    *box_refs, extra_ref, held = refs
    step = pl.program_id(0)
    held[pl.ds(pl.multiple_of(MARGIN + CHUNK * step, 8), CHUNK), :] = flat_ref[...].reshape(CHUNK, LANES)

    @pl.when(step == steps - 1)
    def _():
        low = lax.broadcasted_iota(jnp.int32, (8, LANES), 1) < 64
        low_one = lax.broadcasted_iota(jnp.int32, (1, LANES), 1) < 64
        extra_ref[...] = jnp.zeros_like(extra_ref)
        for share in range(4):

            @pl.when(shard_ref[0] == share)
            def _(share=share):
                odd = share % 2 == 1

                def tile(first, stride):
                    here = held[pl.ds(first, 8, stride=stride), :]
                    if not odd:
                        return here
                    ahead = held[pl.ds(first - 1, 8, stride=stride), :]
                    return jnp.where(low, pltpu.roll(ahead, 64, 1), pltpu.roll(here, 64, 1))

                for box, groups, box_row, flat_row, stride in block.parts(share):
                    base = MARGIN + block.start[share] + flat_row

                    def body(group, carry, box=box, base=base, box_row=box_row, stride=stride):
                        for j in range(6):
                            first = base + 16 * stride * group + j
                            both = jnp.concatenate([tile(first, stride), tile(first + 8 * stride, stride)], axis=0)
                            at = pl.multiple_of(box_row + 16 * group, 16)
                            box_refs[box][pl.ds(at, 16), LANES * j : LANES * j + LANES] = both.astype(BF)
                        return carry

                    lax.fori_loop(0, groups, body, 0, unroll=8)
                count = flat_rows(block, share)
                for to, row, length in block.extra[share]:
                    for k in range(length):
                        at = MARGIN + row + k
                        value = held[at : at + 1, :]
                        if odd:
                            ahead = held[at - 1 : at, :]
                            value = jnp.where(low_one, pltpu.roll(ahead, 64, 1), pltpu.roll(value, 64, 1))
                            if row + k == 0:
                                value = jnp.where(low_one, 0.0, value)
                        elif row + k == count:
                            value = jnp.where(low_one, value, 0.0)
                        extra_ref[to + k : to + k + 1, :] = value.astype(BF).astype(F32)


def flat_rows(block, share):
    return 4615 if block is ATTN else 9226


def prep(block, flat, shard):
    steps = -(-flat.shape[0] // (CHUNK * LANES))
    return pl.pallas_call(
        functools.partial(prep_kernel, block, steps),
        grid=(steps,),
        in_specs=[SMEM, pl.BlockSpec((CHUNK * LANES,), lambda i: (i,))],
        out_specs=[pl.BlockSpec((D, D), lambda i: (0, 0))] * block.boxes
        + [pl.BlockSpec((EXTRA, LANES), lambda i: (0, 0))],
        out_shape=[sds((D, D), BF)] * block.boxes + [sds((EXTRA, LANES), F32)],
        scratch_shapes=[pltpu.VMEM((MARGIN + CHUNK * steps + MARGIN, LANES), F32)],
        compiler_params=params(),
    )(shard, flat)


def spread_row(extra_ref, first, count):
    return jnp.concatenate([extra_ref[first + k : first + k + 1, :] for k in range(count)], axis=1)


def patch_row(ref, row, values):
    at = row // 16 * 16
    rows = lax.broadcasted_iota(jnp.int32, (16, values.shape[1]), 0)
    old = ref[at : at + 16, :].astype(F32)
    ref[at : at + 16, :] = jnp.where(rows == row - at, values, old).astype(BF)


def load_attn(shard, boxes, qkv_ref, proj_ref, sems):
    for wait in (False, True):
        for k, box in enumerate(boxes):
            share = jnp.bitwise_xor(shard, k)

            @pl.when(share == 3)
            def _(box=box, k=k):
                copy = pltpu.make_async_copy(box, proj_ref, sems.at[k, 0])
                copy.wait() if wait else copy.start()

            @pl.when(share != 3)
            def _(box=box, k=k, share=share):
                for part in range(3):
                    copy = pltpu.make_async_copy(
                        box.at[pl.ds(256 * part, 256), :],
                        qkv_ref.at[pl.ds(pl.multiple_of(768 * part + 256 * share, 256), 256), :],
                        sems.at[k, part],
                    )
                    copy.wait() if wait else copy.start()


def load_feed(shard, boxes, up_ref, down_ref, sems):
    for wait in (False, True):
        for k, box in enumerate(boxes):
            share = jnp.bitwise_xor(shard, k)

            @pl.when(share >= 2)
            def _(box=box, k=k, share=share):
                at = pl.multiple_of(768 * (share - 2), 256)
                copy = pltpu.make_async_copy(box, down_ref.at[pl.ds(at, 768), :], sems.at[k, 0])
                copy.wait() if wait else copy.start()

            @pl.when(share < 2)
            def _(box=box, k=k, share=share):
                for h in range(2):
                    copy = pltpu.make_async_copy(
                        box.at[pl.ds(384 * h, 384), :],
                        up_ref.at[pl.ds(pl.multiple_of(768 * h + 384 * share, 128), 384), :],
                        sems.at[k, h],
                    )
                    copy.wait() if wait else copy.start()


ANYWHERE = pl.BlockSpec(memory_space=pl.ANY)


def half_masks():
    lane = lax.broadcasted_iota(jnp.int32, (1, LANES), 1)
    return (lane < 64).astype(F32).astype(BF), (lane >= 64).astype(F32).astype(BF)


def two_heads(pair, masks):
    return jnp.concatenate([pair * masks[0], pair * masks[1]], axis=0)


def attn_forward(seq, x_ref, shard_ref, extra_ref, a0, a1, a2, a3, *refs):
    *refs, qkv_w, proj_w, vec_ref, bias_ref, sems = refs

    @pl.when(pl.program_id(0) == 0)
    def _():
        load_attn(shard_ref[0], (a0, a1, a2, a3), qkv_w, proj_w, sems)
        for part in range(3):
            patch_row(qkv_w, 768 * part + 255, spread_row(extra_ref, 12 + 6 * part, 6))
            patch_row(qkv_w, 768 * part + 512, spread_row(extra_ref, 30 + 6 * part, 6))
        vec_ref[...] = jnp.zeros_like(vec_ref)
        for row, first in enumerate((0, 6, 60, EXTRA + 0, EXTRA + 6)):
            vec_ref[row : row + 1, :] = spread_row(extra_ref, first, 6)
        bias_ref[...] = jnp.zeros_like(bias_ref)
        bias_ref[0:1, 0:768] = spread_row(extra_ref, 48, 6)
        bias_ref[0:1, 1536:2304] = spread_row(extra_ref, 54, 6)

    first_ref, qkv_ref, log_ref, att_ref, hid_ref, second_ref = refs
    x = x_ref[...].astype(F32)
    normed, _ = normed_of(x)
    first = (normed * vec_ref[0:1, :] + vec_ref[1:2, :]).astype(BF)
    first_ref[...] = first
    for part in range(3):
        cols = slice(768 * part, 768 * part + 768)
        qkv_ref[:, cols] = (dot(first, qkv_w[cols, :]) + bias_ref[0:1, cols]).astype(BF)
    masks = half_masks()
    real = lax.broadcasted_iota(jnp.int32, (2, T, T), 1) < seq
    for pair in range(HEADS // 2):
        at = LANES * pair
        for image in range(x_ref.shape[0] // T):
            own = slice(T * image, T * image + T)
            q = qkv_ref[own, at : at + LANES] * jnp.asarray(0.125, BF)
            k = two_heads(qkv_ref[own, 768 + at : 768 + at + LANES], masks)
            v = two_heads(qkv_ref[own, 1536 + at : 1536 + at + LANES], masks)
            scores = dot_nt(k, q).reshape(2, T, T)
            scores = jnp.where(real, scores, -1e30)
            top = jnp.max(scores, axis=1, keepdims=True)
            weight = jnp.exp(scores - top)
            total = jnp.sum(weight, axis=1, keepdims=True)
            logs = top + jnp.log(total)
            log_ref[image, 2 * pair : 2 * pair + 1, :] = logs[0]
            log_ref[image, 2 * pair + 1 : 2 * pair + 2, :] = logs[1]
            probs = (weight * (1.0 / total)).astype(BF).reshape(2 * T, T)
            att_ref[own, at : at + LANES] = dot_tn(probs, v).astype(BF)
    hidden = x + dot(att_ref[...], proj_w[...]) + vec_ref[2:3, :]
    hid_ref[...] = hidden
    normed, _ = normed_of(hidden)
    second_ref[...] = (normed * vec_ref[3:4, :] + vec_ref[4:5, :]).astype(BF)


FORWARD_IMAGES = 2


def call_attn_forward(seq, x, weights, boxes):
    shard, extra = weights
    rows = x.shape[0]
    images = rows // T
    step = FORWARD_IMAGES if images % FORWARD_IMAGES == 0 else 1
    tall = step * T
    made = [sds((2304, D), BF), sds((D, D), BF), sds((8, D), F32), sds((8, 2304), F32)]
    return pl.pallas_call(
        functools.partial(attn_forward, seq),
        grid=(images // step,),
        in_specs=[rows_of(tall, D), SMEM, whole(extra)] + [ANYWHERE] * 4,
        out_specs=[
            rows_of(tall, D),
            rows_of(tall, 2304),
            pl.BlockSpec((step, HEADS, T), lambda i: (i, 0, 0)),
            rows_of(tall, D),
            rows_of(tall, D),
            rows_of(tall, D),
        ]
        + [pl.BlockSpec(shape.shape, lambda i: (0, 0)) for shape in made],
        out_shape=[
            sds((rows, D), BF),
            sds((rows, 2304), BF),
            sds((images, HEADS, T), F32),
            sds((rows, D), BF),
            sds((rows, D), F32),
            sds((rows, D), BF),
        ]
        + made,
        scratch_shapes=[pltpu.SemaphoreType.DMA((4, 3))],
        compiler_params=params(),
    )(x, shard, extra, *boxes)


def hand_out(index, box, outs, sems):
    copies = [pltpu.make_async_copy(box.at[k], out, sems.at[k]) for k, out in enumerate(outs)]
    for k, copy in enumerate(copies):

        @pl.when(index == k)
        def _(copy=copy):
            copy.start()

    @pl.when(index == len(outs) - 1)
    def _():
        for copy in copies:
            copy.wait()


HALF = FF // 2
ROW_STEPS = 4


def feed(seq, part, tall, shard_ref, extra_ref, a0, a1, a2, a3, second_ref, cot_ref, result_ref, *refs):
    last = part == 1
    if last:
        before_ref, out_ref, gs_ref, *refs = refs
    else:
        out_ref, gs_ref, cot_sum, *refs = refs
    sum_ref, edge_ref, *outs, up_w, down_w, bias, second_all, cot_all, act_all, pre_all, box, sems, box_sems = refs
    step = pl.program_id(0)
    shard = shard_ref[0]

    @pl.when(step == 0)
    def _():
        load_feed(shard, (a0, a1, a2, a3), up_w, down_w, sems)
        for h in range(2):
            patch_row(up_w, 768 * h + 383, spread_row(extra_ref, EXTRA + 12 + 12 * h + 6 * part, 6))
            bias[0:1, 768 * h : 768 * h + 768] = spread_row(extra_ref, EXTRA + 36 + 12 * h + 6 * part, 6)
        if last:
            patch_row(down_w, 767, spread_row(extra_ref, EXTRA + 60, 6))
        sum_ref[...] = jnp.zeros_like(sum_ref)
        edge_ref[...] = jnp.zeros_like(edge_ref)
        if not last:
            cot_sum[...] = jnp.zeros_like(cot_sum)

    @pl.when(step < ROW_STEPS)
    def _():
        at = pl.ds(pl.multiple_of(step * tall, 16), tall)
        second = second_ref[...]
        cot = cot_ref[...]
        second_all[at, :] = second
        cot_all[at, :] = cot
        if last:
            result = result_ref[...]
            grad_second = before_ref[...]
        else:
            result = result_ref[...] + spread_row(extra_ref, EXTRA + 66, 6)
            grad_second = jnp.zeros_like(result)
            cot_sum[0:1, :] += jnp.sum(cot.astype(F32), axis=0, keepdims=True)
        for h in range(2):
            cols = slice(768 * h, 768 * h + 768)
            pre = dot(second, up_w[cols, :]) + bias[0:1, cols]
            grad_act = dot_nt(cot, down_w[cols, :])
            half = 0.5 * (1.0 + lax.erf(pre * root_half))
            act = (pre * half).astype(BF)
            grad_pre = grad_act * (half + pre * jnp.exp(-0.5 * pre * pre) * inv_root_tau)
            low = grad_pre.astype(BF)
            act_all[at, cols] = act
            pre_all[at, cols] = low
            sum_ref[0:1, cols] += jnp.sum(grad_pre, axis=0, keepdims=True)
            result = result + dot(act, down_w[cols, :])
            grad_second = grad_second + dot_nt(low, up_w[cols, :])
        if last:
            for image in range(tall // T):
                out_ref[image] = result[T * image : T * image + seq].astype(BF)
        else:
            out_ref[...] = result
        gs_ref[...] = grad_second

    index = step - ROW_STEPS
    side = jnp.bitwise_xor(shard // 2, 1 - index % 2)
    core = jnp.where(index >= 2, shard % 2, 1 - shard % 2)

    @pl.when((index >= 0) & (side == 0))
    def _():
        left = second_all[:, pl.ds(pl.multiple_of(384 * core, 128), 384)]
        for h in range(2):
            grad = dot_tn(left, pre_all[:, 768 * h : 768 * h + 768])
            box[index, 384 * h : 384 * h + 384, :] = grad.astype(BF)

            @pl.when(core == 0)
            def _(grad=grad, h=h):
                edge_ref[0:1, 768 * h : 768 * h + 768] = grad[383:384]

    @pl.when((index >= 0) & (side == 1))
    def _():
        left = act_all[:, pl.ds(pl.multiple_of(768 * core, 128), 768)]
        grad = dot_tn(left, cot_all[...])
        box[index] = grad.astype(BF)

        @pl.when(core == 0)
        def _():
            edge_ref[1:2, 0:768] = grad[767:768]

    hand_out(index, box, outs, box_sems)


def call_feed(seq, part, shard, extra, boxes, second, cot, result, before=None):
    rows = second.shape[0]
    images = rows // T
    tall = rows // ROW_STEPS
    last = part == 1
    row = lambda i: jnp.minimum(i, ROW_STEPS - 1)
    block = pl.BlockSpec((tall, D), lambda i: (row(i), 0))
    out = pl.BlockSpec((tall // T, seq, D), lambda i: (row(i), 0, 0)) if last else block
    small = lambda width: pl.BlockSpec((8, width), lambda i: (0, 0))
    return pl.pallas_call(
        functools.partial(feed, seq, part, tall),
        grid=(ROW_STEPS + 4,),
        in_specs=[SMEM, whole(extra)] + [ANYWHERE] * 4 + [block] * (4 if last else 3),
        out_specs=[out, block] + ([] if last else [small(D)]) + [small(HALF), small(HALF)] + [ANYWHERE] * 4,
        out_shape=[sds((images, seq, D), BF) if last else sds((rows, D), F32), sds((rows, D), F32)]
        + ([] if last else [sds((8, D), F32)])
        + [sds((8, HALF), F32), sds((8, HALF), F32)] + [sds((D, D), BF)] * 4,
        scratch_shapes=[
            pltpu.VMEM((HALF, D), BF),
            pltpu.VMEM((HALF, D), BF),
            pltpu.VMEM((8, HALF), F32),
            pltpu.VMEM((rows, D), BF),
            pltpu.VMEM((rows, D), BF),
            pltpu.VMEM((rows, HALF), BF),
            pltpu.VMEM((rows, HALF), BF),
            pltpu.VMEM((4, D, D), BF),
            pltpu.SemaphoreType.DMA((4, 2)),
            pltpu.SemaphoreType.DMA((4,)),
        ],
        compiler_params=params(60),
    )(shard, extra, *boxes, second, cot, result, *([before] if last else []))


WIDE = 384


def attn_backward(seq, group, base, count, last, shard_ref, log_ref, qkv_ref, first_ref, att_ref, *refs):
    step = pl.program_id(0)
    shard = shard_ref[0]
    if group == 0:
        gs_ref, hid_ref, cot_ref, vec_ref, proj_w, *refs = refs
    else:
        low_ref, ga_ref, *refs = refs
    if last:
        if group == 0:
            head_before, sum_before, first_any, att_any, low_any, grad_any, _, _, *refs = refs
        else:
            head_before, first_any, att_any, low_any, grad_any, *refs = refs
    grad_ref, head_sum, *refs = refs
    if group == 0:
        low_ref, ga_ref, gh_ref, sum_ref, *refs = refs
    if last:
        edge_ref, *outs, grad_all, first_all, low_all, att_all, box, box_sems, load_sems = refs
        done = pl.ds(0, base * T)
        loads = [
            pltpu.make_async_copy(grad_any.at[done], grad_all.at[done], load_sems.at[0]),
            pltpu.make_async_copy(first_any.at[done], first_all.at[done], load_sems.at[1]),
            pltpu.make_async_copy(low_any.at[done], low_all.at[done], load_sems.at[2]),
            pltpu.make_async_copy(
                att_any.at[done, pl.ds(WIDE * group, WIDE)], att_all.at[done], load_sems.at[3]
            ),
        ]

    @pl.when(step == 0)
    def _():
        if last:
            for load in loads:
                load.start()
            edge_ref[...] = jnp.zeros_like(edge_ref)
            head_sum[...] = head_before[...]
        else:
            head_sum[...] = jnp.zeros_like(head_sum)
        if group == 0:
            sum_ref[...] = sum_before[...] if last else jnp.zeros_like(sum_ref)

    @pl.when(step < count)
    def _():
        at_rows = pl.ds(pl.multiple_of((step + base) * T, 16), T)
        if last:
            first_all[at_rows, :] = first_ref[...]
            att_all[at_rows, :] = att_ref[...]
        if group == 0:
            gs = gs_ref[...]
            normed, spread = normed_of(hid_ref[...])
            gn = gs * vec_ref[3:4, :]
            gh = cot_ref[...].astype(F32) + spread * (
                gn - jnp.mean(gn, axis=-1, keepdims=True) - normed * jnp.mean(gn * normed, axis=-1, keepdims=True)
            )
            sum_ref[0:1, :] += jnp.sum(gs * normed, axis=0, keepdims=True)
            sum_ref[1:2, :] += jnp.sum(gs, axis=0, keepdims=True)
            sum_ref[2:3, :] += jnp.sum(gh, axis=0, keepdims=True)
            gh_ref[...] = gh
            gh_low = gh.astype(BF)
            low_ref[...] = gh_low
            ga_ref[...] = dot_nt(gh_low, proj_w[...]).astype(BF)
        if last:
            low_all[at_rows, :] = low_ref[...]
        low = lax.broadcasted_iota(jnp.int32, (T, LANES), 1) < 64
        real = lax.broadcasted_iota(jnp.int32, (2, T, T), 1) < seq
        eighth = jnp.asarray(0.125, BF)
        masks = half_masks()
        for pair in range(3):
            at = LANES * pair
            full = WIDE * group + at
            head = 6 * group + 2 * pair
            q = qkv_ref[:, full : full + LANES] * eighth
            k = two_heads(qkv_ref[:, 768 + full : 768 + full + LANES], masks)
            v = two_heads(qkv_ref[:, 1536 + full : 1536 + full + LANES], masks)
            grad_out = ga_ref[:, at : at + LANES]
            scores = dot_nt(k, q).reshape(2, T, T)
            logs = jnp.concatenate([log_ref[0:1, head : head + 1, :], log_ref[0:1, head + 1 : head + 2, :]], axis=0)
            probs = jnp.where(real, jnp.exp(scores - logs), 0.0)
            grad_v = dot(probs.astype(BF).reshape(2 * T, T), grad_out)
            grad_probs = dot_nt(v, grad_out).reshape(2, T, T)
            delta = jnp.sum(probs * grad_probs, axis=1, keepdims=True)
            grad_scores = (probs * (grad_probs - delta)).astype(BF).reshape(2 * T, T)
            grad_k = dot(grad_scores, q)
            grads = (
                dot_tn(grad_scores, k * eighth),
                jnp.where(low, grad_k[:T], grad_k[T:]),
                jnp.where(low, grad_v[:T], grad_v[T:]),
            )
            for part, grad in enumerate(grads):
                if part != 1:
                    row = part // 2
                    head_sum[row : row + 1, at : at + LANES] += jnp.sum(grad, axis=0, keepdims=True)
                cols = slice(WIDE * part + at, WIDE * part + at + LANES)
                grad = grad.astype(BF)
                grad_ref[:, cols] = grad
                if last:
                    grad_all[at_rows, cols] = grad

    if not last:
        return

    @pl.when(step == count)
    def _():
        for load in loads:
            load.wait()

    index = step - count
    side = jnp.bitwise_xor(shard // 2, 1 - index % 2)
    core = jnp.where(index >= 2, shard % 2, 1 - shard % 2)
    share = 2 * side + core

    @pl.when((index >= 0) & (share == 3))
    def _():
        box[index] = dot_tn(att_all[...], low_all[...]).astype(BF)

    @pl.when((index >= 0) & (share != 3))
    def _():
        grad = dot_tn(first_all[:, pl.ds(pl.multiple_of(256 * share, 256), 256)], grad_all[...])
        for part in range(3):
            cols = slice(WIDE * part, WIDE * part + WIDE)
            for u in range(2):
                box[index, 128 * part : 128 * part + 128, WIDE * u : WIDE * u + WIDE] = grad[
                    128 * u : 128 * u + 128, cols
                ].astype(BF)

        @pl.when(share == 0)
        def _():
            edge_ref[0:1, :] = grad[255:256]

        @pl.when(share == 2)
        def _():
            edge_ref[1:2, :] = grad[0:1]

    hand_out(index, box, outs, box_sems)


def call_attn_backward(seq, group, base, count, shard, log_total, qkv, first, attended, *more, before=()):
    rows = first.shape[0]
    last = len(before) > 0
    row = lambda i: jnp.minimum(i, count - 1) + base
    block = lambda width, col=0: pl.BlockSpec((T, width), lambda i: (row(i), col))
    small = lambda width: pl.BlockSpec((8, width), lambda i: (0, 0))
    in_specs = [SMEM, pl.BlockSpec((1, HEADS, T), lambda i: (row(i), 0, 0)), block(2304), block(D), block(WIDE, group)]
    out_specs = [block(3 * WIDE), small(WIDE)]
    out_shape = [sds((rows, 3 * WIDE), BF), sds((8, WIDE), F32)]
    if group == 0:
        in_specs += [block(D)] * 3 + [whole(more[3]), whole(more[4])]
        out_specs += [block(D), block(D), block(D), small(D)]
        out_shape += [sds((rows, D), BF), sds((rows, D), BF), sds((rows, D), F32), sds((8, D), F32)]
    else:
        in_specs += [block(D), block(WIDE, 1)]
    aliases, scratch, extra = {}, [], []
    if last:
        at = len(in_specs)
        if group == 0:
            grad, head, low, ga, gh, total = before
            extra = [head, total, first, attended, low, grad, ga, gh]
            in_specs += [whole(head), whole(total)] + [ANYWHERE] * 6
            aliases = {at + 4: 2, at + 5: 0, at + 6: 3, at + 7: 4}
        else:
            grad, head = before
            extra = [head, first, attended, more[0], grad]
            in_specs += [whole(head)] + [ANYWHERE] * 4
            aliases = {at + 4: 0}
        out_specs += [small(3 * WIDE)] + [ANYWHERE] * 4
        out_shape += [sds((8, 3 * WIDE), F32)] + [sds((WIDE, D), BF)] * 4
        scratch = [
            pltpu.VMEM((rows, 3 * WIDE), BF),
            pltpu.VMEM((rows, D), BF),
            pltpu.VMEM((rows, D), BF),
            pltpu.VMEM((rows, WIDE), BF),
            pltpu.VMEM((4, WIDE, D), BF),
            pltpu.SemaphoreType.DMA((4,)),
            pltpu.SemaphoreType.DMA((4,)),
        ]
    return pl.pallas_call(
        functools.partial(attn_backward, seq, group, base, count, last),
        grid=(count + 4 if last else count,),
        in_specs=in_specs,
        out_specs=out_specs,
        out_shape=out_shape,
        input_output_aliases=aliases,
        scratch_shapes=scratch,
        compiler_params=params(),
    )(shard, log_total, qkv, first, attended, *more, *extra)


def input_backward(seq, grad0, grad1, gh_ref, x_ref, vec_ref, qkv_w, out_ref, sum_ref):
    @pl.when(pl.program_id(0) == 0)
    def _():
        sum_ref[...] = jnp.zeros_like(sum_ref)

    grad_first = None
    for part in range(3):
        cols = slice(WIDE * part, WIDE * part + WIDE)
        both = jnp.concatenate([grad0[:, cols], grad1[:, cols]], axis=1)
        term = dot_nt(both, qkv_w[768 * part : 768 * part + 768, :])
        grad_first = term if part == 0 else grad_first + term
    normed, spread = normed_of(x_ref[...].astype(F32))
    gn = grad_first * vec_ref[0:1, :]
    grad = gh_ref[...] + spread * (
        gn - jnp.mean(gn, axis=-1, keepdims=True) - normed * jnp.mean(gn * normed, axis=-1, keepdims=True)
    )
    sum_ref[0:1, :] += jnp.sum(grad_first * normed, axis=0, keepdims=True)
    sum_ref[1:2, :] += jnp.sum(grad_first, axis=0, keepdims=True)
    for image in range(grad.shape[0] // T):
        out_ref[image] = grad[T * image : T * image + seq].astype(BF)


def call_input_backward(seq, grads, gh, x, vec, qkv_w):
    rows = gh.shape[0]
    images = rows // T
    step = 2 if images % 2 == 0 else 1
    tall = step * T
    return pl.pallas_call(
        functools.partial(input_backward, seq),
        grid=(images // step,),
        in_specs=[rows_of(tall, 3 * WIDE)] * 2 + [rows_of(tall, D), rows_of(tall, D), whole(vec), whole(qkv_w)],
        out_specs=[pl.BlockSpec((step, seq, D), lambda i: (i, 0, 0)), pl.BlockSpec((8, D), lambda i: (0, 0))],
        out_shape=[sds((images, seq, D), BF), sds((8, D), F32)],
        compiler_params=params(),
    )(*grads, gh, x, vec, qkv_w)


def putter(out_ref):
    out_ref[...] = jnp.zeros_like(out_ref)

    def put(first, ref, row, col, width):
        for k in range(width // LANES):
            at = col + LANES * k
            out_ref[first + k : first + k + 1, :] = ref[row : row + 1, at : at + LANES]

    return put


def pack(last_sum, back_sum, head0, head1, edge0, edge1, pre0, pre1, up0, up1, cot_sum, out_ref):
    put = putter(out_ref)
    put(0, last_sum, 0, 0, D)
    put(6, last_sum, 1, 0, D)
    for group, (head, edge) in enumerate(((head0, edge0), (head1, edge1))):
        for part in range(3):
            put(12 + 6 * part + 3 * group, edge, 0, WIDE * part, WIDE)
            put(30 + 6 * part + 3 * group, edge, 1, WIDE * part, WIDE)
        put(48 + 3 * group, head, 0, 0, WIDE)
        put(54 + 3 * group, head, 1, 0, WIDE)
    put(60, back_sum, 2, 0, D)
    put(EXTRA, back_sum, 0, 0, D)
    put(EXTRA + 6, back_sum, 1, 0, D)
    for j, (pre, up) in enumerate(((pre0, up0), (pre1, up1))):
        for h in range(2):
            put(EXTRA + 12 + 12 * h + 6 * j, up, 0, 768 * h, D)
            put(EXTRA + 36 + 12 * h + 6 * j, pre, 0, 768 * h, D)
    put(EXTRA + 60, up1, 1, 0, D)
    put(EXTRA + 66, cot_sum, 0, 0, D)


def call_pack(*arrays):
    return pl.pallas_call(
        pack,
        in_specs=[pl.BlockSpec(memory_space=pltpu.VMEM)] * len(arrays),
        out_specs=pl.BlockSpec(memory_space=pltpu.VMEM),
        out_shape=sds((2 * EXTRA, LANES), F32),
        compiler_params=params(),
    )(*arrays)


def adam_kernel(block, share_size, scale, boxes, shard_ref, power_ref, extra_ref, *refs):
    box_refs = refs[:boxes]
    flat_ref, mom_ref, grad_ref, change_ref, new_ref, held = refs[boxes:]
    step = pl.program_id(0)

    @pl.when(step == 0)
    def _():
        for share in range(4):

            @pl.when(shard_ref[0] == share)
            def _(share=share):
                for box, groups, box_row, col, cols, flat_row, stride in block.grad_parts(share):
                    base = MARGIN + block.start[share] + flat_row

                    def body(group, carry, box=box, box_row=box_row, col=col, cols=cols, base=base, stride=stride):
                        row = pl.multiple_of(box_row + 16 * group, 16)
                        for j in range(cols):
                            at = LANES * (col + j)
                            both = box_refs[box][pl.ds(row, 16), at : at + LANES].astype(F32)
                            to = base + 16 * stride * group + j
                            held[pl.ds(to, 8, stride=stride), :] = both[0:8]
                            held[pl.ds(to + 8 * stride, 8, stride=stride), :] = both[8:16]
                        return carry

                    lax.fori_loop(0, groups, body, 0, unroll=8)
                for source, row, length in block.put[share]:
                    held[MARGIN + row : MARGIN + row + length, :] = extra_ref[block.base + source : block.base + source + length, :]

    start = pl.multiple_of(MARGIN + CHUNK * step, 8)
    shard = shard_ref[0]
    low = lax.broadcasted_iota(jnp.int32, (CHUNK, LANES), 1) < 64
    here = held[pl.ds(start, CHUNK), :]
    after = held[pl.ds(start + 1, CHUNK), :]
    shifted = jnp.where(low, pltpu.roll(here, 64, 1), pltpu.roll(after, 64, 1))
    grad = jnp.where(shard % 2 == 1, shifted, here) * scale
    position = (
        shard * share_size
        + step * (CHUNK * LANES)
        + lax.broadcasted_iota(jnp.int32, (CHUNK, LANES), 0) * LANES
        + lax.broadcasted_iota(jnp.int32, (CHUNK, LANES), 1)
    )
    matrix = jnp.zeros((CHUNK, LANES), jnp.bool_)
    for first, end in block.matrices:
        matrix = matrix | ((position >= first) & (position < end))
    size = CHUNK * LANES
    p = flat_ref[...].reshape(CHUNK, LANES)
    m = beta_one * mom_ref[0, :].reshape(CHUNK, LANES) + (1.0 - beta_one) * grad
    s = beta_two * mom_ref[1, :].reshape(CHUNK, LANES) + (1.0 - beta_two) * grad * grad
    ratio = (m * power_ref[0]) / (jnp.sqrt(s * power_ref[1]) + adam_eps)
    change = jnp.where(matrix, rate_matrix, rate_vector) * (ratio + jnp.where(matrix, decay_matrix, 0.0) * p)
    grad_ref[...] = grad.reshape(size)
    change_ref[...] = change.reshape(size)
    new_ref[0, :] = m.reshape(size)
    new_ref[1, :] = s.reshape(size)


def adam(block, shard, powers, extra, boxes, flat, moments, scale):
    count = flat.shape[0]
    steps = -(-count // (CHUNK * LANES))
    line = pl.BlockSpec((CHUNK * LANES,), lambda i: (i,))
    two = pl.BlockSpec((2, CHUNK * LANES), lambda i: (0, i))
    return pl.pallas_call(
        functools.partial(adam_kernel, block, count, scale, len(boxes)),
        grid=(steps,),
        in_specs=[SMEM, SMEM, whole(extra)] + [whole(box) for box in boxes] + [line, two],
        out_specs=[line, line, two],
        out_shape=[sds((count,), F32), sds((count,), F32), sds((2, count), F32)],
        scratch_shapes=[pltpu.VMEM((MARGIN + CHUNK * steps + MARGIN, LANES), F32)],
        compiler_params=params(),
    )(shard, powers, extra, *boxes, flat, moments)


def swap(value, axis, bit):
    pairs = [(i, i ^ bit) for i in range(lax.axis_size(axis))]
    return lax.ppermute(value, axis, pairs)


def turn(value, axis, unit, distance):
    size = lax.axis_size(axis)
    return lax.ppermute(value, axis, [(i, (i + unit * distance) % size) for i in range(size)])


def pick(array, index, axis=0):
    return lax.dynamic_index_in_dim(array, index, axis, keepdims=False)


class Line:
    def __init__(self):
        self.last = None

    def __call__(self, step, *args):
        if self.last is not None:
            flat, tree = jax.tree.flatten(args)
            flat = lax.optimization_barrier((self.last, *flat))[1:]
            args = jax.tree.unflatten(tree, flat)
        out = step(*args)
        self.last = min(jax.tree.leaves(out), key=lambda leaf: leaf.size)
        return out


def pause_kernel(in_ref, out_ref):
    out_ref[...] = in_ref[...]


def pause(line, value):
    return line(
        pl.pallas_call(
            pause_kernel,
            out_shape=sds(value.shape, value.dtype),
            cost_estimate=pl.CostEstimate(flops=10**11, bytes_accessed=10**8, transcendentals=0),
        ),
        value,
    )


class Sum:
    def __init__(self, line, across, same, mine_across, mine):
        self.line, self.mine_across, self.mine = line, mine_across, mine
        self.rows = mine.shape[0]
        rep = lax.axis_index("rep")
        self.near, self.far = rep % 2, rep // 2
        self.count = lax.axis_size("rep") // 2
        self.came_across, self.here = swap(across, "shard", 1), swap(same, "shard", 1)

    def side(self):
        add = lambda a, b: (a.astype(F32) + b.astype(F32)).astype(BF)
        send = self.line(add, self.mine_across, self.came_across)
        self.came = swap(send, "shard", 2)
        self.here = self.line(lambda a: a, self.here)

    def close(self):
        def step(*terms):
            def half(index):
                parts = [pick(term.reshape(2, self.rows // 2, D), index).astype(F32) for term in terms]
                return parts[0] + parts[1] + parts[2]

            return half(1 - self.near).astype(BF), half(self.near)

        send, self.half = self.line(step, self.mine, self.here, self.came)
        self.came = swap(send, "rep", 1)

    def level(self, bit):
        if bit == 2:
            self.part = self.line(lambda a, b: (a + b.astype(F32)).astype(BF), self.half, self.came)
        else:
            self.part = self.line(lambda a, b: (a.astype(F32) + b.astype(F32)).astype(BF), self.part, self.came)
        self.came = swap(self.part, "rep", bit)

    def back_level(self):
        self.half = self.line(lambda a, b: (a.astype(F32) + b.astype(F32)).astype(BF), self.part, self.came)
        self.came = swap(self.half, "rep", 1)

    def along(self):
        def step(half, came):
            parts = (half + came.astype(F32)).reshape(self.count, self.rows // 2 // self.count, D)
            sends = [pick(parts, (self.far + d) % self.count).astype(BF) for d in range(1, self.count)]
            return sends, pick(parts, self.far)

        sends, self.part = self.line(step, self.half, self.came)
        self.came = [turn(send, "rep", 2, d + 1) for d, send in enumerate(sends)]

    def back_along(self):
        def step(part, came):
            for value in came:
                part = part + value.astype(F32)
            return part.astype(BF)

        self.part = self.line(step, self.part, self.came)
        self.came = [turn(self.part, "rep", 2, d) for d in range(1, self.count)]

    def back_close(self):
        def step(part, came):
            full = jnp.zeros((self.count,) + part.shape, BF)
            for d, value in enumerate([part] + came):
                full = lax.dynamic_update_slice_in_dim(full, value[None], (self.far + self.count - d) % self.count, 0)
            return full.reshape(self.rows // 2, D)

        self.half = self.line(step, self.part, self.came)
        self.came = swap(self.half, "rep", 1)

    def end(self):
        def step(half, came):
            first = self.near == 0
            return jnp.concatenate([jnp.where(first, half, came), jnp.where(first, came, half)], axis=0)

        return self.line(step, self.half, self.came)


class SumAll:
    def __init__(self, line, value):
        self.line, self.value = line, value
        self.hops = [("shard", 1), ("shard", 2)]
        bit = 2
        while bit < lax.axis_size("rep"):
            self.hops.append(("rep", bit))
            bit *= 2
        self.hops.append(("rep", 1))
        self.came = swap(value, *self.hops.pop(0))

    def hop(self):
        self.value = self.line(lambda a, b: a + b, self.value, self.came)
        if self.hops:
            self.came = swap(self.value, *self.hops.pop(0))
            return False
        return True


def body(layer_input, out_cotangent, attention_params, attention_moments, feedforward_params, feedforward_moments, step_count):
    images, seq, _ = layer_input.shape
    rows = images * T
    image_total = images * lax.axis_size("shard") * lax.axis_size("rep")
    scale = 1.0 / image_total
    shard = lax.axis_index("shard").astype(jnp.int32).reshape(1)
    time = step_count[0].astype(F32)
    powers = jnp.stack([1.0 / (1.0 - jnp.power(beta_one, time)), 1.0 / (1.0 - jnp.power(beta_two, time))])
    pad = ((0, 0), (0, T - seq), (0, 0))
    turned = lambda tokens: jnp.swapaxes(tokens, 0, 1)
    laid = lambda tokens: with_layout_constraint(turned(tokens), Layout((0, 1, 2)))
    padded = lambda tokens: jnp.pad(tokens, pad).reshape(rows, D)
    line = Line()

    attn_box, attn_extra = line(functools.partial(prep, ATTN), attention_params, shard)
    attn_across = swap(attn_box, "shard", 2)
    attn_near = swap(attn_box, "shard", 1)
    box0, box1, feed_extra = line(functools.partial(prep, FEED), feedforward_params, shard)
    extra = line(lambda a, b: jnp.concatenate([a, b], axis=0), attn_extra, feed_extra)
    came = swap(extra, "shard", 1)
    x = line(padded, layer_input)
    extra = line(lambda a, b: a + b, extra, came)
    came = swap(extra, "shard", 2)
    cot = line(padded, out_cotangent)
    extra = line(lambda a, b: a + b, extra, came)
    near0, near1 = swap(box0, "shard", 1), swap(box1, "shard", 1)
    across, send0 = line(lambda a, b: lax.optimization_barrier((a, b)), attn_across, box0)
    attn_both = swap(across, "shard", 1)
    across0 = swap(send0, "shard", 2)
    boxes = (attn_box, attn_near, attn_across, attn_both)
    first, qkv, log_total, attended, hidden, second, qkv_w, proj_w, vec, bias = line(
        lambda x, w, b: call_attn_forward(seq, x, w, b), x, (shard, extra), boxes
    )
    across, send1 = line(lambda a, b: lax.optimization_barrier((a, b)), across0, box1)
    both0 = swap(across, "shard", 1)
    across1 = swap(send1, "shard", 2)
    boxes = (box0, near0, across0, both0)
    result, gs, cot_sum, pre0, up0, *grads = line(
        lambda *a: call_feed(seq, 0, *a), shard, extra, boxes, second, cot, hidden
    )
    feed0 = Sum(line, *grads)
    both1 = swap(line(lambda a: a, across1), "shard", 1)
    feed0.side()
    boxes = (box1, near1, across1, both1)
    layer_output, gs, pre1, up1, *grads = line(
        lambda *a: call_feed(seq, 1, *a), shard, extra, boxes, second, cot, result, gs
    )
    feed1 = Sum(line, *grads)
    feed0.close()
    layer_output = line(laid, layer_output)
    feed1.side()
    half = images // 2
    common = (shard, log_total, qkv, first, attended)
    more = (gs, hidden, cot, vec, proj_w)
    before = line(lambda *a: call_attn_backward(seq, 0, 0, half, *a), *common, *more)
    feed0.along()
    grad0, head0, gh_low, ga, gh, back_sum, edge0, *grads = line(
        lambda b, *a: call_attn_backward(seq, 0, half, images - half, *a, before=b), tuple(before), *common, *more
    )
    attn0 = Sum(line, *grads)
    feed1.close()
    feed0.back_along()
    head0 = pause(line, head0)
    attn0.side()
    more = (gh_low, ga)
    before = line(lambda *a: call_attn_backward(seq, 1, 0, half, *a), *common, *more)
    feed0.back_close()
    feed1.along()
    grad1, head1, edge1, *grads = line(
        lambda b, *a: call_attn_backward(seq, 1, half, images - half, *a, before=b), tuple(before), *common, *more
    )
    attn1 = Sum(line, *grads)
    feed1.back_along()
    attn0.close()
    feed_box0 = feed0.end()
    head1 = pause(line, head1)
    attn1.side()
    input_grad, last_sum = line(lambda *a: call_input_backward(seq, *a), (grad0, grad1), gh, x, vec, qkv_w)
    sums = line(call_pack, last_sum, back_sum, head0, head1, edge0, edge1, pre0, pre1, up0, up1, cot_sum)
    bits = [2 << k for k in range((lax.axis_size("rep") // 2).bit_length() - 1)]
    sums = SumAll(line, sums)
    attn1.close()
    attn0.level(2)
    feed1.back_close()
    sums.hop()
    input_grad = line(laid, input_grad)
    sums.hop()
    attn1.level(2)
    for bit in bits[1:]:
        attn0.level(bit)
    sums.hop()
    feed_box1 = feed1.end()
    sums.hop()
    for bit in bits[1:]:
        attn1.level(bit)
    while not sums.hop():
        pass
    feed_grad, feed_change, feed_new = line(
        lambda *a: adam(FEED, *a, scale), shard, powers, sums.value, [feed_box0, feed_box1], feedforward_params, feedforward_moments
    )
    attn0.back_level()
    attn1.back_level()
    attn_box0 = attn0.end()
    attn_grad, attn_change, attn_new = line(
        lambda *a: adam(ATTN, *a, scale), shard, powers, sums.value, [attn_box0, attn1.end()], attention_params, attention_moments
    )
    return (turned(layer_output), turned(input_grad), attn_grad, feed_grad, attn_change, attn_new, feed_change, feed_new)


def solution(mesh):
    tokens = P(("shard", "rep"), None, None)
    in_specs = (tokens, tokens, P("shard"), P(None, "shard"), P("shard"), P(None, "shard"), P())
    out_specs = (tokens, tokens, P("shard"), P("shard"), P("shard"), P(None, "shard"), P("shard"), P(None, "shard"))
    return jax.shard_map(body, mesh=mesh, in_specs=in_specs, out_specs=out_specs, check_vma=False)
```

```python
import functools

import jax
import jax.numpy as jnp
from jax import lax
from jax.experimental import pallas as pl
from jax.experimental.pallas import tpu as pltpu
from jax.sharding import PartitionSpec as P

D = 768
HEADS = 12
FF = 3072
T = 208

F32 = jnp.float32
BF = jnp.bfloat16

ln_eps = 1e-06
beta_one = 0.9
beta_two = 0.999
adam_eps = 1e-08
rate_matrix = 0.01
rate_vector = 0.1
decay_matrix = 0.05
root_half = 0.7071067811865476
inv_root_tau = 0.3989422804014327

MB = 1 << 20
LANES = 128
MARGIN = 8

ATTN_START = (12, 5, -3, 2)
FEED_START = (12, 2, 15, 5)


def attn_parts(share):
    if share < 3:
        return [(0, 16, 256 * part, 6 * part, 18) for part in range(3)]
    return [(0, 48, 0, 0, 6)]


def feed_parts(share):
    if share < 2:
        return [(j, 24, 384 * h, 12 * h + 6 * j, 24) for j in range(2) for h in range(2)]
    return [(j, 48, 0, 4608 * j, 6) for j in range(2)]


def attn_grad_parts(share):
    if share < 3:
        return [
            (g, 8, 128 * part, 3 * u, 3, 18 * 128 * u + 6 * part + 3 * g, 18)
            for g in range(2)
            for part in range(3)
            for u in range(2)
        ]
    return [(g, 24, 0, 0, 6, 6 * 384 * g, 6) for g in range(2)]


def feed_grad_parts(share):
    return [(box, groups, row, 0, 6, flat, stride) for box, groups, row, flat, stride in feed_parts(share)]


ATTN_EXTRA = (
    [(0, 0, 12), (12, 4602, 14)],
    [(25, 0, 5), (30, 4613, 3)],
    [(33, 0, 15), (48, 4605, 11)],
    [(58, 0, 2), (60, 4610, 6)],
)
FEED_EXTRA = (
    [(0, 0, 12), (12, 9204, 23)],
    [(34, 0, 2), (36, 9218, 9)],
    [(45, 0, 15), (60, 9225, 2)],
    [(61, 0, 5), (66, 9221, 6)],
)
ATTN_PUT = (
    [(0, 0, 12)],
    [(25, 0, 5), (30, 4613, 3)],
    [(48, 4605, 12)],
    [(58, 0, 2), (60, 4610, 6)],
)
FEED_PUT = (
    [(0, 0, 12)],
    [(34, 0, 2), (36, 9218, 9)],
    [(45, 0, 15)],
    [(61, 0, 5), (66, 9221, 6)],
)
EXTRA = 72


class Block:
    def __init__(self, base, boxes, start, parts, grad_parts, extra, put, matrices):
        self.base = base
        self.boxes, self.start, self.parts, self.grad_parts = boxes, start, parts, grad_parts
        self.extra, self.put = extra, put
        self.matrices = matrices


ATTN = Block(
    0, 1, ATTN_START, attn_parts, attn_grad_parts, ATTN_EXTRA, ATTN_PUT, ((1536, 1771008), (1772544, 2362368))
)
FEED = Block(
    EXTRA, 2, FEED_START, feed_parts, feed_grad_parts, FEED_EXTRA, FEED_PUT, ((1536, 2360832), (2363904, 4723200))
)


def params(limit=56):
    return pltpu.CompilerParams(vmem_limit_bytes=limit * MB)


def dot(a, b):
    return lax.dot_general(a, b, (((1,), (0,)), ((), ())), preferred_element_type=F32)


def dot_nt(a, b):
    return lax.dot_general(a, b, (((1,), (1,)), ((), ())), preferred_element_type=F32)


def dot_tn(a, b):
    return lax.dot_general(a, b, (((0,), (0,)), ((), ())), preferred_element_type=F32)


def normed_of(values):
    center = values - jnp.mean(values, axis=-1, keepdims=True)
    spread = lax.rsqrt(jnp.mean(center * center, axis=-1, keepdims=True) + ln_eps)
    return center * spread, spread


def whole(array):
    rank = len(array.shape)
    return pl.BlockSpec(array.shape, lambda *i: (0,) * rank, pipeline_mode=pl.Buffered(1))


def rows_of(count, width):
    return pl.BlockSpec((count, width), lambda i: (i, 0))


SMEM = pl.BlockSpec(memory_space=pltpu.SMEM)


def sds(shape, dtype):
    return jax.ShapeDtypeStruct(shape, dtype)


CHUNK = 2368


def prep_kernel(block, steps, shard_ref, flat_ref, *refs):
    *box_refs, extra_ref, held = refs
    step = pl.program_id(0)
    held[pl.ds(pl.multiple_of(MARGIN + CHUNK * step, 8), CHUNK), :] = flat_ref[...].reshape(CHUNK, LANES)

    @pl.when(step == steps - 1)
    def _():
        low = lax.broadcasted_iota(jnp.int32, (8, LANES), 1) < 64
        low_one = lax.broadcasted_iota(jnp.int32, (1, LANES), 1) < 64
        extra_ref[...] = jnp.zeros_like(extra_ref)
        for share in range(4):

            @pl.when(shard_ref[0] == share)
            def _(share=share):
                odd = share % 2 == 1

                def tile(first, stride):
                    here = held[pl.ds(first, 8, stride=stride), :]
                    if not odd:
                        return here
                    ahead = held[pl.ds(first - 1, 8, stride=stride), :]
                    return jnp.where(low, pltpu.roll(ahead, 64, 1), pltpu.roll(here, 64, 1))

                for box, groups, box_row, flat_row, stride in block.parts(share):
                    base = MARGIN + block.start[share] + flat_row

                    def body(group, carry, box=box, base=base, box_row=box_row, stride=stride):
                        for j in range(6):
                            first = base + 16 * stride * group + j
                            both = jnp.concatenate([tile(first, stride), tile(first + 8 * stride, stride)], axis=0)
                            at = pl.multiple_of(box_row + 16 * group, 16)
                            box_refs[box][pl.ds(at, 16), LANES * j : LANES * j + LANES] = both.astype(BF)
                        return carry

                    lax.fori_loop(0, groups, body, 0, unroll=8)
                count = flat_rows(block, share)
                for to, row, length in block.extra[share]:
                    for k in range(length):
                        at = MARGIN + row + k
                        value = held[at : at + 1, :]
                        if odd:
                            ahead = held[at - 1 : at, :]
                            value = jnp.where(low_one, pltpu.roll(ahead, 64, 1), pltpu.roll(value, 64, 1))
                            if row + k == 0:
                                value = jnp.where(low_one, 0.0, value)
                        elif row + k == count:
                            value = jnp.where(low_one, value, 0.0)
                        extra_ref[to + k : to + k + 1, :] = value.astype(BF).astype(F32)


def flat_rows(block, share):
    return 4615 if block is ATTN else 9226


def prep(block, flat, shard):
    steps = -(-flat.shape[0] // (CHUNK * LANES))
    return pl.pallas_call(
        functools.partial(prep_kernel, block, steps),
        grid=(steps,),
        in_specs=[SMEM, pl.BlockSpec((CHUNK * LANES,), lambda i: (i,))],
        out_specs=[pl.BlockSpec((D, D), lambda i: (0, 0))] * block.boxes
        + [pl.BlockSpec((EXTRA, LANES), lambda i: (0, 0))],
        out_shape=[sds((D, D), BF)] * block.boxes + [sds((EXTRA, LANES), F32)],
        scratch_shapes=[pltpu.VMEM((MARGIN + CHUNK * steps + MARGIN, LANES), F32)],
        compiler_params=params(),
    )(shard, flat)


def spread_row(extra_ref, first, count):
    return jnp.concatenate([extra_ref[first + k : first + k + 1, :] for k in range(count)], axis=1)


def patch_row(ref, row, values):
    at = row // 16 * 16
    rows = lax.broadcasted_iota(jnp.int32, (16, values.shape[1]), 0)
    old = ref[at : at + 16, :].astype(F32)
    ref[at : at + 16, :] = jnp.where(rows == row - at, values, old).astype(BF)


def load_attn(shard, boxes, qkv_ref, proj_ref, sems):
    for wait in (False, True):
        for k, box in enumerate(boxes):
            share = jnp.bitwise_xor(shard, k)

            @pl.when(share == 3)
            def _(box=box, k=k):
                copy = pltpu.make_async_copy(box, proj_ref, sems.at[k, 0])
                copy.wait() if wait else copy.start()

            @pl.when(share != 3)
            def _(box=box, k=k, share=share):
                for part in range(3):
                    copy = pltpu.make_async_copy(
                        box.at[pl.ds(256 * part, 256), :],
                        qkv_ref.at[pl.ds(pl.multiple_of(768 * part + 256 * share, 256), 256), :],
                        sems.at[k, part],
                    )
                    copy.wait() if wait else copy.start()


def load_feed(shard, boxes, up_ref, down_ref, sems):
    for wait in (False, True):
        for k, box in enumerate(boxes):
            share = jnp.bitwise_xor(shard, k)

            @pl.when(share >= 2)
            def _(box=box, k=k, share=share):
                at = pl.multiple_of(768 * (share - 2), 256)
                copy = pltpu.make_async_copy(box, down_ref.at[pl.ds(at, 768), :], sems.at[k, 0])
                copy.wait() if wait else copy.start()

            @pl.when(share < 2)
            def _(box=box, k=k, share=share):
                for h in range(2):
                    copy = pltpu.make_async_copy(
                        box.at[pl.ds(384 * h, 384), :],
                        up_ref.at[pl.ds(pl.multiple_of(768 * h + 384 * share, 128), 384), :],
                        sems.at[k, h],
                    )
                    copy.wait() if wait else copy.start()


ANYWHERE = pl.BlockSpec(memory_space=pl.ANY)


def half_masks():
    lane = lax.broadcasted_iota(jnp.int32, (1, LANES), 1)
    return (lane < 64).astype(F32).astype(BF), (lane >= 64).astype(F32).astype(BF)


def two_heads(pair, masks):
    return jnp.concatenate([pair * masks[0], pair * masks[1]], axis=0)


def attn_forward(seq, x_ref, shard_ref, extra_ref, a0, a1, a2, a3, *refs):
    *refs, qkv_w, proj_w, vec_ref, bias_ref, sems = refs

    @pl.when(pl.program_id(0) == 0)
    def _():
        load_attn(shard_ref[0], (a0, a1, a2, a3), qkv_w, proj_w, sems)
        for part in range(3):
            patch_row(qkv_w, 768 * part + 255, spread_row(extra_ref, 12 + 6 * part, 6))
            patch_row(qkv_w, 768 * part + 512, spread_row(extra_ref, 30 + 6 * part, 6))
        vec_ref[...] = jnp.zeros_like(vec_ref)
        for row, first in enumerate((0, 6, 60, EXTRA + 0, EXTRA + 6)):
            vec_ref[row : row + 1, :] = spread_row(extra_ref, first, 6)
        bias_ref[...] = jnp.zeros_like(bias_ref)
        bias_ref[0:1, 0:768] = spread_row(extra_ref, 48, 6)
        bias_ref[0:1, 1536:2304] = spread_row(extra_ref, 54, 6)

    first_ref, qkv_ref, log_ref, att_ref, hid_ref, second_ref = refs
    x = x_ref[...].astype(F32)
    normed, _ = normed_of(x)
    first = (normed * vec_ref[0:1, :] + vec_ref[1:2, :]).astype(BF)
    first_ref[...] = first
    for part in range(3):
        cols = slice(768 * part, 768 * part + 768)
        qkv_ref[:, cols] = (dot(first, qkv_w[cols, :]) + bias_ref[0:1, cols]).astype(BF)
    masks = half_masks()
    real = lax.broadcasted_iota(jnp.int32, (2, T, T), 1) < seq
    for pair in range(HEADS // 2):
        at = LANES * pair
        for image in range(x_ref.shape[0] // T):
            own = slice(T * image, T * image + T)
            q = qkv_ref[own, at : at + LANES] * jnp.asarray(0.125, BF)
            k = two_heads(qkv_ref[own, 768 + at : 768 + at + LANES], masks)
            v = two_heads(qkv_ref[own, 1536 + at : 1536 + at + LANES], masks)
            scores = dot_nt(k, q).reshape(2, T, T)
            scores = jnp.where(real, scores, -1e30)
            top = jnp.max(scores, axis=1, keepdims=True)
            weight = jnp.exp(scores - top)
            total = jnp.sum(weight, axis=1, keepdims=True)
            logs = top + jnp.log(total)
            log_ref[image, 2 * pair : 2 * pair + 1, :] = logs[0]
            log_ref[image, 2 * pair + 1 : 2 * pair + 2, :] = logs[1]
            probs = (weight * (1.0 / total)).astype(BF).reshape(2 * T, T)
            att_ref[own, at : at + LANES] = dot_tn(probs, v).astype(BF)
    hidden = x + dot(att_ref[...], proj_w[...]) + vec_ref[2:3, :]
    hid_ref[...] = hidden
    normed, _ = normed_of(hidden)
    second_ref[...] = (normed * vec_ref[3:4, :] + vec_ref[4:5, :]).astype(BF)


FORWARD_IMAGES = 2


def call_attn_forward(seq, x, weights, boxes):
    shard, extra = weights
    rows = x.shape[0]
    images = rows // T
    step = FORWARD_IMAGES if images % FORWARD_IMAGES == 0 else 1
    tall = step * T
    made = [sds((2304, D), BF), sds((D, D), BF), sds((8, D), F32), sds((8, 2304), F32)]
    return pl.pallas_call(
        functools.partial(attn_forward, seq),
        grid=(images // step,),
        in_specs=[rows_of(tall, D), SMEM, whole(extra)] + [ANYWHERE] * 4,
        out_specs=[
            rows_of(tall, D),
            rows_of(tall, 2304),
            pl.BlockSpec((step, HEADS, T), lambda i: (i, 0, 0)),
            rows_of(tall, D),
            rows_of(tall, D),
            rows_of(tall, D),
        ]
        + [pl.BlockSpec(shape.shape, lambda i: (0, 0)) for shape in made],
        out_shape=[
            sds((rows, D), BF),
            sds((rows, 2304), BF),
            sds((images, HEADS, T), F32),
            sds((rows, D), BF),
            sds((rows, D), F32),
            sds((rows, D), BF),
        ]
        + made,
        scratch_shapes=[pltpu.SemaphoreType.DMA((4, 3))],
        compiler_params=params(),
    )(x, shard, extra, *boxes)


def hand_out(index, box, outs, sems):
    copies = [pltpu.make_async_copy(box.at[k], out, sems.at[k]) for k, out in enumerate(outs)]
    for k, copy in enumerate(copies):

        @pl.when(index == k)
        def _(copy=copy):
            copy.start()

    @pl.when(index == len(outs) - 1)
    def _():
        for copy in copies:
            copy.wait()


HALF = FF // 2
ROW_STEPS = 4


def feed(seq, part, tall, shard_ref, extra_ref, a0, a1, a2, a3, second_ref, cot_ref, result_ref, *refs):
    last = part == 1
    if last:
        before_ref, out_ref, gs_ref, *refs = refs
    else:
        out_ref, gs_ref, cot_sum, *refs = refs
    sum_ref, edge_ref, *outs, up_w, down_w, bias, second_all, cot_all, act_all, pre_all, box, sems, box_sems = refs
    step = pl.program_id(0)
    shard = shard_ref[0]

    @pl.when(step == 0)
    def _():
        load_feed(shard, (a0, a1, a2, a3), up_w, down_w, sems)
        for h in range(2):
            patch_row(up_w, 768 * h + 383, spread_row(extra_ref, EXTRA + 12 + 12 * h + 6 * part, 6))
            bias[0:1, 768 * h : 768 * h + 768] = spread_row(extra_ref, EXTRA + 36 + 12 * h + 6 * part, 6)
        if last:
            patch_row(down_w, 767, spread_row(extra_ref, EXTRA + 60, 6))
        sum_ref[...] = jnp.zeros_like(sum_ref)
        edge_ref[...] = jnp.zeros_like(edge_ref)
        if not last:
            cot_sum[...] = jnp.zeros_like(cot_sum)

    @pl.when(step < ROW_STEPS)
    def _():
        at = pl.ds(pl.multiple_of(step * tall, 16), tall)
        second = second_ref[...]
        cot = cot_ref[...]
        second_all[at, :] = second
        cot_all[at, :] = cot
        if last:
            result = result_ref[...]
            grad_second = before_ref[...]
        else:
            result = result_ref[...] + spread_row(extra_ref, EXTRA + 66, 6)
            grad_second = jnp.zeros_like(result)
            cot_sum[0:1, :] += jnp.sum(cot.astype(F32), axis=0, keepdims=True)
        for h in range(2):
            cols = slice(768 * h, 768 * h + 768)
            pre = dot(second, up_w[cols, :]) + bias[0:1, cols]
            grad_act = dot_nt(cot, down_w[cols, :])
            half = 0.5 * (1.0 + lax.erf(pre * root_half))
            act = (pre * half).astype(BF)
            grad_pre = grad_act * (half + pre * jnp.exp(-0.5 * pre * pre) * inv_root_tau)
            low = grad_pre.astype(BF)
            act_all[at, cols] = act
            pre_all[at, cols] = low
            sum_ref[0:1, cols] += jnp.sum(grad_pre, axis=0, keepdims=True)
            result = result + dot(act, down_w[cols, :])
            grad_second = grad_second + dot_nt(low, up_w[cols, :])
        if last:
            for image in range(tall // T):
                out_ref[image] = result[T * image : T * image + seq].astype(BF)
        else:
            out_ref[...] = result
        gs_ref[...] = grad_second

    index = step - ROW_STEPS
    side = jnp.bitwise_xor(shard // 2, 1 - index % 2)
    core = jnp.where(index >= 2, shard % 2, 1 - shard % 2)

    @pl.when((index >= 0) & (side == 0))
    def _():
        left = second_all[:, pl.ds(pl.multiple_of(384 * core, 128), 384)]
        for h in range(2):
            grad = dot_tn(left, pre_all[:, 768 * h : 768 * h + 768])
            box[index, 384 * h : 384 * h + 384, :] = grad.astype(BF)

            @pl.when(core == 0)
            def _(grad=grad, h=h):
                edge_ref[0:1, 768 * h : 768 * h + 768] = grad[383:384]

    @pl.when((index >= 0) & (side == 1))
    def _():
        left = act_all[:, pl.ds(pl.multiple_of(768 * core, 128), 768)]
        grad = dot_tn(left, cot_all[...])
        box[index] = grad.astype(BF)

        @pl.when(core == 0)
        def _():
            edge_ref[1:2, 0:768] = grad[767:768]

    hand_out(index, box, outs, box_sems)


def call_feed(seq, part, shard, extra, boxes, second, cot, result, before=None):
    rows = second.shape[0]
    images = rows // T
    tall = rows // ROW_STEPS
    last = part == 1
    row = lambda i: jnp.minimum(i, ROW_STEPS - 1)
    block = pl.BlockSpec((tall, D), lambda i: (row(i), 0))
    out = pl.BlockSpec((tall // T, seq, D), lambda i: (row(i), 0, 0)) if last else block
    small = lambda width: pl.BlockSpec((8, width), lambda i: (0, 0))
    return pl.pallas_call(
        functools.partial(feed, seq, part, tall),
        grid=(ROW_STEPS + 4,),
        in_specs=[SMEM, whole(extra)] + [ANYWHERE] * 4 + [block] * (4 if last else 3),
        out_specs=[out, block] + ([] if last else [small(D)]) + [small(HALF), small(HALF)] + [ANYWHERE] * 4,
        out_shape=[sds((images, seq, D), BF) if last else sds((rows, D), F32), sds((rows, D), F32)]
        + ([] if last else [sds((8, D), F32)])
        + [sds((8, HALF), F32), sds((8, HALF), F32)] + [sds((D, D), BF)] * 4,
        scratch_shapes=[
            pltpu.VMEM((HALF, D), BF),
            pltpu.VMEM((HALF, D), BF),
            pltpu.VMEM((8, HALF), F32),
            pltpu.VMEM((rows, D), BF),
            pltpu.VMEM((rows, D), BF),
            pltpu.VMEM((rows, HALF), BF),
            pltpu.VMEM((rows, HALF), BF),
            pltpu.VMEM((4, D, D), BF),
            pltpu.SemaphoreType.DMA((4, 2)),
            pltpu.SemaphoreType.DMA((4,)),
        ],
        compiler_params=params(60),
    )(shard, extra, *boxes, second, cot, result, *([before] if last else []))


WIDE = 384


def attn_backward(seq, group, base, count, last, shard_ref, log_ref, qkv_ref, first_ref, att_ref, *refs):
    step = pl.program_id(0)
    shard = shard_ref[0]
    if group == 0:
        gs_ref, hid_ref, cot_ref, vec_ref, proj_w, *refs = refs
    else:
        low_ref, ga_ref, *refs = refs
    if last:
        if group == 0:
            head_before, sum_before, first_any, att_any, low_any, grad_any, _, _, *refs = refs
        else:
            head_before, first_any, att_any, low_any, grad_any, *refs = refs
    grad_ref, head_sum, *refs = refs
    if group == 0:
        low_ref, ga_ref, gh_ref, sum_ref, *refs = refs
    if last:
        edge_ref, *outs, grad_all, first_all, low_all, att_all, box, box_sems, load_sems = refs
        done = pl.ds(0, base * T)
        loads = [
            pltpu.make_async_copy(grad_any.at[done], grad_all.at[done], load_sems.at[0]),
            pltpu.make_async_copy(first_any.at[done], first_all.at[done], load_sems.at[1]),
            pltpu.make_async_copy(low_any.at[done], low_all.at[done], load_sems.at[2]),
            pltpu.make_async_copy(
                att_any.at[done, pl.ds(WIDE * group, WIDE)], att_all.at[done], load_sems.at[3]
            ),
        ]

    @pl.when(step == 0)
    def _():
        if last:
            for load in loads:
                load.start()
            edge_ref[...] = jnp.zeros_like(edge_ref)
            head_sum[...] = head_before[...]
        else:
            head_sum[...] = jnp.zeros_like(head_sum)
        if group == 0:
            sum_ref[...] = sum_before[...] if last else jnp.zeros_like(sum_ref)

    @pl.when(step < count)
    def _():
        at_rows = pl.ds(pl.multiple_of((step + base) * T, 16), T)
        if last:
            first_all[at_rows, :] = first_ref[...]
            att_all[at_rows, :] = att_ref[...]
        if group == 0:
            gs = gs_ref[...]
            normed, spread = normed_of(hid_ref[...])
            gn = gs * vec_ref[3:4, :]
            gh = cot_ref[...].astype(F32) + spread * (
                gn - jnp.mean(gn, axis=-1, keepdims=True) - normed * jnp.mean(gn * normed, axis=-1, keepdims=True)
            )
            sum_ref[0:1, :] += jnp.sum(gs * normed, axis=0, keepdims=True)
            sum_ref[1:2, :] += jnp.sum(gs, axis=0, keepdims=True)
            sum_ref[2:3, :] += jnp.sum(gh, axis=0, keepdims=True)
            gh_ref[...] = gh
            gh_low = gh.astype(BF)
            low_ref[...] = gh_low
            ga_ref[...] = dot_nt(gh_low, proj_w[...]).astype(BF)
        if last:
            low_all[at_rows, :] = low_ref[...]
        low = lax.broadcasted_iota(jnp.int32, (T, LANES), 1) < 64
        real = lax.broadcasted_iota(jnp.int32, (2, T, T), 1) < seq
        eighth = jnp.asarray(0.125, BF)
        masks = half_masks()
        for pair in range(3):
            at = LANES * pair
            full = WIDE * group + at
            head = 6 * group + 2 * pair
            q = qkv_ref[:, full : full + LANES] * eighth
            k = two_heads(qkv_ref[:, 768 + full : 768 + full + LANES], masks)
            v = two_heads(qkv_ref[:, 1536 + full : 1536 + full + LANES], masks)
            grad_out = ga_ref[:, at : at + LANES]
            scores = dot_nt(k, q).reshape(2, T, T)
            logs = jnp.concatenate([log_ref[0:1, head : head + 1, :], log_ref[0:1, head + 1 : head + 2, :]], axis=0)
            probs = jnp.where(real, jnp.exp(scores - logs), 0.0)
            grad_v = dot(probs.astype(BF).reshape(2 * T, T), grad_out)
            grad_probs = dot_nt(v, grad_out).reshape(2, T, T)
            delta = jnp.sum(probs * grad_probs, axis=1, keepdims=True)
            grad_scores = (probs * (grad_probs - delta)).astype(BF).reshape(2 * T, T)
            grad_k = dot(grad_scores, q)
            grads = (
                dot_tn(grad_scores, k * eighth),
                jnp.where(low, grad_k[:T], grad_k[T:]),
                jnp.where(low, grad_v[:T], grad_v[T:]),
            )
            for part, grad in enumerate(grads):
                if part != 1:
                    row = part // 2
                    head_sum[row : row + 1, at : at + LANES] += jnp.sum(grad, axis=0, keepdims=True)
                cols = slice(WIDE * part + at, WIDE * part + at + LANES)
                grad = grad.astype(BF)
                grad_ref[:, cols] = grad
                if last:
                    grad_all[at_rows, cols] = grad

    if not last:
        return

    @pl.when(step == count)
    def _():
        for load in loads:
            load.wait()

    index = step - count
    side = jnp.bitwise_xor(shard // 2, 1 - index % 2)
    core = jnp.where(index >= 2, shard % 2, 1 - shard % 2)
    share = 2 * side + core

    @pl.when((index >= 0) & (share == 3))
    def _():
        box[index] = dot_tn(att_all[...], low_all[...]).astype(BF)

    @pl.when((index >= 0) & (share != 3))
    def _():
        grad = dot_tn(first_all[:, pl.ds(pl.multiple_of(256 * share, 256), 256)], grad_all[...])
        for part in range(3):
            cols = slice(WIDE * part, WIDE * part + WIDE)
            for u in range(2):
                box[index, 128 * part : 128 * part + 128, WIDE * u : WIDE * u + WIDE] = grad[
                    128 * u : 128 * u + 128, cols
                ].astype(BF)

        @pl.when(share == 0)
        def _():
            edge_ref[0:1, :] = grad[255:256]

        @pl.when(share == 2)
        def _():
            edge_ref[1:2, :] = grad[0:1]

    hand_out(index, box, outs, box_sems)


def call_attn_backward(seq, group, base, count, shard, log_total, qkv, first, attended, *more, before=()):
    rows = first.shape[0]
    last = len(before) > 0
    row = lambda i: jnp.minimum(i, count - 1) + base
    block = lambda width, col=0: pl.BlockSpec((T, width), lambda i: (row(i), col))
    small = lambda width: pl.BlockSpec((8, width), lambda i: (0, 0))
    in_specs = [SMEM, pl.BlockSpec((1, HEADS, T), lambda i: (row(i), 0, 0)), block(2304), block(D), block(WIDE, group)]
    out_specs = [block(3 * WIDE), small(WIDE)]
    out_shape = [sds((rows, 3 * WIDE), BF), sds((8, WIDE), F32)]
    if group == 0:
        in_specs += [block(D)] * 3 + [whole(more[3]), whole(more[4])]
        out_specs += [block(D), block(D), block(D), small(D)]
        out_shape += [sds((rows, D), BF), sds((rows, D), BF), sds((rows, D), F32), sds((8, D), F32)]
    else:
        in_specs += [block(D), block(WIDE, 1)]
    aliases, scratch, extra = {}, [], []
    if last:
        at = len(in_specs)
        if group == 0:
            grad, head, low, ga, gh, total = before
            extra = [head, total, first, attended, low, grad, ga, gh]
            in_specs += [whole(head), whole(total)] + [ANYWHERE] * 6
            aliases = {at + 4: 2, at + 5: 0, at + 6: 3, at + 7: 4}
        else:
            grad, head = before
            extra = [head, first, attended, more[0], grad]
            in_specs += [whole(head)] + [ANYWHERE] * 4
            aliases = {at + 4: 0}
        out_specs += [small(3 * WIDE)] + [ANYWHERE] * 4
        out_shape += [sds((8, 3 * WIDE), F32)] + [sds((WIDE, D), BF)] * 4
        scratch = [
            pltpu.VMEM((rows, 3 * WIDE), BF),
            pltpu.VMEM((rows, D), BF),
            pltpu.VMEM((rows, D), BF),
            pltpu.VMEM((rows, WIDE), BF),
            pltpu.VMEM((4, WIDE, D), BF),
            pltpu.SemaphoreType.DMA((4,)),
            pltpu.SemaphoreType.DMA((4,)),
        ]
    return pl.pallas_call(
        functools.partial(attn_backward, seq, group, base, count, last),
        grid=(count + 4 if last else count,),
        in_specs=in_specs,
        out_specs=out_specs,
        out_shape=out_shape,
        input_output_aliases=aliases,
        scratch_shapes=scratch,
        compiler_params=params(),
    )(shard, log_total, qkv, first, attended, *more, *extra)


def input_backward(seq, grad0, grad1, gh_ref, x_ref, vec_ref, qkv_w, out_ref, sum_ref):
    @pl.when(pl.program_id(0) == 0)
    def _():
        sum_ref[...] = jnp.zeros_like(sum_ref)

    grad_first = None
    for part in range(3):
        cols = slice(WIDE * part, WIDE * part + WIDE)
        both = jnp.concatenate([grad0[:, cols], grad1[:, cols]], axis=1)
        term = dot_nt(both, qkv_w[768 * part : 768 * part + 768, :])
        grad_first = term if part == 0 else grad_first + term
    normed, spread = normed_of(x_ref[...].astype(F32))
    gn = grad_first * vec_ref[0:1, :]
    grad = gh_ref[...] + spread * (
        gn - jnp.mean(gn, axis=-1, keepdims=True) - normed * jnp.mean(gn * normed, axis=-1, keepdims=True)
    )
    sum_ref[0:1, :] += jnp.sum(grad_first * normed, axis=0, keepdims=True)
    sum_ref[1:2, :] += jnp.sum(grad_first, axis=0, keepdims=True)
    for image in range(grad.shape[0] // T):
        out_ref[image] = grad[T * image : T * image + seq].astype(BF)


def call_input_backward(seq, grads, gh, x, vec, qkv_w):
    rows = gh.shape[0]
    images = rows // T
    step = 2 if images % 2 == 0 else 1
    tall = step * T
    return pl.pallas_call(
        functools.partial(input_backward, seq),
        grid=(images // step,),
        in_specs=[rows_of(tall, 3 * WIDE)] * 2 + [rows_of(tall, D), rows_of(tall, D), whole(vec), whole(qkv_w)],
        out_specs=[pl.BlockSpec((step, seq, D), lambda i: (i, 0, 0)), pl.BlockSpec((8, D), lambda i: (0, 0))],
        out_shape=[sds((images, seq, D), BF), sds((8, D), F32)],
        compiler_params=params(),
    )(*grads, gh, x, vec, qkv_w)


def putter(out_ref):
    out_ref[...] = jnp.zeros_like(out_ref)

    def put(first, ref, row, col, width):
        for k in range(width // LANES):
            at = col + LANES * k
            out_ref[first + k : first + k + 1, :] = ref[row : row + 1, at : at + LANES]

    return put


def pack(last_sum, back_sum, head0, head1, edge0, edge1, pre0, pre1, up0, up1, cot_sum, out_ref):
    put = putter(out_ref)
    put(0, last_sum, 0, 0, D)
    put(6, last_sum, 1, 0, D)
    for group, (head, edge) in enumerate(((head0, edge0), (head1, edge1))):
        for part in range(3):
            put(12 + 6 * part + 3 * group, edge, 0, WIDE * part, WIDE)
            put(30 + 6 * part + 3 * group, edge, 1, WIDE * part, WIDE)
        put(48 + 3 * group, head, 0, 0, WIDE)
        put(54 + 3 * group, head, 1, 0, WIDE)
    put(60, back_sum, 2, 0, D)
    put(EXTRA, back_sum, 0, 0, D)
    put(EXTRA + 6, back_sum, 1, 0, D)
    for j, (pre, up) in enumerate(((pre0, up0), (pre1, up1))):
        for h in range(2):
            put(EXTRA + 12 + 12 * h + 6 * j, up, 0, 768 * h, D)
            put(EXTRA + 36 + 12 * h + 6 * j, pre, 0, 768 * h, D)
    put(EXTRA + 60, up1, 1, 0, D)
    put(EXTRA + 66, cot_sum, 0, 0, D)


def call_pack(*arrays):
    return pl.pallas_call(
        pack,
        in_specs=[pl.BlockSpec(memory_space=pltpu.VMEM)] * len(arrays),
        out_specs=pl.BlockSpec(memory_space=pltpu.VMEM),
        out_shape=sds((2 * EXTRA, LANES), F32),
        compiler_params=params(),
    )(*arrays)


def adam_kernel(block, share_size, scale, boxes, shard_ref, power_ref, extra_ref, *refs):
    box_refs = refs[:boxes]
    flat_ref, mom_ref, grad_ref, change_ref, new_ref, held = refs[boxes:]
    step = pl.program_id(0)

    @pl.when(step == 0)
    def _():
        for share in range(4):

            @pl.when(shard_ref[0] == share)
            def _(share=share):
                for box, groups, box_row, col, cols, flat_row, stride in block.grad_parts(share):
                    base = MARGIN + block.start[share] + flat_row

                    def body(group, carry, box=box, box_row=box_row, col=col, cols=cols, base=base, stride=stride):
                        row = pl.multiple_of(box_row + 16 * group, 16)
                        for j in range(cols):
                            at = LANES * (col + j)
                            both = box_refs[box][pl.ds(row, 16), at : at + LANES].astype(F32)
                            to = base + 16 * stride * group + j
                            held[pl.ds(to, 8, stride=stride), :] = both[0:8]
                            held[pl.ds(to + 8 * stride, 8, stride=stride), :] = both[8:16]
                        return carry

                    lax.fori_loop(0, groups, body, 0, unroll=8)
                for source, row, length in block.put[share]:
                    held[MARGIN + row : MARGIN + row + length, :] = extra_ref[block.base + source : block.base + source + length, :]

    start = pl.multiple_of(MARGIN + CHUNK * step, 8)
    shard = shard_ref[0]
    low = lax.broadcasted_iota(jnp.int32, (CHUNK, LANES), 1) < 64
    here = held[pl.ds(start, CHUNK), :]
    after = held[pl.ds(start + 1, CHUNK), :]
    shifted = jnp.where(low, pltpu.roll(here, 64, 1), pltpu.roll(after, 64, 1))
    grad = jnp.where(shard % 2 == 1, shifted, here) * scale
    position = (
        shard * share_size
        + step * (CHUNK * LANES)
        + lax.broadcasted_iota(jnp.int32, (CHUNK, LANES), 0) * LANES
        + lax.broadcasted_iota(jnp.int32, (CHUNK, LANES), 1)
    )
    matrix = jnp.zeros((CHUNK, LANES), jnp.bool_)
    for first, end in block.matrices:
        matrix = matrix | ((position >= first) & (position < end))
    size = CHUNK * LANES
    p = flat_ref[...].reshape(CHUNK, LANES)
    m = beta_one * mom_ref[0, :].reshape(CHUNK, LANES) + (1.0 - beta_one) * grad
    s = beta_two * mom_ref[1, :].reshape(CHUNK, LANES) + (1.0 - beta_two) * grad * grad
    ratio = (m * power_ref[0]) / (jnp.sqrt(s * power_ref[1]) + adam_eps)
    change = jnp.where(matrix, rate_matrix, rate_vector) * (ratio + jnp.where(matrix, decay_matrix, 0.0) * p)
    grad_ref[...] = grad.reshape(size)
    change_ref[...] = change.reshape(size)
    new_ref[0, :] = m.reshape(size)
    new_ref[1, :] = s.reshape(size)


def adam(block, shard, powers, extra, boxes, flat, moments, scale):
    count = flat.shape[0]
    steps = -(-count // (CHUNK * LANES))
    line = pl.BlockSpec((CHUNK * LANES,), lambda i: (i,))
    two = pl.BlockSpec((2, CHUNK * LANES), lambda i: (0, i))
    return pl.pallas_call(
        functools.partial(adam_kernel, block, count, scale, len(boxes)),
        grid=(steps,),
        in_specs=[SMEM, SMEM, whole(extra)] + [whole(box) for box in boxes] + [line, two],
        out_specs=[line, line, two],
        out_shape=[sds((count,), F32), sds((count,), F32), sds((2, count), F32)],
        scratch_shapes=[pltpu.VMEM((MARGIN + CHUNK * steps + MARGIN, LANES), F32)],
        compiler_params=params(),
    )(shard, powers, extra, *boxes, flat, moments)


def swap(value, axis, bit):
    pairs = [(i, i ^ bit) for i in range(lax.axis_size(axis))]
    return lax.ppermute(value, axis, pairs)


def turn(value, axis, unit, distance):
    size = lax.axis_size(axis)
    return lax.ppermute(value, axis, [(i, (i + unit * distance) % size) for i in range(size)])


def pick(array, index, axis=0):
    return lax.dynamic_index_in_dim(array, index, axis, keepdims=False)


class Line:
    def __init__(self):
        self.last = None

    def __call__(self, step, *args):
        if self.last is not None:
            flat, tree = jax.tree.flatten(args)
            flat = lax.optimization_barrier((self.last, *flat))[1:]
            args = jax.tree.unflatten(tree, flat)
        out = step(*args)
        self.last = min(jax.tree.leaves(out), key=lambda leaf: leaf.size)
        return out


def pause_kernel(in_ref, out_ref):
    out_ref[...] = in_ref[...]


def pause(line, value):
    return line(
        pl.pallas_call(
            pause_kernel,
            out_shape=sds(value.shape, value.dtype),
            cost_estimate=pl.CostEstimate(flops=10**11, bytes_accessed=10**8, transcendentals=0),
        ),
        value,
    )


class Sum:
    def __init__(self, line, across, same, mine_across, mine):
        self.line, self.mine_across, self.mine = line, mine_across, mine
        self.rows = mine.shape[0]
        rep = lax.axis_index("rep")
        self.near, self.far = rep % 2, rep // 2
        self.count = lax.axis_size("rep") // 2
        self.came_across, self.here = swap(across, "shard", 1), swap(same, "shard", 1)

    def side(self):
        add = lambda a, b: (a.astype(F32) + b.astype(F32)).astype(BF)
        send = self.line(add, self.mine_across, self.came_across)
        self.came = swap(send, "shard", 2)
        self.here = self.line(lambda a: a, self.here)

    def close(self):
        def step(mine, here, came):
            total = mine.astype(F32) + here.astype(F32) + came.astype(F32)
            halves = total.reshape(2, self.rows // 2, D)
            return pick(halves, 1 - self.near).astype(BF), pick(halves, self.near)

        send, self.half = self.line(step, self.mine, self.here, self.came)
        self.came = swap(send, "rep", 1)

    def level(self, bit):
        if bit == 2:
            self.part = self.line(lambda a, b: (a + b.astype(F32)).astype(BF), self.half, self.came)
        else:
            self.part = self.line(lambda a, b: (a.astype(F32) + b.astype(F32)).astype(BF), self.part, self.came)
        self.came = swap(self.part, "rep", bit)

    def back_level(self):
        self.half = self.line(lambda a, b: (a.astype(F32) + b.astype(F32)).astype(BF), self.part, self.came)
        self.came = swap(self.half, "rep", 1)

    def along(self):
        def step(half, came):
            parts = (half + came.astype(F32)).reshape(self.count, self.rows // 2 // self.count, D)
            sends = [pick(parts, (self.far + d) % self.count).astype(BF) for d in range(1, self.count)]
            return sends, pick(parts, self.far)

        sends, self.part = self.line(step, self.half, self.came)
        self.came = [turn(send, "rep", 2, d + 1) for d, send in enumerate(sends)]

    def back_along(self):
        def step(part, came):
            for value in came:
                part = part + value.astype(F32)
            return part.astype(BF)

        self.part = self.line(step, self.part, self.came)
        self.came = [turn(self.part, "rep", 2, d) for d in range(1, self.count)]

    def back_close(self):
        def step(part, came):
            full = jnp.zeros((self.count,) + part.shape, BF)
            for d, value in enumerate([part] + came):
                full = lax.dynamic_update_slice_in_dim(full, value[None], (self.far + self.count - d) % self.count, 0)
            return full.reshape(self.rows // 2, D)

        self.half = self.line(step, self.part, self.came)
        self.came = swap(self.half, "rep", 1)

    def end(self):
        def step(half, came):
            first = self.near == 0
            return jnp.concatenate([jnp.where(first, half, came), jnp.where(first, came, half)], axis=0)

        return self.line(step, self.half, self.came)


class SumAll:
    def __init__(self, line, value):
        self.line, self.value = line, value
        self.hops = [("shard", 1)]
        bit = 2
        while bit < lax.axis_size("rep"):
            self.hops.append(("rep", bit))
            bit *= 2
        self.hops += [("shard", 2), ("rep", 1)]
        self.came = swap(value, *self.hops.pop(0))

    def hop(self):
        self.value = self.line(lambda a, b: a + b, self.value, self.came)
        if self.hops:
            self.came = swap(self.value, *self.hops.pop(0))
            return False
        return True


def body(layer_input, out_cotangent, attention_params, attention_moments, feedforward_params, feedforward_moments, step_count):
    images, seq, _ = layer_input.shape
    rows = images * T
    image_total = images * lax.axis_size("shard") * lax.axis_size("rep")
    scale = 1.0 / image_total
    shard = lax.axis_index("shard").astype(jnp.int32).reshape(1)
    time = step_count[0].astype(F32)
    powers = jnp.stack([1.0 / (1.0 - jnp.power(beta_one, time)), 1.0 / (1.0 - jnp.power(beta_two, time))])
    pad = ((0, 0), (0, T - seq), (0, 0))
    padded = lambda tokens: jnp.pad(tokens, pad).reshape(rows, D)
    line = Line()

    attn_box, attn_extra = line(functools.partial(prep, ATTN), attention_params, shard)
    attn_across = swap(attn_box, "shard", 2)
    attn_near = swap(attn_box, "shard", 1)
    box0, box1, feed_extra = line(functools.partial(prep, FEED), feedforward_params, shard)
    extra = line(lambda a, b: jnp.concatenate([a, b], axis=0), attn_extra, feed_extra)
    came = swap(extra, "shard", 1)
    x = line(padded, layer_input)
    extra = line(lambda a, b: a + b, extra, came)
    came = swap(extra, "shard", 2)
    cot = line(padded, out_cotangent)
    extra = line(lambda a, b: a + b, extra, came)
    near0, near1 = swap(box0, "shard", 1), swap(box1, "shard", 1)
    across, send0 = line(lambda a, b: lax.optimization_barrier((a, b)), attn_across, box0)
    attn_both = swap(across, "shard", 1)
    across0 = swap(send0, "shard", 2)
    boxes = (attn_box, attn_near, attn_across, attn_both)
    first, qkv, log_total, attended, hidden, second, qkv_w, proj_w, vec, bias = line(
        lambda x, w, b: call_attn_forward(seq, x, w, b), x, (shard, extra), boxes
    )
    across, send1 = line(lambda a, b: lax.optimization_barrier((a, b)), across0, box1)
    both0 = swap(across, "shard", 1)
    across1 = swap(send1, "shard", 2)
    boxes = (box0, near0, across0, both0)
    result, gs, cot_sum, pre0, up0, *grads = line(
        lambda *a: call_feed(seq, 0, *a), shard, extra, boxes, second, cot, hidden
    )
    feed0 = Sum(line, *grads)
    both1 = swap(line(lambda a: a, across1), "shard", 1)
    feed0.side()
    boxes = (box1, near1, across1, both1)
    layer_output, gs, pre1, up1, *grads = line(
        lambda *a: call_feed(seq, 1, *a), shard, extra, boxes, second, cot, result, gs
    )
    feed1 = Sum(line, *grads)
    feed0.close()
    feed1.side()
    half = images // 2
    common = (shard, log_total, qkv, first, attended)
    more = (gs, hidden, cot, vec, proj_w)
    before = line(lambda *a: call_attn_backward(seq, 0, 0, half, *a), *common, *more)
    feed0.along()
    grad0, head0, gh_low, ga, gh, back_sum, edge0, *grads = line(
        lambda b, *a: call_attn_backward(seq, 0, half, images - half, *a, before=b), tuple(before), *common, *more
    )
    attn0 = Sum(line, *grads)
    feed1.close()
    feed0.back_along()
    attn0.side()
    more = (gh_low, ga)
    before = line(lambda *a: call_attn_backward(seq, 1, 0, half, *a), *common, *more)
    feed0.back_close()
    feed1.along()
    grad1, head1, edge1, *grads = line(
        lambda b, *a: call_attn_backward(seq, 1, half, images - half, *a, before=b), tuple(before), *common, *more
    )
    attn1 = Sum(line, *grads)
    feed1.back_along()
    attn0.close()
    feed_box0 = feed0.end()
    head1 = pause(line, head1)
    attn1.side()
    input_grad, last_sum = line(lambda *a: call_input_backward(seq, *a), (grad0, grad1), gh, x, vec, qkv_w)
    sums = line(call_pack, last_sum, back_sum, head0, head1, edge0, edge1, pre0, pre1, up0, up1, cot_sum)
    bits = [2 << k for k in range((lax.axis_size("rep") // 2).bit_length() - 1)]
    sums = SumAll(line, sums)
    attn1.close()
    sums.hop()
    attn0.level(2)
    feed1.back_close()
    sums.hop()
    attn1.level(2)
    for bit in bits[1:]:
        attn0.level(bit)
    sums.hop()
    feed_box1 = feed1.end()
    sums.hop()
    for bit in bits[1:]:
        attn1.level(bit)
    while not sums.hop():
        pass
    feed_grad, feed_change, feed_new = line(
        lambda *a: adam(FEED, *a, scale), shard, powers, sums.value, [feed_box0, feed_box1], feedforward_params, feedforward_moments
    )
    attn0.back_level()
    attn1.back_level()
    layer_output, input_grad = line(lambda *a: a, layer_output, input_grad)
    attn_box0 = attn0.end()
    attn_grad, attn_change, attn_new = line(
        lambda *a: adam(ATTN, *a, scale), shard, powers, sums.value, [attn_box0, attn1.end()], attention_params, attention_moments
    )
    return (layer_output, input_grad, attn_grad, feed_grad, attn_change, attn_new, feed_change, feed_new)


def solution(mesh):
    tokens = P(("shard", "rep"), None, None)
    in_specs = (tokens, tokens, P("shard"), P(None, "shard"), P("shard"), P(None, "shard"), P())
    out_specs = (tokens, tokens, P("shard"), P("shard"), P("shard"), P(None, "shard"), P("shard"), P(None, "shard"))
    return jax.shard_map(body, mesh=mesh, in_specs=in_specs, out_specs=out_specs, check_vma=False)
```

```python
import functools

import jax
import jax.numpy as jnp
from jax import lax
from jax.experimental import pallas as pl
from jax.experimental.pallas import tpu as pltpu
from jax.sharding import PartitionSpec as P

D = 768
HEADS = 12
FF = 3072
T = 208

F32 = jnp.float32
BF = jnp.bfloat16

ln_eps = 1e-06
beta_one = 0.9
beta_two = 0.999
adam_eps = 1e-08
rate_matrix = 0.01
rate_vector = 0.1
decay_matrix = 0.05
root_half = 0.7071067811865476
inv_root_tau = 0.3989422804014327

MB = 1 << 20
LANES = 128
MARGIN = 8

ATTN_START = (12, 5, -3, 2)
FEED_START = (12, 2, 15, 5)


def attn_parts(share):
    if share < 3:
        return [(0, 16, 256 * part, 6 * part, 18) for part in range(3)]
    return [(0, 48, 0, 0, 6)]


def feed_parts(share):
    if share < 2:
        return [(j, 24, 384 * h, 12 * h + 6 * j, 24) for j in range(2) for h in range(2)]
    return [(j, 48, 0, 4608 * j, 6) for j in range(2)]


def attn_grad_parts(share):
    if share < 3:
        return [
            (g, 8, 128 * part, 3 * u, 3, 18 * 128 * u + 6 * part + 3 * g, 18)
            for g in range(2)
            for part in range(3)
            for u in range(2)
        ]
    return [(g, 24, 0, 0, 6, 6 * 384 * g, 6) for g in range(2)]


def feed_grad_parts(share):
    return [(box, groups, row, 0, 6, flat, stride) for box, groups, row, flat, stride in feed_parts(share)]


ATTN_EXTRA = (
    [(0, 0, 12), (12, 4602, 14)],
    [(25, 0, 5), (30, 4613, 3)],
    [(33, 0, 15), (48, 4605, 11)],
    [(58, 0, 2), (60, 4610, 6)],
)
FEED_EXTRA = (
    [(0, 0, 12), (12, 9204, 23)],
    [(34, 0, 2), (36, 9218, 9)],
    [(45, 0, 15), (60, 9225, 2)],
    [(61, 0, 5), (66, 9221, 6)],
)
ATTN_PUT = (
    [(0, 0, 12)],
    [(25, 0, 5), (30, 4613, 3)],
    [(48, 4605, 12)],
    [(58, 0, 2), (60, 4610, 6)],
)
FEED_PUT = (
    [(0, 0, 12)],
    [(34, 0, 2), (36, 9218, 9)],
    [(45, 0, 15)],
    [(61, 0, 5), (66, 9221, 6)],
)
EXTRA = 72


class Block:
    def __init__(self, base, boxes, start, parts, grad_parts, extra, put, matrices):
        self.base = base
        self.boxes, self.start, self.parts, self.grad_parts = boxes, start, parts, grad_parts
        self.extra, self.put = extra, put
        self.matrices = matrices


ATTN = Block(
    0, 1, ATTN_START, attn_parts, attn_grad_parts, ATTN_EXTRA, ATTN_PUT, ((1536, 1771008), (1772544, 2362368))
)
FEED = Block(
    EXTRA, 2, FEED_START, feed_parts, feed_grad_parts, FEED_EXTRA, FEED_PUT, ((1536, 2360832), (2363904, 4723200))
)


def params(limit=56):
    return pltpu.CompilerParams(vmem_limit_bytes=limit * MB)


def dot(a, b):
    return lax.dot_general(a, b, (((1,), (0,)), ((), ())), preferred_element_type=F32)


def dot_nt(a, b):
    return lax.dot_general(a, b, (((1,), (1,)), ((), ())), preferred_element_type=F32)


def dot_tn(a, b):
    return lax.dot_general(a, b, (((0,), (0,)), ((), ())), preferred_element_type=F32)


def normed_of(values):
    center = values - jnp.mean(values, axis=-1, keepdims=True)
    spread = lax.rsqrt(jnp.mean(center * center, axis=-1, keepdims=True) + ln_eps)
    return center * spread, spread


def whole(array):
    rank = len(array.shape)
    return pl.BlockSpec(array.shape, lambda *i: (0,) * rank, pipeline_mode=pl.Buffered(1))


def rows_of(count, width):
    return pl.BlockSpec((count, width), lambda i: (i, 0))


SMEM = pl.BlockSpec(memory_space=pltpu.SMEM)


def sds(shape, dtype):
    return jax.ShapeDtypeStruct(shape, dtype)


CHUNK = 2368


def prep_kernel(block, steps, shard_ref, flat_ref, *refs):
    *box_refs, extra_ref, held = refs
    step = pl.program_id(0)
    held[pl.ds(pl.multiple_of(MARGIN + CHUNK * step, 8), CHUNK), :] = flat_ref[...].reshape(CHUNK, LANES)

    @pl.when(step == steps - 1)
    def _():
        low = lax.broadcasted_iota(jnp.int32, (8, LANES), 1) < 64
        low_one = lax.broadcasted_iota(jnp.int32, (1, LANES), 1) < 64
        extra_ref[...] = jnp.zeros_like(extra_ref)
        for share in range(4):

            @pl.when(shard_ref[0] == share)
            def _(share=share):
                odd = share % 2 == 1

                def tile(first, stride):
                    here = held[pl.ds(first, 8, stride=stride), :]
                    if not odd:
                        return here
                    ahead = held[pl.ds(first - 1, 8, stride=stride), :]
                    return jnp.where(low, pltpu.roll(ahead, 64, 1), pltpu.roll(here, 64, 1))

                for box, groups, box_row, flat_row, stride in block.parts(share):
                    base = MARGIN + block.start[share] + flat_row

                    def body(group, carry, box=box, base=base, box_row=box_row, stride=stride):
                        for j in range(6):
                            first = base + 16 * stride * group + j
                            both = jnp.concatenate([tile(first, stride), tile(first + 8 * stride, stride)], axis=0)
                            at = pl.multiple_of(box_row + 16 * group, 16)
                            box_refs[box][pl.ds(at, 16), LANES * j : LANES * j + LANES] = both.astype(BF)
                        return carry

                    lax.fori_loop(0, groups, body, 0, unroll=8)
                count = flat_rows(block, share)
                for to, row, length in block.extra[share]:
                    for k in range(length):
                        at = MARGIN + row + k
                        value = held[at : at + 1, :]
                        if odd:
                            ahead = held[at - 1 : at, :]
                            value = jnp.where(low_one, pltpu.roll(ahead, 64, 1), pltpu.roll(value, 64, 1))
                            if row + k == 0:
                                value = jnp.where(low_one, 0.0, value)
                        elif row + k == count:
                            value = jnp.where(low_one, value, 0.0)
                        extra_ref[to + k : to + k + 1, :] = value.astype(BF).astype(F32)


def flat_rows(block, share):
    return 4615 if block is ATTN else 9226


def prep(block, flat, shard):
    steps = -(-flat.shape[0] // (CHUNK * LANES))
    return pl.pallas_call(
        functools.partial(prep_kernel, block, steps),
        grid=(steps,),
        in_specs=[SMEM, pl.BlockSpec((CHUNK * LANES,), lambda i: (i,))],
        out_specs=[pl.BlockSpec((D, D), lambda i: (0, 0))] * block.boxes
        + [pl.BlockSpec((EXTRA, LANES), lambda i: (0, 0))],
        out_shape=[sds((D, D), BF)] * block.boxes + [sds((EXTRA, LANES), F32)],
        scratch_shapes=[pltpu.VMEM((MARGIN + CHUNK * steps + MARGIN, LANES), F32)],
        compiler_params=params(),
    )(shard, flat)


def spread_row(extra_ref, first, count):
    return jnp.concatenate([extra_ref[first + k : first + k + 1, :] for k in range(count)], axis=1)


def patch_row(ref, row, values):
    at = row // 16 * 16
    rows = lax.broadcasted_iota(jnp.int32, (16, values.shape[1]), 0)
    old = ref[at : at + 16, :].astype(F32)
    ref[at : at + 16, :] = jnp.where(rows == row - at, values, old).astype(BF)


def load_attn(shard, boxes, qkv_ref, proj_ref, sems):
    for wait in (False, True):
        for k, box in enumerate(boxes):
            share = jnp.bitwise_xor(shard, k)

            @pl.when(share == 3)
            def _(box=box, k=k):
                copy = pltpu.make_async_copy(box, proj_ref, sems.at[k, 0])
                copy.wait() if wait else copy.start()

            @pl.when(share != 3)
            def _(box=box, k=k, share=share):
                for part in range(3):
                    copy = pltpu.make_async_copy(
                        box.at[pl.ds(256 * part, 256), :],
                        qkv_ref.at[pl.ds(pl.multiple_of(768 * part + 256 * share, 256), 256), :],
                        sems.at[k, part],
                    )
                    copy.wait() if wait else copy.start()


def load_feed(shard, boxes, up_ref, down_ref, sems):
    for wait in (False, True):
        for k, box in enumerate(boxes):
            share = jnp.bitwise_xor(shard, k)

            @pl.when(share >= 2)
            def _(box=box, k=k, share=share):
                at = pl.multiple_of(768 * (share - 2), 256)
                copy = pltpu.make_async_copy(box, down_ref.at[pl.ds(at, 768), :], sems.at[k, 0])
                copy.wait() if wait else copy.start()

            @pl.when(share < 2)
            def _(box=box, k=k, share=share):
                for h in range(2):
                    copy = pltpu.make_async_copy(
                        box.at[pl.ds(384 * h, 384), :],
                        up_ref.at[pl.ds(pl.multiple_of(768 * h + 384 * share, 128), 384), :],
                        sems.at[k, h],
                    )
                    copy.wait() if wait else copy.start()


ANYWHERE = pl.BlockSpec(memory_space=pl.ANY)


def half_masks():
    lane = lax.broadcasted_iota(jnp.int32, (1, LANES), 1)
    return (lane < 64).astype(F32).astype(BF), (lane >= 64).astype(F32).astype(BF)


def two_heads(pair, masks):
    return jnp.concatenate([pair * masks[0], pair * masks[1]], axis=0)


def attn_forward(seq, x_ref, shard_ref, extra_ref, a0, a1, a2, a3, *refs):
    *refs, qkv_w, proj_w, vec_ref, bias_ref, sems = refs

    @pl.when(pl.program_id(0) == 0)
    def _():
        load_attn(shard_ref[0], (a0, a1, a2, a3), qkv_w, proj_w, sems)
        for part in range(3):
            patch_row(qkv_w, 768 * part + 255, spread_row(extra_ref, 12 + 6 * part, 6))
            patch_row(qkv_w, 768 * part + 512, spread_row(extra_ref, 30 + 6 * part, 6))
        vec_ref[...] = jnp.zeros_like(vec_ref)
        for row, first in enumerate((0, 6, 60, EXTRA + 0, EXTRA + 6)):
            vec_ref[row : row + 1, :] = spread_row(extra_ref, first, 6)
        bias_ref[...] = jnp.zeros_like(bias_ref)
        bias_ref[0:1, 0:768] = spread_row(extra_ref, 48, 6)
        bias_ref[0:1, 1536:2304] = spread_row(extra_ref, 54, 6)

    first_ref, qkv_ref, log_ref, att_ref, hid_ref, second_ref = refs
    x = x_ref[...].astype(F32)
    normed, _ = normed_of(x)
    first = (normed * vec_ref[0:1, :] + vec_ref[1:2, :]).astype(BF)
    first_ref[...] = first
    for part in range(3):
        cols = slice(768 * part, 768 * part + 768)
        qkv_ref[:, cols] = (dot(first, qkv_w[cols, :]) + bias_ref[0:1, cols]).astype(BF)
    masks = half_masks()
    real = lax.broadcasted_iota(jnp.int32, (2, T, T), 1) < seq
    for pair in range(HEADS // 2):
        at = LANES * pair
        for image in range(x_ref.shape[0] // T):
            own = slice(T * image, T * image + T)
            q = qkv_ref[own, at : at + LANES] * jnp.asarray(0.125, BF)
            k = two_heads(qkv_ref[own, 768 + at : 768 + at + LANES], masks)
            v = two_heads(qkv_ref[own, 1536 + at : 1536 + at + LANES], masks)
            scores = dot_nt(k, q).reshape(2, T, T)
            scores = jnp.where(real, scores, -1e30)
            top = jnp.max(scores, axis=1, keepdims=True)
            weight = jnp.exp(scores - top)
            total = jnp.sum(weight, axis=1, keepdims=True)
            logs = top + jnp.log(total)
            log_ref[image, 2 * pair : 2 * pair + 1, :] = logs[0]
            log_ref[image, 2 * pair + 1 : 2 * pair + 2, :] = logs[1]
            probs = (weight * (1.0 / total)).astype(BF).reshape(2 * T, T)
            att_ref[own, at : at + LANES] = dot_tn(probs, v).astype(BF)
    hidden = x + dot(att_ref[...], proj_w[...]) + vec_ref[2:3, :]
    hid_ref[...] = hidden
    normed, _ = normed_of(hidden)
    second_ref[...] = (normed * vec_ref[3:4, :] + vec_ref[4:5, :]).astype(BF)


FORWARD_IMAGES = 2


def call_attn_forward(seq, x, weights, boxes):
    shard, extra = weights
    rows = x.shape[0]
    images = rows // T
    step = FORWARD_IMAGES if images % FORWARD_IMAGES == 0 else 1
    tall = step * T
    made = [sds((2304, D), BF), sds((D, D), BF), sds((8, D), F32), sds((8, 2304), F32)]
    return pl.pallas_call(
        functools.partial(attn_forward, seq),
        grid=(images // step,),
        in_specs=[rows_of(tall, D), SMEM, whole(extra)] + [ANYWHERE] * 4,
        out_specs=[
            rows_of(tall, D),
            rows_of(tall, 2304),
            pl.BlockSpec((step, HEADS, T), lambda i: (i, 0, 0)),
            rows_of(tall, D),
            rows_of(tall, D),
            rows_of(tall, D),
        ]
        + [pl.BlockSpec(shape.shape, lambda i: (0, 0)) for shape in made],
        out_shape=[
            sds((rows, D), BF),
            sds((rows, 2304), BF),
            sds((images, HEADS, T), F32),
            sds((rows, D), BF),
            sds((rows, D), F32),
            sds((rows, D), BF),
        ]
        + made,
        scratch_shapes=[pltpu.SemaphoreType.DMA((4, 3))],
        compiler_params=params(),
    )(x, shard, extra, *boxes)


def hand_out(index, box, outs, sems):
    copies = [pltpu.make_async_copy(box.at[k], out, sems.at[k]) for k, out in enumerate(outs)]
    for k, copy in enumerate(copies):

        @pl.when(index == k)
        def _(copy=copy):
            copy.start()

    @pl.when(index == len(outs) - 1)
    def _():
        for copy in copies:
            copy.wait()


HALF = FF // 2
ROW_STEPS = 4


def feed(seq, part, tall, shard_ref, extra_ref, a0, a1, a2, a3, second_ref, cot_ref, result_ref, *refs):
    last = part == 1
    if last:
        before_ref, out_ref, gs_ref, *refs = refs
    else:
        out_ref, gs_ref, cot_sum, *refs = refs
    sum_ref, edge_ref, *outs, up_w, down_w, bias, second_all, cot_all, act_all, pre_all, box, sems, box_sems = refs
    step = pl.program_id(0)
    shard = shard_ref[0]

    @pl.when(step == 0)
    def _():
        load_feed(shard, (a0, a1, a2, a3), up_w, down_w, sems)
        for h in range(2):
            patch_row(up_w, 768 * h + 383, spread_row(extra_ref, EXTRA + 12 + 12 * h + 6 * part, 6))
            bias[0:1, 768 * h : 768 * h + 768] = spread_row(extra_ref, EXTRA + 36 + 12 * h + 6 * part, 6)
        if last:
            patch_row(down_w, 767, spread_row(extra_ref, EXTRA + 60, 6))
        sum_ref[...] = jnp.zeros_like(sum_ref)
        edge_ref[...] = jnp.zeros_like(edge_ref)
        if not last:
            cot_sum[...] = jnp.zeros_like(cot_sum)

    @pl.when(step < ROW_STEPS)
    def _():
        at = pl.ds(pl.multiple_of(step * tall, 16), tall)
        second = second_ref[...]
        cot = cot_ref[...]
        second_all[at, :] = second
        cot_all[at, :] = cot
        if last:
            result = result_ref[...]
            grad_second = before_ref[...]
        else:
            result = result_ref[...] + spread_row(extra_ref, EXTRA + 66, 6)
            grad_second = jnp.zeros_like(result)
            cot_sum[0:1, :] += jnp.sum(cot.astype(F32), axis=0, keepdims=True)
        for h in range(2):
            cols = slice(768 * h, 768 * h + 768)
            pre = dot(second, up_w[cols, :]) + bias[0:1, cols]
            grad_act = dot_nt(cot, down_w[cols, :])
            half = 0.5 * (1.0 + lax.erf(pre * root_half))
            act = (pre * half).astype(BF)
            grad_pre = grad_act * (half + pre * jnp.exp(-0.5 * pre * pre) * inv_root_tau)
            low = grad_pre.astype(BF)
            act_all[at, cols] = act
            pre_all[at, cols] = low
            sum_ref[0:1, cols] += jnp.sum(grad_pre, axis=0, keepdims=True)
            result = result + dot(act, down_w[cols, :])
            grad_second = grad_second + dot_nt(low, up_w[cols, :])
        if last:
            for image in range(tall // T):
                out_ref[image] = result[T * image : T * image + seq].astype(BF)
        else:
            out_ref[...] = result
        gs_ref[...] = grad_second

    index = step - ROW_STEPS
    side = jnp.bitwise_xor(shard // 2, 1 - index % 2)
    core = jnp.where(index >= 2, shard % 2, 1 - shard % 2)

    @pl.when((index >= 0) & (side == 0))
    def _():
        left = second_all[:, pl.ds(pl.multiple_of(384 * core, 128), 384)]
        for h in range(2):
            grad = dot_tn(left, pre_all[:, 768 * h : 768 * h + 768])
            box[index, 384 * h : 384 * h + 384, :] = grad.astype(BF)

            @pl.when(core == 0)
            def _(grad=grad, h=h):
                edge_ref[0:1, 768 * h : 768 * h + 768] = grad[383:384]

    @pl.when((index >= 0) & (side == 1))
    def _():
        left = act_all[:, pl.ds(pl.multiple_of(768 * core, 128), 768)]
        grad = dot_tn(left, cot_all[...])
        box[index] = grad.astype(BF)

        @pl.when(core == 0)
        def _():
            edge_ref[1:2, 0:768] = grad[767:768]

    hand_out(index, box, outs, box_sems)


def call_feed(seq, part, shard, extra, boxes, second, cot, result, before=None):
    rows = second.shape[0]
    images = rows // T
    tall = rows // ROW_STEPS
    last = part == 1
    row = lambda i: jnp.minimum(i, ROW_STEPS - 1)
    block = pl.BlockSpec((tall, D), lambda i: (row(i), 0))
    out = pl.BlockSpec((tall // T, seq, D), lambda i: (row(i), 0, 0)) if last else block
    small = lambda width: pl.BlockSpec((8, width), lambda i: (0, 0))
    return pl.pallas_call(
        functools.partial(feed, seq, part, tall),
        grid=(ROW_STEPS + 4,),
        in_specs=[SMEM, whole(extra)] + [ANYWHERE] * 4 + [block] * (4 if last else 3),
        out_specs=[out, block] + ([] if last else [small(D)]) + [small(HALF), small(HALF)] + [ANYWHERE] * 4,
        out_shape=[sds((images, seq, D), BF) if last else sds((rows, D), F32), sds((rows, D), F32)]
        + ([] if last else [sds((8, D), F32)])
        + [sds((8, HALF), F32), sds((8, HALF), F32)] + [sds((D, D), BF)] * 4,
        scratch_shapes=[
            pltpu.VMEM((HALF, D), BF),
            pltpu.VMEM((HALF, D), BF),
            pltpu.VMEM((8, HALF), F32),
            pltpu.VMEM((rows, D), BF),
            pltpu.VMEM((rows, D), BF),
            pltpu.VMEM((rows, HALF), BF),
            pltpu.VMEM((rows, HALF), BF),
            pltpu.VMEM((4, D, D), BF),
            pltpu.SemaphoreType.DMA((4, 2)),
            pltpu.SemaphoreType.DMA((4,)),
        ],
        compiler_params=params(60),
    )(shard, extra, *boxes, second, cot, result, *([before] if last else []))


WIDE = 384


def attn_backward(seq, group, base, count, last, shard_ref, log_ref, qkv_ref, first_ref, att_ref, *refs):
    step = pl.program_id(0)
    shard = shard_ref[0]
    if group == 0:
        gs_ref, hid_ref, cot_ref, vec_ref, proj_w, *refs = refs
    else:
        low_ref, ga_ref, *refs = refs
    if last:
        if group == 0:
            head_before, sum_before, first_any, att_any, low_any, grad_any, _, _, *refs = refs
        else:
            head_before, first_any, att_any, low_any, grad_any, *refs = refs
    grad_ref, head_sum, *refs = refs
    if group == 0:
        low_ref, ga_ref, gh_ref, sum_ref, *refs = refs
    if last:
        edge_ref, *outs, grad_all, first_all, low_all, att_all, box, box_sems, load_sems = refs
        done = pl.ds(0, base * T)
        loads = [
            pltpu.make_async_copy(grad_any.at[done], grad_all.at[done], load_sems.at[0]),
            pltpu.make_async_copy(first_any.at[done], first_all.at[done], load_sems.at[1]),
            pltpu.make_async_copy(low_any.at[done], low_all.at[done], load_sems.at[2]),
            pltpu.make_async_copy(
                att_any.at[done, pl.ds(WIDE * group, WIDE)], att_all.at[done], load_sems.at[3]
            ),
        ]

    @pl.when(step == 0)
    def _():
        if last:
            for load in loads:
                load.start()
            edge_ref[...] = jnp.zeros_like(edge_ref)
            head_sum[...] = head_before[...]
        else:
            head_sum[...] = jnp.zeros_like(head_sum)
        if group == 0:
            sum_ref[...] = sum_before[...] if last else jnp.zeros_like(sum_ref)

    @pl.when(step < count)
    def _():
        at_rows = pl.ds(pl.multiple_of((step + base) * T, 16), T)
        if last:
            first_all[at_rows, :] = first_ref[...]
            att_all[at_rows, :] = att_ref[...]
        if group == 0:
            gs = gs_ref[...]
            normed, spread = normed_of(hid_ref[...])
            gn = gs * vec_ref[3:4, :]
            gh = cot_ref[...].astype(F32) + spread * (
                gn - jnp.mean(gn, axis=-1, keepdims=True) - normed * jnp.mean(gn * normed, axis=-1, keepdims=True)
            )
            sum_ref[0:1, :] += jnp.sum(gs * normed, axis=0, keepdims=True)
            sum_ref[1:2, :] += jnp.sum(gs, axis=0, keepdims=True)
            sum_ref[2:3, :] += jnp.sum(gh, axis=0, keepdims=True)
            gh_ref[...] = gh
            gh_low = gh.astype(BF)
            low_ref[...] = gh_low
            ga_ref[...] = dot_nt(gh_low, proj_w[...]).astype(BF)
        if last:
            low_all[at_rows, :] = low_ref[...]
        low = lax.broadcasted_iota(jnp.int32, (T, LANES), 1) < 64
        real = lax.broadcasted_iota(jnp.int32, (2, T, T), 1) < seq
        eighth = jnp.asarray(0.125, BF)
        masks = half_masks()
        for pair in range(3):
            at = LANES * pair
            full = WIDE * group + at
            head = 6 * group + 2 * pair
            q = qkv_ref[:, full : full + LANES] * eighth
            k = two_heads(qkv_ref[:, 768 + full : 768 + full + LANES], masks)
            v = two_heads(qkv_ref[:, 1536 + full : 1536 + full + LANES], masks)
            grad_out = ga_ref[:, at : at + LANES]
            scores = dot_nt(k, q).reshape(2, T, T)
            logs = jnp.concatenate([log_ref[0:1, head : head + 1, :], log_ref[0:1, head + 1 : head + 2, :]], axis=0)
            probs = jnp.where(real, jnp.exp(scores - logs), 0.0)
            grad_v = dot(probs.astype(BF).reshape(2 * T, T), grad_out)
            grad_probs = dot_nt(v, grad_out).reshape(2, T, T)
            delta = jnp.sum(probs * grad_probs, axis=1, keepdims=True)
            grad_scores = (probs * (grad_probs - delta)).astype(BF).reshape(2 * T, T)
            grad_k = dot(grad_scores, q)
            grads = (
                dot_tn(grad_scores, k * eighth),
                jnp.where(low, grad_k[:T], grad_k[T:]),
                jnp.where(low, grad_v[:T], grad_v[T:]),
            )
            for part, grad in enumerate(grads):
                if part != 1:
                    row = part // 2
                    head_sum[row : row + 1, at : at + LANES] += jnp.sum(grad, axis=0, keepdims=True)
                cols = slice(WIDE * part + at, WIDE * part + at + LANES)
                grad = grad.astype(BF)
                grad_ref[:, cols] = grad
                if last:
                    grad_all[at_rows, cols] = grad

    if not last:
        return

    @pl.when(step == count)
    def _():
        for load in loads:
            load.wait()

    index = step - count
    side = jnp.bitwise_xor(shard // 2, 1 - index % 2)
    core = jnp.where(index >= 2, shard % 2, 1 - shard % 2)
    share = 2 * side + core

    @pl.when((index >= 0) & (share == 3))
    def _():
        box[index] = dot_tn(att_all[...], low_all[...]).astype(BF)

    @pl.when((index >= 0) & (share != 3))
    def _():
        grad = dot_tn(first_all[:, pl.ds(pl.multiple_of(256 * share, 256), 256)], grad_all[...])
        for part in range(3):
            cols = slice(WIDE * part, WIDE * part + WIDE)
            for u in range(2):
                box[index, 128 * part : 128 * part + 128, WIDE * u : WIDE * u + WIDE] = grad[
                    128 * u : 128 * u + 128, cols
                ].astype(BF)

        @pl.when(share == 0)
        def _():
            edge_ref[0:1, :] = grad[255:256]

        @pl.when(share == 2)
        def _():
            edge_ref[1:2, :] = grad[0:1]

    hand_out(index, box, outs, box_sems)


def call_attn_backward(seq, group, base, count, shard, log_total, qkv, first, attended, *more, before=()):
    rows = first.shape[0]
    last = len(before) > 0
    row = lambda i: jnp.minimum(i, count - 1) + base
    block = lambda width, col=0: pl.BlockSpec((T, width), lambda i: (row(i), col))
    small = lambda width: pl.BlockSpec((8, width), lambda i: (0, 0))
    in_specs = [SMEM, pl.BlockSpec((1, HEADS, T), lambda i: (row(i), 0, 0)), block(2304), block(D), block(WIDE, group)]
    out_specs = [block(3 * WIDE), small(WIDE)]
    out_shape = [sds((rows, 3 * WIDE), BF), sds((8, WIDE), F32)]
    if group == 0:
        in_specs += [block(D)] * 3 + [whole(more[3]), whole(more[4])]
        out_specs += [block(D), block(D), block(D), small(D)]
        out_shape += [sds((rows, D), BF), sds((rows, D), BF), sds((rows, D), F32), sds((8, D), F32)]
    else:
        in_specs += [block(D), block(WIDE, 1)]
    aliases, scratch, extra = {}, [], []
    if last:
        at = len(in_specs)
        if group == 0:
            grad, head, low, ga, gh, total = before
            extra = [head, total, first, attended, low, grad, ga, gh]
            in_specs += [whole(head), whole(total)] + [ANYWHERE] * 6
            aliases = {at + 4: 2, at + 5: 0, at + 6: 3, at + 7: 4}
        else:
            grad, head = before
            extra = [head, first, attended, more[0], grad]
            in_specs += [whole(head)] + [ANYWHERE] * 4
            aliases = {at + 4: 0}
        out_specs += [small(3 * WIDE)] + [ANYWHERE] * 4
        out_shape += [sds((8, 3 * WIDE), F32)] + [sds((WIDE, D), BF)] * 4
        scratch = [
            pltpu.VMEM((rows, 3 * WIDE), BF),
            pltpu.VMEM((rows, D), BF),
            pltpu.VMEM((rows, D), BF),
            pltpu.VMEM((rows, WIDE), BF),
            pltpu.VMEM((4, WIDE, D), BF),
            pltpu.SemaphoreType.DMA((4,)),
            pltpu.SemaphoreType.DMA((4,)),
        ]
    return pl.pallas_call(
        functools.partial(attn_backward, seq, group, base, count, last),
        grid=(count + 4 if last else count,),
        in_specs=in_specs,
        out_specs=out_specs,
        out_shape=out_shape,
        input_output_aliases=aliases,
        scratch_shapes=scratch,
        compiler_params=params(),
    )(shard, log_total, qkv, first, attended, *more, *extra)


def input_backward(seq, grad0, grad1, gh_ref, x_ref, vec_ref, qkv_w, out_ref, sum_ref):
    @pl.when(pl.program_id(0) == 0)
    def _():
        sum_ref[...] = jnp.zeros_like(sum_ref)

    grad_first = None
    for part in range(3):
        cols = slice(WIDE * part, WIDE * part + WIDE)
        both = jnp.concatenate([grad0[:, cols], grad1[:, cols]], axis=1)
        term = dot_nt(both, qkv_w[768 * part : 768 * part + 768, :])
        grad_first = term if part == 0 else grad_first + term
    normed, spread = normed_of(x_ref[...].astype(F32))
    gn = grad_first * vec_ref[0:1, :]
    grad = gh_ref[...] + spread * (
        gn - jnp.mean(gn, axis=-1, keepdims=True) - normed * jnp.mean(gn * normed, axis=-1, keepdims=True)
    )
    sum_ref[0:1, :] += jnp.sum(grad_first * normed, axis=0, keepdims=True)
    sum_ref[1:2, :] += jnp.sum(grad_first, axis=0, keepdims=True)
    for image in range(grad.shape[0] // T):
        out_ref[image] = grad[T * image : T * image + seq].astype(BF)


def call_input_backward(seq, grads, gh, x, vec, qkv_w):
    rows = gh.shape[0]
    images = rows // T
    step = 2 if images % 2 == 0 else 1
    tall = step * T
    return pl.pallas_call(
        functools.partial(input_backward, seq),
        grid=(images // step,),
        in_specs=[rows_of(tall, 3 * WIDE)] * 2 + [rows_of(tall, D), rows_of(tall, D), whole(vec), whole(qkv_w)],
        out_specs=[pl.BlockSpec((step, seq, D), lambda i: (i, 0, 0)), pl.BlockSpec((8, D), lambda i: (0, 0))],
        out_shape=[sds((images, seq, D), BF), sds((8, D), F32)],
        compiler_params=params(),
    )(*grads, gh, x, vec, qkv_w)


def putter(out_ref):
    out_ref[...] = jnp.zeros_like(out_ref)

    def put(first, ref, row, col, width):
        for k in range(width // LANES):
            at = col + LANES * k
            out_ref[first + k : first + k + 1, :] = ref[row : row + 1, at : at + LANES]

    return put


def pack(last_sum, back_sum, head0, head1, edge0, edge1, pre0, pre1, up0, up1, cot_sum, out_ref):
    put = putter(out_ref)
    put(0, last_sum, 0, 0, D)
    put(6, last_sum, 1, 0, D)
    for group, (head, edge) in enumerate(((head0, edge0), (head1, edge1))):
        for part in range(3):
            put(12 + 6 * part + 3 * group, edge, 0, WIDE * part, WIDE)
            put(30 + 6 * part + 3 * group, edge, 1, WIDE * part, WIDE)
        put(48 + 3 * group, head, 0, 0, WIDE)
        put(54 + 3 * group, head, 1, 0, WIDE)
    put(60, back_sum, 2, 0, D)
    put(EXTRA, back_sum, 0, 0, D)
    put(EXTRA + 6, back_sum, 1, 0, D)
    for j, (pre, up) in enumerate(((pre0, up0), (pre1, up1))):
        for h in range(2):
            put(EXTRA + 12 + 12 * h + 6 * j, up, 0, 768 * h, D)
            put(EXTRA + 36 + 12 * h + 6 * j, pre, 0, 768 * h, D)
    put(EXTRA + 60, up1, 1, 0, D)
    put(EXTRA + 66, cot_sum, 0, 0, D)


def call_pack(*arrays):
    return pl.pallas_call(
        pack,
        in_specs=[pl.BlockSpec(memory_space=pltpu.VMEM)] * len(arrays),
        out_specs=pl.BlockSpec(memory_space=pltpu.VMEM),
        out_shape=sds((2 * EXTRA, LANES), F32),
        compiler_params=params(),
    )(*arrays)


def adam_kernel(block, share_size, scale, boxes, shard_ref, power_ref, extra_ref, *refs):
    box_refs = refs[:boxes]
    flat_ref, mom_ref, grad_ref, change_ref, new_ref, held = refs[boxes:]
    step = pl.program_id(0)

    @pl.when(step == 0)
    def _():
        for share in range(4):

            @pl.when(shard_ref[0] == share)
            def _(share=share):
                for box, groups, box_row, col, cols, flat_row, stride in block.grad_parts(share):
                    base = MARGIN + block.start[share] + flat_row

                    def body(group, carry, box=box, box_row=box_row, col=col, cols=cols, base=base, stride=stride):
                        row = pl.multiple_of(box_row + 16 * group, 16)
                        for j in range(cols):
                            at = LANES * (col + j)
                            both = box_refs[box][pl.ds(row, 16), at : at + LANES].astype(F32)
                            to = base + 16 * stride * group + j
                            held[pl.ds(to, 8, stride=stride), :] = both[0:8]
                            held[pl.ds(to + 8 * stride, 8, stride=stride), :] = both[8:16]
                        return carry

                    lax.fori_loop(0, groups, body, 0, unroll=8)
                for source, row, length in block.put[share]:
                    held[MARGIN + row : MARGIN + row + length, :] = extra_ref[block.base + source : block.base + source + length, :]

    start = pl.multiple_of(MARGIN + CHUNK * step, 8)
    shard = shard_ref[0]
    low = lax.broadcasted_iota(jnp.int32, (CHUNK, LANES), 1) < 64
    here = held[pl.ds(start, CHUNK), :]
    after = held[pl.ds(start + 1, CHUNK), :]
    shifted = jnp.where(low, pltpu.roll(here, 64, 1), pltpu.roll(after, 64, 1))
    grad = jnp.where(shard % 2 == 1, shifted, here) * scale
    position = (
        shard * share_size
        + step * (CHUNK * LANES)
        + lax.broadcasted_iota(jnp.int32, (CHUNK, LANES), 0) * LANES
        + lax.broadcasted_iota(jnp.int32, (CHUNK, LANES), 1)
    )
    matrix = jnp.zeros((CHUNK, LANES), jnp.bool_)
    for first, end in block.matrices:
        matrix = matrix | ((position >= first) & (position < end))
    size = CHUNK * LANES
    p = flat_ref[...].reshape(CHUNK, LANES)
    m = beta_one * mom_ref[0, :].reshape(CHUNK, LANES) + (1.0 - beta_one) * grad
    s = beta_two * mom_ref[1, :].reshape(CHUNK, LANES) + (1.0 - beta_two) * grad * grad
    ratio = (m * power_ref[0]) / (jnp.sqrt(s * power_ref[1]) + adam_eps)
    change = jnp.where(matrix, rate_matrix, rate_vector) * (ratio + jnp.where(matrix, decay_matrix, 0.0) * p)
    grad_ref[...] = grad.reshape(size)
    change_ref[...] = change.reshape(size)
    new_ref[0, :] = m.reshape(size)
    new_ref[1, :] = s.reshape(size)


def adam(block, shard, powers, extra, boxes, flat, moments, scale):
    count = flat.shape[0]
    steps = -(-count // (CHUNK * LANES))
    line = pl.BlockSpec((CHUNK * LANES,), lambda i: (i,))
    two = pl.BlockSpec((2, CHUNK * LANES), lambda i: (0, i))
    return pl.pallas_call(
        functools.partial(adam_kernel, block, count, scale, len(boxes)),
        grid=(steps,),
        in_specs=[SMEM, SMEM, whole(extra)] + [whole(box) for box in boxes] + [line, two],
        out_specs=[line, line, two],
        out_shape=[sds((count,), F32), sds((count,), F32), sds((2, count), F32)],
        scratch_shapes=[pltpu.VMEM((MARGIN + CHUNK * steps + MARGIN, LANES), F32)],
        compiler_params=params(),
    )(shard, powers, extra, *boxes, flat, moments)


def swap(value, axis, bit):
    pairs = [(i, i ^ bit) for i in range(lax.axis_size(axis))]
    return lax.ppermute(value, axis, pairs)


def turn(value, axis, unit, distance):
    size = lax.axis_size(axis)
    return lax.ppermute(value, axis, [(i, (i + unit * distance) % size) for i in range(size)])


def pick(array, index, axis=0):
    return lax.dynamic_index_in_dim(array, index, axis, keepdims=False)


class Line:
    def __init__(self):
        self.last = None

    def __call__(self, step, *args):
        if self.last is not None:
            flat, tree = jax.tree.flatten(args)
            flat = lax.optimization_barrier((self.last, *flat))[1:]
            args = jax.tree.unflatten(tree, flat)
        out = step(*args)
        self.last = min(jax.tree.leaves(out), key=lambda leaf: leaf.size)
        return out


def pause_kernel(in_ref, out_ref):
    out_ref[...] = in_ref[...]


def pause(line, value):
    return line(
        pl.pallas_call(
            pause_kernel,
            out_shape=sds(value.shape, value.dtype),
            cost_estimate=pl.CostEstimate(flops=10**11, bytes_accessed=10**8, transcendentals=0),
        ),
        value,
    )


class Sum:
    def __init__(self, line, across, same, mine_across, mine):
        self.line, self.mine_across, self.mine = line, mine_across, mine
        self.rows = mine.shape[0]
        rep = lax.axis_index("rep")
        self.near, self.far = rep % 2, rep // 2
        self.count = lax.axis_size("rep") // 2
        self.came_across, self.here = swap(across, "shard", 1), swap(same, "shard", 1)

    def side(self):
        add = lambda a, b: (a.astype(F32) + b.astype(F32)).astype(BF)
        send = self.line(add, self.mine_across, self.came_across)
        self.came = swap(send, "shard", 2)
        self.here = self.line(lambda a: a, self.here)

    def close(self):
        def step(mine, here, came):
            total = mine.astype(F32) + here.astype(F32) + came.astype(F32)
            halves = total.reshape(2, self.rows // 2, D)
            return pick(halves, 1 - self.near).astype(BF), pick(halves, self.near)

        send, self.half = self.line(step, self.mine, self.here, self.came)
        self.came = swap(send, "rep", 1)

    def level(self, bit):
        if bit == 2:
            self.part = self.line(lambda a, b: (a + b.astype(F32)).astype(BF), self.half, self.came)
        else:
            self.part = self.line(lambda a, b: (a.astype(F32) + b.astype(F32)).astype(BF), self.part, self.came)
        self.came = swap(self.part, "rep", bit)

    def back_level(self):
        self.half = self.line(lambda a, b: (a.astype(F32) + b.astype(F32)).astype(BF), self.part, self.came)
        self.came = swap(self.half, "rep", 1)

    def along(self):
        def step(half, came):
            parts = (half + came.astype(F32)).reshape(self.count, self.rows // 2 // self.count, D)
            sends = [pick(parts, (self.far + d) % self.count).astype(BF) for d in range(1, self.count)]
            return sends, pick(parts, self.far)

        sends, self.part = self.line(step, self.half, self.came)
        self.came = [turn(send, "rep", 2, d + 1) for d, send in enumerate(sends)]

    def back_along(self):
        def step(part, came):
            for value in came:
                part = part + value.astype(F32)
            return part.astype(BF)

        self.part = self.line(step, self.part, self.came)
        self.came = [turn(self.part, "rep", 2, d) for d in range(1, self.count)]

    def back_close(self):
        def step(part, came):
            full = jnp.zeros((self.count,) + part.shape, BF)
            for d, value in enumerate([part] + came):
                full = lax.dynamic_update_slice_in_dim(full, value[None], (self.far + self.count - d) % self.count, 0)
            return full.reshape(self.rows // 2, D)

        self.half = self.line(step, self.part, self.came)
        self.came = swap(self.half, "rep", 1)

    def end(self):
        def step(half, came):
            first = self.near == 0
            return jnp.concatenate([jnp.where(first, half, came), jnp.where(first, came, half)], axis=0)

        return self.line(step, self.half, self.came)


class SumAll:
    def __init__(self, line, value):
        self.line, self.value = line, value
        self.hops = [("shard", 1)]
        bit = 2
        while bit < lax.axis_size("rep"):
            self.hops.append(("rep", bit))
            bit *= 2
        self.hops += [("shard", 2), ("rep", 1)]
        self.came = swap(value, *self.hops.pop(0))

    def hop(self):
        self.value = self.line(lambda a, b: a + b, self.value, self.came)
        if self.hops:
            self.came = swap(self.value, *self.hops.pop(0))
            return False
        return True


def body(layer_input, out_cotangent, attention_params, attention_moments, feedforward_params, feedforward_moments, step_count):
    images, seq, _ = layer_input.shape
    rows = images * T
    image_total = images * lax.axis_size("shard") * lax.axis_size("rep")
    scale = 1.0 / image_total
    shard = lax.axis_index("shard").astype(jnp.int32).reshape(1)
    time = step_count[0].astype(F32)
    powers = jnp.stack([1.0 / (1.0 - jnp.power(beta_one, time)), 1.0 / (1.0 - jnp.power(beta_two, time))])
    pad = ((0, 0), (0, T - seq), (0, 0))
    padded = lambda tokens: jnp.pad(tokens, pad).reshape(rows, D)
    line = Line()

    attn_box, attn_extra = line(functools.partial(prep, ATTN), attention_params, shard)
    attn_across = swap(attn_box, "shard", 2)
    attn_near = swap(attn_box, "shard", 1)
    box0, box1, feed_extra = line(functools.partial(prep, FEED), feedforward_params, shard)
    extra = line(lambda a, b: jnp.concatenate([a, b], axis=0), attn_extra, feed_extra)
    came = swap(extra, "shard", 1)
    x = line(padded, layer_input)
    extra = line(lambda a, b: a + b, extra, came)
    came = swap(extra, "shard", 2)
    cot = line(padded, out_cotangent)
    extra = line(lambda a, b: a + b, extra, came)
    near0, near1 = swap(box0, "shard", 1), swap(box1, "shard", 1)
    across, send0 = line(lambda a, b: lax.optimization_barrier((a, b)), attn_across, box0)
    attn_both = swap(across, "shard", 1)
    across0 = swap(send0, "shard", 2)
    boxes = (attn_box, attn_near, attn_across, attn_both)
    first, qkv, log_total, attended, hidden, second, qkv_w, proj_w, vec, bias = line(
        lambda x, w, b: call_attn_forward(seq, x, w, b), x, (shard, extra), boxes
    )
    across, send1, near0, near1 = line(lambda *a: lax.optimization_barrier(a), across0, box1, near0, near1)
    both0 = swap(across, "shard", 1)
    across1 = swap(send1, "shard", 2)
    boxes = (box0, near0, across0, both0)
    result, gs, cot_sum, pre0, up0, *grads = line(
        lambda *a: call_feed(seq, 0, *a), shard, extra, boxes, second, cot, hidden
    )
    both1 = swap(line(lambda a: a, across1), "shard", 1)
    feed0 = Sum(line, *grads)
    feed0.side()
    boxes = (box1, near1, across1, both1)
    layer_output, gs, pre1, up1, *grads = line(
        lambda *a: call_feed(seq, 1, *a), shard, extra, boxes, second, cot, result, gs
    )
    feed1 = Sum(line, *grads)
    feed0.close()
    feed1.side()
    half = images // 2
    common = (shard, log_total, qkv, first, attended)
    more = (gs, hidden, cot, vec, proj_w)
    before = line(lambda *a: call_attn_backward(seq, 0, 0, half, *a), *common, *more)
    feed0.along()
    grad0, head0, gh_low, ga, gh, back_sum, edge0, *grads = line(
        lambda b, *a: call_attn_backward(seq, 0, half, images - half, *a, before=b), tuple(before), *common, *more
    )
    attn0 = Sum(line, *grads)
    feed1.close()
    feed0.back_along()
    attn0.side()
    more = (gh_low, ga)
    before = line(lambda *a: call_attn_backward(seq, 1, 0, half, *a), *common, *more)
    feed0.back_close()
    feed1.along()
    grad1, head1, edge1, *grads = line(
        lambda b, *a: call_attn_backward(seq, 1, half, images - half, *a, before=b), tuple(before), *common, *more
    )
    attn1 = Sum(line, *grads)
    feed1.back_along()
    attn0.close()
    feed_box0 = feed0.end()
    head1 = pause(line, head1)
    attn1.side()
    input_grad, last_sum = line(lambda *a: call_input_backward(seq, *a), (grad0, grad1), gh, x, vec, qkv_w)
    sums = line(call_pack, last_sum, back_sum, head0, head1, edge0, edge1, pre0, pre1, up0, up1, cot_sum)
    bits = [2 << k for k in range((lax.axis_size("rep") // 2).bit_length() - 1)]
    sums = SumAll(line, sums)
    attn1.close()
    sums.hop()
    attn0.level(2)
    feed1.back_close()
    sums.hop()
    attn1.level(2)
    sums.hop()
    for bit in bits[1:]:
        attn0.level(bit)
    sums.hop()
    feed_box1 = feed1.end()
    for bit in bits[1:]:
        attn1.level(bit)
    while not sums.hop():
        pass
    feed_grad, feed_change, feed_new = line(
        lambda *a: adam(FEED, *a, scale), shard, powers, sums.value, [feed_box0, feed_box1], feedforward_params, feedforward_moments
    )
    attn0.back_level()
    attn1.back_level()
    layer_output, input_grad = line(lambda *a: a, layer_output, input_grad)
    attn_box0 = attn0.end()
    attn_grad, attn_change, attn_new = line(
        lambda *a: adam(ATTN, *a, scale), shard, powers, sums.value, [attn_box0, attn1.end()], attention_params, attention_moments
    )
    return (layer_output, input_grad, attn_grad, feed_grad, attn_change, attn_new, feed_change, feed_new)


def solution(mesh):
    tokens = P(("shard", "rep"), None, None)
    in_specs = (tokens, tokens, P("shard"), P(None, "shard"), P("shard"), P(None, "shard"), P())
    out_specs = (tokens, tokens, P("shard"), P("shard"), P("shard"), P(None, "shard"), P("shard"), P(None, "shard"))
    return jax.shard_map(body, mesh=mesh, in_specs=in_specs, out_specs=out_specs, check_vma=False)
```

```python
import functools

import jax
import jax.numpy as jnp
from jax import lax
from jax.experimental import pallas as pl
from jax.experimental.pallas import tpu as pltpu
from jax.sharding import PartitionSpec as P

D = 768
HEADS = 12
FF = 3072
T = 208

F32 = jnp.float32
BF = jnp.bfloat16

ln_eps = 1e-06
beta_one = 0.9
beta_two = 0.999
adam_eps = 1e-08
rate_matrix = 0.01
rate_vector = 0.1
decay_matrix = 0.05
root_half = 0.7071067811865476
inv_root_tau = 0.3989422804014327

MB = 1 << 20
LANES = 128
MARGIN = 8

ATTN_START = (12, 5, -3, 2)
FEED_START = (12, 2, 15, 5)


def attn_parts(share):
    if share < 3:
        return [(0, 16, 256 * part, 6 * part, 18) for part in range(3)]
    return [(0, 48, 0, 0, 6)]


def feed_parts(share):
    if share < 2:
        return [(j, 24, 384 * h, 12 * h + 6 * j, 24) for j in range(2) for h in range(2)]
    return [(j, 48, 0, 4608 * j, 6) for j in range(2)]


def attn_grad_parts(share):
    if share < 3:
        return [
            (g, 8, 128 * part, 3 * u, 3, 18 * 128 * u + 6 * part + 3 * g, 18)
            for g in range(2)
            for part in range(3)
            for u in range(2)
        ]
    return [(g, 24, 0, 0, 6, 6 * 384 * g, 6) for g in range(2)]


def feed_grad_parts(share):
    return [(box, groups, row, 0, 6, flat, stride) for box, groups, row, flat, stride in feed_parts(share)]


ATTN_EXTRA = (
    [(0, 0, 12), (12, 4602, 14)],
    [(25, 0, 5), (30, 4613, 3)],
    [(33, 0, 15), (48, 4605, 11)],
    [(58, 0, 2), (60, 4610, 6)],
)
FEED_EXTRA = (
    [(0, 0, 12), (12, 9204, 23)],
    [(34, 0, 2), (36, 9218, 9)],
    [(45, 0, 15), (60, 9225, 2)],
    [(61, 0, 5), (66, 9221, 6)],
)
ATTN_PUT = (
    [(0, 0, 12)],
    [(25, 0, 5), (30, 4613, 3)],
    [(48, 4605, 12)],
    [(58, 0, 2), (60, 4610, 6)],
)
FEED_PUT = (
    [(0, 0, 12)],
    [(34, 0, 2), (36, 9218, 9)],
    [(45, 0, 15)],
    [(61, 0, 5), (66, 9221, 6)],
)
EXTRA = 72


class Block:
    def __init__(self, base, boxes, start, parts, grad_parts, extra, put, matrices):
        self.base = base
        self.boxes, self.start, self.parts, self.grad_parts = boxes, start, parts, grad_parts
        self.extra, self.put = extra, put
        self.matrices = matrices


ATTN = Block(
    0, 1, ATTN_START, attn_parts, attn_grad_parts, ATTN_EXTRA, ATTN_PUT, ((1536, 1771008), (1772544, 2362368))
)
FEED = Block(
    EXTRA, 2, FEED_START, feed_parts, feed_grad_parts, FEED_EXTRA, FEED_PUT, ((1536, 2360832), (2363904, 4723200))
)


def params(limit=56):
    return pltpu.CompilerParams(vmem_limit_bytes=limit * MB)


def dot(a, b):
    return lax.dot_general(a, b, (((1,), (0,)), ((), ())), preferred_element_type=F32)


def dot_nt(a, b):
    return lax.dot_general(a, b, (((1,), (1,)), ((), ())), preferred_element_type=F32)


def dot_tn(a, b):
    return lax.dot_general(a, b, (((0,), (0,)), ((), ())), preferred_element_type=F32)


def normed_of(values):
    center = values - jnp.mean(values, axis=-1, keepdims=True)
    spread = lax.rsqrt(jnp.mean(center * center, axis=-1, keepdims=True) + ln_eps)
    return center * spread, spread


def whole(array):
    rank = len(array.shape)
    return pl.BlockSpec(array.shape, lambda *i: (0,) * rank, pipeline_mode=pl.Buffered(1))


def rows_of(count, width):
    return pl.BlockSpec((count, width), lambda i: (i, 0))


SMEM = pl.BlockSpec(memory_space=pltpu.SMEM)


def sds(shape, dtype):
    return jax.ShapeDtypeStruct(shape, dtype)


CHUNK = 2368


def prep_kernel(block, steps, shard_ref, flat_ref, *refs):
    *box_refs, extra_ref, held = refs
    step = pl.program_id(0)
    held[pl.ds(pl.multiple_of(MARGIN + CHUNK * step, 8), CHUNK), :] = flat_ref[...].reshape(CHUNK, LANES)

    @pl.when(step == steps - 1)
    def _():
        low = lax.broadcasted_iota(jnp.int32, (8, LANES), 1) < 64
        low_one = lax.broadcasted_iota(jnp.int32, (1, LANES), 1) < 64
        extra_ref[...] = jnp.zeros_like(extra_ref)
        for share in range(4):

            @pl.when(shard_ref[0] == share)
            def _(share=share):
                odd = share % 2 == 1

                def tile(first, stride):
                    here = held[pl.ds(first, 8, stride=stride), :]
                    if not odd:
                        return here
                    ahead = held[pl.ds(first - 1, 8, stride=stride), :]
                    return jnp.where(low, pltpu.roll(ahead, 64, 1), pltpu.roll(here, 64, 1))

                for box, groups, box_row, flat_row, stride in block.parts(share):
                    base = MARGIN + block.start[share] + flat_row

                    def body(group, carry, box=box, base=base, box_row=box_row, stride=stride):
                        for j in range(6):
                            first = base + 16 * stride * group + j
                            both = jnp.concatenate([tile(first, stride), tile(first + 8 * stride, stride)], axis=0)
                            at = pl.multiple_of(box_row + 16 * group, 16)
                            box_refs[box][pl.ds(at, 16), LANES * j : LANES * j + LANES] = both.astype(BF)
                        return carry

                    lax.fori_loop(0, groups, body, 0, unroll=8)
                count = flat_rows(block, share)
                for to, row, length in block.extra[share]:
                    for k in range(length):
                        at = MARGIN + row + k
                        value = held[at : at + 1, :]
                        if odd:
                            ahead = held[at - 1 : at, :]
                            value = jnp.where(low_one, pltpu.roll(ahead, 64, 1), pltpu.roll(value, 64, 1))
                            if row + k == 0:
                                value = jnp.where(low_one, 0.0, value)
                        elif row + k == count:
                            value = jnp.where(low_one, value, 0.0)
                        extra_ref[to + k : to + k + 1, :] = value.astype(BF).astype(F32)


def flat_rows(block, share):
    return 4615 if block is ATTN else 9226


def prep(block, flat, shard):
    steps = -(-flat.shape[0] // (CHUNK * LANES))
    return pl.pallas_call(
        functools.partial(prep_kernel, block, steps),
        grid=(steps,),
        in_specs=[SMEM, pl.BlockSpec((CHUNK * LANES,), lambda i: (i,))],
        out_specs=[pl.BlockSpec((D, D), lambda i: (0, 0))] * block.boxes
        + [pl.BlockSpec((EXTRA, LANES), lambda i: (0, 0))],
        out_shape=[sds((D, D), BF)] * block.boxes + [sds((EXTRA, LANES), F32)],
        scratch_shapes=[pltpu.VMEM((MARGIN + CHUNK * steps + MARGIN, LANES), F32)],
        compiler_params=params(),
    )(shard, flat)


def spread_row(extra_ref, first, count):
    return jnp.concatenate([extra_ref[first + k : first + k + 1, :] for k in range(count)], axis=1)


def patch_row(ref, row, values):
    at = row // 16 * 16
    rows = lax.broadcasted_iota(jnp.int32, (16, values.shape[1]), 0)
    old = ref[at : at + 16, :].astype(F32)
    ref[at : at + 16, :] = jnp.where(rows == row - at, values, old).astype(BF)


def load_attn(shard, boxes, qkv_ref, proj_ref, sems):
    for wait in (False, True):
        for k, box in enumerate(boxes):
            share = jnp.bitwise_xor(shard, k)

            @pl.when(share == 3)
            def _(box=box, k=k):
                copy = pltpu.make_async_copy(box, proj_ref, sems.at[k, 0])
                copy.wait() if wait else copy.start()

            @pl.when(share != 3)
            def _(box=box, k=k, share=share):
                for part in range(3):
                    copy = pltpu.make_async_copy(
                        box.at[pl.ds(256 * part, 256), :],
                        qkv_ref.at[pl.ds(pl.multiple_of(768 * part + 256 * share, 256), 256), :],
                        sems.at[k, part],
                    )
                    copy.wait() if wait else copy.start()


def load_feed(shard, boxes, up_ref, down_ref, sems):
    for wait in (False, True):
        for k, box in enumerate(boxes):
            share = jnp.bitwise_xor(shard, k)

            @pl.when(share >= 2)
            def _(box=box, k=k, share=share):
                at = pl.multiple_of(768 * (share - 2), 256)
                copy = pltpu.make_async_copy(box, down_ref.at[pl.ds(at, 768), :], sems.at[k, 0])
                copy.wait() if wait else copy.start()

            @pl.when(share < 2)
            def _(box=box, k=k, share=share):
                for h in range(2):
                    copy = pltpu.make_async_copy(
                        box.at[pl.ds(384 * h, 384), :],
                        up_ref.at[pl.ds(pl.multiple_of(768 * h + 384 * share, 128), 384), :],
                        sems.at[k, h],
                    )
                    copy.wait() if wait else copy.start()


ANYWHERE = pl.BlockSpec(memory_space=pl.ANY)


def half_masks():
    lane = lax.broadcasted_iota(jnp.int32, (1, LANES), 1)
    return (lane < 64).astype(F32).astype(BF), (lane >= 64).astype(F32).astype(BF)


def two_heads(pair, masks):
    return jnp.concatenate([pair * masks[0], pair * masks[1]], axis=0)


def attn_forward(seq, x_ref, shard_ref, extra_ref, a0, a1, a2, a3, *refs):
    *refs, qkv_w, proj_w, vec_ref, bias_ref, sems = refs

    @pl.when(pl.program_id(0) == 0)
    def _():
        load_attn(shard_ref[0], (a0, a1, a2, a3), qkv_w, proj_w, sems)
        for part in range(3):
            patch_row(qkv_w, 768 * part + 255, spread_row(extra_ref, 12 + 6 * part, 6))
            patch_row(qkv_w, 768 * part + 512, spread_row(extra_ref, 30 + 6 * part, 6))
        vec_ref[...] = jnp.zeros_like(vec_ref)
        for row, first in enumerate((0, 6, 60, EXTRA + 0, EXTRA + 6)):
            vec_ref[row : row + 1, :] = spread_row(extra_ref, first, 6)
        bias_ref[...] = jnp.zeros_like(bias_ref)
        bias_ref[0:1, 0:768] = spread_row(extra_ref, 48, 6)
        bias_ref[0:1, 1536:2304] = spread_row(extra_ref, 54, 6)

    first_ref, qkv_ref, log_ref, att_ref, hid_ref, second_ref = refs
    x = x_ref[...].astype(F32)
    normed, _ = normed_of(x)
    first = (normed * vec_ref[0:1, :] + vec_ref[1:2, :]).astype(BF)
    first_ref[...] = first
    for part in range(3):
        cols = slice(768 * part, 768 * part + 768)
        qkv_ref[:, cols] = (dot(first, qkv_w[cols, :]) + bias_ref[0:1, cols]).astype(BF)
    masks = half_masks()
    real = lax.broadcasted_iota(jnp.int32, (2, T, T), 1) < seq
    for pair in range(HEADS // 2):
        at = LANES * pair
        for image in range(x_ref.shape[0] // T):
            own = slice(T * image, T * image + T)
            q = qkv_ref[own, at : at + LANES] * jnp.asarray(0.125, BF)
            k = two_heads(qkv_ref[own, 768 + at : 768 + at + LANES], masks)
            v = two_heads(qkv_ref[own, 1536 + at : 1536 + at + LANES], masks)
            scores = dot_nt(k, q).reshape(2, T, T)
            scores = jnp.where(real, scores, -1e30)
            top = jnp.max(scores, axis=1, keepdims=True)
            weight = jnp.exp(scores - top)
            total = jnp.sum(weight, axis=1, keepdims=True)
            logs = top + jnp.log(total)
            log_ref[image, 2 * pair : 2 * pair + 1, :] = logs[0]
            log_ref[image, 2 * pair + 1 : 2 * pair + 2, :] = logs[1]
            probs = (weight * (1.0 / total)).astype(BF).reshape(2 * T, T)
            att_ref[own, at : at + LANES] = dot_tn(probs, v).astype(BF)
    hidden = x + dot(att_ref[...], proj_w[...]) + vec_ref[2:3, :]
    hid_ref[...] = hidden
    normed, _ = normed_of(hidden)
    second_ref[...] = (normed * vec_ref[3:4, :] + vec_ref[4:5, :]).astype(BF)


FORWARD_IMAGES = 2


def call_attn_forward(seq, x, weights, boxes):
    shard, extra = weights
    rows = x.shape[0]
    images = rows // T
    step = FORWARD_IMAGES if images % FORWARD_IMAGES == 0 else 1
    tall = step * T
    made = [sds((2304, D), BF), sds((D, D), BF), sds((8, D), F32), sds((8, 2304), F32)]
    return pl.pallas_call(
        functools.partial(attn_forward, seq),
        grid=(images // step,),
        in_specs=[rows_of(tall, D), SMEM, whole(extra)] + [ANYWHERE] * 4,
        out_specs=[
            rows_of(tall, D),
            rows_of(tall, 2304),
            pl.BlockSpec((step, HEADS, T), lambda i: (i, 0, 0)),
            rows_of(tall, D),
            rows_of(tall, D),
            rows_of(tall, D),
        ]
        + [pl.BlockSpec(shape.shape, lambda i: (0, 0)) for shape in made],
        out_shape=[
            sds((rows, D), BF),
            sds((rows, 2304), BF),
            sds((images, HEADS, T), F32),
            sds((rows, D), BF),
            sds((rows, D), F32),
            sds((rows, D), BF),
        ]
        + made,
        scratch_shapes=[pltpu.SemaphoreType.DMA((4, 3))],
        compiler_params=params(),
    )(x, shard, extra, *boxes)


def hand_out(index, box, outs, sems):
    copies = [pltpu.make_async_copy(box.at[k], out, sems.at[k]) for k, out in enumerate(outs)]
    for k, copy in enumerate(copies):

        @pl.when(index == k)
        def _(copy=copy):
            copy.start()

    @pl.when(index == len(outs) - 1)
    def _():
        for copy in copies:
            copy.wait()


HALF = FF // 2
ROW_STEPS = 4


def feed(seq, part, tall, shard_ref, extra_ref, a0, a1, a2, a3, second_ref, cot_ref, result_ref, *refs):
    last = part == 1
    if last:
        before_ref, out_ref, gs_ref, *refs = refs
    else:
        out_ref, gs_ref, cot_sum, *refs = refs
    sum_ref, edge_ref, *outs, up_w, down_w, bias, second_all, cot_all, act_all, pre_all, box, sems, box_sems = refs
    step = pl.program_id(0)
    shard = shard_ref[0]

    @pl.when(step == 0)
    def _():
        load_feed(shard, (a0, a1, a2, a3), up_w, down_w, sems)
        for h in range(2):
            patch_row(up_w, 768 * h + 383, spread_row(extra_ref, EXTRA + 12 + 12 * h + 6 * part, 6))
            bias[0:1, 768 * h : 768 * h + 768] = spread_row(extra_ref, EXTRA + 36 + 12 * h + 6 * part, 6)
        if last:
            patch_row(down_w, 767, spread_row(extra_ref, EXTRA + 60, 6))
        sum_ref[...] = jnp.zeros_like(sum_ref)
        edge_ref[...] = jnp.zeros_like(edge_ref)
        if not last:
            cot_sum[...] = jnp.zeros_like(cot_sum)

    @pl.when(step < ROW_STEPS)
    def _():
        at = pl.ds(pl.multiple_of(step * tall, 16), tall)
        second = second_ref[...]
        cot = cot_ref[...]
        second_all[at, :] = second
        cot_all[at, :] = cot
        if last:
            result = result_ref[...]
            grad_second = before_ref[...]
        else:
            result = result_ref[...] + spread_row(extra_ref, EXTRA + 66, 6)
            grad_second = jnp.zeros_like(result)
            cot_sum[0:1, :] += jnp.sum(cot.astype(F32), axis=0, keepdims=True)
        for h in range(2):
            cols = slice(768 * h, 768 * h + 768)
            pre = dot(second, up_w[cols, :]) + bias[0:1, cols]
            grad_act = dot_nt(cot, down_w[cols, :])
            half = 0.5 * (1.0 + lax.erf(pre * root_half))
            act = (pre * half).astype(BF)
            grad_pre = grad_act * (half + pre * jnp.exp(-0.5 * pre * pre) * inv_root_tau)
            low = grad_pre.astype(BF)
            act_all[at, cols] = act
            pre_all[at, cols] = low
            sum_ref[0:1, cols] += jnp.sum(grad_pre, axis=0, keepdims=True)
            result = result + dot(act, down_w[cols, :])
            grad_second = grad_second + dot_nt(low, up_w[cols, :])
        if last:
            for image in range(tall // T):
                out_ref[image] = result[T * image : T * image + seq].astype(BF)
        else:
            out_ref[...] = result
        gs_ref[...] = grad_second

    index = step - ROW_STEPS
    side = jnp.bitwise_xor(shard // 2, 1 - index % 2)
    core = jnp.where(index >= 2, shard % 2, 1 - shard % 2)

    @pl.when((index >= 0) & (side == 0))
    def _():
        left = second_all[:, pl.ds(pl.multiple_of(384 * core, 128), 384)]
        for h in range(2):
            grad = dot_tn(left, pre_all[:, 768 * h : 768 * h + 768])
            box[index, 384 * h : 384 * h + 384, :] = grad.astype(BF)

            @pl.when(core == 0)
            def _(grad=grad, h=h):
                edge_ref[0:1, 768 * h : 768 * h + 768] = grad[383:384]

    @pl.when((index >= 0) & (side == 1))
    def _():
        left = act_all[:, pl.ds(pl.multiple_of(768 * core, 128), 768)]
        grad = dot_tn(left, cot_all[...])
        box[index] = grad.astype(BF)

        @pl.when(core == 0)
        def _():
            edge_ref[1:2, 0:768] = grad[767:768]

    hand_out(index, box, outs, box_sems)


def call_feed(seq, part, shard, extra, boxes, second, cot, result, before=None):
    rows = second.shape[0]
    images = rows // T
    tall = rows // ROW_STEPS
    last = part == 1
    row = lambda i: jnp.minimum(i, ROW_STEPS - 1)
    block = pl.BlockSpec((tall, D), lambda i: (row(i), 0))
    out = pl.BlockSpec((tall // T, seq, D), lambda i: (row(i), 0, 0)) if last else block
    small = lambda width: pl.BlockSpec((8, width), lambda i: (0, 0))
    return pl.pallas_call(
        functools.partial(feed, seq, part, tall),
        grid=(ROW_STEPS + 4,),
        in_specs=[SMEM, whole(extra)] + [ANYWHERE] * 4 + [block] * (4 if last else 3),
        out_specs=[out, block] + ([] if last else [small(D)]) + [small(HALF), small(HALF)] + [ANYWHERE] * 4,
        out_shape=[sds((images, seq, D), BF) if last else sds((rows, D), F32), sds((rows, D), F32)]
        + ([] if last else [sds((8, D), F32)])
        + [sds((8, HALF), F32), sds((8, HALF), F32)] + [sds((D, D), BF)] * 4,
        scratch_shapes=[
            pltpu.VMEM((HALF, D), BF),
            pltpu.VMEM((HALF, D), BF),
            pltpu.VMEM((8, HALF), F32),
            pltpu.VMEM((rows, D), BF),
            pltpu.VMEM((rows, D), BF),
            pltpu.VMEM((rows, HALF), BF),
            pltpu.VMEM((rows, HALF), BF),
            pltpu.VMEM((4, D, D), BF),
            pltpu.SemaphoreType.DMA((4, 2)),
            pltpu.SemaphoreType.DMA((4,)),
        ],
        compiler_params=params(60),
    )(shard, extra, *boxes, second, cot, result, *([before] if last else []))


WIDE = 384


def attn_backward(seq, group, base, count, last, shard_ref, log_ref, qkv_ref, first_ref, att_ref, *refs):
    step = pl.program_id(0)
    shard = shard_ref[0]
    if group == 0:
        gs_ref, hid_ref, cot_ref, vec_ref, proj_w, *refs = refs
    else:
        low_ref, ga_ref, *refs = refs
    if last:
        if group == 0:
            head_before, sum_before, first_any, att_any, low_any, grad_any, _, _, *refs = refs
        else:
            head_before, first_any, att_any, low_any, grad_any, *refs = refs
    grad_ref, head_sum, *refs = refs
    if group == 0:
        low_ref, ga_ref, gh_ref, sum_ref, *refs = refs
    if last:
        edge_ref, *outs, grad_all, first_all, low_all, att_all, box, box_sems, load_sems = refs
        done = pl.ds(0, base * T)
        loads = [
            pltpu.make_async_copy(grad_any.at[done], grad_all.at[done], load_sems.at[0]),
            pltpu.make_async_copy(first_any.at[done], first_all.at[done], load_sems.at[1]),
            pltpu.make_async_copy(low_any.at[done], low_all.at[done], load_sems.at[2]),
            pltpu.make_async_copy(
                att_any.at[done, pl.ds(WIDE * group, WIDE)], att_all.at[done], load_sems.at[3]
            ),
        ]

    @pl.when(step == 0)
    def _():
        if last:
            for load in loads:
                load.start()
            edge_ref[...] = jnp.zeros_like(edge_ref)
            head_sum[...] = head_before[...]
        else:
            head_sum[...] = jnp.zeros_like(head_sum)
        if group == 0:
            sum_ref[...] = sum_before[...] if last else jnp.zeros_like(sum_ref)

    @pl.when(step < count)
    def _():
        at_rows = pl.ds(pl.multiple_of((step + base) * T, 16), T)
        if last:
            first_all[at_rows, :] = first_ref[...]
            att_all[at_rows, :] = att_ref[...]
        if group == 0:
            gs = gs_ref[...]
            normed, spread = normed_of(hid_ref[...])
            gn = gs * vec_ref[3:4, :]
            gh = cot_ref[...].astype(F32) + spread * (
                gn - jnp.mean(gn, axis=-1, keepdims=True) - normed * jnp.mean(gn * normed, axis=-1, keepdims=True)
            )
            sum_ref[0:1, :] += jnp.sum(gs * normed, axis=0, keepdims=True)
            sum_ref[1:2, :] += jnp.sum(gs, axis=0, keepdims=True)
            sum_ref[2:3, :] += jnp.sum(gh, axis=0, keepdims=True)
            gh_ref[...] = gh
            gh_low = gh.astype(BF)
            low_ref[...] = gh_low
            ga_ref[...] = dot_nt(gh_low, proj_w[...]).astype(BF)
        if last:
            low_all[at_rows, :] = low_ref[...]
        low = lax.broadcasted_iota(jnp.int32, (T, LANES), 1) < 64
        real = lax.broadcasted_iota(jnp.int32, (2, T, T), 1) < seq
        eighth = jnp.asarray(0.125, BF)
        masks = half_masks()
        for pair in range(3):
            at = LANES * pair
            full = WIDE * group + at
            head = 6 * group + 2 * pair
            q = qkv_ref[:, full : full + LANES] * eighth
            k = two_heads(qkv_ref[:, 768 + full : 768 + full + LANES], masks)
            v = two_heads(qkv_ref[:, 1536 + full : 1536 + full + LANES], masks)
            grad_out = ga_ref[:, at : at + LANES]
            scores = dot_nt(k, q).reshape(2, T, T)
            logs = jnp.concatenate([log_ref[0:1, head : head + 1, :], log_ref[0:1, head + 1 : head + 2, :]], axis=0)
            probs = jnp.where(real, jnp.exp(scores - logs), 0.0)
            grad_v = dot(probs.astype(BF).reshape(2 * T, T), grad_out)
            grad_probs = dot_nt(v, grad_out).reshape(2, T, T)
            delta = jnp.sum(probs * grad_probs, axis=1, keepdims=True)
            grad_scores = (probs * (grad_probs - delta)).astype(BF).reshape(2 * T, T)
            grad_k = dot(grad_scores, q)
            grads = (
                dot_tn(grad_scores, k * eighth),
                jnp.where(low, grad_k[:T], grad_k[T:]),
                jnp.where(low, grad_v[:T], grad_v[T:]),
            )
            for part, grad in enumerate(grads):
                if part != 1:
                    row = part // 2
                    head_sum[row : row + 1, at : at + LANES] += jnp.sum(grad, axis=0, keepdims=True)
                cols = slice(WIDE * part + at, WIDE * part + at + LANES)
                grad = grad.astype(BF)
                grad_ref[:, cols] = grad
                if last:
                    grad_all[at_rows, cols] = grad

    if not last:
        return

    @pl.when(step == count)
    def _():
        for load in loads:
            load.wait()

    index = step - count
    side = jnp.bitwise_xor(shard // 2, 1 - index % 2)
    core = jnp.where(index >= 2, shard % 2, 1 - shard % 2)
    share = 2 * side + core

    @pl.when((index >= 0) & (share == 3))
    def _():
        box[index] = dot_tn(att_all[...], low_all[...]).astype(BF)

    @pl.when((index >= 0) & (share != 3))
    def _():
        grad = dot_tn(first_all[:, pl.ds(pl.multiple_of(256 * share, 256), 256)], grad_all[...])
        for part in range(3):
            cols = slice(WIDE * part, WIDE * part + WIDE)
            for u in range(2):
                box[index, 128 * part : 128 * part + 128, WIDE * u : WIDE * u + WIDE] = grad[
                    128 * u : 128 * u + 128, cols
                ].astype(BF)

        @pl.when(share == 0)
        def _():
            edge_ref[0:1, :] = grad[255:256]

        @pl.when(share == 2)
        def _():
            edge_ref[1:2, :] = grad[0:1]

    hand_out(index, box, outs, box_sems)


def call_attn_backward(seq, group, base, count, shard, log_total, qkv, first, attended, *more, before=()):
    rows = first.shape[0]
    last = len(before) > 0
    row = lambda i: jnp.minimum(i, count - 1) + base
    block = lambda width, col=0: pl.BlockSpec((T, width), lambda i: (row(i), col))
    small = lambda width: pl.BlockSpec((8, width), lambda i: (0, 0))
    in_specs = [SMEM, pl.BlockSpec((1, HEADS, T), lambda i: (row(i), 0, 0)), block(2304), block(D), block(WIDE, group)]
    out_specs = [block(3 * WIDE), small(WIDE)]
    out_shape = [sds((rows, 3 * WIDE), BF), sds((8, WIDE), F32)]
    if group == 0:
        in_specs += [block(D)] * 3 + [whole(more[3]), whole(more[4])]
        out_specs += [block(D), block(D), block(D), small(D)]
        out_shape += [sds((rows, D), BF), sds((rows, D), BF), sds((rows, D), F32), sds((8, D), F32)]
    else:
        in_specs += [block(D), block(WIDE, 1)]
    aliases, scratch, extra = {}, [], []
    if last:
        at = len(in_specs)
        if group == 0:
            grad, head, low, ga, gh, total = before
            extra = [head, total, first, attended, low, grad, ga, gh]
            in_specs += [whole(head), whole(total)] + [ANYWHERE] * 6
            aliases = {at + 4: 2, at + 5: 0, at + 6: 3, at + 7: 4}
        else:
            grad, head = before
            extra = [head, first, attended, more[0], grad]
            in_specs += [whole(head)] + [ANYWHERE] * 4
            aliases = {at + 4: 0}
        out_specs += [small(3 * WIDE)] + [ANYWHERE] * 4
        out_shape += [sds((8, 3 * WIDE), F32)] + [sds((WIDE, D), BF)] * 4
        scratch = [
            pltpu.VMEM((rows, 3 * WIDE), BF),
            pltpu.VMEM((rows, D), BF),
            pltpu.VMEM((rows, D), BF),
            pltpu.VMEM((rows, WIDE), BF),
            pltpu.VMEM((4, WIDE, D), BF),
            pltpu.SemaphoreType.DMA((4,)),
            pltpu.SemaphoreType.DMA((4,)),
        ]
    return pl.pallas_call(
        functools.partial(attn_backward, seq, group, base, count, last),
        grid=(count + 4 if last else count,),
        in_specs=in_specs,
        out_specs=out_specs,
        out_shape=out_shape,
        input_output_aliases=aliases,
        scratch_shapes=scratch,
        compiler_params=params(),
    )(shard, log_total, qkv, first, attended, *more, *extra)


def input_backward(seq, grad0, grad1, gh_ref, x_ref, vec_ref, qkv_w, out_ref, sum_ref):
    @pl.when(pl.program_id(0) == 0)
    def _():
        sum_ref[...] = jnp.zeros_like(sum_ref)

    grad_first = None
    for part in range(3):
        cols = slice(WIDE * part, WIDE * part + WIDE)
        both = jnp.concatenate([grad0[:, cols], grad1[:, cols]], axis=1)
        term = dot_nt(both, qkv_w[768 * part : 768 * part + 768, :])
        grad_first = term if part == 0 else grad_first + term
    normed, spread = normed_of(x_ref[...].astype(F32))
    gn = grad_first * vec_ref[0:1, :]
    grad = gh_ref[...] + spread * (
        gn - jnp.mean(gn, axis=-1, keepdims=True) - normed * jnp.mean(gn * normed, axis=-1, keepdims=True)
    )
    sum_ref[0:1, :] += jnp.sum(grad_first * normed, axis=0, keepdims=True)
    sum_ref[1:2, :] += jnp.sum(grad_first, axis=0, keepdims=True)
    for image in range(grad.shape[0] // T):
        out_ref[image] = grad[T * image : T * image + seq].astype(BF)


def call_input_backward(seq, grads, gh, x, vec, qkv_w):
    rows = gh.shape[0]
    images = rows // T
    step = 2 if images % 2 == 0 else 1
    tall = step * T
    return pl.pallas_call(
        functools.partial(input_backward, seq),
        grid=(images // step,),
        in_specs=[rows_of(tall, 3 * WIDE)] * 2 + [rows_of(tall, D), rows_of(tall, D), whole(vec), whole(qkv_w)],
        out_specs=[pl.BlockSpec((step, seq, D), lambda i: (i, 0, 0)), pl.BlockSpec((8, D), lambda i: (0, 0))],
        out_shape=[sds((images, seq, D), BF), sds((8, D), F32)],
        compiler_params=params(),
    )(*grads, gh, x, vec, qkv_w)


def putter(out_ref):
    out_ref[...] = jnp.zeros_like(out_ref)

    def put(first, ref, row, col, width):
        for k in range(width // LANES):
            at = col + LANES * k
            out_ref[first + k : first + k + 1, :] = ref[row : row + 1, at : at + LANES]

    return put


def pack(last_sum, back_sum, head0, head1, edge0, edge1, pre0, pre1, up0, up1, cot_sum, out_ref):
    put = putter(out_ref)
    put(0, last_sum, 0, 0, D)
    put(6, last_sum, 1, 0, D)
    for group, (head, edge) in enumerate(((head0, edge0), (head1, edge1))):
        for part in range(3):
            put(12 + 6 * part + 3 * group, edge, 0, WIDE * part, WIDE)
            put(30 + 6 * part + 3 * group, edge, 1, WIDE * part, WIDE)
        put(48 + 3 * group, head, 0, 0, WIDE)
        put(54 + 3 * group, head, 1, 0, WIDE)
    put(60, back_sum, 2, 0, D)
    put(EXTRA, back_sum, 0, 0, D)
    put(EXTRA + 6, back_sum, 1, 0, D)
    for j, (pre, up) in enumerate(((pre0, up0), (pre1, up1))):
        for h in range(2):
            put(EXTRA + 12 + 12 * h + 6 * j, up, 0, 768 * h, D)
            put(EXTRA + 36 + 12 * h + 6 * j, pre, 0, 768 * h, D)
    put(EXTRA + 60, up1, 1, 0, D)
    put(EXTRA + 66, cot_sum, 0, 0, D)


def call_pack(*arrays):
    return pl.pallas_call(
        pack,
        in_specs=[pl.BlockSpec(memory_space=pltpu.VMEM)] * len(arrays),
        out_specs=pl.BlockSpec(memory_space=pltpu.VMEM),
        out_shape=sds((2 * EXTRA, LANES), F32),
        compiler_params=params(),
    )(*arrays)


def adam_kernel(block, share_size, scale, boxes, shard_ref, power_ref, extra_ref, *refs):
    box_refs = refs[:boxes]
    flat_ref, mom_ref, grad_ref, change_ref, new_ref, held = refs[boxes:]
    step = pl.program_id(0)

    @pl.when(step == 0)
    def _():
        for share in range(4):

            @pl.when(shard_ref[0] == share)
            def _(share=share):
                for box, groups, box_row, col, cols, flat_row, stride in block.grad_parts(share):
                    base = MARGIN + block.start[share] + flat_row

                    def body(group, carry, box=box, box_row=box_row, col=col, cols=cols, base=base, stride=stride):
                        row = pl.multiple_of(box_row + 16 * group, 16)
                        for j in range(cols):
                            at = LANES * (col + j)
                            both = box_refs[box][pl.ds(row, 16), at : at + LANES].astype(F32)
                            to = base + 16 * stride * group + j
                            held[pl.ds(to, 8, stride=stride), :] = both[0:8]
                            held[pl.ds(to + 8 * stride, 8, stride=stride), :] = both[8:16]
                        return carry

                    lax.fori_loop(0, groups, body, 0, unroll=8)
                for source, row, length in block.put[share]:
                    held[MARGIN + row : MARGIN + row + length, :] = extra_ref[block.base + source : block.base + source + length, :]

    start = pl.multiple_of(MARGIN + CHUNK * step, 8)
    shard = shard_ref[0]
    low = lax.broadcasted_iota(jnp.int32, (CHUNK, LANES), 1) < 64
    here = held[pl.ds(start, CHUNK), :]
    after = held[pl.ds(start + 1, CHUNK), :]
    shifted = jnp.where(low, pltpu.roll(here, 64, 1), pltpu.roll(after, 64, 1))
    grad = jnp.where(shard % 2 == 1, shifted, here) * scale
    position = (
        shard * share_size
        + step * (CHUNK * LANES)
        + lax.broadcasted_iota(jnp.int32, (CHUNK, LANES), 0) * LANES
        + lax.broadcasted_iota(jnp.int32, (CHUNK, LANES), 1)
    )
    matrix = jnp.zeros((CHUNK, LANES), jnp.bool_)
    for first, end in block.matrices:
        matrix = matrix | ((position >= first) & (position < end))
    size = CHUNK * LANES
    p = flat_ref[...].reshape(CHUNK, LANES)
    m = beta_one * mom_ref[0, :].reshape(CHUNK, LANES) + (1.0 - beta_one) * grad
    s = beta_two * mom_ref[1, :].reshape(CHUNK, LANES) + (1.0 - beta_two) * grad * grad
    ratio = (m * power_ref[0]) / (jnp.sqrt(s * power_ref[1]) + adam_eps)
    change = jnp.where(matrix, rate_matrix, rate_vector) * (ratio + jnp.where(matrix, decay_matrix, 0.0) * p)
    grad_ref[...] = grad.reshape(size)
    change_ref[...] = change.reshape(size)
    new_ref[0, :] = m.reshape(size)
    new_ref[1, :] = s.reshape(size)


def adam(block, shard, powers, extra, boxes, flat, moments, scale):
    count = flat.shape[0]
    steps = -(-count // (CHUNK * LANES))
    line = pl.BlockSpec((CHUNK * LANES,), lambda i: (i,))
    two = pl.BlockSpec((2, CHUNK * LANES), lambda i: (0, i))
    return pl.pallas_call(
        functools.partial(adam_kernel, block, count, scale, len(boxes)),
        grid=(steps,),
        in_specs=[SMEM, SMEM, whole(extra)] + [whole(box) for box in boxes] + [line, two],
        out_specs=[line, line, two],
        out_shape=[sds((count,), F32), sds((count,), F32), sds((2, count), F32)],
        scratch_shapes=[pltpu.VMEM((MARGIN + CHUNK * steps + MARGIN, LANES), F32)],
        compiler_params=params(),
    )(shard, powers, extra, *boxes, flat, moments)


def swap(value, axis, bit):
    pairs = [(i, i ^ bit) for i in range(lax.axis_size(axis))]
    return lax.ppermute(value, axis, pairs)


def turn(value, axis, unit, distance):
    size = lax.axis_size(axis)
    return lax.ppermute(value, axis, [(i, (i + unit * distance) % size) for i in range(size)])


def pick(array, index, axis=0):
    return lax.dynamic_index_in_dim(array, index, axis, keepdims=False)


class Line:
    def __init__(self):
        self.last = None

    def __call__(self, step, *args):
        if self.last is not None:
            flat, tree = jax.tree.flatten(args)
            flat = lax.optimization_barrier((self.last, *flat))[1:]
            args = jax.tree.unflatten(tree, flat)
        out = step(*args)
        self.last = min(jax.tree.leaves(out), key=lambda leaf: leaf.size)
        return out


class Sum:
    def __init__(self, line, across, same, mine_across, mine):
        self.line, self.mine_across, self.mine = line, mine_across, mine
        self.rows = mine.shape[0]
        rep = lax.axis_index("rep")
        self.near, self.far = rep % 2, rep // 2
        self.count = lax.axis_size("rep") // 2
        self.came_across, self.here = swap(across, "shard", 1), swap(same, "shard", 1)

    def side(self):
        add = lambda a, b: (a.astype(F32) + b.astype(F32)).astype(BF)
        send = self.line(add, self.mine_across, self.came_across)
        self.came = swap(send, "shard", 2)
        self.here = self.line(lambda a: a, self.here)

    def close(self):
        def step(mine, here, came):
            total = mine.astype(F32) + here.astype(F32) + came.astype(F32)
            halves = total.reshape(2, self.rows // 2, D)
            return pick(halves, 1 - self.near).astype(BF), pick(halves, self.near)

        send, self.half = self.line(step, self.mine, self.here, self.came)
        self.came = swap(send, "rep", 1)

    def level(self, bit):
        if bit == 2:
            self.part = self.line(lambda a, b: (a + b.astype(F32)).astype(BF), self.half, self.came)
        else:
            self.part = self.line(lambda a, b: (a.astype(F32) + b.astype(F32)).astype(BF), self.part, self.came)
        self.came = swap(self.part, "rep", bit)

    def back_level(self):
        self.half = self.line(lambda a, b: (a.astype(F32) + b.astype(F32)).astype(BF), self.part, self.came)
        self.came = swap(self.half, "rep", 1)

    def along(self):
        def step(half, came):
            parts = (half + came.astype(F32)).reshape(self.count, self.rows // 2 // self.count, D)
            sends = [pick(parts, (self.far + d) % self.count).astype(BF) for d in range(1, self.count)]
            return sends, pick(parts, self.far)

        sends, self.part = self.line(step, self.half, self.came)
        self.came = [turn(send, "rep", 2, d + 1) for d, send in enumerate(sends)]

    def back_along(self):
        def step(part, came):
            for value in came:
                part = part + value.astype(F32)
            return part.astype(BF)

        self.part = self.line(step, self.part, self.came)
        self.came = [turn(self.part, "rep", 2, d) for d in range(1, self.count)]

    def back_close(self):
        def step(part, came):
            full = jnp.zeros((self.count,) + part.shape, BF)
            for d, value in enumerate([part] + came):
                full = lax.dynamic_update_slice_in_dim(full, value[None], (self.far + self.count - d) % self.count, 0)
            return full.reshape(self.rows // 2, D)

        self.half = self.line(step, self.part, self.came)
        self.came = swap(self.half, "rep", 1)

    def end(self):
        def step(half, came):
            first = self.near == 0
            return jnp.concatenate([jnp.where(first, half, came), jnp.where(first, came, half)], axis=0)

        return self.line(step, self.half, self.came)


class SumAll:
    def __init__(self, line, value):
        self.line, self.value = line, value
        self.hops = [("shard", 1)]
        bit = 2
        while bit < lax.axis_size("rep"):
            self.hops.append(("rep", bit))
            bit *= 2
        self.hops += [("shard", 2), ("rep", 1)]
        self.came = swap(value, *self.hops.pop(0))

    def hop(self):
        self.value = self.line(lambda a, b: a + b, self.value, self.came)
        if self.hops:
            self.came = swap(self.value, *self.hops.pop(0))
            return False
        return True


def body(layer_input, out_cotangent, attention_params, attention_moments, feedforward_params, feedforward_moments, step_count):
    images, seq, _ = layer_input.shape
    rows = images * T
    image_total = images * lax.axis_size("shard") * lax.axis_size("rep")
    scale = 1.0 / image_total
    shard = lax.axis_index("shard").astype(jnp.int32).reshape(1)
    time = step_count[0].astype(F32)
    powers = jnp.stack([1.0 / (1.0 - jnp.power(beta_one, time)), 1.0 / (1.0 - jnp.power(beta_two, time))])
    pad = ((0, 0), (0, T - seq), (0, 0))
    padded = lambda tokens: jnp.pad(tokens, pad).reshape(rows, D)
    line = Line()

    attn_box, attn_extra = line(functools.partial(prep, ATTN), attention_params, shard)
    attn_across = swap(attn_box, "shard", 2)
    attn_near = swap(attn_box, "shard", 1)
    box0, box1, feed_extra = line(functools.partial(prep, FEED), feedforward_params, shard)
    extra = line(lambda a, b: jnp.concatenate([a, b], axis=0), attn_extra, feed_extra)
    came = swap(extra, "shard", 1)
    x = line(padded, layer_input)
    extra = line(lambda a, b: a + b, extra, came)
    came = swap(extra, "shard", 2)
    cot = line(padded, out_cotangent)
    extra = line(lambda a, b: a + b, extra, came)
    near0, near1 = swap(box0, "shard", 1), swap(box1, "shard", 1)
    across, send0 = line(lambda a, b: lax.optimization_barrier((a, b)), attn_across, box0)
    attn_both = swap(across, "shard", 1)
    across0 = swap(send0, "shard", 2)
    boxes = (attn_box, attn_near, attn_across, attn_both)
    first, qkv, log_total, attended, hidden, second, qkv_w, proj_w, vec, bias = line(
        lambda x, w, b: call_attn_forward(seq, x, w, b), x, (shard, extra), boxes
    )
    across, send1, near0, near1 = line(lambda *a: lax.optimization_barrier(a), across0, box1, near0, near1)
    both0 = swap(across, "shard", 1)
    across1 = swap(send1, "shard", 2)
    boxes = (box0, near0, across0, both0)
    result, gs, cot_sum, pre0, up0, *grads = line(
        lambda *a: call_feed(seq, 0, *a), shard, extra, boxes, second, cot, hidden
    )
    both1 = swap(line(lambda a: a, across1), "shard", 1)
    feed0 = Sum(line, *grads)
    feed0.side()
    boxes = (box1, near1, across1, both1)
    layer_output, gs, pre1, up1, *grads = line(
        lambda *a: call_feed(seq, 1, *a), shard, extra, boxes, second, cot, result, gs
    )
    feed1 = Sum(line, *grads)
    feed0.close()
    feed1.side()
    half = images // 2
    common = (shard, log_total, qkv, first, attended)
    more = (gs, hidden, cot, vec, proj_w)
    before = line(lambda *a: call_attn_backward(seq, 0, 0, half, *a), *common, *more)
    feed0.along()
    grad0, head0, gh_low, ga, gh, back_sum, edge0, *grads = line(
        lambda b, *a: call_attn_backward(seq, 0, half, images - half, *a, before=b), tuple(before), *common, *more
    )
    attn0 = Sum(line, *grads)
    feed1.close()
    feed0.back_along()
    attn0.side()
    more = (gh_low, ga)
    before = line(lambda *a: call_attn_backward(seq, 1, 0, half, *a), *common, *more)
    feed0.back_close()
    feed1.along()
    grad1, head1, edge1, *grads = line(
        lambda b, *a: call_attn_backward(seq, 1, half, images - half, *a, before=b), tuple(before), *common, *more
    )
    attn1 = Sum(line, *grads)
    feed1.back_along()
    attn0.close()
    feed_box0 = feed0.end()
    attn1.side()
    input_grad, last_sum = line(lambda *a: call_input_backward(seq, *a), (grad0, grad1), gh, x, vec, qkv_w)
    sums = line(call_pack, last_sum, back_sum, head0, head1, edge0, edge1, pre0, pre1, up0, up1, cot_sum)
    bits = [2 << k for k in range((lax.axis_size("rep") // 2).bit_length() - 1)]
    sums = SumAll(line, sums)
    attn1.close()
    sums.hop()
    attn0.level(2)
    feed1.back_close()
    sums.hop()
    attn1.level(2)
    sums.hop()
    for bit in bits[1:]:
        attn0.level(bit)
    sums.hop()
    feed_box1 = feed1.end()
    for bit in bits[1:]:
        attn1.level(bit)
    while not sums.hop():
        pass
    feed_grad, feed_change, feed_new = line(
        lambda *a: adam(FEED, *a, scale), shard, powers, sums.value, [feed_box0, feed_box1], feedforward_params, feedforward_moments
    )
    attn0.back_level()
    attn1.back_level()
    layer_output, input_grad = line(lambda *a: a, layer_output, input_grad)
    attn_box0 = attn0.end()
    attn_grad, attn_change, attn_new = line(
        lambda *a: adam(ATTN, *a, scale), shard, powers, sums.value, [attn_box0, attn1.end()], attention_params, attention_moments
    )
    return (layer_output, input_grad, attn_grad, feed_grad, attn_change, attn_new, feed_change, feed_new)


def solution(mesh):
    tokens = P(("shard", "rep"), None, None)
    in_specs = (tokens, tokens, P("shard"), P(None, "shard"), P("shard"), P(None, "shard"), P())
    out_specs = (tokens, tokens, P("shard"), P("shard"), P("shard"), P(None, "shard"), P("shard"), P(None, "shard"))
    return jax.shard_map(body, mesh=mesh, in_specs=in_specs, out_specs=out_specs, check_vma=False)
```
